32 devices in a mesh: dp: 8 (over z, x), tensor: 4 (over y, core).
Axes of the slice: x: 2, y: 2, z: 4, core: 2. Of those that a mesh axis runs over, the one named last changes fastest.
Arguments:
- residual_in: float32 [4096, 2048], P('dp', 'tensor'), may hold values from -6 to 6
- lengths: int32 [8, 4], P('dp'), may hold values from 1 to 384, 512 in all within a row
- head_bucket: int32 [8, 4], P('dp'), may hold values from 0 to 3, as said below
- width_bucket: int32 [8, 4], P('dp'), may hold values from 0 to 3, as said below
- norm1_gain: float32 [2048], replicated, may hold values from 0.25 to 1.75
- norm1_shift: float32 [2048], replicated, may hold values from -3 to 3
- w_qkv: bfloat16 [2048, 3, 2048], P('dp', None, 'tensor'), may hold values from -0.125 to 0.125
- w_out: bfloat16 [2048, 2048], P('tensor', 'dp'), may hold values from -1 to 1
- norm2_gain: float32 [2048], replicated, may hold values from 0.25 to 1.75
- norm2_shift: float32 [2048], replicated, may hold values from -3 to 3
- w_up: bfloat16 [2048, 8192], P('dp', 'tensor'), may hold values from -0.125 to 0.125
- w_down: bfloat16 [8192, 2048], P('tensor', 'dp'), may hold values from -0.0625 to 0.0625
- cotangent: float32 [4096, 2048], P('dp', 'tensor'), may hold values from -6 to 6
Outputs:
- output: float32 [4096, 2048], P('dp', 'tensor')
- grad_input: float32 [4096, 2048], P('dp', 'tensor')
- grad_norm1_gain: float32 [2048], replicated
- grad_norm1_shift: float32 [2048], replicated
- grad_w_qkv: float32 [2048, 3, 2048], P('dp', None, 'tensor')
- grad_w_out: float32 [2048, 2048], P('tensor', 'dp')
- grad_norm2_gain: float32 [2048], replicated
- grad_norm2_shift: float32 [2048], replicated
- grad_w_up: float32 [2048, 8192], P('dp', 'tensor')
- grad_w_down: float32 [8192, 2048], P('tensor', 'dp')
- bucket_counts: int32 [4], replicated
The draws below stay inside these ranges and needn't reach their ends.
Inputs may be any that keep to these rules, and one draw needn't show every extreme that they name: `lengths`: each row sums to 512; its largest entry is 384. `head_bucket`: every row of 4 sequences holds at least one bucket 4 - 1. `width_bucket`: every row of 4 sequences holds at least one bucket 4 - 1.
All inputs are finite; a program needn't handle non-finite values.
Results may differ from the reference program's by a relative error of at most 0.033.
Values may be sent and summed in bfloat16 or wider, within the bound.
A program may use at most 192 MiB of HBM per device.

```python
import math
import jax
import jax.numpy as jnp
import numpy as np
from jax import lax

D = 2048
H = 16
HD = 128
FF = 8192
TOK_DEV = 512
SEQ_DEV = 4
MOST_LEN = 384
TOKENS = 4096
N_DP = 8
N_TENSOR = 4


def bucket_rows(key):
    draw_key, pick_key = jax.random.split(key)
    buckets = jax.random.randint(draw_key, (N_DP, SEQ_DEV), 0, N_TENSOR)
    chosen = jax.random.randint(pick_key, (N_DP, 1), 0, SEQ_DEV)
    column = jnp.arange(SEQ_DEV)[None, :]
    return jnp.where(column == chosen, N_TENSOR - 1, buckets).astype(jnp.int32)


def draw_head_bucket(key, part):
    key = jax.random.fold_in(key, 11)
    return bucket_rows(key)


def draw_width_bucket(key, part):
    key = jax.random.fold_in(key, 23)
    return bucket_rows(key)


def levels(rng, dims, cuts, least, high):
    level = 1.0
    for axis_at, blocks in cuts:
        draws = jax.random.uniform(jax.random.fold_in(jax.random.fold_in(rng, 6), axis_at), (blocks,), jnp.float32, least / len(cuts), high / len(cuts))
        level = level * jnp.repeat(jnp.exp(draws), dims[axis_at] // blocks).reshape((-1,) + (1,) * (len(dims) - 1 - axis_at))
    return level


def length_profile(count, total, bound, slope):
    weights = [(1 << 20) // math.isqrt(rank ** slope) + 1 for rank in range(2, count + 1)]
    surplus, given = total - bound - (count - 1), [1] * (count - 1)
    while surplus > 0:
        candidates = [i for i in range(count - 1) if given[i] < bound]
        pool, remaining = sum([weights[i] for i in candidates]), surplus
        for i in candidates:
            extra = min(bound - given[i], max(1, remaining * weights[i] // pool), surplus)
            given[i] = given[i] + extra
            surplus = surplus - extra
    return np.array([bound] + given)


def ragged_sizes(key, amount, total, most, slope):
    if amount == 2:
        one = jax.random.randint(key, (), max(1, total - most), min(most, total - 1) + 1)
        return jnp.stack([one, total - one])
    tallies = jnp.asarray(length_profile(amount, total, most, slope), jnp.int32)
    couples = (amount - 1) // 2
    donor, taker = tallies[1:1 + 2 * couples:2], tallies[2:2 + 2 * couples:2]
    margin = jnp.minimum(donor - 1, most - taker)
    shifted = jax.random.randint(jax.random.fold_in(key, 1), (couples,), 0, 1 << 20) % (margin + 1)
    tallies = tallies.at[1:1 + 2 * couples:2].set(donor - shifted).at[2:2 + 2 * couples:2].set(taker + shifted)
    return tallies[jax.random.permutation(jax.random.fold_in(key, 2), amount)]


def gaussian(rng, extent, width, bound, cuts=(), kind=jnp.bfloat16):
    level = levels(rng, extent, cuts, -0.22, 0.18) if cuts else 1.0
    drawn = jax.random.normal(rng, extent, jnp.float32) * width * level
    return jnp.minimum(jnp.maximum(drawn, -bound), bound).astype(kind)


def setup_inputs(seed: int = 0) -> dict:
    key_list = jax.random.split(jax.random.key(seed), 14)
    return {
        "residual_in": gaussian(key_list[0], (TOKENS, D), 1.0, 6.0, ((0, 8), (1, 4)), jnp.float32),
        "lengths": jax.vmap(lambda own: ragged_sizes(own, SEQ_DEV, TOK_DEV, MOST_LEN, 2))(jax.random.split(key_list[1], N_DP)).reshape((N_DP, SEQ_DEV)).astype(jnp.int32),
        "head_bucket": draw_head_bucket(jax.random.fold_in(key_list[13], 71), 0),
        "width_bucket": draw_width_bucket(jax.random.fold_in(key_list[13], 71), 0),
        "norm1_gain": jnp.clip(1.0 + 0.15 * jax.random.normal(key_list[4], (D,), jnp.float32), 0.25, 1.75),
        "norm1_shift": gaussian(key_list[5], (D,), 0.5, 3.0, (), jnp.float32),
        "w_qkv": gaussian(key_list[6], (D, 3, D), D ** -0.5, 0.125, ((0, 8), (2, 4))),
        "w_out": gaussian(key_list[7], (D, D), (D // 64) ** -0.5, 1.0, ((0, 4), (1, 8))),
        "norm2_gain": jnp.clip(1.0 + 0.15 * jax.random.normal(key_list[8], (D,), jnp.float32), 0.25, 1.75),
        "norm2_shift": gaussian(key_list[9], (D,), 0.5, 3.0, (), jnp.float32),
        "w_up": gaussian(key_list[10], (D, FF), D ** -0.5, 0.125, ((0, 8), (1, 4))),
        "w_down": gaussian(key_list[11], (FF, D), FF ** -0.5, 0.0625, ((0, 4), (1, 8))),
        "cotangent": gaussian(key_list[12], (TOKENS, D), 1.0, 6.0, ((0, 8), (1, 4)), jnp.float32),
    }


@jax.custom_vjp
def low(v):
    return lax.optimization_barrier(v.astype(jnp.bfloat16)).astype(jnp.float32)

@jax.custom_vjp
def low_back(v):
    return v

def low_keep(v):
    return (low(v), None)

def low_pass(kept, grad):
    return (grad,)

def back_keep(v):
    return (v, None)

def back_low(kept, grad):
    return (low(grad),)
low.defvjp(low_keep, low_pass)
low_back.defvjp(back_keep, back_low)
epsilon = 1e-05
highest = lax.Precision.HIGHEST

def token_info(length_row, head_row, width_row, row_count):
    seq_ends = jnp.cumsum(length_row).astype(jnp.int32)
    seq_starts = (seq_ends - length_row).astype(jnp.int32)
    places = jnp.arange(row_count, dtype=jnp.int32)
    segment = lax.optimization_barrier(jnp.sum((places[:, None] >= seq_ends[None, :]).astype(jnp.int32), axis=1)).astype(jnp.int32)
    labels = jnp.arange(length_row.shape[0], dtype=jnp.int32)
    onehot = (segment[:, None] == labels[None, :]).astype(jnp.int32)
    offset = (places - lax.optimization_barrier(jnp.sum(onehot * seq_starts[None, :], axis=1))).astype(jnp.int32)
    head_tok = lax.optimization_barrier(jnp.sum(onehot * head_row[None, :], axis=1)).astype(jnp.int32)
    width_tok = lax.optimization_barrier(jnp.sum(onehot * width_row[None, :], axis=1)).astype(jnp.int32)
    return (segment, offset, head_tok, width_tok)

def rotary_tables(offset, head_size):
    half_size = head_size // 2
    ladder = jnp.arange(half_size, dtype=jnp.float32)
    inverse = jnp.exp(ladder * (-2.0 * math.log(10000.0) / head_size))
    angles = offset.astype(jnp.float32)[:, None] * inverse[None, :]
    return (jnp.cos(angles)[:, None, :], jnp.sin(angles)[:, None, :])

def rotate(values, cosine, sine_part):
    half_size = values.shape[-1] // 2
    front_half = values[..., :half_size]
    back_half = values[..., half_size:]
    return jnp.concatenate([front_half * cosine - back_half * sine_part, back_half * cosine + front_half * sine_part], axis=-1)

def layer_norm(values, norm_gain, norm_shift):
    center = values - lax.optimization_barrier(jnp.mean(values, axis=-1, keepdims=True))
    spread = lax.optimization_barrier(jnp.mean(center * center, axis=-1, keepdims=True))
    return center * lax.rsqrt(spread + epsilon) * norm_gain + norm_shift

def group_product(left, right):
    row_count = left.shape[0]
    inner = left.shape[1] // N_TENSOR
    left_groups = left.reshape(row_count, N_TENSOR, inner)
    right_groups = right.reshape(N_TENSOR, inner, right.shape[1])
    partials = jnp.einsum('rgk,gkd->grd', left_groups, right_groups, precision=highest)
    return lax.optimization_barrier(jnp.sum(low(partials), axis=0))

def shard_forward(inputs, weight_list, info):
    norm1_gain, norm1_shift, w_qkv, w_out, norm2_gain, norm2_shift, w_up, w_down = weight_list
    segment, offset, head_tok, width_tok = info
    row_count = inputs.shape[0]
    places = jnp.arange(row_count, dtype=jnp.int32)
    normed = low(layer_norm(inputs, norm1_gain, norm1_shift))
    projected = low_back(jnp.dot(normed, w_qkv.reshape(D, 3 * D), precision=highest)).reshape(row_count, 3, H, HD)
    cosine, sine_part = rotary_tables(offset, HD)
    query_rows = low(rotate(projected[:, 0], cosine, sine_part))
    key_rows = low(rotate(projected[:, 1], cosine, sine_part))
    value_rows = low(projected[:, 2])
    raw_scores = low_back(jnp.einsum('qhd,khd->hqk', query_rows, key_rows, precision=highest))
    allowed = (segment[:, None] == segment[None, :]) & (places[:, None] >= places[None, :])
    scores = jnp.where(allowed[None], raw_scores * HD ** (-0.5), -1000000000.0)
    row_max = lax.optimization_barrier(jnp.max(scores, axis=-1, keepdims=True))
    exp_scores = jnp.exp(scores - row_max)
    weights = exp_scores / lax.optimization_barrier(jnp.sum(exp_scores, axis=-1, keepdims=True))
    mixed = jnp.einsum('hqk,khd->qhd', low(weights), value_rows, precision=highest)
    head_owner = jnp.arange(H, dtype=jnp.int32) // (H // N_TENSOR)
    head_mask = (head_tok[:, None] >= head_owner[None, :]).astype(jnp.float32)
    mixed = low(low_back(mixed * head_mask[:, :, None]))
    middle = inputs + low_back(group_product(mixed.reshape(row_count, D), w_out))
    normed2 = low(layer_norm(middle, norm2_gain, norm2_shift))
    upper = low_back(jnp.dot(normed2, w_up, precision=highest))
    column_owner = jnp.arange(FF, dtype=jnp.int32) // (FF // N_TENSOR)
    width_mask = (width_tok[:, None] >= column_owner[None, :]).astype(jnp.float32)
    active = low(jnp.square(jnp.maximum(upper, 0.0)) * width_mask)
    return middle + low_back(group_product(active, w_down))

def reference(residual_in, lengths, head_bucket, width_bucket, norm1_gain, norm1_shift, w_qkv, w_out, norm2_gain, norm2_shift, w_up, w_down, cotangent):
    token_infos = jax.vmap(lambda length_row, head_row, width_row: token_info(length_row, head_row, width_row, TOK_DEV))(lengths, head_bucket, width_bucket)
    shard_step = jax.checkpoint(shard_forward)

    def forward(inputs, gain_one, shift_one, qkv_weight, out_weight, gain_two, shift_two, up_weight, down_weight):
        weight_list = (gain_one, shift_one, qkv_weight, out_weight, gain_two, shift_two, up_weight, down_weight)
        row_blocks = inputs.reshape(N_DP, TOK_DEV, D)
        results = lax.map(lambda block_pair: shard_step(block_pair[0], weight_list, block_pair[1]), (row_blocks, token_infos))
        return results.reshape(N_DP * TOK_DEV, D)
    output, pull_back = jax.vjp(forward, residual_in.astype(jnp.float32), norm1_gain.astype(jnp.float32), norm1_shift.astype(jnp.float32), w_qkv.astype(jnp.float32), w_out.astype(jnp.float32), norm2_gain.astype(jnp.float32), norm2_shift.astype(jnp.float32), w_up.astype(jnp.float32), w_down.astype(jnp.float32))
    gradients = pull_back(cotangent.astype(jnp.float32))
    matches = (width_bucket[:, :, None] == jnp.arange(N_TENSOR, dtype=jnp.int32)[None, None, :]).astype(jnp.int32)
    counts = lax.optimization_barrier(jnp.sum(lengths[:, :, None] * matches, axis=(0, 1))).astype(jnp.int32)
    return (output, gradients[0], gradients[1], gradients[2], gradients[3], gradients[4], gradients[5], gradients[6], gradients[7], gradients[8], counts)
```

```python
import functools
import math

import jax
import jax.numpy as jnp
from jax import lax
from jax.experimental import pallas as pl
from jax.experimental.pallas import tpu as pltpu
from jax.sharding import PartitionSpec as P

HD = 128
HIDDEN_BIT = 2

epsilon = 1e-05


def dp_swap(value, bit):
    count = lax.axis_size("dp")
    return lax.ppermute(value, "dp", [(i, i ^ bit) for i in range(count)])


def tensor_swap(value, bit):
    count = lax.axis_size("tensor")
    return lax.ppermute(value, "tensor", [(i, i ^ bit) for i in range(count)])


def bits_of(count):
    return [1 << i for i in range(count.bit_length() - 1)]


def replica_bits():
    bits = bits_of(lax.axis_size("dp"))
    return [b for b in bits if b > HIDDEN_BIT] + [b for b in bits if b < HIDDEN_BIT]


def gather_weight(mine, other):
    blocks = {0: mine, HIDDEN_BIT: dp_swap(other, HIDDEN_BIT)}
    for bit in replica_bits():
        blocks.update({m | bit: dp_swap(blocks[m], bit) for m in list(blocks)})
    return blocks


def add_low(left, right):
    return (left.astype(jnp.float32) + right.astype(jnp.float32)).astype(jnp.bfloat16)


def scatter_weight(blocks):
    for bit in reversed(replica_bits()):
        arrived = {m ^ bit: dp_swap(blocks[m], bit) for m in blocks if m & bit}
        blocks = {m: add_low(blocks[m], arrived[m]) for m in arrived}
    return blocks[0], dp_swap(blocks[HIDDEN_BIT], HIDDEN_BIT)


def gather_act(rows):
    blocks = {(0, 0): rows, (1, 0): dp_swap(rows, HIDDEN_BIT)}
    for bit in reversed(bits_of(lax.axis_size("tensor"))):
        blocks.update({(b, m | bit): tensor_swap(v, bit) for (b, m), v in list(blocks.items())})
    return blocks


def scatter_act(blocks):
    for bit in bits_of(lax.axis_size("tensor")):
        arrived = {(b, m ^ bit): tensor_swap(v, bit) for (b, m), v in blocks.items() if m & bit}
        blocks = {k: add_low(blocks[k], arrived[k]) for k in arrived}
    return blocks[(0, 0)].astype(jnp.float32) + dp_swap(blocks[(1, 0)], HIDDEN_BIT).astype(
        jnp.float32
    )


def lay(blocks, shape, spots):
    count = len(blocks)

    def kernel(*refs):
        ins, out, sems = refs[:count], refs[count], refs[count + 1]
        copies = []
        for i, spot in enumerate(spots()):
            r, c = blocks[i].shape
            copies.append(
                pltpu.make_async_copy(
                    ins[i],
                    out.at[pl.ds(pl.multiple_of(spot[0], 16), r), pl.ds(pl.multiple_of(spot[1], 128), c)],
                    sems.at[i],
                )
            )
        for copy in copies:
            copy.start()
        for copy in copies:
            copy.wait()

    return pl.pallas_call(
        kernel,
        out_shape=jax.ShapeDtypeStruct(shape, jnp.bfloat16),
        in_specs=[pl.BlockSpec(memory_space=pl.ANY)] * count,
        out_specs=pl.BlockSpec(memory_space=pltpu.VMEM),
        scratch_shapes=[pltpu.SemaphoreType.DMA((count,))],
        compiler_params=pltpu.CompilerParams(vmem_limit_bytes=24 << 20),
    )(*blocks)


def cut(whole, block_shape, count, spots):
    def kernel(*refs):
        src, outs, sems = refs[0], refs[1 : 1 + count], refs[1 + count]
        r, c = block_shape
        copies = []
        for i, spot in enumerate(spots()):
            copies.append(
                pltpu.make_async_copy(
                    src.at[pl.ds(pl.multiple_of(spot[0], 16), r), pl.ds(pl.multiple_of(spot[1], 128), c)],
                    outs[i],
                    sems.at[i],
                )
            )
        for copy in copies:
            copy.start()
        for copy in copies:
            copy.wait()

    return pl.pallas_call(
        kernel,
        out_shape=[jax.ShapeDtypeStruct(block_shape, jnp.bfloat16)] * count,
        in_specs=[pl.BlockSpec(memory_space=pltpu.VMEM)],
        out_specs=[pl.BlockSpec(memory_space=pl.ANY)] * count,
        scratch_shapes=[pltpu.SemaphoreType.DMA((count,))],
        compiler_params=pltpu.CompilerParams(vmem_limit_bytes=24 << 20),
    )(whole)


def lay_weight(blocks, axis):
    count = len(blocks)
    r, c = blocks[0].shape
    if axis == 1 and c % 128:
        order = jnp.bitwise_xor(lax.axis_index("dp"), jnp.arange(count))
        stacked = jnp.stack([blocks[m] for m in range(count)])[order]
        return jnp.swapaxes(stacked, 0, 1).reshape(r, count * c)

    def spots():
        place = lax.axis_index("dp")
        at = [jnp.bitwise_xor(place, m) for m in range(count)]
        return [(d * r, 0) if axis == 0 else (0, d * c) for d in at]

    shape = (r * count, c) if axis == 0 else (r, c * count)
    return lay([blocks[m] for m in range(count)], shape, spots)


def cut_weight(whole, axis):
    count = lax.axis_size("dp")
    r, c = whole.shape
    r, c = (r // count, c) if axis == 0 else (r, c // count)
    if axis == 1 and c % 128:
        order = jnp.bitwise_xor(lax.axis_index("dp"), jnp.arange(count))
        stacked = jnp.swapaxes(whole.reshape(r, count, c), 0, 1)[order]
        return {m: stacked[m] for m in range(count)}

    def spots():
        place = lax.axis_index("dp")
        at = [jnp.bitwise_xor(place, m) for m in range(count)]
        return [(d * r, 0) if axis == 0 else (0, d * c) for d in at]

    return dict(enumerate(cut(whole, (r, c), count, spots)))


def act_keys():
    return [(b, m) for b in range(2) for m in range(lax.axis_size("tensor"))]


def act_spots(r, c):
    place = lax.axis_index("tensor")
    return [(b * r, jnp.bitwise_xor(place, m) * c) for b, m in act_keys()]


def lay_act(blocks):
    r, c = blocks[(0, 0)].shape
    shape = (2 * r, c * lax.axis_size("tensor"))
    return lay([blocks[k] for k in act_keys()], shape, lambda: act_spots(r, c))


def cut_act(whole):
    r, c = whole.shape[0] // 2, whole.shape[1] // lax.axis_size("tensor")
    keys = act_keys()
    return dict(zip(keys, cut(whole, (r, c), len(keys), lambda: act_spots(r, c))))


def whole_stream(rows):
    return lay_act(gather_act(rows.astype(jnp.bfloat16)))


def stream_sum(rows):
    return scatter_act(cut_act(rows.astype(jnp.bfloat16)))


def sum_all(value, axes):
    if "dp" in axes:
        for bit in bits_of(lax.axis_size("dp")):
            value = value + dp_swap(value, bit)
    if "tensor" in axes:
        for bit in bits_of(lax.axis_size("tensor")):
            value = value + tensor_swap(value, bit)
    return value


def token_info(length_row, head_row, width_row, row_count):
    seq_ends = jnp.cumsum(length_row)
    seq_starts = seq_ends - length_row
    places = jnp.arange(row_count, dtype=jnp.int32)
    segment = jnp.sum((places[:, None] >= seq_ends[None, :]).astype(jnp.int32), axis=1)
    labels = jnp.arange(length_row.shape[0], dtype=jnp.int32)
    onehot = (segment[:, None] == labels[None, :]).astype(jnp.int32)
    offset = places - jnp.sum(onehot * seq_starts[None, :], axis=1)
    head_tok = jnp.sum(onehot * head_row[None, :], axis=1)
    width_tok = jnp.sum(onehot * width_row[None, :], axis=1)
    return (segment, offset, head_tok, width_tok)


def rotary_tables(offset, head_size):
    half_size = head_size // 2
    ladder = jnp.arange(half_size, dtype=jnp.float32)
    inverse = jnp.exp(ladder * (-2.0 * math.log(10000.0) / head_size))
    angles = offset.astype(jnp.float32)[:, None] * inverse[None, :]
    return (jnp.cos(angles)[:, None, :], jnp.sin(angles)[:, None, :])


def rotate(values, cosine, sine_part):
    half_size = values.shape[-1] // 2
    front_half = values[..., :half_size]
    back_half = values[..., half_size:]
    return jnp.concatenate(
        [front_half * cosine - back_half * sine_part, back_half * cosine + front_half * sine_part],
        axis=-1,
    )


def norm_forward(values, norm_gain, norm_shift):
    values = values.astype(jnp.float32)
    center = values - jnp.mean(values, axis=-1, keepdims=True)
    spread = jnp.mean(center * center, axis=-1, keepdims=True)
    inverse = lax.rsqrt(spread + epsilon)
    unit_rows = center * inverse
    return (unit_rows * norm_gain + norm_shift, unit_rows, inverse)


def norm_backward(grad_rows, unit_rows, inverse, norm_gain):
    scaled = grad_rows * norm_gain
    grad_in = inverse * (
        scaled
        - jnp.mean(scaled, axis=-1, keepdims=True)
        - unit_rows * jnp.mean(scaled * unit_rows, axis=-1, keepdims=True)
    )
    return (grad_in, jnp.sum(grad_rows * unit_rows, axis=0), jnp.sum(grad_rows, axis=0))


def heads_of(rows, blocks):
    rows = rows.reshape(blocks, rows.shape[0] // blocks, -1, HD)
    return jnp.transpose(rows, (2, 0, 1, 3)).reshape(-1, rows.shape[1], HD)


def rows_of(heads, blocks):
    heads = heads.reshape(-1, blocks, heads.shape[1], HD)
    return jnp.transpose(heads, (1, 2, 0, 3)).reshape(blocks * heads.shape[2], -1)


def local(
    residual_in,
    lengths,
    head_bucket,
    width_bucket,
    norm1_gain,
    norm1_shift,
    w_qkv,
    w_out,
    norm2_gain,
    norm2_shift,
    w_up,
    w_down,
    cotangent,
):
    f32, bf16 = jnp.float32, jnp.bfloat16
    dot = functools.partial(jnp.dot, preferred_element_type=f32)
    tensor_index = lax.axis_index("tensor")
    bucket_total = lax.axis_size("tensor")
    tokens = residual_in.shape[0]
    side = (lax.axis_index("dp") // HIDDEN_BIT) % 2

    def halves(weight, axis):
        left, right = jnp.split(weight, 2, axis=axis)
        return jnp.where(side == 0, left, right), jnp.where(side == 0, right, left)

    info = jnp.stack([lengths[0], head_bucket[0], width_bucket[0]])
    far_info = dp_swap(info, HIDDEN_BIT)
    pair = [token_info(i[0], i[1], i[2], tokens) for i in (info, far_info)]
    segment, offset, head_tok, width_tok = [jnp.stack([a, b]) for a, b in zip(*pair)]
    matches = (
        width_bucket[0][:, None] == jnp.arange(bucket_total, dtype=jnp.int32)[None, :]
    ).astype(jnp.int32)
    bucket_counts = sum_all(jnp.sum(lengths[0][:, None] * matches, axis=0), ("dp",))
    head_mask = (head_tok.reshape(-1) >= tensor_index).astype(f32)[:, None]
    width_mask = (width_tok.reshape(-1) >= tensor_index).astype(f32)[:, None]
    places = jnp.arange(tokens, dtype=jnp.int32)
    allowed = (segment[:, :, None] == segment[:, None, :]) & (
        places[:, None] >= places[None, :]
    )
    cosine, sine_part = rotary_tables(offset.reshape(-1), HD)
    score_scale = HD ** (-0.5)

    qkv_halves = [h.reshape(h.shape[0], -1) for h in halves(w_qkv, 2)]
    full_qkv = lay_weight(gather_weight(*qkv_halves), 0)
    full_out = lay_weight(gather_weight(*halves(w_out, 0)), 1)
    full_up = lay_weight(gather_weight(*halves(w_up, 1)), 0)
    full_down = lay_weight(gather_weight(*halves(w_down, 0)), 1)

    inputs = whole_stream(residual_in)
    normed1, unit1, inverse1 = norm_forward(inputs, norm1_gain, norm1_shift)
    normed1 = normed1.astype(bf16)
    projected = dot(normed1, full_qkv).reshape(2 * tokens, 3, -1, HD)
    width = projected.shape[2] * HD
    query = rotate(projected[:, 0], cosine, sine_part).astype(bf16).reshape(-1, width)
    key = rotate(projected[:, 1], cosine, sine_part).astype(bf16).reshape(-1, width)
    value = projected[:, 2].astype(bf16).reshape(-1, width)
    query, key, value = heads_of(query, 2), heads_of(key, 2), heads_of(value, 2)
    allowed = jnp.tile(allowed, (query.shape[0] // 2, 1, 1))
    scores = jnp.einsum("nqd,nkd->nqk", query, key, preferred_element_type=f32) * score_scale
    scores = jnp.where(allowed, scores, -1000000000.0)
    scores = jnp.exp(scores - jnp.max(scores, axis=-1, keepdims=True))
    weights = (scores / jnp.sum(scores, axis=-1, keepdims=True)).astype(bf16)
    mixed = jnp.einsum("nqk,nkd->nqd", weights, value, preferred_element_type=f32)
    mixed = (rows_of(mixed, 2) * head_mask).astype(bf16)
    middle = residual_in + stream_sum(dot(mixed, full_out))
    middle_rows = whole_stream(middle)
    normed2, unit2, inverse2 = norm_forward(middle_rows, norm2_gain, norm2_shift)
    normed2 = normed2.astype(bf16)
    upper = jnp.maximum(dot(normed2, full_up), 0.0) * width_mask
    active = jnp.square(upper).astype(bf16)
    upper = upper.astype(bf16)
    output = middle + stream_sum(dot(active, full_down))

    grad_top = whole_stream(cotangent)
    grad_down = scatter_weight(cut_weight(dot(active.T, grad_top).astype(bf16), 1))
    grad_active = dot(grad_top, full_down.T)
    grad_upper = (grad_active * 2.0 * upper.astype(f32)).astype(bf16)
    grad_normed2 = dot(grad_upper, full_up.T)
    part_middle, gain2_grad, shift2_grad = norm_backward(
        grad_normed2, unit2, inverse2, norm2_gain
    )
    grad_middle = cotangent + stream_sum(part_middle)
    grad_up = scatter_weight(cut_weight(dot(normed2.T, grad_upper).astype(bf16), 0))
    grad_branch = whole_stream(grad_middle)
    grad_wout = scatter_weight(cut_weight(dot(mixed.T, grad_branch).astype(bf16), 1))
    grad_mixed = (dot(grad_branch, full_out.T) * head_mask).astype(bf16)
    grad_mixed = heads_of(grad_mixed, 2)
    grad_weights = jnp.einsum("nqd,nkd->nqk", grad_mixed, value, preferred_element_type=f32)
    grad_value = jnp.einsum("nqk,nqd->nkd", weights, grad_mixed, preferred_element_type=f32)
    wide = weights.astype(f32)
    grad_scores = wide * (grad_weights - jnp.sum(grad_weights * wide, axis=-1, keepdims=True))
    grad_raw = (grad_scores * score_scale).astype(bf16)
    grad_query = jnp.einsum("nqk,nkd->nqd", grad_raw, key, preferred_element_type=f32)
    grad_key = jnp.einsum("nqk,nqd->nkd", grad_raw, query, preferred_element_type=f32)
    grad_query, grad_key = [
        rotate(rows_of(g, 2).reshape(2 * tokens, -1, HD), cosine, -sine_part).reshape(-1, width)
        for g in (grad_query, grad_key)
    ]
    grad_projected = jnp.concatenate([grad_query, grad_key, rows_of(grad_value, 2)], axis=1)
    grad_projected = grad_projected.astype(bf16)
    grad_normed1 = dot(grad_projected, full_qkv.T)
    part_input, gain1_grad, shift1_grad = norm_backward(
        grad_normed1, unit1, inverse1, norm1_gain
    )
    grad_input = grad_middle + stream_sum(part_input)
    grad_qkv = scatter_weight(cut_weight(dot(normed1.T, grad_projected).astype(bf16), 0))

    def join(pair, axis):
        left = jnp.where(side == 0, pair[0], pair[1])
        right = jnp.where(side == 0, pair[1], pair[0])
        return jnp.concatenate([left, right], axis=axis).astype(f32)

    grad_qkv = join([g.reshape(g.shape[0], 3, width) for g in grad_qkv], 2)
    grad_wout, grad_up, grad_down = join(grad_wout, 0), join(grad_up, 1), join(grad_down, 0)
    gain2_grad, shift2_grad = sum_all(jnp.stack([gain2_grad, shift2_grad]), ("dp", "tensor"))
    gain1_grad, shift1_grad = sum_all(jnp.stack([gain1_grad, shift1_grad]), ("dp", "tensor"))
    return (
        output,
        grad_input,
        gain1_grad,
        shift1_grad,
        grad_qkv,
        grad_wout,
        gain2_grad,
        shift2_grad,
        grad_up,
        grad_down,
        bucket_counts,
    )


def solution(mesh):
    placed = (
        P("dp", "tensor"),
        P("dp", None),
        P("dp", None),
        P("dp", None),
        P(),
        P(),
        P("dp", None, "tensor"),
        P("tensor", "dp"),
        P(),
        P(),
        P("dp", "tensor"),
        P("tensor", "dp"),
        P("dp", "tensor"),
    )
    return jax.shard_map(
        local,
        mesh=mesh,
        in_specs=placed,
        out_specs=(
            P("dp", "tensor"),
            P("dp", "tensor"),
            P(),
            P(),
            P("dp", None, "tensor"),
            P("tensor", "dp"),
            P(),
            P(),
            P("dp", "tensor"),
            P("tensor", "dp"),
            P(),
        ),
        check_vma=False,
    )
```

```python
import functools
import math

import jax
import jax.numpy as jnp
from jax import lax
from jax.experimental import pallas as pl
from jax.experimental.pallas import tpu as pltpu
from jax.sharding import PartitionSpec as P

HD = 128
HIDDEN_BIT = 2

epsilon = 1e-05


def dp_swap(value, bit):
    count = lax.axis_size("dp")
    return lax.ppermute(value, "dp", [(i, i ^ bit) for i in range(count)])


def tensor_swap(value, bit):
    count = lax.axis_size("tensor")
    return lax.ppermute(value, "tensor", [(i, i ^ bit) for i in range(count)])


def bits_of(count):
    return [1 << i for i in range(count.bit_length() - 1)]


def replica_bits():
    bits = bits_of(lax.axis_size("dp"))
    return [b for b in bits if b > HIDDEN_BIT] + [b for b in bits if b < HIDDEN_BIT]


def gather_weight(mine, other):
    blocks = {0: mine, HIDDEN_BIT: dp_swap(other, HIDDEN_BIT)}
    for bit in replica_bits():
        blocks.update({m | bit: dp_swap(blocks[m], bit) for m in list(blocks)})
    return blocks


def add_low(left, right):
    return (left.astype(jnp.float32) + right.astype(jnp.float32)).astype(jnp.bfloat16)


def scatter_weight(blocks):
    for bit in reversed(replica_bits()):
        arrived = {m ^ bit: dp_swap(blocks[m], bit) for m in blocks if m & bit}
        blocks = {m: add_low(blocks[m], arrived[m]) for m in arrived}
    return blocks[0], dp_swap(blocks[HIDDEN_BIT], HIDDEN_BIT)


def gather_act(rows):
    blocks = {(0, 0): rows, (1, 0): dp_swap(rows, HIDDEN_BIT)}
    for bit in reversed(bits_of(lax.axis_size("tensor"))):
        blocks.update({(b, m | bit): tensor_swap(v, bit) for (b, m), v in list(blocks.items())})
    return blocks


def scatter_act(blocks):
    for bit in bits_of(lax.axis_size("tensor")):
        arrived = {(b, m ^ bit): tensor_swap(v, bit) for (b, m), v in blocks.items() if m & bit}
        blocks = {k: add_low(blocks[k], arrived[k]) for k in arrived}
    return blocks[(0, 0)].astype(jnp.float32) + dp_swap(blocks[(1, 0)], HIDDEN_BIT).astype(
        jnp.float32
    )


def lay(blocks, shape, spots):
    count = len(blocks)

    def kernel(*refs):
        ins, out, sems = refs[:count], refs[count], refs[count + 1]
        copies = []
        for i, spot in enumerate(spots()):
            r, c = blocks[i].shape
            copies.append(
                pltpu.make_async_copy(
                    ins[i],
                    out.at[pl.ds(pl.multiple_of(spot[0], 16), r), pl.ds(pl.multiple_of(spot[1], 128), c)],
                    sems.at[i],
                )
            )
        for copy in copies:
            copy.start()
        for copy in copies:
            copy.wait()

    return pl.pallas_call(
        kernel,
        out_shape=jax.ShapeDtypeStruct(shape, jnp.bfloat16),
        in_specs=[pl.BlockSpec(memory_space=pl.ANY)] * count,
        out_specs=pl.BlockSpec(memory_space=pltpu.VMEM),
        scratch_shapes=[pltpu.SemaphoreType.DMA((count,))],
        compiler_params=pltpu.CompilerParams(vmem_limit_bytes=24 << 20),
    )(*blocks)


def cut(whole, block_shape, count, spots):
    def kernel(*refs):
        src, outs, sems = refs[0], refs[1 : 1 + count], refs[1 + count]
        r, c = block_shape
        copies = []
        for i, spot in enumerate(spots()):
            copies.append(
                pltpu.make_async_copy(
                    src.at[pl.ds(pl.multiple_of(spot[0], 16), r), pl.ds(pl.multiple_of(spot[1], 128), c)],
                    outs[i],
                    sems.at[i],
                )
            )
        for copy in copies:
            copy.start()
        for copy in copies:
            copy.wait()

    return pl.pallas_call(
        kernel,
        out_shape=[jax.ShapeDtypeStruct(block_shape, jnp.bfloat16)] * count,
        in_specs=[pl.BlockSpec(memory_space=pltpu.VMEM)],
        out_specs=[pl.BlockSpec(memory_space=pl.ANY)] * count,
        scratch_shapes=[pltpu.SemaphoreType.DMA((count,))],
        compiler_params=pltpu.CompilerParams(vmem_limit_bytes=24 << 20),
    )(whole)


def lay_weight(blocks, axis):
    count = len(blocks)
    r, c = blocks[0].shape
    if axis == 1 and c % 128:
        order = jnp.bitwise_xor(lax.axis_index("dp"), jnp.arange(count))
        stacked = jnp.stack([blocks[m] for m in range(count)])[order]
        return jnp.swapaxes(stacked, 0, 1).reshape(r, count * c)

    def spots():
        place = lax.axis_index("dp")
        at = [jnp.bitwise_xor(place, m) for m in range(count)]
        return [(d * r, 0) if axis == 0 else (0, d * c) for d in at]

    shape = (r * count, c) if axis == 0 else (r, c * count)
    return lay([blocks[m] for m in range(count)], shape, spots)


def cut_weight(whole, axis):
    count = lax.axis_size("dp")
    r, c = whole.shape
    r, c = (r // count, c) if axis == 0 else (r, c // count)
    if axis == 1 and c % 128:
        order = jnp.bitwise_xor(lax.axis_index("dp"), jnp.arange(count))
        stacked = jnp.swapaxes(whole.reshape(r, count, c), 0, 1)[order]
        return {m: stacked[m] for m in range(count)}

    def spots():
        place = lax.axis_index("dp")
        at = [jnp.bitwise_xor(place, m) for m in range(count)]
        return [(d * r, 0) if axis == 0 else (0, d * c) for d in at]

    return dict(enumerate(cut(whole, (r, c), count, spots)))


def act_keys():
    return [(b, m) for b in range(2) for m in range(lax.axis_size("tensor"))]


def act_spots(r, c):
    place = lax.axis_index("tensor")
    return [(b * r, jnp.bitwise_xor(place, m) * c) for b, m in act_keys()]


def lay_act(blocks):
    r, c = blocks[(0, 0)].shape
    shape = (2 * r, c * lax.axis_size("tensor"))
    return lay([blocks[k] for k in act_keys()], shape, lambda: act_spots(r, c))


def cut_act(whole):
    r, c = whole.shape[0] // 2, whole.shape[1] // lax.axis_size("tensor")
    keys = act_keys()
    return dict(zip(keys, cut(whole, (r, c), len(keys), lambda: act_spots(r, c))))


def whole_stream(rows):
    return lay_act(gather_act(rows.astype(jnp.bfloat16)))


def stream_sum(rows):
    return scatter_act(cut_act(rows.astype(jnp.bfloat16)))


def sum_all(value, axes):
    if "dp" in axes:
        for bit in bits_of(lax.axis_size("dp")):
            value = value + dp_swap(value, bit)
    if "tensor" in axes:
        for bit in bits_of(lax.axis_size("tensor")):
            value = value + tensor_swap(value, bit)
    return value


def token_info(length_row, head_row, width_row, row_count):
    seq_ends = jnp.cumsum(length_row)
    seq_starts = seq_ends - length_row
    places = jnp.arange(row_count, dtype=jnp.int32)
    segment = jnp.sum((places[:, None] >= seq_ends[None, :]).astype(jnp.int32), axis=1)
    labels = jnp.arange(length_row.shape[0], dtype=jnp.int32)
    onehot = (segment[:, None] == labels[None, :]).astype(jnp.int32)
    offset = places - jnp.sum(onehot * seq_starts[None, :], axis=1)
    head_tok = jnp.sum(onehot * head_row[None, :], axis=1)
    width_tok = jnp.sum(onehot * width_row[None, :], axis=1)
    return (segment, offset, head_tok, width_tok)


def rotary_tables(offset, head_size):
    half_size = head_size // 2
    ladder = jnp.arange(half_size, dtype=jnp.float32)
    inverse = jnp.exp(ladder * (-2.0 * math.log(10000.0) / head_size))
    angles = offset.astype(jnp.float32)[:, None] * inverse[None, :]
    return (jnp.cos(angles)[:, None, :], jnp.sin(angles)[:, None, :])


def rotate(values, cosine, sine_part):
    half_size = values.shape[-1] // 2
    front_half = values[..., :half_size]
    back_half = values[..., half_size:]
    return jnp.concatenate(
        [front_half * cosine - back_half * sine_part, back_half * cosine + front_half * sine_part],
        axis=-1,
    )


def norm_forward(values, norm_gain, norm_shift):
    values = values.astype(jnp.float32)
    center = values - jnp.mean(values, axis=-1, keepdims=True)
    spread = jnp.mean(center * center, axis=-1, keepdims=True)
    inverse = lax.rsqrt(spread + epsilon)
    unit_rows = center * inverse
    return (unit_rows * norm_gain + norm_shift, unit_rows, inverse)


def norm_backward(grad_rows, unit_rows, inverse, norm_gain):
    scaled = grad_rows * norm_gain
    grad_in = inverse * (
        scaled
        - jnp.mean(scaled, axis=-1, keepdims=True)
        - unit_rows * jnp.mean(scaled * unit_rows, axis=-1, keepdims=True)
    )
    return (grad_in, jnp.sum(grad_rows * unit_rows, axis=0), jnp.sum(grad_rows, axis=0))


def heads_of(rows, blocks):
    rows = rows.reshape(blocks, rows.shape[0] // blocks, -1, HD)
    return jnp.transpose(rows, (2, 0, 1, 3)).reshape(-1, rows.shape[1], HD)


def rows_of(heads, blocks):
    heads = heads.reshape(-1, blocks, heads.shape[1], HD)
    return jnp.transpose(heads, (1, 2, 0, 3)).reshape(blocks * heads.shape[2], -1)


def local_general(
    residual_in,
    lengths,
    head_bucket,
    width_bucket,
    norm1_gain,
    norm1_shift,
    w_qkv,
    w_out,
    norm2_gain,
    norm2_shift,
    w_up,
    w_down,
    cotangent,
):
    f32, bf16 = jnp.float32, jnp.bfloat16
    dot = functools.partial(jnp.dot, preferred_element_type=f32)
    tensor_index = lax.axis_index("tensor")
    bucket_total = lax.axis_size("tensor")
    tokens = residual_in.shape[0]
    side = (lax.axis_index("dp") // HIDDEN_BIT) % 2

    def halves(weight, axis):
        left, right = jnp.split(weight, 2, axis=axis)
        return jnp.where(side == 0, left, right), jnp.where(side == 0, right, left)

    info = jnp.stack([lengths[0], head_bucket[0], width_bucket[0]])
    far_info = dp_swap(info, HIDDEN_BIT)
    pair = [token_info(i[0], i[1], i[2], tokens) for i in (info, far_info)]
    segment, offset, head_tok, width_tok = [jnp.stack([a, b]) for a, b in zip(*pair)]
    matches = (
        width_bucket[0][:, None] == jnp.arange(bucket_total, dtype=jnp.int32)[None, :]
    ).astype(jnp.int32)
    bucket_counts = sum_all(jnp.sum(lengths[0][:, None] * matches, axis=0), ("dp",))
    head_mask = (head_tok.reshape(-1) >= tensor_index).astype(f32)[:, None]
    width_mask = (width_tok.reshape(-1) >= tensor_index).astype(f32)[:, None]
    places = jnp.arange(tokens, dtype=jnp.int32)
    allowed = (segment[:, :, None] == segment[:, None, :]) & (
        places[:, None] >= places[None, :]
    )
    cosine, sine_part = rotary_tables(offset.reshape(-1), HD)
    score_scale = HD ** (-0.5)

    qkv_halves = [h.reshape(h.shape[0], -1) for h in halves(w_qkv, 2)]
    full_qkv = lay_weight(gather_weight(*qkv_halves), 0)
    full_out = lay_weight(gather_weight(*halves(w_out, 0)), 1)
    full_up = lay_weight(gather_weight(*halves(w_up, 1)), 0)
    full_down = lay_weight(gather_weight(*halves(w_down, 0)), 1)

    inputs = whole_stream(residual_in)
    normed1, unit1, inverse1 = norm_forward(inputs, norm1_gain, norm1_shift)
    normed1 = normed1.astype(bf16)
    projected = dot(normed1, full_qkv).reshape(2 * tokens, 3, -1, HD)
    width = projected.shape[2] * HD
    query = rotate(projected[:, 0], cosine, sine_part).astype(bf16).reshape(-1, width)
    key = rotate(projected[:, 1], cosine, sine_part).astype(bf16).reshape(-1, width)
    value = projected[:, 2].astype(bf16).reshape(-1, width)
    query, key, value = heads_of(query, 2), heads_of(key, 2), heads_of(value, 2)
    allowed = jnp.tile(allowed, (query.shape[0] // 2, 1, 1))
    scores = jnp.einsum("nqd,nkd->nqk", query, key, preferred_element_type=f32) * score_scale
    scores = jnp.where(allowed, scores, -1000000000.0)
    scores = jnp.exp(scores - jnp.max(scores, axis=-1, keepdims=True))
    weights = (scores / jnp.sum(scores, axis=-1, keepdims=True)).astype(bf16)
    mixed = jnp.einsum("nqk,nkd->nqd", weights, value, preferred_element_type=f32)
    mixed = (rows_of(mixed, 2) * head_mask).astype(bf16)
    middle = residual_in + stream_sum(dot(mixed, full_out))
    middle_rows = whole_stream(middle)
    normed2, unit2, inverse2 = norm_forward(middle_rows, norm2_gain, norm2_shift)
    normed2 = normed2.astype(bf16)
    upper = jnp.maximum(dot(normed2, full_up), 0.0) * width_mask
    active = jnp.square(upper).astype(bf16)
    upper = upper.astype(bf16)
    output = middle + stream_sum(dot(active, full_down))

    grad_top = whole_stream(cotangent)
    grad_down = scatter_weight(cut_weight(dot(active.T, grad_top).astype(bf16), 1))
    grad_active = dot(grad_top, full_down.T)
    grad_upper = (grad_active * 2.0 * upper.astype(f32)).astype(bf16)
    grad_normed2 = dot(grad_upper, full_up.T)
    part_middle, gain2_grad, shift2_grad = norm_backward(
        grad_normed2, unit2, inverse2, norm2_gain
    )
    grad_middle = cotangent + stream_sum(part_middle)
    grad_up = scatter_weight(cut_weight(dot(normed2.T, grad_upper).astype(bf16), 0))
    grad_branch = whole_stream(grad_middle)
    grad_wout = scatter_weight(cut_weight(dot(mixed.T, grad_branch).astype(bf16), 1))
    grad_mixed = (dot(grad_branch, full_out.T) * head_mask).astype(bf16)
    grad_mixed = heads_of(grad_mixed, 2)
    grad_weights = jnp.einsum("nqd,nkd->nqk", grad_mixed, value, preferred_element_type=f32)
    grad_value = jnp.einsum("nqk,nqd->nkd", weights, grad_mixed, preferred_element_type=f32)
    wide = weights.astype(f32)
    grad_scores = wide * (grad_weights - jnp.sum(grad_weights * wide, axis=-1, keepdims=True))
    grad_raw = (grad_scores * score_scale).astype(bf16)
    grad_query = jnp.einsum("nqk,nkd->nqd", grad_raw, key, preferred_element_type=f32)
    grad_key = jnp.einsum("nqk,nqd->nkd", grad_raw, query, preferred_element_type=f32)
    grad_query, grad_key = [
        rotate(rows_of(g, 2).reshape(2 * tokens, -1, HD), cosine, -sine_part).reshape(-1, width)
        for g in (grad_query, grad_key)
    ]
    grad_projected = jnp.concatenate([grad_query, grad_key, rows_of(grad_value, 2)], axis=1)
    grad_projected = grad_projected.astype(bf16)
    grad_normed1 = dot(grad_projected, full_qkv.T)
    part_input, gain1_grad, shift1_grad = norm_backward(
        grad_normed1, unit1, inverse1, norm1_gain
    )
    grad_input = grad_middle + stream_sum(part_input)
    grad_qkv = scatter_weight(cut_weight(dot(normed1.T, grad_projected).astype(bf16), 0))

    def join(pair, axis):
        left = jnp.where(side == 0, pair[0], pair[1])
        right = jnp.where(side == 0, pair[1], pair[0])
        return jnp.concatenate([left, right], axis=axis).astype(f32)

    grad_qkv = join([g.reshape(g.shape[0], 3, width) for g in grad_qkv], 2)
    grad_wout, grad_up, grad_down = join(grad_wout, 0), join(grad_up, 1), join(grad_down, 0)
    gain2_grad, shift2_grad = sum_all(jnp.stack([gain2_grad, shift2_grad]), ("dp", "tensor"))
    gain1_grad, shift1_grad = sum_all(jnp.stack([gain1_grad, shift1_grad]), ("dp", "tensor"))
    return (
        output,
        grad_input,
        gain1_grad,
        shift1_grad,
        grad_qkv,
        grad_wout,
        gain2_grad,
        shift2_grad,
        grad_up,
        grad_down,
        bucket_counts,
    )


def flip(i, bit):
    return i + bit - 2 * bit * ((i // bit) % 2)


class Traffic:
    def __init__(self, send_sems, recv_sems):
        self.send_sems, self.recv_sems = send_sems, recv_sems
        self.copies = {}

    def send(self, name, src, dst, device):
        k = len(self.copies)
        copy = pltpu.make_async_remote_copy(
            src_ref=src,
            dst_ref=dst,
            send_sem=self.send_sems.at[k],
            recv_sem=self.recv_sems.at[k],
            device_id=device,
            device_id_type=pl.DeviceIdType.MESH,
        )
        copy.start()
        self.copies[name] = copy

    def wait(self, *names):
        for name in names:
            self.copies[name].wait_recv()

    def finish(self):
        for copy in self.copies.values():
            copy.wait_send()


class Moves:
    def __init__(self, sems):
        self.sems, self.copies = sems, {}

    def start(self, name, src, dst):
        copy = pltpu.make_async_copy(src, dst, self.sems.at[len(self.copies)])
        copy.start()
        self.copies[name] = [copy, False]

    def wait(self, *names):
        for name in names:
            if not self.copies[name][1]:
                self.copies[name][0].wait()
                self.copies[name][1] = True

    def finish(self):
        self.wait(*self.copies)


class Place:
    def __init__(self):
        self.i, self.t = lax.axis_index("dp"), lax.axis_index("tensor")
        self.side = (self.i // HIDDEN_BIT) % 2
        self.x, self.z, self.far = [(flip(self.i, b), self.t) for b in (1, 2, 4)]
        self.c, self.y = [(self.i, flip(self.t, b)) for b in (1, 2)]

    def greet(self):
        barrier = pltpu.get_barrier_semaphore()
        partners = (self.x, self.z, self.far, self.c, self.y)
        for device in partners:
            pl.semaphore_signal(
                barrier, inc=1, device_id=device, device_id_type=pl.DeviceIdType.MESH
            )
        pl.semaphore_wait(barrier, len(partners))

    def block(self, m):
        d = self.i
        for bit in (1, 2, 4):
            if m & bit:
                d = flip(d, bit)
        return d

    def stripe(self, m):
        s = self.t
        for bit in (1, 2):
            if m & bit:
                s = flip(s, bit)
        return s


class WeightGather:
    def __init__(self, name, place, traffic, moves, halves, slot):
        self.name, self.p, self.tr, self.mv = name, place, traffic, moves
        self.halves, self.slot = halves, slot

    def begin(self):
        p, n = self.p, self.name
        own, other = self.halves.at[p.side], self.halves.at[1 - p.side]
        self.tr.send(n + "2", other, self.slot(p.i), p.z)
        self.tr.send(n + "4", own, self.slot(p.i), p.far)
        self.tr.send(n + "1", own, self.slot(p.i), p.x)
        self.mv.start(n + "0", own, self.slot(p.i))

    def mid(self):
        p, n = self.p, self.name
        self.tr.wait(n + "2")
        block = self.slot(p.block(2))
        self.tr.send(n + "6", block, block, p.far)
        self.tr.send(n + "3", block, block, p.x)

    def late(self, m):
        p, n = self.p, self.name
        self.tr.wait(n + str(m))
        block = self.slot(p.block(m))
        self.tr.send(n + str(m + 1), block, block, p.x)

    def end(self):
        n = self.name
        self.mv.wait(n + "0")
        self.tr.wait(n + "1", n + "3", n + "5", n + "7")


class ActGather:
    def __init__(self, name, place, traffic, slots):
        self.name, self.p, self.tr, self.slots = name, place, traffic, slots

    def at(self, b, m):
        return self.slots.at[b, self.p.stripe(m)]

    def begin(self):
        p, n, own = self.p, self.name, self.at(0, 0)
        self.tr.send(n + "10", own, self.slots.at[1, p.t], p.z)
        self.tr.send(n + "02", own, own, p.y)
        self.tr.send(n + "01", own, own, p.c)

    def mid(self):
        p, n = self.p, self.name
        self.tr.wait(n + "10")
        block = self.at(1, 0)
        self.tr.send(n + "12", block, block, p.y)
        self.tr.send(n + "11", block, block, p.c)
        self.tr.wait(n + "02")
        block = self.at(0, 2)
        self.tr.send(n + "03", block, block, p.c)

    def end(self):
        p, n = self.p, self.name
        self.tr.wait(n + "12")
        block = self.at(1, 2)
        self.tr.send(n + "13", block, block, p.c)
        self.tr.wait(n + "01", n + "11", n + "03", n + "13")


def loop_rows(count, step, body):
    def run(k, carry):
        body(pl.multiple_of(k * step, step))
        return carry

    lax.fori_loop(0, count // step, run, 0)


def wide(value):
    return value.astype(jnp.float32)


def add_blocks(out, left, right, rows):
    def body(r):
        at = pl.ds(r, 64)
        out[at, :] = (wide(left[at, :]) + wide(right[at, :])).astype(out.dtype)

    loop_rows(rows, 64, body)


class ActScatter:
    def __init__(self, name, place, traffic, part, got_c, got_y, got_z):
        self.name, self.p, self.tr = name, place, traffic
        self.part, self.got_c, self.got_y, self.got_z = part, got_c, got_y, got_z
        self.rows = part.shape[2]

    def at(self, b, m):
        return self.part.at[b, self.p.stripe(m)]

    def begin(self):
        p, n = self.p, self.name
        for j, m in ((1, 3), (0, 1)):
            for b in (1, 0):
                self.tr.send(n + "c" + str(b) + str(j), self.at(b, m), self.got_c.at[b, j], p.c)

    def mid(self):
        p, n = self.p, self.name
        for b in (1, 0):
            self.tr.wait(n + "c" + str(b) + "1")
            add_blocks(self.at(b, 2), self.at(b, 2), self.got_c.at[b, 1], self.rows)
            self.tr.send(n + "y" + str(b), self.at(b, 2), self.got_y.at[b], p.y)
        for b in (1, 0):
            self.tr.wait(n + "c" + str(b) + "0")
            add_blocks(self.at(b, 0), self.at(b, 0), self.got_c.at[b, 0], self.rows)

    def late(self):
        p, n = self.p, self.name
        self.tr.wait(n + "y1")
        add_blocks(self.at(1, 0), self.at(1, 0), self.got_y.at[1], self.rows)
        self.tr.send(n + "z", self.at(1, 0), self.got_z, p.z)
        self.tr.wait(n + "y0")
        add_blocks(self.at(0, 0), self.at(0, 0), self.got_y.at[0], self.rows)

    def end(self, out, base):
        self.tr.wait(self.name + "z")
        own = self.at(0, 0)

        def body(r):
            at = pl.ds(r, 64)
            out[at, :] = base[at, :] + (wide(own[at, :]) + wide(self.got_z[at, :]))

        loop_rows(self.rows, 64, body)


def round_rows(src, dst, rows):
    def body(r):
        at = pl.ds(r, 64)
        dst[at, :] = src[at, :].astype(dst.dtype)

    loop_rows(rows, 64, body)


def dot_f32(left, right):
    return jnp.dot(left, right, preferred_element_type=jnp.float32)


def dot_nt(left, right):
    return lax.dot_general(
        left, right, (((1,), (1,)), ((), ())), preferred_element_type=jnp.float32
    )


def dot_tn(left, right):
    return lax.dot_general(
        left, right, (((0,), (0,)), ((), ())), preferred_element_type=jnp.float32
    )


def center_rows(slots, b, at):
    stripes = slots.shape[1]
    rows = jnp.concatenate([wide(slots[b, s, at, :]) for s in range(stripes)], axis=1)
    center = rows - jnp.mean(rows, axis=1, keepdims=True)
    spread = jnp.mean(center * center, axis=1, keepdims=True)
    return center, lax.rsqrt(spread + epsilon)


def norm_rows(slots, gain, shift, out):
    rows = slots.shape[2]
    for b in range(2):

        def body(r, b=b):
            center, inverse = center_rows(slots, b, pl.ds(r, 32))
            out[pl.ds(b * rows + r, 32), :] = (
                center * inverse * gain[...] + shift[...]
            ).astype(jnp.bfloat16)

        loop_rows(rows, 32, body)


def attend(qkv, seg_col, seg_row, head_mask, weights, mixed, scale):
    tokens = seg_row.shape[2]
    heads = qkv.shape[2] // HD
    half = tokens // 2

    def body(b, carry):
        start = pl.multiple_of(b * tokens, tokens)
        for h in range(heads):
            cols = pl.ds(h * HD, HD)
            for part in range(2):
                rows = pl.ds(start + part * half, half)
                reach = half * (part + 1)
                query = qkv[0, rows, cols]
                key = qkv[1, pl.ds(start, reach), cols]
                value = qkv[2, pl.ds(start, reach), cols]
                scores = dot_nt(query, key) * scale
                row_id = lax.broadcasted_iota(jnp.int32, (half, reach), 0) + part * half
                col_id = lax.broadcasted_iota(jnp.int32, (half, reach), 1)
                allowed = (seg_col[rows, :] == seg_row[b, :, pl.ds(0, reach)]) & (
                    row_id >= col_id
                )
                scores = jnp.where(allowed, scores, -1000000000.0)
                scores = jnp.exp(scores - jnp.max(scores, axis=1, keepdims=True))
                total = jnp.sum(scores, axis=1, keepdims=True)
                chosen = (scores / total).astype(jnp.bfloat16)
                weights[b * heads + h, pl.ds(part * half, half), pl.ds(0, reach)] = chosen
                mixed[rows, cols] = (dot_f32(chosen, value) * head_mask[rows, :]).astype(
                    jnp.bfloat16
                )
        return carry

    lax.fori_loop(0, 2, body, 0)


def forward_kernel(
    residual,
    cotangent,
    gain1,
    shift1,
    gain2,
    shift2,
    cosine,
    sine,
    seg_col,
    seg_row,
    head_mask,
    width_mask,
    half_qkv,
    half_out,
    half_up,
    half_down,
    all_qkv,
    all_out,
    all_up,
    all_down,
    stream1,
    stream2,
    stream_c,
    normed1,
    normed2,
    heads_out,
    weights_out,
    mixed_out,
    upper_out,
    middle_out,
    w_qkv,
    w_out,
    w_up,
    rows1,
    rows2,
    rows_c,
    normed,
    qkv,
    weights,
    mixed,
    part,
    got_c,
    got_y,
    got_z,
    upper,
    middle,
    send_sems,
    recv_sems,
    move_sems,
):
    p = Place()
    tr, mv = Traffic(send_sems, recv_sems), Moves(move_sems)
    tokens = residual.shape[0]
    rows_d = half_qkv.shape[1]
    head_cols = half_out.shape[1]

    def row_slot(ref):
        return lambda d: ref.at[pl.ds(pl.multiple_of(d * rows_d, rows_d), rows_d)]

    def first_slot(ref):
        return lambda d: ref.at[d]

    g_qkv = WeightGather("q", p, tr, mv, half_qkv, row_slot(w_qkv))
    g_out = WeightGather("o", p, tr, mv, half_out, first_slot(w_out))
    g_up = WeightGather("u", p, tr, mv, half_up, row_slot(w_up))
    g_down = WeightGather("d", p, tr, mv, half_down, first_slot(all_down))
    a1 = ActGather("a", p, tr, rows1)
    a2 = ActGather("b", p, tr, rows2)
    ac = ActGather("c", p, tr, rows_c)
    s1 = ActScatter("s", p, tr, part, got_c, got_y, got_z)

    p.greet()
    round_rows(residual, rows1.at[0, p.t], tokens)
    a1.begin()
    g_qkv.begin()
    round_rows(cotangent, rows_c.at[0, p.t], tokens)
    a1.mid()
    g_qkv.mid()
    a1.end()
    g_out.begin()
    ac.begin()
    norm_rows(rows1, gain1, shift1, normed)
    mv.start("stream1", rows1, stream1)
    mv.start("normed1", normed, normed1)
    g_qkv.late(4)
    g_out.mid()
    g_qkv.late(6)
    g_up.begin()
    ac.mid()
    g_qkv.end()

    def project(r):
        at = pl.ds(r, 256)
        for k in range(3):
            got = dot_f32(normed[at, :], w_qkv[:, pl.ds(k * head_cols, head_cols)])
            for h in range(head_cols // HD):
                cols = pl.ds(h * HD, HD)
                one = got[:, h * HD : (h + 1) * HD]
                if k < 2:
                    one = one * cosine[at, :] + pltpu.roll(one, HD // 2, 1) * sine[at, :]
                qkv[k, at, cols] = one.astype(jnp.bfloat16)

    loop_rows(2 * tokens, 256, project)
    mv.start("all_qkv", w_qkv, all_qkv)
    g_out.late(4)
    g_up.mid()
    attend(qkv, seg_col, seg_row, head_mask, weights, mixed, HD ** (-0.5))
    mv.start("heads", qkv, heads_out)
    mv.start("weights", weights, weights_out)
    mv.start("mixed", mixed, mixed_out)
    g_out.late(6)
    ac.end()
    mv.start("stream_c", rows_c, stream_c)
    g_out.end()

    blocks = w_out.shape[0]
    stripes = part.shape[1]
    per = blocks // stripes

    def branch(k, carry):
        b = k // stripes
        s = k % stripes
        at = pl.ds(pl.multiple_of(b * tokens, tokens), tokens)
        for j in range(per):
            got = dot_f32(mixed[at, :], w_out[s * per + j])
            part[b, s, :, pl.ds(j * rows_d, rows_d)] = got.astype(jnp.bfloat16)
        return carry

    lax.fori_loop(0, 2 * stripes, branch, 0)
    mv.start("all_out", w_out, all_out)
    s1.begin()
    s1.mid()
    g_up.late(4)
    s1.late()
    g_down.begin()
    s1.end(middle, residual)
    round_rows(middle, rows2.at[0, p.t], tokens)
    a2.begin()
    mv.start("middle", middle, middle_out)
    g_up.late(6)
    a2.mid()
    g_down.mid()
    g_up.end()
    mv.start("all_up", w_up, all_up)
    a2.end()
    mv.wait("normed1")
    norm_rows(rows2, gain2, shift2, normed)
    mv.start("stream2", rows2, stream2)
    mv.start("normed2", normed, normed2)

    def rise(r):
        at = pl.ds(r, 256)
        for k in range(upper.shape[1] // 256):
            cols = pl.ds(k * 256, 256)
            got = dot_f32(normed[at, :], w_up[:, cols])
            upper[at, cols] = (jnp.maximum(got, 0.0) * width_mask[at, :]).astype(jnp.bfloat16)

    loop_rows(2 * tokens, 256, rise)
    mv.start("upper", upper, upper_out)
    g_down.late(4)
    g_down.late(6)
    g_down.end()
    tr.finish()
    mv.finish()


def forward_call(arrays, half_weights):
    bf16, f32 = jnp.bfloat16, jnp.float32
    tokens, columns = arrays[0].shape
    half_qkv, half_out, half_up, half_down = half_weights
    count, stripes = lax.axis_size("dp"), lax.axis_size("tensor")
    rows_d = half_qkv.shape[1]
    head_cols = half_out.shape[1]
    hidden = half_up.shape[2]
    width = rows_d * count
    heads = head_cols // HD
    slots = (2, stripes, tokens, columns)
    shapes = dict(
        all_qkv=((width, 3 * head_cols), bf16),
        all_out=((count, head_cols, rows_d), bf16),
        all_up=((width, hidden), bf16),
        all_down=((count, hidden, rows_d), bf16),
        stream1=(slots, bf16),
        stream2=(slots, bf16),
        stream_c=(slots, bf16),
        normed1=((2 * tokens, width), bf16),
        normed2=((2 * tokens, width), bf16),
        heads=((3, 2 * tokens, head_cols), bf16),
        weights=((2 * heads, tokens, tokens), bf16),
        mixed=((2 * tokens, head_cols), bf16),
        upper=((2 * tokens, hidden), bf16),
        middle=((tokens, columns), f32),
    )

    def vmem(name):
        return pltpu.VMEM(*shapes[name])

    scratch = [
        vmem("all_qkv"),
        vmem("all_out"),
        vmem("all_up"),
        vmem("stream1"),
        vmem("stream2"),
        vmem("stream_c"),
        vmem("normed1"),
        vmem("heads"),
        vmem("weights"),
        vmem("mixed"),
        pltpu.VMEM(slots, bf16),
        pltpu.VMEM((2, 2, tokens, columns), bf16),
        pltpu.VMEM((2, tokens, columns), bf16),
        pltpu.VMEM((tokens, columns), bf16),
        vmem("upper"),
        vmem("middle"),
        pltpu.SemaphoreType.DMA((56,)),
        pltpu.SemaphoreType.DMA((56,)),
        pltpu.SemaphoreType.DMA((24,)),
    ]
    any_spec = pl.BlockSpec(memory_space=pl.ANY)
    vmem_spec = pl.BlockSpec(memory_space=pltpu.VMEM)
    outs = pl.pallas_call(
        forward_kernel,
        out_shape=[jax.ShapeDtypeStruct(*s) for s in shapes.values()],
        in_specs=[vmem_spec] * len(arrays) + [any_spec] * 4,
        out_specs=[any_spec] * len(shapes),
        scratch_shapes=scratch,
        compiler_params=pltpu.CompilerParams(
            collective_id=0, has_side_effects=True, vmem_limit_bytes=62 << 20
        ),
    )(*arrays, *half_weights)
    return dict(zip(shapes, outs))

def token_tables(lengths, head_bucket, width_bucket, tokens, tensor_index):
    info = jnp.stack([lengths[0], head_bucket[0], width_bucket[0]])
    far_info = dp_swap(info, HIDDEN_BIT)
    pair = [token_info(i[0], i[1], i[2], tokens) for i in (info, far_info)]
    segment, offset, head_tok, width_tok = [jnp.stack([a, b]) for a, b in zip(*pair)]
    head_mask = (head_tok.reshape(-1) >= tensor_index).astype(jnp.float32)[:, None]
    width_mask = (width_tok.reshape(-1) >= tensor_index).astype(jnp.float32)[:, None]
    cosine, sine_part = [v[:, 0] for v in rotary_tables(offset.reshape(-1), HD)]
    return (
        segment,
        head_mask,
        width_mask,
        jnp.concatenate([cosine, cosine], axis=1),
        jnp.concatenate([-sine_part, sine_part], axis=1),
    )


def count_buckets(lengths, width_bucket, total):
    matches = (width_bucket[0][:, None] == jnp.arange(total, dtype=jnp.int32)[None, :]).astype(
        jnp.int32
    )
    return sum_all(jnp.sum(lengths[0][:, None] * matches, axis=0), ("dp",))


def side_first(weight, axis):
    shape = weight.shape
    split = weight.reshape(shape[:axis] + (2, shape[axis] // 2) + shape[axis + 1 :])
    return jnp.moveaxis(split, axis, 0)


def local_fast(
    residual_in,
    lengths,
    head_bucket,
    width_bucket,
    norm1_gain,
    norm1_shift,
    w_qkv,
    w_out,
    norm2_gain,
    norm2_shift,
    w_up,
    w_down,
    cotangent,
):
    f32, bf16 = jnp.float32, jnp.bfloat16
    dot = functools.partial(jnp.dot, preferred_element_type=f32)
    tokens = residual_in.shape[0]
    tensor_index = lax.axis_index("tensor")
    side = (lax.axis_index("dp") // HIDDEN_BIT) % 2
    segment, head_mask, width_mask, cosine, sine = token_tables(
        lengths, head_bucket, width_bucket, tokens, tensor_index
    )
    bucket_counts = count_buckets(lengths, width_bucket, lax.axis_size("tensor"))
    half_qkv = side_first(w_qkv, 2).reshape(2, w_qkv.shape[0], -1)
    half_weights = (half_qkv, side_first(w_out, 0), side_first(w_up, 1), side_first(w_down, 0))
    arrays = (
        residual_in,
        cotangent,
        norm1_gain[None],
        norm1_shift[None],
        norm2_gain[None],
        norm2_shift[None],
        cosine,
        sine,
        segment.reshape(-1, 1),
        segment[:, None, :],
        head_mask,
        width_mask,
    )
    got = forward_call(arrays, half_weights)

    def rows_of_stream(s):
        return jnp.swapaxes(s, 1, 2).reshape(2 * tokens, -1)

    full_qkv, full_up = got["all_qkv"], got["all_up"]
    full_out, full_down = [
        jnp.swapaxes(got[k], 0, 1).reshape(got[k].shape[1], -1) for k in ("all_out", "all_down")
    ]
    normed1, normed2, mixed, middle = [got[k] for k in ("normed1", "normed2", "mixed", "middle")]
    query, key, value = [heads_of(h, 2) for h in got["heads"]]
    weights = jnp.where(jnp.tril(jnp.ones((tokens, tokens), bool)), got["weights"], 0)
    weights = jnp.swapaxes(weights.reshape(2, -1, tokens, tokens), 0, 1).reshape(weights.shape)
    _, unit1, inverse1 = norm_forward(rows_of_stream(got["stream1"]), norm1_gain, norm1_shift)
    _, unit2, inverse2 = norm_forward(rows_of_stream(got["stream2"]), norm2_gain, norm2_shift)
    upper = got["upper"]
    active = jnp.square(upper.astype(f32)).astype(bf16)
    width = mixed.shape[1]
    score_scale = HD ** (-0.5)
    output = middle + stream_sum(dot(active, full_down))
    cosine, sine_part = cosine[:, None, : HD // 2], sine[:, None, HD // 2 :]

    grad_top = rows_of_stream(got["stream_c"])
    grad_down = scatter_weight(cut_weight(dot(active.T, grad_top).astype(bf16), 1))
    grad_active = dot(grad_top, full_down.T)
    grad_upper = (grad_active * 2.0 * upper.astype(f32)).astype(bf16)
    grad_normed2 = dot(grad_upper, full_up.T)
    part_middle, gain2_grad, shift2_grad = norm_backward(
        grad_normed2, unit2, inverse2, norm2_gain
    )
    grad_middle = cotangent + stream_sum(part_middle)
    grad_up = scatter_weight(cut_weight(dot(normed2.T, grad_upper).astype(bf16), 0))
    grad_branch = whole_stream(grad_middle)
    grad_wout = scatter_weight(cut_weight(dot(mixed.T, grad_branch).astype(bf16), 1))
    grad_mixed = (dot(grad_branch, full_out.T) * head_mask).astype(bf16)
    grad_mixed = heads_of(grad_mixed, 2)
    grad_weights = jnp.einsum("nqd,nkd->nqk", grad_mixed, value, preferred_element_type=f32)
    grad_value = jnp.einsum("nqk,nqd->nkd", weights, grad_mixed, preferred_element_type=f32)
    wide = weights.astype(f32)
    grad_scores = wide * (grad_weights - jnp.sum(grad_weights * wide, axis=-1, keepdims=True))
    grad_raw = (grad_scores * score_scale).astype(bf16)
    grad_query = jnp.einsum("nqk,nkd->nqd", grad_raw, key, preferred_element_type=f32)
    grad_key = jnp.einsum("nqk,nqd->nkd", grad_raw, query, preferred_element_type=f32)
    grad_query, grad_key = [
        rotate(rows_of(g, 2).reshape(2 * tokens, -1, HD), cosine, -sine_part).reshape(-1, width)
        for g in (grad_query, grad_key)
    ]
    grad_projected = jnp.concatenate([grad_query, grad_key, rows_of(grad_value, 2)], axis=1)
    grad_projected = grad_projected.astype(bf16)
    grad_normed1 = dot(grad_projected, full_qkv.T)
    part_input, gain1_grad, shift1_grad = norm_backward(
        grad_normed1, unit1, inverse1, norm1_gain
    )
    grad_input = grad_middle + stream_sum(part_input)
    grad_qkv = scatter_weight(cut_weight(dot(normed1.T, grad_projected).astype(bf16), 0))

    def join(pair, axis):
        left = jnp.where(side == 0, pair[0], pair[1])
        right = jnp.where(side == 0, pair[1], pair[0])
        return jnp.concatenate([left, right], axis=axis).astype(f32)

    grad_qkv = join([g.reshape(g.shape[0], 3, width) for g in grad_qkv], 2)
    grad_wout, grad_up, grad_down = join(grad_wout, 0), join(grad_up, 1), join(grad_down, 0)
    gain2_grad, shift2_grad = sum_all(jnp.stack([gain2_grad, shift2_grad]), ("dp", "tensor"))
    gain1_grad, shift1_grad = sum_all(jnp.stack([gain1_grad, shift1_grad]), ("dp", "tensor"))
    return (
        output,
        grad_input,
        gain1_grad,
        shift1_grad,
        grad_qkv,
        grad_wout,
        gain2_grad,
        shift2_grad,
        grad_up,
        grad_down,
        bucket_counts,
    )


def local(*args):
    w_out = args[7]
    if lax.axis_size("dp") == 8 and lax.axis_size("tensor") == 4 and w_out.shape[1] % 128 == 0:
        return local_fast(*args)
    return local_general(*args)


def solution(mesh):
    placed = (
        P("dp", "tensor"),
        P("dp", None),
        P("dp", None),
        P("dp", None),
        P(),
        P(),
        P("dp", None, "tensor"),
        P("tensor", "dp"),
        P(),
        P(),
        P("dp", "tensor"),
        P("tensor", "dp"),
        P("dp", "tensor"),
    )
    return jax.shard_map(
        local,
        mesh=mesh,
        in_specs=placed,
        out_specs=(
            P("dp", "tensor"),
            P("dp", "tensor"),
            P(),
            P(),
            P("dp", None, "tensor"),
            P("tensor", "dp"),
            P(),
            P(),
            P("dp", "tensor"),
            P("tensor", "dp"),
            P(),
        ),
        check_vma=False,
    )
```

```python
import functools
import math

import jax
import jax.numpy as jnp
import numpy as np
from jax import lax
from jax.experimental import pallas as pl
from jax.experimental.pallas import tpu as pltpu
from jax.sharding import PartitionSpec as P

HD = 128
HIDDEN_BIT = 2

epsilon = 1e-05


def dp_swap(value, bit):
    count = lax.axis_size("dp")
    return lax.ppermute(value, "dp", [(i, i ^ bit) for i in range(count)])


def tensor_swap(value, bit):
    count = lax.axis_size("tensor")
    return lax.ppermute(value, "tensor", [(i, i ^ bit) for i in range(count)])


def bits_of(count):
    return [1 << i for i in range(count.bit_length() - 1)]


def replica_bits():
    bits = bits_of(lax.axis_size("dp"))
    return [b for b in bits if b > HIDDEN_BIT] + [b for b in bits if b < HIDDEN_BIT]


def gather_weight(mine, other):
    blocks = {0: mine, HIDDEN_BIT: dp_swap(other, HIDDEN_BIT)}
    for bit in replica_bits():
        blocks.update({m | bit: dp_swap(blocks[m], bit) for m in list(blocks)})
    return blocks


def add_low(left, right):
    return (left.astype(jnp.float32) + right.astype(jnp.float32)).astype(jnp.bfloat16)


def scatter_weight(blocks):
    for bit in reversed(replica_bits()):
        arrived = {m ^ bit: dp_swap(blocks[m], bit) for m in blocks if m & bit}
        blocks = {m: add_low(blocks[m], arrived[m]) for m in arrived}
    return blocks[0], dp_swap(blocks[HIDDEN_BIT], HIDDEN_BIT)


def gather_act(rows):
    blocks = {(0, 0): rows, (1, 0): dp_swap(rows, HIDDEN_BIT)}
    for bit in reversed(bits_of(lax.axis_size("tensor"))):
        blocks.update({(b, m | bit): tensor_swap(v, bit) for (b, m), v in list(blocks.items())})
    return blocks


def scatter_act(blocks):
    for bit in bits_of(lax.axis_size("tensor")):
        arrived = {(b, m ^ bit): tensor_swap(v, bit) for (b, m), v in blocks.items() if m & bit}
        blocks = {k: add_low(blocks[k], arrived[k]) for k in arrived}
    return blocks[(0, 0)].astype(jnp.float32) + dp_swap(blocks[(1, 0)], HIDDEN_BIT).astype(
        jnp.float32
    )


def lay(blocks, shape, spots):
    count = len(blocks)

    def kernel(*refs):
        ins, out, sems = refs[:count], refs[count], refs[count + 1]
        copies = []
        for i, spot in enumerate(spots()):
            r, c = blocks[i].shape
            copies.append(
                pltpu.make_async_copy(
                    ins[i],
                    out.at[pl.ds(pl.multiple_of(spot[0], 16), r), pl.ds(pl.multiple_of(spot[1], 128), c)],
                    sems.at[i],
                )
            )
        for copy in copies:
            copy.start()
        for copy in copies:
            copy.wait()

    return pl.pallas_call(
        kernel,
        out_shape=jax.ShapeDtypeStruct(shape, jnp.bfloat16),
        in_specs=[pl.BlockSpec(memory_space=pl.ANY)] * count,
        out_specs=pl.BlockSpec(memory_space=pltpu.VMEM),
        scratch_shapes=[pltpu.SemaphoreType.DMA((count,))],
        compiler_params=pltpu.CompilerParams(vmem_limit_bytes=24 << 20),
    )(*blocks)


def cut(whole, block_shape, count, spots):
    def kernel(*refs):
        src, outs, sems = refs[0], refs[1 : 1 + count], refs[1 + count]
        r, c = block_shape
        copies = []
        for i, spot in enumerate(spots()):
            copies.append(
                pltpu.make_async_copy(
                    src.at[pl.ds(pl.multiple_of(spot[0], 16), r), pl.ds(pl.multiple_of(spot[1], 128), c)],
                    outs[i],
                    sems.at[i],
                )
            )
        for copy in copies:
            copy.start()
        for copy in copies:
            copy.wait()

    return pl.pallas_call(
        kernel,
        out_shape=[jax.ShapeDtypeStruct(block_shape, jnp.bfloat16)] * count,
        in_specs=[pl.BlockSpec(memory_space=pltpu.VMEM)],
        out_specs=[pl.BlockSpec(memory_space=pl.ANY)] * count,
        scratch_shapes=[pltpu.SemaphoreType.DMA((count,))],
        compiler_params=pltpu.CompilerParams(vmem_limit_bytes=24 << 20),
    )(whole)


def lay_weight(blocks, axis):
    count = len(blocks)
    r, c = blocks[0].shape
    if axis == 1 and c % 128:
        order = jnp.bitwise_xor(lax.axis_index("dp"), jnp.arange(count))
        stacked = jnp.stack([blocks[m] for m in range(count)])[order]
        return jnp.swapaxes(stacked, 0, 1).reshape(r, count * c)

    def spots():
        place = lax.axis_index("dp")
        at = [jnp.bitwise_xor(place, m) for m in range(count)]
        return [(d * r, 0) if axis == 0 else (0, d * c) for d in at]

    shape = (r * count, c) if axis == 0 else (r, c * count)
    return lay([blocks[m] for m in range(count)], shape, spots)


def cut_weight(whole, axis):
    count = lax.axis_size("dp")
    r, c = whole.shape
    r, c = (r // count, c) if axis == 0 else (r, c // count)
    if axis == 1 and c % 128:
        order = jnp.bitwise_xor(lax.axis_index("dp"), jnp.arange(count))
        stacked = jnp.swapaxes(whole.reshape(r, count, c), 0, 1)[order]
        return {m: stacked[m] for m in range(count)}

    def spots():
        place = lax.axis_index("dp")
        at = [jnp.bitwise_xor(place, m) for m in range(count)]
        return [(d * r, 0) if axis == 0 else (0, d * c) for d in at]

    return dict(enumerate(cut(whole, (r, c), count, spots)))


def act_keys():
    return [(b, m) for b in range(2) for m in range(lax.axis_size("tensor"))]


def act_spots(r, c):
    place = lax.axis_index("tensor")
    return [(b * r, jnp.bitwise_xor(place, m) * c) for b, m in act_keys()]


def lay_act(blocks):
    r, c = blocks[(0, 0)].shape
    shape = (2 * r, c * lax.axis_size("tensor"))
    return lay([blocks[k] for k in act_keys()], shape, lambda: act_spots(r, c))


def cut_act(whole):
    r, c = whole.shape[0] // 2, whole.shape[1] // lax.axis_size("tensor")
    keys = act_keys()
    return dict(zip(keys, cut(whole, (r, c), len(keys), lambda: act_spots(r, c))))


def whole_stream(rows):
    return lay_act(gather_act(rows.astype(jnp.bfloat16)))


def stream_sum(rows):
    return scatter_act(cut_act(rows.astype(jnp.bfloat16)))


def sum_all(value, axes):
    if "dp" in axes:
        for bit in bits_of(lax.axis_size("dp")):
            value = value + dp_swap(value, bit)
    if "tensor" in axes:
        for bit in bits_of(lax.axis_size("tensor")):
            value = value + tensor_swap(value, bit)
    return value


def token_info(length_row, head_row, width_row, row_count):
    seq_ends = jnp.cumsum(length_row)
    seq_starts = seq_ends - length_row
    places = jnp.arange(row_count, dtype=jnp.int32)
    segment = jnp.sum((places[:, None] >= seq_ends[None, :]).astype(jnp.int32), axis=1)
    labels = jnp.arange(length_row.shape[0], dtype=jnp.int32)
    onehot = (segment[:, None] == labels[None, :]).astype(jnp.int32)
    offset = places - jnp.sum(onehot * seq_starts[None, :], axis=1)
    head_tok = jnp.sum(onehot * head_row[None, :], axis=1)
    width_tok = jnp.sum(onehot * width_row[None, :], axis=1)
    return (segment, offset, head_tok, width_tok)


def rotary_tables(offset, head_size):
    half_size = head_size // 2
    ladder = jnp.arange(half_size, dtype=jnp.float32)
    inverse = jnp.exp(ladder * (-2.0 * math.log(10000.0) / head_size))
    angles = offset.astype(jnp.float32)[:, None] * inverse[None, :]
    return (jnp.cos(angles)[:, None, :], jnp.sin(angles)[:, None, :])


def rotate(values, cosine, sine_part):
    half_size = values.shape[-1] // 2
    front_half = values[..., :half_size]
    back_half = values[..., half_size:]
    return jnp.concatenate(
        [front_half * cosine - back_half * sine_part, back_half * cosine + front_half * sine_part],
        axis=-1,
    )


def norm_forward(values, norm_gain, norm_shift):
    values = values.astype(jnp.float32)
    center = values - jnp.mean(values, axis=-1, keepdims=True)
    spread = jnp.mean(center * center, axis=-1, keepdims=True)
    inverse = lax.rsqrt(spread + epsilon)
    unit_rows = center * inverse
    return (unit_rows * norm_gain + norm_shift, unit_rows, inverse)


def norm_backward(grad_rows, unit_rows, inverse, norm_gain):
    scaled = grad_rows * norm_gain
    grad_in = inverse * (
        scaled
        - jnp.mean(scaled, axis=-1, keepdims=True)
        - unit_rows * jnp.mean(scaled * unit_rows, axis=-1, keepdims=True)
    )
    return (grad_in, jnp.sum(grad_rows * unit_rows, axis=0), jnp.sum(grad_rows, axis=0))


def heads_of(rows, blocks):
    rows = rows.reshape(blocks, rows.shape[0] // blocks, -1, HD)
    return jnp.transpose(rows, (2, 0, 1, 3)).reshape(-1, rows.shape[1], HD)


def rows_of(heads, blocks):
    heads = heads.reshape(-1, blocks, heads.shape[1], HD)
    return jnp.transpose(heads, (1, 2, 0, 3)).reshape(blocks * heads.shape[2], -1)


def local_general(
    residual_in,
    lengths,
    head_bucket,
    width_bucket,
    norm1_gain,
    norm1_shift,
    w_qkv,
    w_out,
    norm2_gain,
    norm2_shift,
    w_up,
    w_down,
    cotangent,
):
    f32, bf16 = jnp.float32, jnp.bfloat16
    dot = functools.partial(jnp.dot, preferred_element_type=f32)
    tensor_index = lax.axis_index("tensor")
    bucket_total = lax.axis_size("tensor")
    tokens = residual_in.shape[0]
    side = (lax.axis_index("dp") // HIDDEN_BIT) % 2

    def halves(weight, axis):
        left, right = jnp.split(weight, 2, axis=axis)
        return jnp.where(side == 0, left, right), jnp.where(side == 0, right, left)

    info = jnp.stack([lengths[0], head_bucket[0], width_bucket[0]])
    far_info = dp_swap(info, HIDDEN_BIT)
    pair = [token_info(i[0], i[1], i[2], tokens) for i in (info, far_info)]
    segment, offset, head_tok, width_tok = [jnp.stack([a, b]) for a, b in zip(*pair)]
    matches = (
        width_bucket[0][:, None] == jnp.arange(bucket_total, dtype=jnp.int32)[None, :]
    ).astype(jnp.int32)
    bucket_counts = sum_all(jnp.sum(lengths[0][:, None] * matches, axis=0), ("dp",))
    head_mask = (head_tok.reshape(-1) >= tensor_index).astype(f32)[:, None]
    width_mask = (width_tok.reshape(-1) >= tensor_index).astype(f32)[:, None]
    places = jnp.arange(tokens, dtype=jnp.int32)
    allowed = (segment[:, :, None] == segment[:, None, :]) & (
        places[:, None] >= places[None, :]
    )
    cosine, sine_part = rotary_tables(offset.reshape(-1), HD)
    score_scale = HD ** (-0.5)

    qkv_halves = [h.reshape(h.shape[0], -1) for h in halves(w_qkv, 2)]
    full_qkv = lay_weight(gather_weight(*qkv_halves), 0)
    full_out = lay_weight(gather_weight(*halves(w_out, 0)), 1)
    full_up = lay_weight(gather_weight(*halves(w_up, 1)), 0)
    full_down = lay_weight(gather_weight(*halves(w_down, 0)), 1)

    inputs = whole_stream(residual_in)
    normed1, unit1, inverse1 = norm_forward(inputs, norm1_gain, norm1_shift)
    normed1 = normed1.astype(bf16)
    projected = dot(normed1, full_qkv).reshape(2 * tokens, 3, -1, HD)
    width = projected.shape[2] * HD
    query = rotate(projected[:, 0], cosine, sine_part).astype(bf16).reshape(-1, width)
    key = rotate(projected[:, 1], cosine, sine_part).astype(bf16).reshape(-1, width)
    value = projected[:, 2].astype(bf16).reshape(-1, width)
    query, key, value = heads_of(query, 2), heads_of(key, 2), heads_of(value, 2)
    allowed = jnp.tile(allowed, (query.shape[0] // 2, 1, 1))
    scores = jnp.einsum("nqd,nkd->nqk", query, key, preferred_element_type=f32) * score_scale
    scores = jnp.where(allowed, scores, -1000000000.0)
    scores = jnp.exp(scores - jnp.max(scores, axis=-1, keepdims=True))
    weights = (scores / jnp.sum(scores, axis=-1, keepdims=True)).astype(bf16)
    mixed = jnp.einsum("nqk,nkd->nqd", weights, value, preferred_element_type=f32)
    mixed = (rows_of(mixed, 2) * head_mask).astype(bf16)
    middle = residual_in + stream_sum(dot(mixed, full_out))
    middle_rows = whole_stream(middle)
    normed2, unit2, inverse2 = norm_forward(middle_rows, norm2_gain, norm2_shift)
    normed2 = normed2.astype(bf16)
    upper = jnp.maximum(dot(normed2, full_up), 0.0) * width_mask
    active = jnp.square(upper).astype(bf16)
    upper = upper.astype(bf16)
    output = middle + stream_sum(dot(active, full_down))

    grad_top = whole_stream(cotangent)
    grad_down = scatter_weight(cut_weight(dot(active.T, grad_top).astype(bf16), 1))
    grad_active = dot(grad_top, full_down.T)
    grad_upper = (grad_active * 2.0 * upper.astype(f32)).astype(bf16)
    grad_normed2 = dot(grad_upper, full_up.T)
    part_middle, gain2_grad, shift2_grad = norm_backward(
        grad_normed2, unit2, inverse2, norm2_gain
    )
    grad_middle = cotangent + stream_sum(part_middle)
    grad_up = scatter_weight(cut_weight(dot(normed2.T, grad_upper).astype(bf16), 0))
    grad_branch = whole_stream(grad_middle)
    grad_wout = scatter_weight(cut_weight(dot(mixed.T, grad_branch).astype(bf16), 1))
    grad_mixed = (dot(grad_branch, full_out.T) * head_mask).astype(bf16)
    grad_mixed = heads_of(grad_mixed, 2)
    grad_weights = jnp.einsum("nqd,nkd->nqk", grad_mixed, value, preferred_element_type=f32)
    grad_value = jnp.einsum("nqk,nqd->nkd", weights, grad_mixed, preferred_element_type=f32)
    wide = weights.astype(f32)
    grad_scores = wide * (grad_weights - jnp.sum(grad_weights * wide, axis=-1, keepdims=True))
    grad_raw = (grad_scores * score_scale).astype(bf16)
    grad_query = jnp.einsum("nqk,nkd->nqd", grad_raw, key, preferred_element_type=f32)
    grad_key = jnp.einsum("nqk,nqd->nkd", grad_raw, query, preferred_element_type=f32)
    grad_query, grad_key = [
        rotate(rows_of(g, 2).reshape(2 * tokens, -1, HD), cosine, -sine_part).reshape(-1, width)
        for g in (grad_query, grad_key)
    ]
    grad_projected = jnp.concatenate([grad_query, grad_key, rows_of(grad_value, 2)], axis=1)
    grad_projected = grad_projected.astype(bf16)
    grad_normed1 = dot(grad_projected, full_qkv.T)
    part_input, gain1_grad, shift1_grad = norm_backward(
        grad_normed1, unit1, inverse1, norm1_gain
    )
    grad_input = grad_middle + stream_sum(part_input)
    grad_qkv = scatter_weight(cut_weight(dot(normed1.T, grad_projected).astype(bf16), 0))

    def join(pair, axis):
        left = jnp.where(side == 0, pair[0], pair[1])
        right = jnp.where(side == 0, pair[1], pair[0])
        return jnp.concatenate([left, right], axis=axis).astype(f32)

    grad_qkv = join([g.reshape(g.shape[0], 3, width) for g in grad_qkv], 2)
    grad_wout, grad_up, grad_down = join(grad_wout, 0), join(grad_up, 1), join(grad_down, 0)
    gain2_grad, shift2_grad = sum_all(jnp.stack([gain2_grad, shift2_grad]), ("dp", "tensor"))
    gain1_grad, shift1_grad = sum_all(jnp.stack([gain1_grad, shift1_grad]), ("dp", "tensor"))
    return (
        output,
        grad_input,
        gain1_grad,
        shift1_grad,
        grad_qkv,
        grad_wout,
        gain2_grad,
        shift2_grad,
        grad_up,
        grad_down,
        bucket_counts,
    )


def flip(i, bit):
    return i + bit - 2 * bit * ((i // bit) % 2)


class Traffic:
    def __init__(self, send_sems, recv_sems):
        self.send_sems, self.recv_sems = send_sems, recv_sems
        self.copies, self.gone, self.come = {}, set(), set()

    def send(self, name, src, dst, device):
        k = len(self.copies)
        copy = pltpu.make_async_remote_copy(
            src_ref=src,
            dst_ref=dst,
            send_sem=self.send_sems.at[k],
            recv_sem=self.recv_sems.at[k],
            device_id=device,
            device_id_type=pl.DeviceIdType.MESH,
        )
        copy.start()
        self.copies[name] = copy

    def wait(self, *names):
        for name in names:
            if name not in self.come:
                self.copies[name].wait_recv()
                self.come.add(name)

    def sent(self, *names):
        for name in names:
            if name not in self.gone:
                self.copies[name].wait_send()
                self.gone.add(name)

    def finish(self):
        self.sent(*self.copies)


class Moves:
    def __init__(self, sems):
        self.sems, self.copies = sems, {}

    def start(self, name, src, dst):
        copy = pltpu.make_async_copy(src, dst, self.sems.at[len(self.copies)])
        copy.start()
        self.copies[name] = [copy, False]

    def wait(self, *names):
        for name in names:
            if not self.copies[name][1]:
                self.copies[name][0].wait()
                self.copies[name][1] = True

    def finish(self):
        self.wait(*self.copies)


class Place:
    def __init__(self):
        self.i, self.t = lax.axis_index("dp"), lax.axis_index("tensor")
        self.side = (self.i // 2 + self.i // 4) % 2
        self.x, self.z = [(flip(self.i, b), self.t) for b in (1, 2)]
        self.far = (self.block(6), self.t)
        self.c, self.y = [(self.i, flip(self.t, b)) for b in (1, 2)]

    def greet(self):
        barrier = pltpu.get_barrier_semaphore()
        partners = (self.x, self.z, self.far, self.c, self.y)
        for device in partners:
            pl.semaphore_signal(
                barrier, inc=1, device_id=device, device_id_type=pl.DeviceIdType.MESH
            )
        pl.semaphore_wait(barrier, len(partners))

    def block(self, m):
        d = self.i
        for bit in (1, 2, 4):
            if m & bit:
                d = flip(d, bit)
        return d

    def stripe(self, m):
        s = self.t
        for bit in (1, 2):
            if m & bit:
                s = flip(s, bit)
        return s


class WeightGather:
    def __init__(self, name, place, traffic, moves, half, slot):
        self.name, self.p, self.tr, self.mv = name, place, traffic, moves
        self.half, self.slot = half, slot

    def own(self):
        self.mv.start(self.name + "0", self.half(self.p.side), self.slot(self.p.i))

    def z(self):
        self.tr.send(self.name + "2", self.half(1 - self.p.side), self.slot(self.p.i), self.p.z)

    def far(self):
        self.tr.send(self.name + "6", self.half(self.p.side), self.slot(self.p.i), self.p.far)

    def x(self):
        self.tr.send(self.name + "1", self.half(self.p.side), self.slot(self.p.i), self.p.x)

    def far_next(self):
        self.tr.wait(self.name + "2")
        block = self.slot(self.p.block(2))
        self.tr.send(self.name + "4", block, block, self.p.far)

    def x_next(self, m):
        self.tr.wait(self.name + str(m))
        block = self.slot(self.p.block(m))
        self.tr.send(self.name + str(m + 1), block, block, self.p.x)

    def take(self, *which):
        for m in which:
            if m == 0:
                self.mv.wait(self.name + "0")
            else:
                self.tr.wait(self.name + str(m))

    def end(self):
        self.take(*range(8))


class ActGather:
    def __init__(self, name, place, traffic, slots):
        self.name, self.p, self.tr, self.slots = name, place, traffic, slots

    def at(self, b, m):
        return self.slots.at[b, self.p.stripe(m)]

    def z(self):
        self.tr.send(self.name + "10", self.at(0, 0), self.slots.at[1, self.p.t], self.p.z)

    def y(self):
        self.tr.send(self.name + "02", self.at(0, 0), self.at(0, 0), self.p.y)

    def c(self):
        self.tr.send(self.name + "01", self.at(0, 0), self.at(0, 0), self.p.c)

    def pass_z(self):
        self.tr.wait(self.name + "10")
        block = self.at(1, 0)
        self.tr.send(self.name + "12", block, block, self.p.y)
        self.tr.send(self.name + "11", block, block, self.p.c)

    def pass_y(self, b):
        self.tr.wait(self.name + str(b) + "2")
        block = self.at(b, 2)
        self.tr.send(self.name + str(b) + "3", block, block, self.p.c)

    def take(self, b):
        for m in range(1 - b, 4):
            self.tr.wait(self.name + str(b) + str(m))


def loop_rows(count, step, body):
    def run(k, carry):
        body(pl.multiple_of(k * step, step))
        return carry

    lax.fori_loop(0, count // step, run, 0)


def wide(value):
    return value.astype(jnp.float32)


def add_blocks(out, left, right, rows):
    def body(r):
        at = pl.ds(r, 64)
        out[at, :] = (wide(left[at, :]) + wide(right[at, :])).astype(out.dtype)

    loop_rows(rows, 64, body)


class ActScatter:
    def __init__(self, name, place, traffic, part, got_c, got_y, got_z):
        self.name, self.p, self.tr = name, place, traffic
        self.part, self.got_c, self.got_y, self.got_z = part, got_c, got_y, got_z
        self.rows = part.shape[2]

    def at(self, b, m):
        return self.part.at[b, self.p.stripe(m)]

    def c(self, b):
        for j, m in ((1, 3), (0, 1)):
            name = self.name + "c" + str(b) + str(j)
            self.tr.send(name, self.at(b, m), self.got_c.at[b, j], self.p.c)

    def add(self, b, m, name, got):
        self.tr.wait(self.name + name)
        add_blocks(self.at(b, m), self.at(b, m), got, self.rows)

    def y(self, b):
        self.add(b, 2, "c" + str(b) + "1", self.got_c.at[b, 1])
        self.tr.send(self.name + "y" + str(b), self.at(b, 2), self.got_y.at[b], self.p.y)

    def own(self, b):
        self.add(b, 0, "c" + str(b) + "0", self.got_c.at[b, 0])

    def z(self):
        self.add(1, 0, "y1", self.got_y.at[1])
        self.tr.send(self.name + "z", self.at(1, 0), self.got_z, self.p.z)

    def home(self):
        self.add(0, 0, "y0", self.got_y.at[0])

    def sent(self):
        for key in ("c11", "c01", "c10", "c00", "y1", "y0", "z"):
            self.tr.sent(self.name + key)

    def end(self, out, base):
        self.tr.wait(self.name + "z")
        own = self.at(0, 0)

        def body(r):
            at = pl.ds(r, 64)
            out[at, :] = base[at, :] + (wide(own[at, :]) + wide(self.got_z[at, :]))

        loop_rows(self.rows, 64, body)


def round_rows(src, dst, rows):
    def body(r):
        at = pl.ds(r, 64)
        dst[at, :] = src[at, :].astype(dst.dtype)

    loop_rows(rows, 64, body)


def dot_f32(left, right):
    return jnp.dot(left, right, preferred_element_type=jnp.float32)


def dot_nt(left, right):
    return lax.dot_general(
        left, right, (((1,), (1,)), ((), ())), preferred_element_type=jnp.float32
    )


def dot_tn(left, right):
    return lax.dot_general(
        left, right, (((0,), (0,)), ((), ())), preferred_element_type=jnp.float32
    )


def center_rows(slots, b, at):
    stripes = slots.shape[1]
    rows = jnp.concatenate([wide(slots[b, s, at, :]) for s in range(stripes)], axis=1)
    center = rows - jnp.mean(rows, axis=1, keepdims=True)
    spread = jnp.mean(center * center, axis=1, keepdims=True)
    return center, lax.rsqrt(spread + epsilon)


def norm_rows(slots, b, gain, shift, out):
    rows = slots.shape[2]

    def body(r):
        center, inverse = center_rows(slots, b, pl.ds(r, 32))
        out[pl.ds(b * rows + r, 32), :] = (center * inverse * gain[...] + shift[...]).astype(
            jnp.bfloat16
        )

    loop_rows(rows, 32, body)


def attend(b, qkv, seg_col, seg_row, head_mask, weights, mixed, scale):
    tokens = seg_row.shape[2]
    heads = qkv.shape[2] // HD
    half = tokens // 2
    start = b * tokens
    for h in range(heads):
        cols = pl.ds(h * HD, HD)
        for part in range(2):
            rows = pl.ds(start + part * half, half)
            reach = half * (part + 1)
            query = qkv[0, rows, cols]
            key = qkv[1, pl.ds(start, reach), cols]
            value = qkv[2, pl.ds(start, reach), cols]
            scores = dot_nt(query, key) * scale
            row_id = lax.broadcasted_iota(jnp.int32, (half, reach), 0) + part * half
            col_id = lax.broadcasted_iota(jnp.int32, (half, reach), 1)
            same = seg_col[rows, :] == seg_row[b, :, pl.ds(0, reach)]
            scores = jnp.where(same & (row_id >= col_id), scores, -1000000000.0)
            scores = jnp.exp(scores - jnp.max(scores, axis=1, keepdims=True))
            total = jnp.sum(scores, axis=1, keepdims=True)
            chosen = (scores / total).astype(jnp.bfloat16)
            weights[b * heads + h, pl.ds(part * half, half), pl.ds(0, reach)] = chosen
            mixed[rows, cols] = (dot_f32(chosen, value) * head_mask[rows, :]).astype(jnp.bfloat16)


def sequences(lengths):
    start = 0
    for s in range(lengths.shape[1]):
        length = lengths[0, s]
        yield s, start, length
        start = start + length


def count_row(lengths, width_bucket, lanes):
    lane = lax.broadcasted_iota(jnp.int32, (1, lanes), 1)
    row = jnp.zeros((1, lanes), jnp.float32)
    for s, _, length in sequences(lengths):
        row = row + jnp.where(lane == width_bucket[0, s], wide(length), 0.0)
    return row


def fill_facts(lengths, head_bucket, width_bucket, place_cosine, place_sine, facts):
    lanes = facts.shape[1]
    row = lax.broadcasted_iota(jnp.int32, (8, lanes), 0)
    lane = lax.broadcasted_iota(jnp.int32, (8, lanes), 1)
    count = lengths.shape[1]
    by_lane = jnp.where((row == 0) & (lane >= count), 1e9, 0.0)
    by_row = jnp.where(row >= count, 1e9, 0.0)
    for s, start, length in sequences(lengths):
        end = wide(start + length)
        here = lane == s
        by_lane = by_lane + jnp.where((row == 0) & here, end, 0.0)
        by_lane = by_lane + jnp.where((row == 2) & here, wide(head_bucket[0, s]), 0.0)
        by_lane = by_lane + jnp.where((row == 3) & here, wide(width_bucket[0, s]), 0.0)
        by_row = by_row + jnp.where(row == s, end, 0.0)
        facts[pl.ds(16 + s, 1), :] = place_cosine[pl.ds(start, 1), :]
        facts[pl.ds(20 + s, 1), :] = place_sine[pl.ds(start, 1), :]
    facts[pl.ds(0, 8), :] = by_lane
    facts[pl.ds(8, 8), :] = by_row


def fill_tables(
    infos, place_cosine, place_sine, t, cosine, sine, head_mask, width_mask, seg_col, seg_row
):
    tokens, lanes = place_cosine.shape
    own = wide(t)
    lane = wide(lax.broadcasted_iota(jnp.int32, (tokens, lanes), 1))
    place = wide(lax.broadcasted_iota(jnp.int32, (tokens, lanes), 0))
    sign = jnp.where(lane < lanes // 2, -1.0, 1.0)
    for b in range(2):
        rows = pl.ds(b * tokens, tokens)

        def row(k, b=b):
            return infos[b, pl.ds(k, 1), :]

        segment = jnp.sum(jnp.where(place >= row(0), 1.0, 0.0), axis=1, keepdims=True)
        seg_col[rows, :] = segment
        chosen = jnp.where(lane == segment, 1.0, 0.0)
        head = jnp.sum(chosen * row(2), axis=1, keepdims=True)
        width = jnp.sum(chosen * row(3), axis=1, keepdims=True)
        head_mask[rows, :] = jnp.where(head >= own, 1.0, 0.0)
        width_mask[rows, :] = jnp.where(width >= own, 1.0, 0.0)
        start_cosine, start_sine = 0.0, 0.0
        for s in range(4):
            here = jnp.where(segment == s, 1.0, 0.0)
            start_cosine = start_cosine + here * row(16 + s)
            start_sine = start_sine + here * row(20 + s)
        at_cosine, at_sine = place_cosine[...], place_sine[...]
        cosine[rows, :] = at_cosine * start_cosine + at_sine * start_sine
        sine[rows, :] = (at_sine * start_cosine - at_cosine * start_sine) * sign
        ends = infos[b, pl.ds(8, 8), pl.ds(0, 1)]
        across = wide(lax.broadcasted_iota(jnp.int32, (8, tokens), 1))
        seg_row[b] = jnp.sum(jnp.where(across >= ends, 1.0, 0.0), axis=0, keepdims=True)


def forward_kernel(
    residual,
    cotangent,
    gain1,
    shift1,
    gain2,
    shift2,
    lengths,
    head_bucket,
    width_bucket,
    place_cosine,
    place_sine,
    half_qkv,
    half_out,
    half_up,
    half_down,
    cosine,
    sine,
    head_mask,
    all_qkv,
    all_out,
    all_up,
    stream1,
    stream2,
    stream_c,
    normed1,
    normed2,
    heads_out,
    weights_out,
    mixed_out,
    active_out,
    grad_upper_out,
    part_out,
    middle_out,
    w_qkv,
    w_out,
    w_up,
    w_down,
    rows1,
    rows2,
    rows_c,
    normed,
    qkv,
    weights,
    mixed,
    part,
    got_c,
    got_y,
    got_z,
    upper,
    active,
    grad_active,
    middle,
    infos,
    seg_col,
    seg_row,
    width_mask,
    send_sems,
    recv_sems,
    move_sems,
):
    p = Place()
    tr, mv = Traffic(send_sems, recv_sems), Moves(move_sems)
    tokens = residual.shape[0]
    rows_d = half_qkv.shape[1]
    head_cols = w_out.shape[1]

    def row_slot(ref):
        return lambda d: ref.at[pl.ds(pl.multiple_of(d * rows_d, rows_d), rows_d)]

    def first_slot(ref):
        return lambda d: ref.at[d]

    def at_side(k, cut, size):
        return pl.ds(pl.multiple_of(k * size + cut.start, 128), cut.size)

    hidden = w_up.shape[1]
    parts = [pl.ds(0, hidden // 2), pl.ds(hidden // 2, hidden // 2)]

    def rows_at(d):
        return pl.ds(pl.multiple_of(d * rows_d, rows_d), rows_d)

    def up_gather(name, cut):
        return WeightGather(
            name,
            p,
            tr,
            mv,
            lambda k: half_up.at[:, at_side(k, cut, hidden)],
            lambda d: w_up.at[rows_at(d), cut],
        )

    def down_gather(name, cut):
        return WeightGather(
            name,
            p,
            tr,
            mv,
            lambda k: half_down.at[at_side(k, cut, hidden), :],
            lambda d: w_down.at[d, cut, :],
        )

    heads_cut = pl.ds(0, head_cols)
    q = WeightGather(
        "q",
        p,
        tr,
        mv,
        lambda k: half_qkv.at[:, :, at_side(k, heads_cut, head_cols)],
        lambda d: w_qkv.at[:, rows_at(d), :],
    )
    o = WeightGather(
        "o",
        p,
        tr,
        mv,
        lambda k: half_out.at[at_side(k, heads_cut, head_cols), :],
        lambda d: w_out.at[d],
    )
    u, v = [up_gather(n, cut) for n, cut in zip("uv", parts)]
    d, e = [down_gather(n, cut) for n, cut in zip("de", parts)]
    a1 = ActGather("a", p, tr, rows1)
    a2 = ActGather("b", p, tr, rows2)
    ac = ActGather("c", p, tr, rows_c)
    s1 = ActScatter("s", p, tr, part, got_c, got_y, got_z)

    fill_facts(lengths, head_bucket, width_bucket, place_cosine, place_sine, infos.at[0])
    p.greet()
    for one in (q, o, u, v, d, e):
        one.own()
    blocks = w_out.shape[0]
    stripes = part.shape[1]
    per = blocks // stripes
    started = []

    def project(b):
        def body(r):
            at = pl.ds(b * tokens + r, 256)
            for k in range(3):
                got = dot_f32(normed[at, :], w_qkv[k])
                for h in range(head_cols // HD):
                    cols = pl.ds(h * HD, HD)
                    one = got[:, h * HD : (h + 1) * HD]
                    if k < 2:
                        one = one * cosine[at, :] + pltpu.roll(one, HD // 2, 1) * sine[at, :]
                    qkv[k, at, cols] = one.astype(jnp.bfloat16)

        loop_rows(tokens, 256, body)

    def branch(b):
        at = pl.ds(b * tokens, tokens)

        def body(s, carry):
            for j in range(per):
                got = dot_f32(mixed[at, :], w_out[s * per + j])
                part[b, s, :, pl.ds(j * rows_d, rows_d)] = got.astype(jnp.bfloat16)
            return carry

        lax.fori_loop(0, stripes, body, 0)

    def rise(b, cut):
        def body(r):
            at = pl.ds(b * tokens + r, 256)
            for k in range(cut.size // 256):
                cols = pl.ds(cut.start + k * 256, 256)
                got = dot_f32(normed[at, :], w_up[:, cols])
                got = jnp.maximum(got, 0.0) * width_mask[at, :]
                upper[at, cols] = got.astype(jnp.bfloat16)
                active[at, cols] = (got * got).astype(jnp.bfloat16)

        loop_rows(tokens, 256, body)

    def fall(m):
        place = p.block(m)
        s = place // per
        cols = pl.ds(pl.multiple_of((place % per) * rows_d, rows_d), rows_d)
        first = not started
        started.append(m)

        def body(r):
            b, at = r // tokens, pl.ds(pl.multiple_of(r % tokens, 256), 256)
            rows = pl.ds(r, 256)
            part[b, s, at, cols] = dot_f32(active[rows, :], w_down[place]).astype(jnp.bfloat16)
            got = dot_nt(rows_c[b, s, at, cols], w_down[place])
            grad_active[rows, :] = got if first else grad_active[rows, :] + got

        loop_rows(2 * tokens, 256, body)

    def turn(r):
        at = pl.ds(r, 64)
        active[at, :] = (grad_active[at, :] * 2.0 * wide(upper[at, :])).astype(jnp.bfloat16)

    q.z()
    v.x()
    round_rows(residual, rows1.at[0, p.t], tokens)
    o.z()
    q.x()
    a1.z()
    o.far()
    tr.send("info", infos.at[0], infos.at[1], p.z)
    q.far()
    a1.c()
    d.x()
    q.x_next(2)
    a1.y()
    q.far_next()
    o.far_next()
    tr.wait("info")
    fill_tables(
        infos, place_cosine, place_sine, p.t, cosine, sine, head_mask, width_mask, seg_col, seg_row
    )
    u.x()
    a1.pass_z()
    q.x_next(6)
    a1.pass_y(1)
    a1.take(1)
    norm_rows(rows1, 1, gain1, shift1, normed)
    round_rows(cotangent, rows_c.at[0, p.t], tokens)
    v.z()
    a1.pass_y(0)
    o.x()
    o.x_next(4)
    ac.y()
    u.z()
    a1.take(0)
    norm_rows(rows1, 0, gain1, shift1, normed)
    mv.start("stream1", rows1, stream1)
    mv.start("normed1", normed, normed1)
    e.z()
    v.far()
    q.x_next(4)
    o.x_next(6)
    o.x_next(2)
    v.far_next()
    q.end()
    project(1)
    attend(
        1, qkv, seg_col, seg_row, head_mask, weights, mixed, HD ** (-0.5)
    )
    o.end()
    branch(1)
    project(0)
    mv.start("all_qkv", w_qkv, all_qkv)
    v.x_next(6)
    s1.c(1)
    s1.y(1)
    s1.own(1)
    d.z()
    u.far_next()
    attend(
        0, qkv, seg_col, seg_row, head_mask, weights, mixed, HD ** (-0.5)
    )
    mv.start("heads", qkv, heads_out)
    mv.start("weights", weights, weights_out)
    mv.start("mixed", mixed, mixed_out)
    ac.c()
    s1.z()
    u.x_next(2)
    branch(0)
    mv.start("all_out", w_out, all_out)
    s1.c(0)
    u.far()
    s1.y(0)
    e.x_next(2)
    e.x()
    v.x_next(4)
    s1.own(0)
    v.x_next(2)
    s1.home()
    s1.end(middle, residual)
    round_rows(middle, rows2.at[0, p.t], tokens)
    mv.start("middle", middle, middle_out)
    a2.z()
    ac.z()
    e.far()
    a2.y()
    d.far_next()
    e.far_next()
    a2.c()
    d.far()
    u.x_next(4)
    a2.pass_y(0)
    d.x_next(2)
    u.x_next(6)
    a2.pass_z()
    ac.pass_z()
    ac.pass_y(0)
    a2.take(0)
    mv.wait("normed1")
    norm_rows(rows2, 0, gain2, shift2, normed)
    a2.pass_y(1)
    a2.take(1)
    norm_rows(rows2, 1, gain2, shift2, normed)
    mv.start("stream2", rows2, stream2)
    mv.start("normed2", normed, normed2)
    e.x_next(6)
    u.end()
    rise(0, parts[0])
    v.end()
    rise(1, parts[1])
    rise(1, parts[0])
    d.x_next(4)
    ac.pass_y(1)
    rise(0, parts[1])
    mv.start("active", active, active_out)
    mv.start("all_up", w_up, all_up)
    ac.take(0)
    ac.take(1)
    s1.sent()
    d.take(3)
    e.take(3)
    fall(3)
    mv.start("stream_c", rows_c, stream_c)
    e.x_next(4)
    d.take(1)
    e.take(1)
    fall(1)
    d.take(4)
    e.take(4)
    fall(4)
    d.take(0)
    e.take(0)
    fall(0)
    d.x_next(6)
    d.take(6)
    e.take(6)
    fall(6)
    d.take(2)
    e.take(2)
    fall(2)
    d.take(5)
    e.take(5)
    fall(5)
    d.take(7)
    e.take(7)
    fall(7)
    mv.start("part", part, part_out)
    mv.wait("active")
    loop_rows(2 * tokens, 64, turn)
    mv.start("grad_upper", active, grad_upper_out)
    tr.finish()
    mv.finish()


def forward_call(arrays, weights):
    bf16, f32 = jnp.bfloat16, jnp.float32
    tokens, columns = arrays[0].shape
    w_qkv, w_out, w_up, w_down = weights
    count, stripes = lax.axis_size("dp"), lax.axis_size("tensor")
    rows_d = w_up.shape[0]
    head_cols = w_out.shape[0] // 2
    hidden = w_up.shape[1] // 2
    width = rows_d * count
    heads = head_cols // HD
    slots = (2, stripes, tokens, columns)
    tables = dict(
        cosine=((2 * tokens, HD), f32),
        sine=((2 * tokens, HD), f32),
        head_mask=((2 * tokens, 1), f32),
    )
    shapes = dict(
        all_qkv=((3, width, head_cols), bf16),
        all_out=((count, head_cols, rows_d), bf16),
        all_up=((width, hidden), bf16),
        stream1=(slots, bf16),
        stream2=(slots, bf16),
        stream_c=(slots, bf16),
        normed1=((2 * tokens, width), bf16),
        normed2=((2 * tokens, width), bf16),
        heads=((3, 2 * tokens, head_cols), bf16),
        weights=((2 * heads, tokens, tokens), bf16),
        mixed=((2 * tokens, head_cols), bf16),
        active=((2 * tokens, hidden), bf16),
        grad_upper=((2 * tokens, hidden), bf16),
        part_out=(slots, bf16),
        middle=((tokens, columns), f32),
    )

    def vmem(name):
        return pltpu.VMEM(*shapes[name])

    scratch = [
        vmem("all_qkv"),
        vmem("all_out"),
        vmem("all_up"),
        pltpu.VMEM((count, hidden, rows_d), bf16),
        vmem("stream1"),
        vmem("stream2"),
        vmem("stream_c"),
        vmem("normed1"),
        vmem("heads"),
        vmem("weights"),
        vmem("mixed"),
        pltpu.VMEM(slots, bf16),
        pltpu.VMEM((2, 2, tokens, columns), bf16),
        pltpu.VMEM((2, tokens, columns), bf16),
        pltpu.VMEM((tokens, columns), bf16),
        vmem("active"),
        vmem("active"),
        pltpu.VMEM((2 * tokens, hidden), f32),
        vmem("middle"),
        pltpu.VMEM((2, 24, 128), f32),
        pltpu.VMEM((2 * tokens, 1), f32),
        pltpu.VMEM((2, 1, tokens), f32),
        pltpu.VMEM((2 * tokens, 1), f32),
        pltpu.SemaphoreType.DMA((72,)),
        pltpu.SemaphoreType.DMA((72,)),
        pltpu.SemaphoreType.DMA((32,)),
    ]
    any_spec = pl.BlockSpec(memory_space=pl.ANY)
    vmem_spec = pl.BlockSpec(memory_space=pltpu.VMEM)
    smem_spec = pl.BlockSpec(memory_space=pltpu.SMEM)
    outs = pl.pallas_call(
        forward_kernel,
        out_shape=[jax.ShapeDtypeStruct(*s) for s in (tables | shapes).values()],
        in_specs=[vmem_spec] * 6 + [smem_spec] * 3 + [vmem_spec] * 2 + [any_spec] * 4,
        out_specs=[vmem_spec] * len(tables) + [any_spec] * len(shapes),
        scratch_shapes=scratch,
        compiler_params=pltpu.CompilerParams(
            collective_id=0, has_side_effects=True, vmem_limit_bytes=62 << 20
        ),
    )(*arrays, *weights)
    split = len(tables)
    return outs[:split], dict(zip(shapes, outs[split:]))


class WeightScatter:
    def __init__(self, name, place, traffic, odd, even, got_x, got_far, out):
        self.name, self.p, self.tr = name, place, traffic
        self.odd, self.even, self.got_x, self.got_far, self.out = odd, even, got_x, got_far, out

    def send_x(self, m):
        self.tr.send(self.name + "x" + str(m), self.odd.at[m // 2], self.got_x.at[m // 2], self.p.x)

    def add_x(self, m):
        k, n = m // 2, self.name
        own = self.even.at[k]
        self.tr.wait(n + "x" + str(m + 1))
        add_blocks(own, own, self.got_x.at[k], own.shape[0])
        if m >= 4:
            self.tr.send(n + "f" + str(m), own, self.got_far.at[3 - k], self.p.far)

    def add_far(self, m):
        k, n = m // 2, self.name
        own = self.even.at[k]
        self.tr.wait(n + "f" + str(6 - m))
        add_blocks(own, own, self.got_far.at[k], own.shape[0])
        if m == 2:
            for j, (cut, spot) in enumerate(self.out(self.p.side)):
                self.tr.send(n + "z" + str(j), own.at[:, cut], spot, self.p.z)

    def end(self, moves):
        for j, (cut, spot) in enumerate(self.out(self.p.side)):
            moves.start(self.name + str(j), self.even.at[0, :, cut], spot)
            self.tr.wait(self.name + "z" + str(j))


class SumAll:
    def __init__(self, name, place, traffic, sums, got):
        self.name, self.tr, self.sums, self.got = name, traffic, sums, got
        self.partners = (place.c, place.y, place.x, place.z, place.far)

    def start(self, k):
        self.tr.send(self.name + str(k), self.sums, self.got.at[k], self.partners[k])

    def step(self, k):
        self.tr.wait(self.name + str(k))
        self.tr.sent(self.name + str(k))
        self.sums[...] += self.got[k]
        if k + 1 < len(self.partners):
            self.start(k + 1)


def norm_back(b, part, slots, gain, total):
    stripes, rows, columns = part.shape[1:]
    fold = (4, 8, stripes * columns)

    def body(r):
        at = pl.ds(r, 32)
        value = wide(slots[pl.ds(b * rows + r, 32), :])
        center = value - jnp.mean(value, axis=1, keepdims=True)
        spread = jnp.mean(center * center, axis=1, keepdims=True)
        inverse = lax.rsqrt(spread + epsilon)
        unit = center * inverse
        grad = jnp.concatenate([wide(part[b, s, at, :]) for s in range(stripes)], axis=1)
        scaled = grad * gain[...]
        push = inverse * (
            scaled
            - jnp.mean(scaled, axis=1, keepdims=True)
            - unit * jnp.mean(scaled * unit, axis=1, keepdims=True)
        )
        for s in range(stripes):
            part[b, s, at, :] = push[:, s * columns : (s + 1) * columns].astype(jnp.bfloat16)
        total[0] += jnp.sum((grad * unit).reshape(fold), axis=0)
        total[1] += jnp.sum(grad.reshape(fold), axis=0)

    if b == 1:
        total[...] = jnp.zeros_like(total)
    loop_rows(rows, 32, body)


def attend_back(b, qkv, weights, grad_mixed, cosine, sine, out, tokens, scale):
    width = grad_mixed.shape[1]
    heads = width // HD
    half = tokens // 2
    start = b * tokens

    def turn_back(grad, rows):
        return (grad * cosine[rows, :] - pltpu.roll(grad, HD // 2, 1) * sine[rows, :]).astype(
            jnp.bfloat16
        )

    for h in range(heads):
        spots = [pl.ds(k * width + h * HD, HD) for k in range(3)]
        grad_key, grad_value = None, None
        for part in (1, 0):
            rows = pl.ds(start + part * half, half)
            reach = pl.ds(start, half * (part + 1))
            query, key, value = qkv[rows, spots[0]], qkv[reach, spots[1]], qkv[reach, spots[2]]
            given = grad_mixed[rows, pl.ds(h * HD, HD)]
            chosen = weights[b * heads + h, pl.ds(part * half, half), pl.ds(0, half * (part + 1))]
            grad = dot_nt(given, value)
            soft = wide(chosen)
            grad = soft * (grad - jnp.sum(grad * soft, axis=1, keepdims=True))
            raw = (grad * scale).astype(jnp.bfloat16)
            out[rows, spots[0]] = turn_back(dot_f32(raw, key), rows)
            key_part, value_part = dot_tn(raw, query), dot_tn(chosen, given)
            if part == 1:
                grad_key, grad_value = key_part, value_part
        low, high = pl.ds(start, half), pl.ds(start + half, half)
        out[low, spots[1]] = turn_back(grad_key[:half] + key_part, low)
        out[high, spots[1]] = turn_back(grad_key[half:], high)
        out[low, spots[2]] = (grad_value[:half] + value_part).astype(jnp.bfloat16)
        out[high, spots[2]] = grad_value[half:].astype(jnp.bfloat16)


def backward_kernel(
    cotangent,
    gain1,
    gain2,
    cosine,
    sine,
    head_mask,
    lengths,
    width_bucket,
    all_qkv,
    all_out,
    all_up,
    stream1,
    stream2,
    stream_c,
    normed1,
    normed2,
    heads,
    weights_in,
    mixed_in,
    active_in,
    grad_upper_in,
    part_in,
    middle_in,
    output,
    grad_input,
    sums2_out,
    sums1_out,
    grad_qkv,
    grad_out,
    grad_up,
    grad_down,
    w_up,
    w_out,
    rows_a,
    rows_b,
    active,
    grad_upper,
    part_a,
    part_b,
    got_ca,
    got_ya,
    got_za,
    got_cb,
    got_yb,
    got_zb,
    stream_b,
    weights,
    mixed,
    grad_mixed,
    odd,
    even_down,
    even_up,
    odd_out,
    even_out,
    gx_down,
    gf_down,
    gx_up,
    gf_up,
    gx_qkv,
    gf_qkv,
    gx_out,
    gf_out,
    middle,
    grad_middle,
    total,
    sums2,
    got2,
    sums1,
    got1,
    send_sems,
    recv_sems,
    move_sems,
):
    p = Place()
    tr, mv = Traffic(send_sems, recv_sems), Moves(move_sems)
    tokens, columns = cotangent.shape
    stripes, blocks = part_a.shape[1], all_out.shape[0]
    rows_d = all_out.shape[2]
    per = blocks // stripes
    head_cols = mixed.shape[1]
    bf16 = jnp.bfloat16

    def load_stream(name, src, dst):
        for b in range(2):
            for s in range(stripes):
                spot = dst.at[pl.ds(b * tokens, tokens), pl.ds(s * columns, columns)]
                mv.start(name + str(b) + str(s), src.at[b, s], spot)

    def wait_stream(name):
        mv.wait(*[name + str(b) + str(s) for b in range(2) for s in range(stripes)])

    s_out = ActScatter("s", p, tr, part_a, got_ca, got_ya, got_za)
    s2 = ActScatter("t", p, tr, part_b, got_cb, got_yb, got_zb)
    s1 = ActScatter("r", p, tr, part_b, got_cb, got_yb, got_zb)
    ab = ActGather("b", p, tr, stream_b)
    qkv_cols = pl.ds(0, 3 * head_cols)
    hidden = active.shape[1]
    parts = [pl.ds(0, hidden // 2), pl.ds(hidden // 2, hidden // 2)]

    def at_side(k, cut, size):
        return pl.ds(pl.multiple_of(k * size + cut.start, 128), cut.size)

    def scatter(name, odd, even, got_x, got_far, out, cols):
        views = [ref.at[:, :, cols] for ref in (odd, even, got_x, got_far)]

        def spots(k):
            if len(out.shape) == 3:
                return [
                    (pl.ds(j * head_cols, head_cols), out.at[j, :, at_side(k, heads_cut, head_cols)])
                    for j in range(3)
                ]
            spot = out.at[:, at_side(k, cols, out.shape[1] // 2)]
            return [(pl.ds(0, cols.size), spot)]

        return WeightScatter(name, p, tr, *views, spots)

    heads_cut = pl.ds(0, head_cols)

    d, e = [
        scatter(n, odd, even_down, gx_down, gf_down, grad_down, cut) for n, cut in zip("de", parts)
    ]
    u, v = [scatter(n, odd, even_up, gx_up, gf_up, grad_up, cut) for n, cut in zip("uv", parts)]
    q = scatter("q", odd, even_down, gx_qkv, gf_qkv, grad_qkv, qkv_cols)
    o = scatter("o", odd_out, even_out, gx_out, gf_out, grad_out, pl.ds(0, head_cols))
    all2 = SumAll("2", p, tr, sums2, got2)
    all1 = SumAll("1", p, tr, sums1, got1)

    load_stream("c", stream_c, rows_a)
    mv.start("active", active_in, active)
    mv.start("grad_upper", grad_upper_in, grad_upper)
    mv.start("all_up", all_up, w_up)
    load_stream("x2", stream2, rows_b)
    mv.start("mixed", mixed_in, mixed)
    mv.start("weights", weights_in, weights)
    for k in range(blocks):
        mv.start("p" + str(k), all_out.at[k], w_out.at[:, pl.ds(k * rows_d, rows_d)])
    mv.start("part", part_in, part_a)
    mv.start("middle", middle_in, middle)
    p.greet()

    def block_cols(m):
        return pl.ds(pl.multiple_of(p.block(m) * rows_d, rows_d), rows_d)

    def grad_block(left, right, m, spot, cols=None):
        value = right[...] if cols is None else right[:, cols]
        spot[...] = dot_tn(left[:, block_cols(m)], value).astype(bf16)

    def down_block(m, spot):
        grad_block(rows_a, active, m, spot)

    def product(b, left, right, cols):
        at = pl.ds(b * tokens, tokens)

        def body(s, carry):
            rows = pl.ds(pl.multiple_of(s * columns, columns), columns)
            part_b[b, s] = dot_nt(left[at, cols], right[rows, cols]).astype(bf16)
            return carry

        lax.fori_loop(0, stripes, body, 0)

    def gather_total(sums):
        sums[...] = jnp.concatenate(
            [
                jnp.sum(total[0], axis=0, keepdims=True),
                jnp.sum(total[1], axis=0, keepdims=True),
                jnp.concatenate(
                    [
                        count_row(lengths, width_bucket, HD),
                        jnp.zeros((1, total.shape[2] - HD), jnp.float32),
                    ],
                    axis=1,
                ),
                jnp.zeros((5, total.shape[2]), jnp.float32),
            ],
            axis=0,
        )

    def up_block(m, spot):
        grad_block(rows_a, grad_upper, m, spot)

    def up_odd(m):
        tr.sent("dx" + str(m), "ex" + str(m))
        up_block(m, odd.at[m // 2])
        u.send_x(m)
        v.send_x(m)

    def mix(b):
        mv.wait(*["p" + str(k) for k in range(blocks)])
        at = pl.ds(b * tokens, tokens)
        got = None
        for s in range(stripes):
            one = dot_nt(stream_b[b, s], w_out[:, pl.ds(s * columns, columns)])
            got = one if got is None else got + one
        grad_mixed[at, :] = (got * head_mask[at, :]).astype(bf16)

    def out_block(m, spot):
        mv.wait("mixed")
        place = p.block(m)
        cols = pl.ds(pl.multiple_of((place % per) * rows_d, rows_d), rows_d)
        near = dot_tn(stream_b[0, place // per, :, cols], mixed[pl.ds(0, tokens), :])
        away = dot_tn(stream_b[1, place // per, :, cols], mixed[pl.ds(tokens, tokens), :])
        spot[...] = (near + away).astype(bf16)

    def qkv_block(m, spot):
        mv.wait("normed1")
        grad_block(rows_b, grad_upper, m, spot, qkv_cols)

    def qkv_odd(m):
        tr.sent("ux" + str(m), "vx" + str(m))
        qkv_block(m, odd.at[m // 2, :, qkv_cols])
        q.send_x(m)

    def qkv_even(m):
        mv.wait("d0", "e0")
        tr.sent("df4", "df6", "dz0", "ef4", "ef6", "ez0")
        qkv_block(m, even_down.at[m // 2, :, qkv_cols])

    wait_stream("c")
    mv.wait("active")
    down_block(5, odd.at[2])
    d.send_x(5)
    e.send_x(5)
    mv.wait("grad_upper", "all_up")
    product(1, grad_upper, w_up, pl.ds(0, w_up.shape[1]))
    wait_stream("x2")
    norm_back(1, part_b, rows_b, gain2, total)
    s2.c(1)
    down_block(4, even_down.at[2])
    d.add_x(4)
    s2.y(1)
    mv.wait("part")
    down_block(3, odd.at[1])
    d.send_x(3)
    e.send_x(3)
    product(0, grad_upper, w_up, pl.ds(0, w_up.shape[1]))
    norm_back(0, part_b, rows_b, gain2, total)
    e.add_x(4)
    s2.c(0)
    down_block(2, even_down.at[1])
    down_block(0, even_down.at[0])
    s2.own(1)
    down_block(7, odd.at[3])
    d.send_x(7)
    e.send_x(7)
    s2.y(0)
    s_out.c(1)
    down_block(6, even_down.at[3])
    s2.own(0)
    down_block(1, odd.at[0])
    d.send_x(1)
    e.send_x(1)
    s2.z()
    d.add_x(6)
    d.add_x(2)
    s2.home()
    s2.end(grad_middle, cotangent)
    round_rows(grad_middle, stream_b.at[0, p.t], tokens)
    for k in range(3):
        mv.start("h" + str(k), heads.at[k], active.at[:, pl.ds(k * head_cols, head_cols)])
    mv.start("normed2", normed2, rows_a)
    mv.wait("normed2")
    e.add_x(2)
    up_block(6, even_up.at[3])
    ab.y()
    up_odd(5)
    up_block(2, even_up.at[1])
    s_out.y(1)
    e.add_far(2)
    ab.z()
    e.add_x(6)
    up_block(0, even_up.at[0])
    gather_total(sums2)
    all2.start(0)
    up_odd(7)
    up_block(4, even_up.at[2])
    s_out.own(1)
    u.add_x(4)
    v.add_x(4)
    s_out.c(0)
    ab.c()
    ab.pass_z()
    up_odd(1)
    d.add_x(0)
    ab.pass_y(0)
    ab.pass_y(1)
    up_odd(3)
    d.add_far(2)
    ab.take(0)
    mix(0)
    e.add_x(0)
    load_stream("x1", stream1, rows_a)
    s_out.z()
    ab.take(1)
    out_block(2, even_out.at[1])
    v.add_x(6)
    e.add_far(0)
    d.add_far(0)
    out_block(3, odd_out.at[1])
    o.send_x(3)
    mix(1)
    mv.wait("weights", "h0", "h1", "h2")
    attend_back(
        1, active, weights, grad_mixed, cosine, sine, grad_upper, tokens, HD ** (-0.5)
    )
    s_out.y(0)
    all2.step(0)
    u.add_x(6)
    d.end(mv)
    attend_back(
        0, active, weights, grad_mixed, cosine, sine, grad_upper, tokens, HD ** (-0.5)
    )
    for k in range(3):
        mv.start("w" + str(k), all_qkv.at[k], w_up.at[:, pl.ds(k * head_cols, head_cols)])
    mv.start("normed1", normed1, rows_b)
    out_block(5, odd_out.at[2])
    o.send_x(5)
    u.add_x(2)
    qkv_odd(7)
    s2.sent()
    mv.wait("w0", "w1", "w2")
    product(1, grad_upper, w_up, qkv_cols)
    wait_stream("x1")
    norm_back(1, part_b, rows_a, gain1, total)
    product(0, grad_upper, w_up, qkv_cols)
    norm_back(0, part_b, rows_a, gain1, total)
    all2.step(1)
    s1.c(0)
    out_block(4, even_out.at[2])
    o.add_x(4)
    s1.c(1)
    u.add_far(2)
    v.add_x(0)
    s1.y(0)
    out_block(6, even_out.at[3])
    o.add_x(2)
    v.add_x(2)
    e.end(mv)
    v.add_far(0)
    out_block(0, even_out.at[0])
    qkv_even(6)
    out_block(7, odd_out.at[3])
    o.send_x(7)
    qkv_odd(5)
    s1.y(1)
    gather_total(sums1)
    all1.start(0)
    v.add_far(2)
    u.add_x(0)
    o.add_far(2)
    qkv_even(2)
    qkv_odd(3)
    s1.own(0)
    q.add_x(6)
    all1.step(0)
    qkv_even(0)
    s1.home()
    qkv_odd(1)
    all2.step(2)
    qkv_even(4)
    s1.own(1)
    s_out.own(0)
    s_out.home()
    q.add_x(2)
    s1.z()
    q.add_x(4)
    o.add_x(6)
    q.add_x(0)
    all1.step(1)
    out_block(1, odd_out.at[0])
    o.send_x(1)
    u.add_far(0)
    all1.step(2)
    all2.step(3)
    all1.step(3)
    s1.end(grad_middle, grad_middle)
    mv.start("grad_input", grad_middle, grad_input)
    u.end(mv)
    o.add_x(0)
    q.add_far(2)
    v.end(mv)
    q.add_far(0)
    all1.step(4)
    all2.step(4)
    mv.wait("middle")
    s_out.end(middle, middle)
    mv.start("output", middle, output)
    o.add_far(0)
    o.end(mv)
    q.end(mv)
    sums2_out[...] = sums2[...]
    sums1_out[...] = sums1[...]
    tr.finish()
    mv.finish()


def backward_call(arrays, saved):
    bf16, f32 = jnp.bfloat16, jnp.float32
    tokens, columns = arrays[0].shape
    count, stripes = lax.axis_size("dp"), lax.axis_size("tensor")
    _, head_cols, rows_d = saved["all_out"].shape
    width, hidden = saved["all_up"].shape
    slots = (2, stripes, tokens, columns)
    wide_rows = (2 * tokens, width)

    def vmem(*shape, dtype=bf16):
        return pltpu.VMEM(shape, dtype)

    def got(cols):
        return [vmem(4, rows_d, cols), vmem(2, rows_d, cols)]

    got_act = [vmem(2, 2, tokens, columns), vmem(2, tokens, columns), vmem(tokens, columns)]
    sums = [vmem(8, width, dtype=f32), vmem(5, 8, width, dtype=f32)]
    qkv = 3 * head_cols
    scratch = [
        vmem(width, hidden),
        vmem(head_cols, width),
        vmem(*wide_rows),
        vmem(*wide_rows),
        vmem(2 * tokens, hidden),
        vmem(2 * tokens, hidden),
        vmem(*slots),
        vmem(*slots),
        *got_act,
        *got_act,
        vmem(*slots),
        vmem(*saved["weights"].shape),
        vmem(2 * tokens, head_cols),
        vmem(2 * tokens, head_cols),
        vmem(4, rows_d, hidden),
        vmem(4, rows_d, hidden),
        vmem(4, rows_d, hidden),
        vmem(4, rows_d, head_cols),
        vmem(4, rows_d, head_cols),
        *got(hidden),
        *got(hidden),
        *got(qkv),
        *got(head_cols),
        vmem(tokens, columns, dtype=f32),
        vmem(tokens, columns, dtype=f32),
        vmem(2, 8, width, dtype=f32),
        *sums,
        *sums,
        pltpu.SemaphoreType.DMA((84,)),
        pltpu.SemaphoreType.DMA((84,)),
        pltpu.SemaphoreType.DMA((72,)),
    ]
    any_spec = pl.BlockSpec(memory_space=pl.ANY)
    vmem_spec = pl.BlockSpec(memory_space=pltpu.VMEM)
    smem_spec = pl.BlockSpec(memory_space=pltpu.SMEM)
    shapes = [
        ((tokens, columns), f32),
        ((tokens, columns), f32),
        ((8, width), f32),
        ((8, width), f32),
        ((3, rows_d, 2 * head_cols), bf16),
        ((rows_d, 2 * head_cols), bf16),
        ((rows_d, 2 * hidden), bf16),
        ((rows_d, 2 * hidden), bf16),
    ]
    names = [k for k in saved]
    return pl.pallas_call(
        backward_kernel,
        out_shape=[jax.ShapeDtypeStruct(*s) for s in shapes],
        in_specs=[vmem_spec] * 6 + [smem_spec] * 2 + [any_spec] * len(names),
        out_specs=[any_spec] * 2 + [vmem_spec] * 2 + [any_spec] * 4,
        scratch_shapes=scratch,
        compiler_params=pltpu.CompilerParams(
            collective_id=1, has_side_effects=True, vmem_limit_bytes=63 << 20
        ),
    )(*arrays, *[saved[n] for n in names])


def local_fast(
    residual_in,
    lengths,
    head_bucket,
    width_bucket,
    norm1_gain,
    norm1_shift,
    w_qkv,
    w_out,
    norm2_gain,
    norm2_shift,
    w_up,
    w_down,
    cotangent,
):
    f32 = jnp.float32
    tokens = residual_in.shape[0]
    steps = np.arange(tokens)[:, None] * 10000.0 ** (-2.0 * (np.arange(HD) % (HD // 2)) / HD)
    arrays = (
        residual_in,
        cotangent,
        norm1_gain[None],
        norm1_shift[None],
        norm2_gain[None],
        norm2_shift[None],
        lengths,
        head_bucket,
        width_bucket,
        jnp.asarray(np.cos(steps), f32),
        jnp.asarray(np.sin(steps), f32),
    )
    weights = (jnp.swapaxes(w_qkv, 0, 1), w_out, w_up, w_down)
    (cosine, sine, head_mask), saved = forward_call(arrays, weights)
    arrays = (cotangent, norm1_gain[None], norm2_gain[None], cosine, sine, head_mask)
    output, grad_input, sums2, sums1, grad_qkv, grad_out, grad_up, grad_down = backward_call(
        (*arrays, lengths, width_bucket), saved
    )
    total = lax.axis_size("tensor")
    return (
        output,
        grad_input,
        sums1[0],
        sums1[1],
        jnp.swapaxes(grad_qkv, 0, 1).astype(f32),
        grad_out.T.astype(f32),
        sums2[0],
        sums2[1],
        grad_up.astype(f32),
        grad_down.T.astype(f32),
        (sums2[2, :total] / total).astype(jnp.int32),
    )


def local(*args):
    w_out = args[7]
    if lax.axis_size("dp") == 8 and lax.axis_size("tensor") == 4 and w_out.shape[1] % 128 == 0:
        return local_fast(*args)
    return local_general(*args)


def solution(mesh):
    placed = (
        P("dp", "tensor"),
        P("dp", None),
        P("dp", None),
        P("dp", None),
        P(),
        P(),
        P("dp", None, "tensor"),
        P("tensor", "dp"),
        P(),
        P(),
        P("dp", "tensor"),
        P("tensor", "dp"),
        P("dp", "tensor"),
    )
    return jax.shard_map(
        local,
        mesh=mesh,
        in_specs=placed,
        out_specs=(
            P("dp", "tensor"),
            P("dp", "tensor"),
            P(),
            P(),
            P("dp", None, "tensor"),
            P("tensor", "dp"),
            P(),
            P(),
            P("dp", "tensor"),
            P("tensor", "dp"),
            P(),
        ),
        check_vma=False,
    )
```

```python
import functools
import math

import jax
import jax.numpy as jnp
import numpy as np
from jax import lax
from jax.experimental import pallas as pl
from jax.experimental.pallas import tpu as pltpu
from jax.sharding import PartitionSpec as P

HD = 128
HIDDEN_BIT = 2

epsilon = 1e-05


def dp_swap(value, bit):
    count = lax.axis_size("dp")
    return lax.ppermute(value, "dp", [(i, i ^ bit) for i in range(count)])


def tensor_swap(value, bit):
    count = lax.axis_size("tensor")
    return lax.ppermute(value, "tensor", [(i, i ^ bit) for i in range(count)])


def bits_of(count):
    return [1 << i for i in range(count.bit_length() - 1)]


def replica_bits():
    bits = bits_of(lax.axis_size("dp"))
    return [b for b in bits if b > HIDDEN_BIT] + [b for b in bits if b < HIDDEN_BIT]


def gather_weight(mine, other):
    blocks = {0: mine, HIDDEN_BIT: dp_swap(other, HIDDEN_BIT)}
    for bit in replica_bits():
        blocks.update({m | bit: dp_swap(blocks[m], bit) for m in list(blocks)})
    return blocks


def add_low(left, right):
    return (left.astype(jnp.float32) + right.astype(jnp.float32)).astype(jnp.bfloat16)


def scatter_weight(blocks):
    for bit in reversed(replica_bits()):
        arrived = {m ^ bit: dp_swap(blocks[m], bit) for m in blocks if m & bit}
        blocks = {m: add_low(blocks[m], arrived[m]) for m in arrived}
    return blocks[0], dp_swap(blocks[HIDDEN_BIT], HIDDEN_BIT)


def gather_act(rows):
    blocks = {(0, 0): rows, (1, 0): dp_swap(rows, HIDDEN_BIT)}
    for bit in reversed(bits_of(lax.axis_size("tensor"))):
        blocks.update({(b, m | bit): tensor_swap(v, bit) for (b, m), v in list(blocks.items())})
    return blocks


def scatter_act(blocks):
    for bit in bits_of(lax.axis_size("tensor")):
        arrived = {(b, m ^ bit): tensor_swap(v, bit) for (b, m), v in blocks.items() if m & bit}
        blocks = {k: add_low(blocks[k], arrived[k]) for k in arrived}
    return blocks[(0, 0)].astype(jnp.float32) + dp_swap(blocks[(1, 0)], HIDDEN_BIT).astype(
        jnp.float32
    )


def lay(blocks, shape, spots):
    count = len(blocks)

    def kernel(*refs):
        ins, out, sems = refs[:count], refs[count], refs[count + 1]
        copies = []
        for i, spot in enumerate(spots()):
            r, c = blocks[i].shape
            copies.append(
                pltpu.make_async_copy(
                    ins[i],
                    out.at[pl.ds(pl.multiple_of(spot[0], 16), r), pl.ds(pl.multiple_of(spot[1], 128), c)],
                    sems.at[i],
                )
            )
        for copy in copies:
            copy.start()
        for copy in copies:
            copy.wait()

    return pl.pallas_call(
        kernel,
        out_shape=jax.ShapeDtypeStruct(shape, jnp.bfloat16),
        in_specs=[pl.BlockSpec(memory_space=pl.ANY)] * count,
        out_specs=pl.BlockSpec(memory_space=pltpu.VMEM),
        scratch_shapes=[pltpu.SemaphoreType.DMA((count,))],
        compiler_params=pltpu.CompilerParams(vmem_limit_bytes=24 << 20),
    )(*blocks)


def cut(whole, block_shape, count, spots):
    def kernel(*refs):
        src, outs, sems = refs[0], refs[1 : 1 + count], refs[1 + count]
        r, c = block_shape
        copies = []
        for i, spot in enumerate(spots()):
            copies.append(
                pltpu.make_async_copy(
                    src.at[pl.ds(pl.multiple_of(spot[0], 16), r), pl.ds(pl.multiple_of(spot[1], 128), c)],
                    outs[i],
                    sems.at[i],
                )
            )
        for copy in copies:
            copy.start()
        for copy in copies:
            copy.wait()

    return pl.pallas_call(
        kernel,
        out_shape=[jax.ShapeDtypeStruct(block_shape, jnp.bfloat16)] * count,
        in_specs=[pl.BlockSpec(memory_space=pltpu.VMEM)],
        out_specs=[pl.BlockSpec(memory_space=pl.ANY)] * count,
        scratch_shapes=[pltpu.SemaphoreType.DMA((count,))],
        compiler_params=pltpu.CompilerParams(vmem_limit_bytes=24 << 20),
    )(whole)


def lay_weight(blocks, axis):
    count = len(blocks)
    r, c = blocks[0].shape
    if axis == 1 and c % 128:
        order = jnp.bitwise_xor(lax.axis_index("dp"), jnp.arange(count))
        stacked = jnp.stack([blocks[m] for m in range(count)])[order]
        return jnp.swapaxes(stacked, 0, 1).reshape(r, count * c)

    def spots():
        place = lax.axis_index("dp")
        at = [jnp.bitwise_xor(place, m) for m in range(count)]
        return [(d * r, 0) if axis == 0 else (0, d * c) for d in at]

    shape = (r * count, c) if axis == 0 else (r, c * count)
    return lay([blocks[m] for m in range(count)], shape, spots)


def cut_weight(whole, axis):
    count = lax.axis_size("dp")
    r, c = whole.shape
    r, c = (r // count, c) if axis == 0 else (r, c // count)
    if axis == 1 and c % 128:
        order = jnp.bitwise_xor(lax.axis_index("dp"), jnp.arange(count))
        stacked = jnp.swapaxes(whole.reshape(r, count, c), 0, 1)[order]
        return {m: stacked[m] for m in range(count)}

    def spots():
        place = lax.axis_index("dp")
        at = [jnp.bitwise_xor(place, m) for m in range(count)]
        return [(d * r, 0) if axis == 0 else (0, d * c) for d in at]

    return dict(enumerate(cut(whole, (r, c), count, spots)))


def act_keys():
    return [(b, m) for b in range(2) for m in range(lax.axis_size("tensor"))]


def act_spots(r, c):
    place = lax.axis_index("tensor")
    return [(b * r, jnp.bitwise_xor(place, m) * c) for b, m in act_keys()]


def lay_act(blocks):
    r, c = blocks[(0, 0)].shape
    shape = (2 * r, c * lax.axis_size("tensor"))
    return lay([blocks[k] for k in act_keys()], shape, lambda: act_spots(r, c))


def cut_act(whole):
    r, c = whole.shape[0] // 2, whole.shape[1] // lax.axis_size("tensor")
    keys = act_keys()
    return dict(zip(keys, cut(whole, (r, c), len(keys), lambda: act_spots(r, c))))


def whole_stream(rows):
    return lay_act(gather_act(rows.astype(jnp.bfloat16)))


def stream_sum(rows):
    return scatter_act(cut_act(rows.astype(jnp.bfloat16)))


def sum_all(value, axes):
    if "dp" in axes:
        for bit in bits_of(lax.axis_size("dp")):
            value = value + dp_swap(value, bit)
    if "tensor" in axes:
        for bit in bits_of(lax.axis_size("tensor")):
            value = value + tensor_swap(value, bit)
    return value


def token_info(length_row, head_row, width_row, row_count):
    seq_ends = jnp.cumsum(length_row)
    seq_starts = seq_ends - length_row
    places = jnp.arange(row_count, dtype=jnp.int32)
    segment = jnp.sum((places[:, None] >= seq_ends[None, :]).astype(jnp.int32), axis=1)
    labels = jnp.arange(length_row.shape[0], dtype=jnp.int32)
    onehot = (segment[:, None] == labels[None, :]).astype(jnp.int32)
    offset = places - jnp.sum(onehot * seq_starts[None, :], axis=1)
    head_tok = jnp.sum(onehot * head_row[None, :], axis=1)
    width_tok = jnp.sum(onehot * width_row[None, :], axis=1)
    return (segment, offset, head_tok, width_tok)


def rotary_tables(offset, head_size):
    half_size = head_size // 2
    ladder = jnp.arange(half_size, dtype=jnp.float32)
    inverse = jnp.exp(ladder * (-2.0 * math.log(10000.0) / head_size))
    angles = offset.astype(jnp.float32)[:, None] * inverse[None, :]
    return (jnp.cos(angles)[:, None, :], jnp.sin(angles)[:, None, :])


def rotate(values, cosine, sine_part):
    half_size = values.shape[-1] // 2
    front_half = values[..., :half_size]
    back_half = values[..., half_size:]
    return jnp.concatenate(
        [front_half * cosine - back_half * sine_part, back_half * cosine + front_half * sine_part],
        axis=-1,
    )


def norm_forward(values, norm_gain, norm_shift):
    values = values.astype(jnp.float32)
    center = values - jnp.mean(values, axis=-1, keepdims=True)
    spread = jnp.mean(center * center, axis=-1, keepdims=True)
    inverse = lax.rsqrt(spread + epsilon)
    unit_rows = center * inverse
    return (unit_rows * norm_gain + norm_shift, unit_rows, inverse)


def norm_backward(grad_rows, unit_rows, inverse, norm_gain):
    scaled = grad_rows * norm_gain
    grad_in = inverse * (
        scaled
        - jnp.mean(scaled, axis=-1, keepdims=True)
        - unit_rows * jnp.mean(scaled * unit_rows, axis=-1, keepdims=True)
    )
    return (grad_in, jnp.sum(grad_rows * unit_rows, axis=0), jnp.sum(grad_rows, axis=0))


def heads_of(rows, blocks):
    rows = rows.reshape(blocks, rows.shape[0] // blocks, -1, HD)
    return jnp.transpose(rows, (2, 0, 1, 3)).reshape(-1, rows.shape[1], HD)


def rows_of(heads, blocks):
    heads = heads.reshape(-1, blocks, heads.shape[1], HD)
    return jnp.transpose(heads, (1, 2, 0, 3)).reshape(blocks * heads.shape[2], -1)


def local_general(
    residual_in,
    lengths,
    head_bucket,
    width_bucket,
    norm1_gain,
    norm1_shift,
    w_qkv,
    w_out,
    norm2_gain,
    norm2_shift,
    w_up,
    w_down,
    cotangent,
):
    f32, bf16 = jnp.float32, jnp.bfloat16
    dot = functools.partial(jnp.dot, preferred_element_type=f32)
    tensor_index = lax.axis_index("tensor")
    bucket_total = lax.axis_size("tensor")
    tokens = residual_in.shape[0]
    side = (lax.axis_index("dp") // HIDDEN_BIT) % 2

    def halves(weight, axis):
        left, right = jnp.split(weight, 2, axis=axis)
        return jnp.where(side == 0, left, right), jnp.where(side == 0, right, left)

    info = jnp.stack([lengths[0], head_bucket[0], width_bucket[0]])
    far_info = dp_swap(info, HIDDEN_BIT)
    pair = [token_info(i[0], i[1], i[2], tokens) for i in (info, far_info)]
    segment, offset, head_tok, width_tok = [jnp.stack([a, b]) for a, b in zip(*pair)]
    matches = (
        width_bucket[0][:, None] == jnp.arange(bucket_total, dtype=jnp.int32)[None, :]
    ).astype(jnp.int32)
    bucket_counts = sum_all(jnp.sum(lengths[0][:, None] * matches, axis=0), ("dp",))
    head_mask = (head_tok.reshape(-1) >= tensor_index).astype(f32)[:, None]
    width_mask = (width_tok.reshape(-1) >= tensor_index).astype(f32)[:, None]
    places = jnp.arange(tokens, dtype=jnp.int32)
    allowed = (segment[:, :, None] == segment[:, None, :]) & (
        places[:, None] >= places[None, :]
    )
    cosine, sine_part = rotary_tables(offset.reshape(-1), HD)
    score_scale = HD ** (-0.5)

    qkv_halves = [h.reshape(h.shape[0], -1) for h in halves(w_qkv, 2)]
    full_qkv = lay_weight(gather_weight(*qkv_halves), 0)
    full_out = lay_weight(gather_weight(*halves(w_out, 0)), 1)
    full_up = lay_weight(gather_weight(*halves(w_up, 1)), 0)
    full_down = lay_weight(gather_weight(*halves(w_down, 0)), 1)

    inputs = whole_stream(residual_in)
    normed1, unit1, inverse1 = norm_forward(inputs, norm1_gain, norm1_shift)
    normed1 = normed1.astype(bf16)
    projected = dot(normed1, full_qkv).reshape(2 * tokens, 3, -1, HD)
    width = projected.shape[2] * HD
    query = rotate(projected[:, 0], cosine, sine_part).astype(bf16).reshape(-1, width)
    key = rotate(projected[:, 1], cosine, sine_part).astype(bf16).reshape(-1, width)
    value = projected[:, 2].astype(bf16).reshape(-1, width)
    query, key, value = heads_of(query, 2), heads_of(key, 2), heads_of(value, 2)
    allowed = jnp.tile(allowed, (query.shape[0] // 2, 1, 1))
    scores = jnp.einsum("nqd,nkd->nqk", query, key, preferred_element_type=f32) * score_scale
    scores = jnp.where(allowed, scores, -1000000000.0)
    scores = jnp.exp(scores - jnp.max(scores, axis=-1, keepdims=True))
    weights = (scores / jnp.sum(scores, axis=-1, keepdims=True)).astype(bf16)
    mixed = jnp.einsum("nqk,nkd->nqd", weights, value, preferred_element_type=f32)
    mixed = (rows_of(mixed, 2) * head_mask).astype(bf16)
    middle = residual_in + stream_sum(dot(mixed, full_out))
    middle_rows = whole_stream(middle)
    normed2, unit2, inverse2 = norm_forward(middle_rows, norm2_gain, norm2_shift)
    normed2 = normed2.astype(bf16)
    upper = jnp.maximum(dot(normed2, full_up), 0.0) * width_mask
    active = jnp.square(upper).astype(bf16)
    upper = upper.astype(bf16)
    output = middle + stream_sum(dot(active, full_down))

    grad_top = whole_stream(cotangent)
    grad_down = scatter_weight(cut_weight(dot(active.T, grad_top).astype(bf16), 1))
    grad_active = dot(grad_top, full_down.T)
    grad_upper = (grad_active * 2.0 * upper.astype(f32)).astype(bf16)
    grad_normed2 = dot(grad_upper, full_up.T)
    part_middle, gain2_grad, shift2_grad = norm_backward(
        grad_normed2, unit2, inverse2, norm2_gain
    )
    grad_middle = cotangent + stream_sum(part_middle)
    grad_up = scatter_weight(cut_weight(dot(normed2.T, grad_upper).astype(bf16), 0))
    grad_branch = whole_stream(grad_middle)
    grad_wout = scatter_weight(cut_weight(dot(mixed.T, grad_branch).astype(bf16), 1))
    grad_mixed = (dot(grad_branch, full_out.T) * head_mask).astype(bf16)
    grad_mixed = heads_of(grad_mixed, 2)
    grad_weights = jnp.einsum("nqd,nkd->nqk", grad_mixed, value, preferred_element_type=f32)
    grad_value = jnp.einsum("nqk,nqd->nkd", weights, grad_mixed, preferred_element_type=f32)
    wide = weights.astype(f32)
    grad_scores = wide * (grad_weights - jnp.sum(grad_weights * wide, axis=-1, keepdims=True))
    grad_raw = (grad_scores * score_scale).astype(bf16)
    grad_query = jnp.einsum("nqk,nkd->nqd", grad_raw, key, preferred_element_type=f32)
    grad_key = jnp.einsum("nqk,nqd->nkd", grad_raw, query, preferred_element_type=f32)
    grad_query, grad_key = [
        rotate(rows_of(g, 2).reshape(2 * tokens, -1, HD), cosine, -sine_part).reshape(-1, width)
        for g in (grad_query, grad_key)
    ]
    grad_projected = jnp.concatenate([grad_query, grad_key, rows_of(grad_value, 2)], axis=1)
    grad_projected = grad_projected.astype(bf16)
    grad_normed1 = dot(grad_projected, full_qkv.T)
    part_input, gain1_grad, shift1_grad = norm_backward(
        grad_normed1, unit1, inverse1, norm1_gain
    )
    grad_input = grad_middle + stream_sum(part_input)
    grad_qkv = scatter_weight(cut_weight(dot(normed1.T, grad_projected).astype(bf16), 0))

    def join(pair, axis):
        left = jnp.where(side == 0, pair[0], pair[1])
        right = jnp.where(side == 0, pair[1], pair[0])
        return jnp.concatenate([left, right], axis=axis).astype(f32)

    grad_qkv = join([g.reshape(g.shape[0], 3, width) for g in grad_qkv], 2)
    grad_wout, grad_up, grad_down = join(grad_wout, 0), join(grad_up, 1), join(grad_down, 0)
    gain2_grad, shift2_grad = sum_all(jnp.stack([gain2_grad, shift2_grad]), ("dp", "tensor"))
    gain1_grad, shift1_grad = sum_all(jnp.stack([gain1_grad, shift1_grad]), ("dp", "tensor"))
    return (
        output,
        grad_input,
        gain1_grad,
        shift1_grad,
        grad_qkv,
        grad_wout,
        gain2_grad,
        shift2_grad,
        grad_up,
        grad_down,
        bucket_counts,
    )


def flip(i, bit):
    return i + bit - 2 * bit * ((i // bit) % 2)


class Traffic:
    def __init__(self, send_sems, recv_sems):
        self.send_sems, self.recv_sems = send_sems, recv_sems
        self.copies, self.gone, self.come = {}, set(), set()

    def send(self, name, src, dst, device):
        k = len(self.copies)
        copy = pltpu.make_async_remote_copy(
            src_ref=src,
            dst_ref=dst,
            send_sem=self.send_sems.at[k],
            recv_sem=self.recv_sems.at[k],
            device_id=device,
            device_id_type=pl.DeviceIdType.MESH,
        )
        copy.start()
        self.copies[name] = copy

    def wait(self, *names):
        for name in names:
            if name not in self.come:
                self.copies[name].wait_recv()
                self.come.add(name)

    def sent(self, *names):
        for name in names:
            if name not in self.gone:
                self.copies[name].wait_send()
                self.gone.add(name)

    def finish(self):
        self.sent(*self.copies)


class Moves:
    def __init__(self, sems):
        self.sems, self.copies = sems, {}

    def start(self, name, src, dst):
        copy = pltpu.make_async_copy(src, dst, self.sems.at[len(self.copies)])
        copy.start()
        self.copies[name] = [copy, False]

    def wait(self, *names):
        for name in names:
            if not self.copies[name][1]:
                self.copies[name][0].wait()
                self.copies[name][1] = True

    def finish(self):
        self.wait(*self.copies)


class Place:
    def __init__(self):
        self.i, self.t = lax.axis_index("dp"), lax.axis_index("tensor")
        self.side = (self.i // 2 + self.i // 4) % 2
        self.x, self.z = [(flip(self.i, b), self.t) for b in (1, 2)]
        self.far = (self.block(6), self.t)
        self.c, self.y = [(self.i, flip(self.t, b)) for b in (1, 2)]

    def greet(self):
        barrier = pltpu.get_barrier_semaphore()
        partners = (self.x, self.z, self.far, self.c, self.y)
        for device in partners:
            pl.semaphore_signal(
                barrier, inc=1, device_id=device, device_id_type=pl.DeviceIdType.MESH
            )
        pl.semaphore_wait(barrier, len(partners))

    def block(self, m):
        d = self.i
        for bit in (1, 2, 4):
            if m & bit:
                d = flip(d, bit)
        return d

    def stripe(self, m):
        s = self.t
        for bit in (1, 2):
            if m & bit:
                s = flip(s, bit)
        return s


class WeightGather:
    def __init__(self, name, place, traffic, moves, half, slot):
        self.name, self.p, self.tr, self.mv = name, place, traffic, moves
        self.half, self.slot = half, slot

    def own(self):
        self.mv.start(self.name + "0", self.half(self.p.side), self.slot(self.p.i))

    def z(self):
        self.tr.send(self.name + "2", self.half(1 - self.p.side), self.slot(self.p.i), self.p.z)

    def far(self):
        self.tr.send(self.name + "6", self.half(self.p.side), self.slot(self.p.i), self.p.far)

    def x(self):
        self.tr.send(self.name + "1", self.half(self.p.side), self.slot(self.p.i), self.p.x)

    def far_next(self):
        self.tr.wait(self.name + "2")
        block = self.slot(self.p.block(2))
        self.tr.send(self.name + "4", block, block, self.p.far)

    def x_next(self, m):
        self.tr.wait(self.name + str(m))
        block = self.slot(self.p.block(m))
        self.tr.send(self.name + str(m + 1), block, block, self.p.x)

    def take(self, *which):
        for m in which:
            if m == 0:
                self.mv.wait(self.name + "0")
            else:
                self.tr.wait(self.name + str(m))

    def end(self):
        self.take(*range(8))


class ActGather:
    def __init__(self, name, place, traffic, slots):
        self.name, self.p, self.tr, self.slots = name, place, traffic, slots

    def at(self, b, m):
        return self.slots.at[b, self.p.stripe(m)]

    def z(self):
        self.tr.send(self.name + "10", self.at(0, 0), self.slots.at[1, self.p.t], self.p.z)

    def y(self):
        self.tr.send(self.name + "02", self.at(0, 0), self.at(0, 0), self.p.y)

    def c(self):
        self.tr.send(self.name + "01", self.at(0, 0), self.at(0, 0), self.p.c)

    def pass_z(self):
        self.tr.wait(self.name + "10")
        block = self.at(1, 0)
        self.tr.send(self.name + "12", block, block, self.p.y)
        self.tr.send(self.name + "11", block, block, self.p.c)

    def pass_y(self, b):
        self.tr.wait(self.name + str(b) + "2")
        block = self.at(b, 2)
        self.tr.send(self.name + str(b) + "3", block, block, self.p.c)

    def take(self, b):
        for m in range(1 - b, 4):
            self.tr.wait(self.name + str(b) + str(m))


def loop_rows(count, step, body):
    def run(k, carry):
        body(pl.multiple_of(k * step, step))
        return carry

    lax.fori_loop(0, count // step, run, 0)


def wide(value):
    return value.astype(jnp.float32)


def add_blocks(out, left, right, rows):
    def body(r):
        at = pl.ds(r, 64)
        out[at, :] = (wide(left[at, :]) + wide(right[at, :])).astype(out.dtype)

    loop_rows(rows, 64, body)


class ActScatter:
    def __init__(self, name, place, traffic, part, got_c, got_y, got_z):
        self.name, self.p, self.tr = name, place, traffic
        self.part, self.got_c, self.got_y, self.got_z = part, got_c, got_y, got_z
        self.rows = part.shape[2]

    def at(self, b, m):
        return self.part.at[b, self.p.stripe(m)]

    def c(self, b):
        for j, m in ((1, 3), (0, 1)):
            name = self.name + "c" + str(b) + str(j)
            self.tr.send(name, self.at(b, m), self.got_c.at[b, j], self.p.c)

    def add(self, b, m, name, got):
        self.tr.wait(self.name + name)
        add_blocks(self.at(b, m), self.at(b, m), got, self.rows)

    def y(self, b):
        self.add(b, 2, "c" + str(b) + "1", self.got_c.at[b, 1])
        self.tr.send(self.name + "y" + str(b), self.at(b, 2), self.got_y.at[b], self.p.y)

    def own(self, b):
        self.add(b, 0, "c" + str(b) + "0", self.got_c.at[b, 0])

    def z(self):
        self.add(1, 0, "y1", self.got_y.at[1])
        self.tr.send(self.name + "z", self.at(1, 0), self.got_z, self.p.z)

    def home(self):
        self.add(0, 0, "y0", self.got_y.at[0])

    def sent(self):
        for key in ("c11", "c01", "c10", "c00", "y1", "y0", "z"):
            self.tr.sent(self.name + key)

    def end(self, out, base):
        self.tr.wait(self.name + "z")
        own = self.at(0, 0)

        def body(r):
            at = pl.ds(r, 64)
            out[at, :] = base[at, :] + (wide(own[at, :]) + wide(self.got_z[at, :]))

        loop_rows(self.rows, 64, body)


def round_rows(src, dst, rows):
    def body(r):
        at = pl.ds(r, 64)
        dst[at, :] = src[at, :].astype(dst.dtype)

    loop_rows(rows, 64, body)


def dot_f32(left, right):
    return jnp.dot(left, right, preferred_element_type=jnp.float32)


def dot_nt(left, right):
    return lax.dot_general(
        left, right, (((1,), (1,)), ((), ())), preferred_element_type=jnp.float32
    )


def dot_tn(left, right):
    return lax.dot_general(
        left, right, (((0,), (0,)), ((), ())), preferred_element_type=jnp.float32
    )


def center_rows(slots, b, at):
    stripes = slots.shape[1]
    rows = jnp.concatenate([wide(slots[b, s, at, :]) for s in range(stripes)], axis=1)
    center = rows - jnp.mean(rows, axis=1, keepdims=True)
    spread = jnp.mean(center * center, axis=1, keepdims=True)
    return center, lax.rsqrt(spread + epsilon)


def norm_rows(slots, b, gain, shift, out):
    rows = slots.shape[2]

    def body(r):
        center, inverse = center_rows(slots, b, pl.ds(r, 128))
        out[pl.ds(b * rows + r, 128), :] = (center * inverse * gain[...] + shift[...]).astype(
            jnp.bfloat16
        )

    loop_rows(rows, 128, body)


def attend(b, qkv, seg_col, seg_row, head_mask, weights, mixed, scale):
    tokens = seg_row.shape[2]
    heads = qkv.shape[2] // HD
    half = tokens // 2
    start = b * tokens
    for h in range(heads):
        cols = pl.ds(h * HD, HD)
        for part in range(2):
            rows = pl.ds(start + part * half, half)
            reach = half * (part + 1)
            query = qkv[0, rows, cols]
            key = qkv[1, pl.ds(start, reach), cols]
            value = qkv[2, pl.ds(start, reach), cols]
            scores = dot_nt(query, key) * scale
            row_id = lax.broadcasted_iota(jnp.int32, (half, reach), 0) + part * half
            col_id = lax.broadcasted_iota(jnp.int32, (half, reach), 1)
            same = seg_col[rows, :] == seg_row[b, :, pl.ds(0, reach)]
            scores = jnp.where(same & (row_id >= col_id), scores, -1000000000.0)
            scores = jnp.exp(scores - jnp.max(scores, axis=1, keepdims=True))
            total = jnp.sum(scores, axis=1, keepdims=True)
            chosen = (scores / total).astype(jnp.bfloat16)
            weights[b * heads + h, pl.ds(part * half, half), pl.ds(0, reach)] = chosen
            mixed[rows, cols] = (dot_f32(chosen, value) * head_mask[rows, :]).astype(jnp.bfloat16)


def sequences(lengths):
    start = 0
    for s in range(lengths.shape[1]):
        length = lengths[0, s]
        yield s, start, length
        start = start + length


def count_row(lengths, width_bucket, lanes):
    lane = lax.broadcasted_iota(jnp.int32, (1, lanes), 1)
    row = jnp.zeros((1, lanes), jnp.float32)
    for s, _, length in sequences(lengths):
        row = row + jnp.where(lane == width_bucket[0, s], wide(length), 0.0)
    return row


def fill_facts(lengths, head_bucket, width_bucket, place_cosine, place_sine, facts):
    lanes = facts.shape[1]
    row = lax.broadcasted_iota(jnp.int32, (8, lanes), 0)
    lane = lax.broadcasted_iota(jnp.int32, (8, lanes), 1)
    count = lengths.shape[1]
    by_lane = jnp.where((row == 0) & (lane >= count), 1e9, 0.0)
    by_row = jnp.where(row >= count, 1e9, 0.0)
    for s, start, length in sequences(lengths):
        end = wide(start + length)
        here = lane == s
        by_lane = by_lane + jnp.where((row == 0) & here, end, 0.0)
        by_lane = by_lane + jnp.where((row == 2) & here, wide(head_bucket[0, s]), 0.0)
        by_lane = by_lane + jnp.where((row == 3) & here, wide(width_bucket[0, s]), 0.0)
        by_row = by_row + jnp.where(row == s, end, 0.0)
        facts[pl.ds(16 + s, 1), :] = place_cosine[pl.ds(start, 1), :]
        facts[pl.ds(20 + s, 1), :] = place_sine[pl.ds(start, 1), :]
    facts[pl.ds(0, 8), :] = by_lane
    facts[pl.ds(8, 8), :] = by_row


def fill_tables(
    infos, place_cosine, place_sine, t, cosine, sine, head_mask, width_mask, seg_col, seg_row
):
    tokens, lanes = place_cosine.shape
    own = wide(t)
    lane = wide(lax.broadcasted_iota(jnp.int32, (tokens, lanes), 1))
    place = wide(lax.broadcasted_iota(jnp.int32, (tokens, lanes), 0))
    sign = jnp.where(lane < lanes // 2, -1.0, 1.0)
    for b in range(2):
        rows = pl.ds(b * tokens, tokens)

        def row(k, b=b):
            return infos[b, pl.ds(k, 1), :]

        segment = jnp.sum(jnp.where(place >= row(0), 1.0, 0.0), axis=1, keepdims=True)
        seg_col[rows, :] = segment
        chosen = jnp.where(lane == segment, 1.0, 0.0)
        head = jnp.sum(chosen * row(2), axis=1, keepdims=True)
        width = jnp.sum(chosen * row(3), axis=1, keepdims=True)
        head_mask[rows, :] = jnp.where(head >= own, 1.0, 0.0)
        width_mask[rows, :] = jnp.where(width >= own, 1.0, 0.0)
        start_cosine, start_sine = 0.0, 0.0
        for s in range(4):
            here = jnp.where(segment == s, 1.0, 0.0)
            start_cosine = start_cosine + here * row(16 + s)
            start_sine = start_sine + here * row(20 + s)
        at_cosine, at_sine = place_cosine[...], place_sine[...]
        cosine[rows, :] = at_cosine * start_cosine + at_sine * start_sine
        sine[rows, :] = (at_sine * start_cosine - at_cosine * start_sine) * sign
        ends = infos[b, pl.ds(8, 8), pl.ds(0, 1)]
        across = wide(lax.broadcasted_iota(jnp.int32, (8, tokens), 1))
        seg_row[b] = jnp.sum(jnp.where(across >= ends, 1.0, 0.0), axis=0, keepdims=True)


def forward_kernel(
    residual,
    cotangent,
    gain1,
    shift1,
    gain2,
    shift2,
    lengths,
    head_bucket,
    width_bucket,
    place_cosine,
    place_sine,
    half_qkv,
    half_out,
    half_up,
    half_down,
    cosine,
    sine,
    head_mask,
    all_qkv,
    all_out,
    all_up,
    stream1,
    stream2,
    stream_c,
    normed1,
    normed2,
    heads_out,
    weights_out,
    mixed_out,
    active_out,
    grad_upper_out,
    part_out,
    middle_out,
    w_qkv,
    w_out,
    w_up,
    w_down,
    rows1,
    rows2,
    rows_c,
    normed,
    qkv,
    weights,
    mixed,
    part,
    got_c,
    got_y,
    got_z,
    upper,
    active,
    grad_active,
    middle,
    infos,
    seg_col,
    seg_row,
    width_mask,
    send_sems,
    recv_sems,
    move_sems,
):
    p = Place()
    tr, mv = Traffic(send_sems, recv_sems), Moves(move_sems)
    tokens = residual.shape[0]
    rows_d = half_qkv.shape[1]
    head_cols = w_out.shape[1]

    def row_slot(ref):
        return lambda d: ref.at[pl.ds(pl.multiple_of(d * rows_d, rows_d), rows_d)]

    def first_slot(ref):
        return lambda d: ref.at[d]

    def at_side(k, cut, size):
        return pl.ds(pl.multiple_of(k * size + cut.start, 128), cut.size)

    hidden = w_up.shape[1]
    parts = [pl.ds(0, hidden // 2), pl.ds(hidden // 2, hidden // 2)]

    def rows_at(d):
        return pl.ds(pl.multiple_of(d * rows_d, rows_d), rows_d)

    def up_gather(name, cut):
        return WeightGather(
            name,
            p,
            tr,
            mv,
            lambda k: half_up.at[:, at_side(k, cut, hidden)],
            lambda d: w_up.at[rows_at(d), cut],
        )

    def down_gather(name, cut):
        return WeightGather(
            name,
            p,
            tr,
            mv,
            lambda k: half_down.at[at_side(k, cut, hidden), :],
            lambda d: w_down.at[d, cut, :],
        )

    heads_cut = pl.ds(0, head_cols)
    q = WeightGather(
        "q",
        p,
        tr,
        mv,
        lambda k: half_qkv.at[:, :, at_side(k, heads_cut, head_cols)],
        lambda d: w_qkv.at[:, rows_at(d), :],
    )
    o = WeightGather(
        "o",
        p,
        tr,
        mv,
        lambda k: half_out.at[at_side(k, heads_cut, head_cols), :],
        lambda d: w_out.at[d],
    )
    u, v = [up_gather(n, cut) for n, cut in zip("uv", parts)]
    d, e = [down_gather(n, cut) for n, cut in zip("de", parts)]
    a1 = ActGather("a", p, tr, rows1)
    a2 = ActGather("b", p, tr, rows2)
    ac = ActGather("c", p, tr, rows_c)
    s1 = ActScatter("s", p, tr, part, got_c, got_y, got_z)

    fill_facts(lengths, head_bucket, width_bucket, place_cosine, place_sine, infos.at[0])
    p.greet()
    for one in (q, o, u, v, d, e):
        one.own()
    blocks = w_out.shape[0]
    stripes = part.shape[1]
    per = blocks // stripes
    started = []

    def project(b):
        def body(r):
            at = pl.ds(b * tokens + r, 256)
            for k in range(3):
                got = dot_f32(normed[at, :], w_qkv[k])
                for h in range(head_cols // HD):
                    cols = pl.ds(h * HD, HD)
                    one = got[:, h * HD : (h + 1) * HD]
                    if k < 2:
                        one = one * cosine[at, :] + pltpu.roll(one, HD // 2, 1) * sine[at, :]
                    qkv[k, at, cols] = one.astype(jnp.bfloat16)

        loop_rows(tokens, 256, body)

    def branch(b):
        at = pl.ds(b * tokens, tokens)

        def body(s, carry):
            for j in range(per):
                got = dot_f32(mixed[at, :], w_out[s * per + j])
                part[b, s, :, pl.ds(j * rows_d, rows_d)] = got.astype(jnp.bfloat16)
            return carry

        lax.fori_loop(0, stripes, body, 0)

    def rise(b, cut):
        def body(r):
            at = pl.ds(b * tokens + r, 256)
            for k in range(cut.size // 256):
                cols = pl.ds(cut.start + k * 256, 256)
                got = dot_f32(normed[at, :], w_up[:, cols])
                got = jnp.maximum(got, 0.0) * width_mask[at, :]
                upper[at, cols] = got.astype(jnp.bfloat16)
                active[at, cols] = (got * got).astype(jnp.bfloat16)

        loop_rows(tokens, 256, body)

    def fall(m):
        place = p.block(m)
        s = place // per
        cols = pl.ds(pl.multiple_of((place % per) * rows_d, rows_d), rows_d)
        first = not started
        started.append(m)

        def body(r):
            b, at = r // tokens, pl.ds(pl.multiple_of(r % tokens, 256), 256)
            rows = pl.ds(r, 256)
            part[b, s, at, cols] = dot_f32(active[rows, :], w_down[place]).astype(jnp.bfloat16)
            got = dot_nt(rows_c[b, s, at, cols], w_down[place])
            grad_active[rows, :] = got if first else grad_active[rows, :] + got

        loop_rows(2 * tokens, 256, body)

    def turn(r):
        at = pl.ds(r, 64)
        active[at, :] = (grad_active[at, :] * 2.0 * wide(upper[at, :])).astype(jnp.bfloat16)

    q.z()
    round_rows(residual, rows1.at[0, p.t], tokens)
    a1.z()
    q.x()
    o.z()
    o.x()
    v.z()
    o.far()
    round_rows(cotangent, rows_c.at[0, p.t], tokens)
    q.far()
    q.far_next()
    u.far()
    ac.y()
    a1.y()
    tr.send("info", infos.at[0], infos.at[1], p.z)
    e.x()
    o.x_next(2)
    q.x_next(2)
    a1.pass_z()
    o.x_next(6)
    q.x_next(6)
    o.far_next()
    q.x_next(4)
    tr.wait("info")
    fill_tables(
        infos, place_cosine, place_sine, p.t, cosine, sine, head_mask, width_mask, seg_col, seg_row
    )
    u.z()
    e.z()
    d.z()
    a1.pass_y(1)
    a1.take(1)
    norm_rows(rows1, 1, gain1, shift1, normed)
    o.x_next(4)
    v.far()
    a1.pass_y(0)
    q.end()
    project(1)
    u.x_next(2)
    attend(
        1, qkv, seg_col, seg_row, head_mask, weights, mixed, HD ** (-0.5)
    )
    o.end()
    branch(1)
    s1.c(1)
    v.far_next()
    s1.y(1)
    a1.c()
    v.x()
    s1.own(1)
    d.x_next(2)
    u.x_next(6)
    a1.take(0)
    norm_rows(rows1, 0, gain1, shift1, normed)
    mv.start("stream1", rows1, stream1)
    mv.start("normed1", normed, normed1)
    project(0)
    mv.start("all_qkv", w_qkv, all_qkv)
    attend(
        0, qkv, seg_col, seg_row, head_mask, weights, mixed, HD ** (-0.5)
    )
    mv.start("heads", qkv, heads_out)
    mv.start("weights", weights, weights_out)
    mv.start("mixed", mixed, mixed_out)
    branch(0)
    mv.start("all_out", w_out, all_out)
    v.x_next(2)
    ac.pass_y(0)
    s1.c(0)
    u.x()
    e.x_next(2)
    s1.z()
    u.far_next()
    s1.y(0)
    s1.own(0)
    s1.home()
    v.x_next(4)
    s1.end(middle, residual)
    round_rows(middle, rows2.at[0, p.t], tokens)
    mv.start("middle", middle, middle_out)
    a2.z()
    ac.z()
    a2.y()
    d.far_next()
    e.far()
    d.far()
    a2.c()
    a2.pass_z()
    a2.pass_y(0)
    v.x_next(6)
    u.x_next(4)
    e.far_next()
    a2.take(0)
    mv.wait("normed1")
    norm_rows(rows2, 0, gain2, shift2, normed)
    d.x()
    v.end()
    rise(0, parts[1])
    ac.pass_z()
    a2.pass_y(1)
    d.x_next(4)
    a2.take(1)
    norm_rows(rows2, 1, gain2, shift2, normed)
    mv.start("stream2", rows2, stream2)
    mv.start("normed2", normed, normed2)
    ac.c()
    rise(1, parts[1])
    u.end()
    rise(0, parts[0])
    e.x_next(6)
    rise(1, parts[0])
    mv.start("active", active, active_out)
    mv.start("all_up", w_up, all_up)
    ac.pass_y(1)
    d.x_next(6)
    ac.take(0)
    ac.take(1)
    s1.sent()
    d.take(3)
    e.take(3)
    fall(3)
    mv.start("stream_c", rows_c, stream_c)
    d.take(6)
    e.take(6)
    fall(6)
    d.take(0)
    e.take(0)
    fall(0)
    e.x_next(4)
    d.take(1)
    e.take(1)
    fall(1)
    d.take(4)
    e.take(4)
    fall(4)
    d.take(2)
    e.take(2)
    fall(2)
    d.take(7)
    e.take(7)
    fall(7)
    d.take(5)
    e.take(5)
    fall(5)
    mv.start("part", part, part_out)
    mv.wait("active")
    loop_rows(2 * tokens, 64, turn)
    mv.start("grad_upper", active, grad_upper_out)
    tr.finish()
    mv.finish()


def forward_call(arrays, weights):
    bf16, f32 = jnp.bfloat16, jnp.float32
    tokens, columns = arrays[0].shape
    w_qkv, w_out, w_up, w_down = weights
    count, stripes = lax.axis_size("dp"), lax.axis_size("tensor")
    rows_d = w_up.shape[0]
    head_cols = w_out.shape[0] // 2
    hidden = w_up.shape[1] // 2
    width = rows_d * count
    heads = head_cols // HD
    slots = (2, stripes, tokens, columns)
    tables = dict(
        cosine=((2 * tokens, HD), f32),
        sine=((2 * tokens, HD), f32),
        head_mask=((2 * tokens, 1), f32),
    )
    shapes = dict(
        all_qkv=((3, width, head_cols), bf16),
        all_out=((count, head_cols, rows_d), bf16),
        all_up=((width, hidden), bf16),
        stream1=(slots, bf16),
        stream2=(slots, bf16),
        stream_c=(slots, bf16),
        normed1=((2 * tokens, width), bf16),
        normed2=((2 * tokens, width), bf16),
        heads=((3, 2 * tokens, head_cols), bf16),
        weights=((2 * heads, tokens, tokens), bf16),
        mixed=((2 * tokens, head_cols), bf16),
        active=((2 * tokens, hidden), bf16),
        grad_upper=((2 * tokens, hidden), bf16),
        part_out=(slots, bf16),
        middle=((tokens, columns), f32),
    )

    def vmem(name):
        return pltpu.VMEM(*shapes[name])

    scratch = [
        vmem("all_qkv"),
        vmem("all_out"),
        vmem("all_up"),
        pltpu.VMEM((count, hidden, rows_d), bf16),
        vmem("stream1"),
        vmem("stream2"),
        vmem("stream_c"),
        vmem("normed1"),
        vmem("heads"),
        vmem("weights"),
        vmem("mixed"),
        pltpu.VMEM(slots, bf16),
        pltpu.VMEM((2, 2, tokens, columns), bf16),
        pltpu.VMEM((2, tokens, columns), bf16),
        pltpu.VMEM((tokens, columns), bf16),
        vmem("active"),
        vmem("active"),
        pltpu.VMEM((2 * tokens, hidden), f32),
        vmem("middle"),
        pltpu.VMEM((2, 24, 128), f32),
        pltpu.VMEM((2 * tokens, 1), f32),
        pltpu.VMEM((2, 1, tokens), f32),
        pltpu.VMEM((2 * tokens, 1), f32),
        pltpu.SemaphoreType.DMA((72,)),
        pltpu.SemaphoreType.DMA((72,)),
        pltpu.SemaphoreType.DMA((32,)),
    ]
    any_spec = pl.BlockSpec(memory_space=pl.ANY)
    vmem_spec = pl.BlockSpec(memory_space=pltpu.VMEM)
    smem_spec = pl.BlockSpec(memory_space=pltpu.SMEM)
    outs = pl.pallas_call(
        forward_kernel,
        out_shape=[jax.ShapeDtypeStruct(*s) for s in (tables | shapes).values()],
        in_specs=[vmem_spec] * 6 + [smem_spec] * 3 + [vmem_spec] * 2 + [any_spec] * 4,
        out_specs=[vmem_spec] * len(tables) + [any_spec] * len(shapes),
        scratch_shapes=scratch,
        compiler_params=pltpu.CompilerParams(
            collective_id=0, has_side_effects=True, vmem_limit_bytes=62 << 20
        ),
    )(*arrays, *weights)
    split = len(tables)
    return outs[:split], dict(zip(shapes, outs[split:]))


class WeightScatter:
    def __init__(self, name, place, traffic, odd, even, got_x, got_far, out):
        self.name, self.p, self.tr = name, place, traffic
        self.odd, self.even, self.got_x, self.got_far, self.out = odd, even, got_x, got_far, out

    def send_x(self, m):
        self.tr.send(self.name + "x" + str(m), self.odd.at[m // 2], self.got_x.at[m // 2], self.p.x)

    def add_x(self, m):
        k, n = m // 2, self.name
        own = self.even.at[k]
        self.tr.wait(n + "x" + str(m + 1))
        add_blocks(own, own, self.got_x.at[k], own.shape[0])
        if m >= 4:
            self.tr.send(n + "f" + str(m), own, self.got_far.at[3 - k], self.p.far)

    def add_far(self, m):
        k, n = m // 2, self.name
        own = self.even.at[k]
        self.tr.wait(n + "f" + str(6 - m))
        add_blocks(own, own, self.got_far.at[k], own.shape[0])
        if m == 2:
            for j, (cut, spot) in enumerate(self.out(self.p.side)):
                self.tr.send(n + "z" + str(j), own.at[:, cut], spot, self.p.z)

    def end(self, moves):
        for j, (cut, spot) in enumerate(self.out(self.p.side)):
            moves.start(self.name + str(j), self.even.at[0, :, cut], spot)
            self.tr.wait(self.name + "z" + str(j))


class SumAll:
    def __init__(self, name, place, traffic, sums, got):
        self.name, self.tr, self.sums, self.got = name, traffic, sums, got
        self.partners = (place.c, place.y, place.x, place.z, place.far)

    def start(self, k):
        self.tr.send(self.name + str(k), self.sums, self.got.at[k], self.partners[k])

    def step(self, k):
        self.tr.wait(self.name + str(k))
        self.tr.sent(self.name + str(k))
        self.sums[...] += self.got[k]
        if k + 1 < len(self.partners):
            self.start(k + 1)


def norm_back(b, part, slots, gain, total):
    stripes, rows, columns = part.shape[1:]
    tile = 64
    fold = (tile // 8, 8, stripes * columns)

    def body(r):
        at = pl.ds(r, tile)
        value = wide(slots[pl.ds(b * rows + r, tile), :])
        center = value - jnp.mean(value, axis=1, keepdims=True)
        spread = jnp.mean(center * center, axis=1, keepdims=True)
        inverse = lax.rsqrt(spread + epsilon)
        unit = center * inverse
        grad = jnp.concatenate([wide(part[b, s, at, :]) for s in range(stripes)], axis=1)
        scaled = grad * gain[...]
        push = inverse * (
            scaled
            - jnp.mean(scaled, axis=1, keepdims=True)
            - unit * jnp.mean(scaled * unit, axis=1, keepdims=True)
        )
        for s in range(stripes):
            part[b, s, at, :] = push[:, s * columns : (s + 1) * columns].astype(jnp.bfloat16)
        total[0] += jnp.sum((grad * unit).reshape(fold), axis=0)
        total[1] += jnp.sum(grad.reshape(fold), axis=0)

    if b == 1:
        total[...] = jnp.zeros_like(total)
    loop_rows(rows, tile, body)


def attend_back(b, qkv, weights, grad_mixed, cosine, sine, out, tokens, scale):
    width = grad_mixed.shape[1]
    heads = width // HD
    half = tokens // 2
    start = b * tokens

    def turn_back(grad, rows):
        return (grad * cosine[rows, :] - pltpu.roll(grad, HD // 2, 1) * sine[rows, :]).astype(
            jnp.bfloat16
        )

    for h in range(heads):
        spots = [pl.ds(k * width + h * HD, HD) for k in range(3)]
        grad_key, grad_value = None, None
        for part in (1, 0):
            rows = pl.ds(start + part * half, half)
            reach = pl.ds(start, half * (part + 1))
            query, key, value = qkv[rows, spots[0]], qkv[reach, spots[1]], qkv[reach, spots[2]]
            given = grad_mixed[rows, pl.ds(h * HD, HD)]
            chosen = weights[b * heads + h, pl.ds(part * half, half), pl.ds(0, half * (part + 1))]
            grad = dot_nt(given, value)
            soft = wide(chosen)
            grad = soft * (grad - jnp.sum(grad * soft, axis=1, keepdims=True))
            raw = (grad * scale).astype(jnp.bfloat16)
            out[rows, spots[0]] = turn_back(dot_f32(raw, key), rows)
            key_part, value_part = dot_tn(raw, query), dot_tn(chosen, given)
            if part == 1:
                grad_key, grad_value = key_part, value_part
        low, high = pl.ds(start, half), pl.ds(start + half, half)
        out[low, spots[1]] = turn_back(grad_key[:half] + key_part, low)
        out[high, spots[1]] = turn_back(grad_key[half:], high)
        out[low, spots[2]] = (grad_value[:half] + value_part).astype(jnp.bfloat16)
        out[high, spots[2]] = grad_value[half:].astype(jnp.bfloat16)


def backward_kernel(
    cotangent,
    gain1,
    gain2,
    cosine,
    sine,
    head_mask,
    lengths,
    width_bucket,
    all_qkv,
    all_out,
    all_up,
    stream1,
    stream2,
    stream_c,
    normed1,
    normed2,
    heads,
    weights_in,
    mixed_in,
    active_in,
    grad_upper_in,
    part_in,
    middle_in,
    output,
    grad_input,
    sums2_out,
    sums1_out,
    grad_qkv,
    grad_out,
    grad_up,
    grad_down,
    w_up,
    w_out,
    rows_a,
    rows_b,
    active,
    grad_upper,
    part_a,
    part_b,
    got_ca,
    got_ya,
    got_za,
    got_cb,
    got_yb,
    got_zb,
    stream_b,
    weights,
    mixed,
    grad_mixed,
    odd,
    even_down,
    even_up,
    odd_out,
    even_out,
    gx_down,
    gf_down,
    gx_up,
    gf_up,
    gx_qkv,
    gf_qkv,
    gx_out,
    gf_out,
    middle,
    grad_middle,
    total,
    sums2,
    got2,
    sums1,
    got1,
    send_sems,
    recv_sems,
    move_sems,
):
    p = Place()
    tr, mv = Traffic(send_sems, recv_sems), Moves(move_sems)
    tokens, columns = cotangent.shape
    stripes, blocks = part_a.shape[1], all_out.shape[0]
    rows_d = all_out.shape[2]
    per = blocks // stripes
    head_cols = mixed.shape[1]
    bf16 = jnp.bfloat16

    def load_stream(name, src, dst):
        for b in range(2):
            for s in range(stripes):
                spot = dst.at[pl.ds(b * tokens, tokens), pl.ds(s * columns, columns)]
                mv.start(name + str(b) + str(s), src.at[b, s], spot)

    def wait_stream(name):
        mv.wait(*[name + str(b) + str(s) for b in range(2) for s in range(stripes)])

    s_out = ActScatter("s", p, tr, part_a, got_ca, got_ya, got_za)
    s2 = ActScatter("t", p, tr, part_b, got_cb, got_yb, got_zb)
    s1 = ActScatter("r", p, tr, part_b, got_cb, got_yb, got_zb)
    ab = ActGather("b", p, tr, stream_b)
    qkv_cols = pl.ds(0, 3 * head_cols)
    hidden = active.shape[1]
    parts = [pl.ds(0, hidden // 2), pl.ds(hidden // 2, hidden // 2)]

    def at_side(k, cut, size):
        return pl.ds(pl.multiple_of(k * size + cut.start, 128), cut.size)

    def scatter(name, odd, even, got_x, got_far, out, cols):
        views = [ref.at[:, :, cols] for ref in (odd, even, got_x, got_far)]

        def spots(k):
            if len(out.shape) == 3:
                return [
                    (pl.ds(j * head_cols, head_cols), out.at[j, :, at_side(k, heads_cut, head_cols)])
                    for j in range(3)
                ]
            spot = out.at[:, at_side(k, cols, out.shape[1] // 2)]
            return [(pl.ds(0, cols.size), spot)]

        return WeightScatter(name, p, tr, *views, spots)

    heads_cut = pl.ds(0, head_cols)

    d, e = [
        scatter(n, odd, even_down, gx_down, gf_down, grad_down, cut) for n, cut in zip("de", parts)
    ]
    u, v = [scatter(n, odd, even_up, gx_up, gf_up, grad_up, cut) for n, cut in zip("uv", parts)]
    q = scatter("q", odd, even_down, gx_qkv, gf_qkv, grad_qkv, qkv_cols)
    o = scatter("o", odd_out, even_out, gx_out, gf_out, grad_out, pl.ds(0, head_cols))
    all2 = SumAll("2", p, tr, sums2, got2)
    all1 = SumAll("1", p, tr, sums1, got1)

    load_stream("c", stream_c, rows_a)
    mv.start("active", active_in, active)
    mv.start("grad_upper", grad_upper_in, grad_upper)
    mv.start("all_up", all_up, w_up)
    load_stream("x2", stream2, rows_b)
    p.greet()

    def load_rest():
        for k in range(blocks):
            mv.start("p" + str(k), all_out.at[k], w_out.at[:, pl.ds(k * rows_d, rows_d)])
        mv.start("mixed", mixed_in, mixed)
        mv.start("weights", weights_in, weights)
        mv.start("part", part_in, part_a)
        mv.start("middle", middle_in, middle)

    def block_cols(m):
        return pl.ds(pl.multiple_of(p.block(m) * rows_d, rows_d), rows_d)

    def grad_block(left, right, m, spot, cols=None):
        value = right[...] if cols is None else right[:, cols]
        spot[...] = dot_tn(left[:, block_cols(m)], value).astype(bf16)

    def down_block(m, spot):
        grad_block(rows_a, active, m, spot)

    def product(b, left, right, cols):
        at = pl.ds(b * tokens, tokens)

        def body(s, carry):
            rows = pl.ds(pl.multiple_of(s * columns, columns), columns)
            part_b[b, s] = dot_nt(left[at, cols], right[rows, cols]).astype(bf16)
            return carry

        lax.fori_loop(0, stripes, body, 0)

    def gather_total(sums):
        depth, lanes = 8, total.shape[2] // 8
        sums[...] = jnp.zeros_like(sums)
        for k in range(2):
            row = jnp.sum(total[k], axis=0, keepdims=True)
            for r in range(depth):
                sums[pl.ds(r, 1), pl.ds(k * lanes, lanes)] = row[:, r * lanes : (r + 1) * lanes]
        sums[pl.ds(0, 1), pl.ds(2 * lanes, HD)] = count_row(lengths, width_bucket, HD)

    def unpack(sums, out):
        depth, lanes = 8, total.shape[2] // 8
        for k in range(2):
            for r in range(depth):
                spot = sums[pl.ds(r, 1), pl.ds(k * lanes, lanes)]
                out[pl.ds(k, 1), pl.ds(r * lanes, lanes)] = spot
        out[pl.ds(2, 1), pl.ds(0, HD)] = sums[pl.ds(0, 1), pl.ds(2 * lanes, HD)]

    def up_block(m, spot):
        grad_block(rows_a, grad_upper, m, spot)

    def up_odd(m):
        tr.sent("dx" + str(m), "ex" + str(m))
        up_block(m, odd.at[m // 2])
        u.send_x(m)
        v.send_x(m)

    def mix(b):
        mv.wait(*["p" + str(k) for k in range(blocks)])
        at = pl.ds(b * tokens, tokens)
        got = None
        for s in range(stripes):
            one = dot_nt(stream_b[b, s], w_out[:, pl.ds(s * columns, columns)])
            got = one if got is None else got + one
        grad_mixed[at, :] = (got * head_mask[at, :]).astype(bf16)

    def out_block(m, spot):
        mv.wait("mixed")
        place = p.block(m)
        cols = pl.ds(pl.multiple_of((place % per) * rows_d, rows_d), rows_d)
        near = dot_tn(stream_b[0, place // per, :, cols], mixed[pl.ds(0, tokens), :])
        away = dot_tn(stream_b[1, place // per, :, cols], mixed[pl.ds(tokens, tokens), :])
        spot[...] = (near + away).astype(bf16)

    def qkv_block(m, spot):
        mv.wait("normed1")
        grad_block(rows_b, grad_upper, m, spot, qkv_cols)

    def qkv_odd(m):
        tr.sent("ux" + str(m), "vx" + str(m))
        qkv_block(m, odd.at[m // 2, :, qkv_cols])
        q.send_x(m)

    def qkv_even(m):
        mv.wait("d0", "e0")
        tr.sent("df4", "df6", "dz0", "ef4", "ef6", "ez0")
        qkv_block(m, even_down.at[m // 2, :, qkv_cols])

    wait_stream("c")
    mv.wait("active")
    down_block(5, odd.at[2])
    d.send_x(5)
    e.send_x(5)
    mv.wait("grad_upper", "all_up")
    product(1, grad_upper, w_up, pl.ds(0, w_up.shape[1]))
    wait_stream("x2")
    norm_back(1, part_b, rows_b, gain2, total)
    s2.c(1)
    down_block(4, even_down.at[2])
    d.add_x(4)
    down_block(7, odd.at[3])
    d.send_x(7)
    e.send_x(7)
    down_block(3, odd.at[1])
    d.send_x(3)
    e.send_x(3)
    s2.y(1)
    product(0, grad_upper, w_up, pl.ds(0, w_up.shape[1]))
    norm_back(0, part_b, rows_b, gain2, total)
    s2.c(0)
    down_block(2, even_down.at[1])
    s2.own(1)
    e.add_x(4)
    down_block(6, even_down.at[3])
    down_block(1, odd.at[0])
    d.send_x(1)
    e.send_x(1)
    down_block(0, even_down.at[0])
    load_rest()
    mv.wait("part")
    for k in range(3):
        mv.start("h" + str(k), heads.at[k], active.at[:, pl.ds(k * head_cols, head_cols)])
    mv.start("normed2", normed2, rows_a)
    mv.wait("normed2")
    up_odd(5)
    s2.y(0)
    s_out.c(1)
    s2.own(0)
    gather_total(sums2)
    all2.start(0)
    s2.z()
    up_block(0, even_up.at[0])
    e.add_x(6)
    all2.step(0)
    s_out.y(1)
    all2.step(1)
    e.add_x(2)
    s2.home()
    s2.end(grad_middle, cotangent)
    round_rows(grad_middle, stream_b.at[0, p.t], tokens)
    up_odd(3)
    up_block(4, even_up.at[2])
    d.add_x(2)
    up_odd(7)
    e.add_far(2)
    for k in range(3):
        mv.start("w" + str(k), all_qkv.at[k], w_up.at[:, pl.ds(k * head_cols, head_cols)])
    mv.start("normed1", normed1, rows_b)
    ab.y()
    ab.z()
    d.add_x(6)
    u.add_x(4)
    v.add_x(4)
    e.add_x(0)
    up_odd(1)
    d.add_x(0)
    ab.pass_z()
    ab.pass_y(1)
    s_out.own(1)
    up_block(6, even_up.at[3])
    d.add_far(2)
    up_block(2, even_up.at[1])
    all2.step(2)
    s_out.c(0)
    ab.pass_y(0)
    v.add_x(2)
    s_out.z()
    ab.take(1)
    mix(1)
    load_stream("x1", stream1, rows_a)
    ab.c()
    mv.wait("weights", "h0", "h1", "h2")
    attend_back(
        1, active, weights, grad_mixed, cosine, sine, grad_upper, tokens, HD ** (-0.5)
    )
    s_out.own(0)
    d.add_far(0)
    ab.take(0)
    mix(0)
    attend_back(
        0, active, weights, grad_mixed, cosine, sine, grad_upper, tokens, HD ** (-0.5)
    )
    u.add_x(6)
    s_out.y(0)
    e.add_far(0)
    s2.sent()
    mv.wait("w0", "w1", "w2")
    product(1, grad_upper, w_up, qkv_cols)
    wait_stream("x1")
    norm_back(1, part_b, rows_a, gain1, total)
    u.add_x(0)
    out_block(4, even_out.at[2])
    d.end(mv)
    all2.step(3)
    s1.c(1)
    e.end(mv)
    out_block(5, odd_out.at[2])
    o.send_x(5)
    qkv_odd(5)
    u.add_x(2)
    s1.y(1)
    product(0, grad_upper, w_up, qkv_cols)
    norm_back(0, part_b, rows_a, gain1, total)
    v.add_far(2)
    qkv_even(6)
    gather_total(sums1)
    all1.start(0)
    qkv_odd(3)
    s1.c(0)
    s1.own(1)
    o.add_x(4)
    s1.z()
    qkv_even(2)
    out_block(2, even_out.at[1])
    u.add_far(2)
    v.add_x(6)
    all1.step(0)
    qkv_even(4)
    out_block(0, even_out.at[0])
    qkv_even(0)
    s_out.home()
    mv.wait("middle")
    s_out.end(middle, middle)
    mv.start("output", middle, output)
    qkv_odd(7)
    s1.y(0)
    out_block(1, odd_out.at[0])
    o.send_x(1)
    q.add_x(4)
    qkv_odd(1)
    v.add_x(0)
    s1.own(0)
    all1.step(1)
    o.add_x(0)
    out_block(3, odd_out.at[1])
    o.send_x(3)
    out_block(7, odd_out.at[3])
    o.send_x(7)
    q.add_x(2)
    o.add_x(2)
    out_block(6, even_out.at[3])
    s1.home()
    o.add_far(2)
    all1.step(2)
    q.add_far(2)
    q.add_x(6)
    u.add_far(0)
    s1.end(grad_middle, grad_middle)
    mv.start("grad_input", grad_middle, grad_input)
    o.add_x(6)
    q.add_x(0)
    all1.step(3)
    o.add_far(0)
    u.end(mv)
    q.add_far(0)
    all2.step(4)
    v.add_far(0)
    o.end(mv)
    v.end(mv)
    q.end(mv)
    all1.step(4)
    unpack(sums2, sums2_out)
    unpack(sums1, sums1_out)
    tr.finish()
    mv.finish()


def backward_call(arrays, saved):
    bf16, f32 = jnp.bfloat16, jnp.float32
    tokens, columns = arrays[0].shape
    count, stripes = lax.axis_size("dp"), lax.axis_size("tensor")
    _, head_cols, rows_d = saved["all_out"].shape
    width, hidden = saved["all_up"].shape
    slots = (2, stripes, tokens, columns)
    wide_rows = (2 * tokens, width)

    def vmem(*shape, dtype=bf16):
        return pltpu.VMEM(shape, dtype)

    def got(cols):
        return [vmem(4, rows_d, cols), vmem(2, rows_d, cols)]

    got_act = [vmem(2, 2, tokens, columns), vmem(2, tokens, columns), vmem(tokens, columns)]
    packed = 2 * width // 8 + HD
    sums = [vmem(8, packed, dtype=f32), vmem(5, 8, packed, dtype=f32)]
    qkv = 3 * head_cols
    scratch = [
        vmem(width, hidden),
        vmem(head_cols, width),
        vmem(*wide_rows),
        vmem(*wide_rows),
        vmem(2 * tokens, hidden),
        vmem(2 * tokens, hidden),
        vmem(*slots),
        vmem(*slots),
        *got_act,
        *got_act,
        vmem(*slots),
        vmem(*saved["weights"].shape),
        vmem(2 * tokens, head_cols),
        vmem(2 * tokens, head_cols),
        vmem(4, rows_d, hidden),
        vmem(4, rows_d, hidden),
        vmem(4, rows_d, hidden),
        vmem(4, rows_d, head_cols),
        vmem(4, rows_d, head_cols),
        *got(hidden),
        *got(hidden),
        *got(qkv),
        *got(head_cols),
        vmem(tokens, columns, dtype=f32),
        vmem(tokens, columns, dtype=f32),
        vmem(2, 8, width, dtype=f32),
        *sums,
        *sums,
        pltpu.SemaphoreType.DMA((84,)),
        pltpu.SemaphoreType.DMA((84,)),
        pltpu.SemaphoreType.DMA((72,)),
    ]
    any_spec = pl.BlockSpec(memory_space=pl.ANY)
    vmem_spec = pl.BlockSpec(memory_space=pltpu.VMEM)
    smem_spec = pl.BlockSpec(memory_space=pltpu.SMEM)
    shapes = [
        ((tokens, columns), f32),
        ((tokens, columns), f32),
        ((8, width), f32),
        ((8, width), f32),
        ((3, rows_d, 2 * head_cols), bf16),
        ((rows_d, 2 * head_cols), bf16),
        ((rows_d, 2 * hidden), bf16),
        ((rows_d, 2 * hidden), bf16),
    ]
    names = [k for k in saved]
    return pl.pallas_call(
        backward_kernel,
        out_shape=[jax.ShapeDtypeStruct(*s) for s in shapes],
        in_specs=[vmem_spec] * 6 + [smem_spec] * 2 + [any_spec] * len(names),
        out_specs=[any_spec] * 2 + [vmem_spec] * 2 + [any_spec] * 4,
        scratch_shapes=scratch,
        compiler_params=pltpu.CompilerParams(
            collective_id=1, has_side_effects=True, vmem_limit_bytes=63 << 20
        ),
    )(*arrays, *[saved[n] for n in names])


def finish_kernel(groups, *refs):
    ins, sums, outs, small = refs[:6], refs[6:8], refs[8:14], refs[14:19]
    raw, done, sems = refs[19:25], refs[25:29], refs[29]
    loads = [pltpu.make_async_copy(ins[k], raw[k], sems.at[k]) for k in range(6)]
    for load in loads:
        load.start()
    for k in range(4):
        small[k][...] = sums[k // 2][pl.ds(k % 2, 1), :]
    count = small[4].shape[1]
    small[4][...] = (sums[1][pl.ds(2, 1), pl.ds(0, count)] / groups).astype(jnp.int32)
    stores = []

    def store(k, src):
        stores.append(pltpu.make_async_copy(src, outs[k], sems.at[6 + k]))
        stores[-1].start()

    loads[0].wait()
    rows, columns = raw[0].shape

    def widen(r):
        done[0][pl.ds(r, 32), :] = wide(raw[0][pl.ds(r, 32), :])

    loop_rows(rows, 32, widen)
    store(0, done[0])
    loads[1].wait()

    def turn(src, dst):
        def body(c):
            dst[pl.ds(c, 256), :] = wide(src[:, pl.ds(c, 256)]).T

        loop_rows(src.shape[1], 256, body)

    turn(raw[1], done[1])
    store(1, done[1])
    loads[2].wait()
    for k in range(raw[2].shape[0]):

        def widen_part(r, k=k):
            done[2][k, pl.ds(r, 64), :] = wide(raw[2][k, pl.ds(r, 64), :])

        loop_rows(raw[2].shape[1], 64, widen_part)
    store(2, done[2])
    loads[3].wait()
    turn(raw[3], done[3])
    store(3, done[3])
    for k in (4, 5):
        loads[k].wait()
        store(k, raw[k])
    for one in stores:
        one.wait()


def finish_call(grad_up, grad_down, grad_qkv, grad_out, output, grad_input, sums1, sums2):
    f32 = jnp.float32
    ins = (grad_up, grad_down, grad_qkv, grad_out, output, grad_input)
    shapes = [a.shape for a in ins]
    shapes[1], shapes[3] = shapes[1][::-1], shapes[3][::-1]
    any_spec = pl.BlockSpec(memory_space=pl.ANY)
    vmem_spec = pl.BlockSpec(memory_space=pltpu.VMEM)
    groups = lax.axis_size("tensor")
    return pl.pallas_call(
        functools.partial(finish_kernel, groups),
        out_shape=[jax.ShapeDtypeStruct(s, f32) for s in shapes]
        + [jax.ShapeDtypeStruct((1, sums1.shape[1]), f32)] * 4
        + [jax.ShapeDtypeStruct((1, groups), jnp.int32)],
        in_specs=[any_spec] * 6 + [vmem_spec] * 2,
        out_specs=[any_spec] * 6 + [vmem_spec] * 5,
        scratch_shapes=[pltpu.VMEM(a.shape, a.dtype) for a in ins]
        + [pltpu.VMEM(s, f32) for s in shapes[:4]]
        + [pltpu.SemaphoreType.DMA((12,))],
        compiler_params=pltpu.CompilerParams(vmem_limit_bytes=62 << 20),
    )(*ins, sums1, sums2)


def local_fast(
    residual_in,
    lengths,
    head_bucket,
    width_bucket,
    norm1_gain,
    norm1_shift,
    w_qkv,
    w_out,
    norm2_gain,
    norm2_shift,
    w_up,
    w_down,
    cotangent,
):
    f32 = jnp.float32
    tokens = residual_in.shape[0]
    steps = np.arange(tokens)[:, None] * 10000.0 ** (-2.0 * (np.arange(HD) % (HD // 2)) / HD)
    arrays = (
        residual_in,
        cotangent,
        norm1_gain[None],
        norm1_shift[None],
        norm2_gain[None],
        norm2_shift[None],
        lengths,
        head_bucket,
        width_bucket,
        jnp.asarray(np.cos(steps), f32),
        jnp.asarray(np.sin(steps), f32),
    )
    weights = (jnp.swapaxes(w_qkv, 0, 1), w_out, w_up, w_down)
    (cosine, sine, head_mask), saved = forward_call(arrays, weights)
    arrays = (cotangent, norm1_gain[None], norm2_gain[None], cosine, sine, head_mask)
    output, grad_input, sums2, sums1, grad_qkv, grad_out, grad_up, grad_down = backward_call(
        (*arrays, lengths, width_bucket), saved
    )
    grad_up, grad_down, grad_qkv, grad_out, output, grad_input, *small = finish_call(
        grad_up, grad_down, grad_qkv, grad_out, output, grad_input, sums1, sums2
    )
    gain1_grad, shift1_grad, gain2_grad, shift2_grad, bucket_counts = [one[0] for one in small]
    return (
        output,
        grad_input,
        gain1_grad,
        shift1_grad,
        jnp.swapaxes(grad_qkv, 0, 1),
        grad_out,
        gain2_grad,
        shift2_grad,
        grad_up,
        grad_down,
        bucket_counts,
    )


def local(*args):
    w_out = args[7]
    if lax.axis_size("dp") == 8 and lax.axis_size("tensor") == 4 and w_out.shape[1] % 128 == 0:
        return local_fast(*args)
    return local_general(*args)


def solution(mesh):
    placed = (
        P("dp", "tensor"),
        P("dp", None),
        P("dp", None),
        P("dp", None),
        P(),
        P(),
        P("dp", None, "tensor"),
        P("tensor", "dp"),
        P(),
        P(),
        P("dp", "tensor"),
        P("tensor", "dp"),
        P("dp", "tensor"),
    )
    return jax.shard_map(
        local,
        mesh=mesh,
        in_specs=placed,
        out_specs=(
            P("dp", "tensor"),
            P("dp", "tensor"),
            P(),
            P(),
            P("dp", None, "tensor"),
            P("tensor", "dp"),
            P(),
            P(),
            P("dp", "tensor"),
            P("tensor", "dp"),
            P(),
        ),
        check_vma=False,
    )
```

```python
import functools
import math

import jax
import jax.numpy as jnp
import numpy as np
from jax import lax
from jax.experimental import pallas as pl
from jax.experimental.pallas import tpu as pltpu
from jax.sharding import PartitionSpec as P

HD = 128
HIDDEN_BIT = 2

epsilon = 1e-05


def dp_swap(value, bit):
    count = lax.axis_size("dp")
    return lax.ppermute(value, "dp", [(i, i ^ bit) for i in range(count)])


def tensor_swap(value, bit):
    count = lax.axis_size("tensor")
    return lax.ppermute(value, "tensor", [(i, i ^ bit) for i in range(count)])


def bits_of(count):
    return [1 << i for i in range(count.bit_length() - 1)]


def replica_bits():
    bits = bits_of(lax.axis_size("dp"))
    return [b for b in bits if b > HIDDEN_BIT] + [b for b in bits if b < HIDDEN_BIT]


def gather_weight(mine, other):
    blocks = {0: mine, HIDDEN_BIT: dp_swap(other, HIDDEN_BIT)}
    for bit in replica_bits():
        blocks.update({m | bit: dp_swap(blocks[m], bit) for m in list(blocks)})
    return blocks


def add_low(left, right):
    return (left.astype(jnp.float32) + right.astype(jnp.float32)).astype(jnp.bfloat16)


def scatter_weight(blocks):
    for bit in reversed(replica_bits()):
        arrived = {m ^ bit: dp_swap(blocks[m], bit) for m in blocks if m & bit}
        blocks = {m: add_low(blocks[m], arrived[m]) for m in arrived}
    return blocks[0], dp_swap(blocks[HIDDEN_BIT], HIDDEN_BIT)


def gather_act(rows):
    blocks = {(0, 0): rows, (1, 0): dp_swap(rows, HIDDEN_BIT)}
    for bit in reversed(bits_of(lax.axis_size("tensor"))):
        blocks.update({(b, m | bit): tensor_swap(v, bit) for (b, m), v in list(blocks.items())})
    return blocks


def scatter_act(blocks):
    for bit in bits_of(lax.axis_size("tensor")):
        arrived = {(b, m ^ bit): tensor_swap(v, bit) for (b, m), v in blocks.items() if m & bit}
        blocks = {k: add_low(blocks[k], arrived[k]) for k in arrived}
    return blocks[(0, 0)].astype(jnp.float32) + dp_swap(blocks[(1, 0)], HIDDEN_BIT).astype(
        jnp.float32
    )


def lay(blocks, shape, spots):
    count = len(blocks)

    def kernel(*refs):
        ins, out, sems = refs[:count], refs[count], refs[count + 1]
        copies = []
        for i, spot in enumerate(spots()):
            r, c = blocks[i].shape
            copies.append(
                pltpu.make_async_copy(
                    ins[i],
                    out.at[pl.ds(pl.multiple_of(spot[0], 16), r), pl.ds(pl.multiple_of(spot[1], 128), c)],
                    sems.at[i],
                )
            )
        for copy in copies:
            copy.start()
        for copy in copies:
            copy.wait()

    return pl.pallas_call(
        kernel,
        out_shape=jax.ShapeDtypeStruct(shape, jnp.bfloat16),
        in_specs=[pl.BlockSpec(memory_space=pl.ANY)] * count,
        out_specs=pl.BlockSpec(memory_space=pltpu.VMEM),
        scratch_shapes=[pltpu.SemaphoreType.DMA((count,))],
        compiler_params=pltpu.CompilerParams(vmem_limit_bytes=24 << 20),
    )(*blocks)


def cut(whole, block_shape, count, spots):
    def kernel(*refs):
        src, outs, sems = refs[0], refs[1 : 1 + count], refs[1 + count]
        r, c = block_shape
        copies = []
        for i, spot in enumerate(spots()):
            copies.append(
                pltpu.make_async_copy(
                    src.at[pl.ds(pl.multiple_of(spot[0], 16), r), pl.ds(pl.multiple_of(spot[1], 128), c)],
                    outs[i],
                    sems.at[i],
                )
            )
        for copy in copies:
            copy.start()
        for copy in copies:
            copy.wait()

    return pl.pallas_call(
        kernel,
        out_shape=[jax.ShapeDtypeStruct(block_shape, jnp.bfloat16)] * count,
        in_specs=[pl.BlockSpec(memory_space=pltpu.VMEM)],
        out_specs=[pl.BlockSpec(memory_space=pl.ANY)] * count,
        scratch_shapes=[pltpu.SemaphoreType.DMA((count,))],
        compiler_params=pltpu.CompilerParams(vmem_limit_bytes=24 << 20),
    )(whole)


def lay_weight(blocks, axis):
    count = len(blocks)
    r, c = blocks[0].shape
    if axis == 1 and c % 128:
        order = jnp.bitwise_xor(lax.axis_index("dp"), jnp.arange(count))
        stacked = jnp.stack([blocks[m] for m in range(count)])[order]
        return jnp.swapaxes(stacked, 0, 1).reshape(r, count * c)

    def spots():
        place = lax.axis_index("dp")
        at = [jnp.bitwise_xor(place, m) for m in range(count)]
        return [(d * r, 0) if axis == 0 else (0, d * c) for d in at]

    shape = (r * count, c) if axis == 0 else (r, c * count)
    return lay([blocks[m] for m in range(count)], shape, spots)


def cut_weight(whole, axis):
    count = lax.axis_size("dp")
    r, c = whole.shape
    r, c = (r // count, c) if axis == 0 else (r, c // count)
    if axis == 1 and c % 128:
        order = jnp.bitwise_xor(lax.axis_index("dp"), jnp.arange(count))
        stacked = jnp.swapaxes(whole.reshape(r, count, c), 0, 1)[order]
        return {m: stacked[m] for m in range(count)}

    def spots():
        place = lax.axis_index("dp")
        at = [jnp.bitwise_xor(place, m) for m in range(count)]
        return [(d * r, 0) if axis == 0 else (0, d * c) for d in at]

    return dict(enumerate(cut(whole, (r, c), count, spots)))


def act_keys():
    return [(b, m) for b in range(2) for m in range(lax.axis_size("tensor"))]


def act_spots(r, c):
    place = lax.axis_index("tensor")
    return [(b * r, jnp.bitwise_xor(place, m) * c) for b, m in act_keys()]


def lay_act(blocks):
    r, c = blocks[(0, 0)].shape
    shape = (2 * r, c * lax.axis_size("tensor"))
    return lay([blocks[k] for k in act_keys()], shape, lambda: act_spots(r, c))


def cut_act(whole):
    r, c = whole.shape[0] // 2, whole.shape[1] // lax.axis_size("tensor")
    keys = act_keys()
    return dict(zip(keys, cut(whole, (r, c), len(keys), lambda: act_spots(r, c))))


def whole_stream(rows):
    return lay_act(gather_act(rows.astype(jnp.bfloat16)))


def stream_sum(rows):
    return scatter_act(cut_act(rows.astype(jnp.bfloat16)))


def sum_all(value, axes):
    if "dp" in axes:
        for bit in bits_of(lax.axis_size("dp")):
            value = value + dp_swap(value, bit)
    if "tensor" in axes:
        for bit in bits_of(lax.axis_size("tensor")):
            value = value + tensor_swap(value, bit)
    return value


def token_info(length_row, head_row, width_row, row_count):
    seq_ends = jnp.cumsum(length_row)
    seq_starts = seq_ends - length_row
    places = jnp.arange(row_count, dtype=jnp.int32)
    segment = jnp.sum((places[:, None] >= seq_ends[None, :]).astype(jnp.int32), axis=1)
    labels = jnp.arange(length_row.shape[0], dtype=jnp.int32)
    onehot = (segment[:, None] == labels[None, :]).astype(jnp.int32)
    offset = places - jnp.sum(onehot * seq_starts[None, :], axis=1)
    head_tok = jnp.sum(onehot * head_row[None, :], axis=1)
    width_tok = jnp.sum(onehot * width_row[None, :], axis=1)
    return (segment, offset, head_tok, width_tok)


def rotary_tables(offset, head_size):
    half_size = head_size // 2
    ladder = jnp.arange(half_size, dtype=jnp.float32)
    inverse = jnp.exp(ladder * (-2.0 * math.log(10000.0) / head_size))
    angles = offset.astype(jnp.float32)[:, None] * inverse[None, :]
    return (jnp.cos(angles)[:, None, :], jnp.sin(angles)[:, None, :])


def rotate(values, cosine, sine_part):
    half_size = values.shape[-1] // 2
    front_half = values[..., :half_size]
    back_half = values[..., half_size:]
    return jnp.concatenate(
        [front_half * cosine - back_half * sine_part, back_half * cosine + front_half * sine_part],
        axis=-1,
    )


def norm_forward(values, norm_gain, norm_shift):
    values = values.astype(jnp.float32)
    center = values - jnp.mean(values, axis=-1, keepdims=True)
    spread = jnp.mean(center * center, axis=-1, keepdims=True)
    inverse = lax.rsqrt(spread + epsilon)
    unit_rows = center * inverse
    return (unit_rows * norm_gain + norm_shift, unit_rows, inverse)


def norm_backward(grad_rows, unit_rows, inverse, norm_gain):
    scaled = grad_rows * norm_gain
    grad_in = inverse * (
        scaled
        - jnp.mean(scaled, axis=-1, keepdims=True)
        - unit_rows * jnp.mean(scaled * unit_rows, axis=-1, keepdims=True)
    )
    return (grad_in, jnp.sum(grad_rows * unit_rows, axis=0), jnp.sum(grad_rows, axis=0))


def heads_of(rows, blocks):
    rows = rows.reshape(blocks, rows.shape[0] // blocks, -1, HD)
    return jnp.transpose(rows, (2, 0, 1, 3)).reshape(-1, rows.shape[1], HD)


def rows_of(heads, blocks):
    heads = heads.reshape(-1, blocks, heads.shape[1], HD)
    return jnp.transpose(heads, (1, 2, 0, 3)).reshape(blocks * heads.shape[2], -1)


def local_general(
    residual_in,
    lengths,
    head_bucket,
    width_bucket,
    norm1_gain,
    norm1_shift,
    w_qkv,
    w_out,
    norm2_gain,
    norm2_shift,
    w_up,
    w_down,
    cotangent,
):
    f32, bf16 = jnp.float32, jnp.bfloat16
    dot = functools.partial(jnp.dot, preferred_element_type=f32)
    tensor_index = lax.axis_index("tensor")
    bucket_total = lax.axis_size("tensor")
    tokens = residual_in.shape[0]
    side = (lax.axis_index("dp") // HIDDEN_BIT) % 2

    def halves(weight, axis):
        left, right = jnp.split(weight, 2, axis=axis)
        return jnp.where(side == 0, left, right), jnp.where(side == 0, right, left)

    info = jnp.stack([lengths[0], head_bucket[0], width_bucket[0]])
    far_info = dp_swap(info, HIDDEN_BIT)
    pair = [token_info(i[0], i[1], i[2], tokens) for i in (info, far_info)]
    segment, offset, head_tok, width_tok = [jnp.stack([a, b]) for a, b in zip(*pair)]
    matches = (
        width_bucket[0][:, None] == jnp.arange(bucket_total, dtype=jnp.int32)[None, :]
    ).astype(jnp.int32)
    bucket_counts = sum_all(jnp.sum(lengths[0][:, None] * matches, axis=0), ("dp",))
    head_mask = (head_tok.reshape(-1) >= tensor_index).astype(f32)[:, None]
    width_mask = (width_tok.reshape(-1) >= tensor_index).astype(f32)[:, None]
    places = jnp.arange(tokens, dtype=jnp.int32)
    allowed = (segment[:, :, None] == segment[:, None, :]) & (
        places[:, None] >= places[None, :]
    )
    cosine, sine_part = rotary_tables(offset.reshape(-1), HD)
    score_scale = HD ** (-0.5)

    qkv_halves = [h.reshape(h.shape[0], -1) for h in halves(w_qkv, 2)]
    full_qkv = lay_weight(gather_weight(*qkv_halves), 0)
    full_out = lay_weight(gather_weight(*halves(w_out, 0)), 1)
    full_up = lay_weight(gather_weight(*halves(w_up, 1)), 0)
    full_down = lay_weight(gather_weight(*halves(w_down, 0)), 1)

    inputs = whole_stream(residual_in)
    normed1, unit1, inverse1 = norm_forward(inputs, norm1_gain, norm1_shift)
    normed1 = normed1.astype(bf16)
    projected = dot(normed1, full_qkv).reshape(2 * tokens, 3, -1, HD)
    width = projected.shape[2] * HD
    query = rotate(projected[:, 0], cosine, sine_part).astype(bf16).reshape(-1, width)
    key = rotate(projected[:, 1], cosine, sine_part).astype(bf16).reshape(-1, width)
    value = projected[:, 2].astype(bf16).reshape(-1, width)
    query, key, value = heads_of(query, 2), heads_of(key, 2), heads_of(value, 2)
    allowed = jnp.tile(allowed, (query.shape[0] // 2, 1, 1))
    scores = jnp.einsum("nqd,nkd->nqk", query, key, preferred_element_type=f32) * score_scale
    scores = jnp.where(allowed, scores, -1000000000.0)
    scores = jnp.exp(scores - jnp.max(scores, axis=-1, keepdims=True))
    weights = (scores / jnp.sum(scores, axis=-1, keepdims=True)).astype(bf16)
    mixed = jnp.einsum("nqk,nkd->nqd", weights, value, preferred_element_type=f32)
    mixed = (rows_of(mixed, 2) * head_mask).astype(bf16)
    middle = residual_in + stream_sum(dot(mixed, full_out))
    middle_rows = whole_stream(middle)
    normed2, unit2, inverse2 = norm_forward(middle_rows, norm2_gain, norm2_shift)
    normed2 = normed2.astype(bf16)
    upper = jnp.maximum(dot(normed2, full_up), 0.0) * width_mask
    active = jnp.square(upper).astype(bf16)
    upper = upper.astype(bf16)
    output = middle + stream_sum(dot(active, full_down))

    grad_top = whole_stream(cotangent)
    grad_down = scatter_weight(cut_weight(dot(active.T, grad_top).astype(bf16), 1))
    grad_active = dot(grad_top, full_down.T)
    grad_upper = (grad_active * 2.0 * upper.astype(f32)).astype(bf16)
    grad_normed2 = dot(grad_upper, full_up.T)
    part_middle, gain2_grad, shift2_grad = norm_backward(
        grad_normed2, unit2, inverse2, norm2_gain
    )
    grad_middle = cotangent + stream_sum(part_middle)
    grad_up = scatter_weight(cut_weight(dot(normed2.T, grad_upper).astype(bf16), 0))
    grad_branch = whole_stream(grad_middle)
    grad_wout = scatter_weight(cut_weight(dot(mixed.T, grad_branch).astype(bf16), 1))
    grad_mixed = (dot(grad_branch, full_out.T) * head_mask).astype(bf16)
    grad_mixed = heads_of(grad_mixed, 2)
    grad_weights = jnp.einsum("nqd,nkd->nqk", grad_mixed, value, preferred_element_type=f32)
    grad_value = jnp.einsum("nqk,nqd->nkd", weights, grad_mixed, preferred_element_type=f32)
    wide = weights.astype(f32)
    grad_scores = wide * (grad_weights - jnp.sum(grad_weights * wide, axis=-1, keepdims=True))
    grad_raw = (grad_scores * score_scale).astype(bf16)
    grad_query = jnp.einsum("nqk,nkd->nqd", grad_raw, key, preferred_element_type=f32)
    grad_key = jnp.einsum("nqk,nqd->nkd", grad_raw, query, preferred_element_type=f32)
    grad_query, grad_key = [
        rotate(rows_of(g, 2).reshape(2 * tokens, -1, HD), cosine, -sine_part).reshape(-1, width)
        for g in (grad_query, grad_key)
    ]
    grad_projected = jnp.concatenate([grad_query, grad_key, rows_of(grad_value, 2)], axis=1)
    grad_projected = grad_projected.astype(bf16)
    grad_normed1 = dot(grad_projected, full_qkv.T)
    part_input, gain1_grad, shift1_grad = norm_backward(
        grad_normed1, unit1, inverse1, norm1_gain
    )
    grad_input = grad_middle + stream_sum(part_input)
    grad_qkv = scatter_weight(cut_weight(dot(normed1.T, grad_projected).astype(bf16), 0))

    def join(pair, axis):
        left = jnp.where(side == 0, pair[0], pair[1])
        right = jnp.where(side == 0, pair[1], pair[0])
        return jnp.concatenate([left, right], axis=axis).astype(f32)

    grad_qkv = join([g.reshape(g.shape[0], 3, width) for g in grad_qkv], 2)
    grad_wout, grad_up, grad_down = join(grad_wout, 0), join(grad_up, 1), join(grad_down, 0)
    gain2_grad, shift2_grad = sum_all(jnp.stack([gain2_grad, shift2_grad]), ("dp", "tensor"))
    gain1_grad, shift1_grad = sum_all(jnp.stack([gain1_grad, shift1_grad]), ("dp", "tensor"))
    return (
        output,
        grad_input,
        gain1_grad,
        shift1_grad,
        grad_qkv,
        grad_wout,
        gain2_grad,
        shift2_grad,
        grad_up,
        grad_down,
        bucket_counts,
    )


def flip(i, bit):
    return i + bit - 2 * bit * ((i // bit) % 2)


class Traffic:
    def __init__(self, send_sems, recv_sems):
        self.send_sems, self.recv_sems = send_sems, recv_sems
        self.copies, self.gone, self.come = {}, set(), set()

    def send(self, name, src, dst, device):
        k = len(self.copies)
        copy = pltpu.make_async_remote_copy(
            src_ref=src,
            dst_ref=dst,
            send_sem=self.send_sems.at[k],
            recv_sem=self.recv_sems.at[k],
            device_id=device,
            device_id_type=pl.DeviceIdType.MESH,
        )
        copy.start()
        self.copies[name] = copy

    def wait(self, *names):
        for name in names:
            if name not in self.come:
                self.copies[name].wait_recv()
                self.come.add(name)

    def sent(self, *names):
        for name in names:
            if name not in self.gone:
                self.copies[name].wait_send()
                self.gone.add(name)

    def finish(self):
        self.sent(*self.copies)


class Moves:
    def __init__(self, sems):
        self.sems, self.copies = sems, {}

    def start(self, name, src, dst):
        copy = pltpu.make_async_copy(src, dst, self.sems.at[len(self.copies)])
        copy.start()
        self.copies[name] = [copy, False]

    def wait(self, *names):
        for name in names:
            if not self.copies[name][1]:
                self.copies[name][0].wait()
                self.copies[name][1] = True

    def finish(self):
        self.wait(*self.copies)


class Place:
    def __init__(self):
        self.i, self.t = lax.axis_index("dp"), lax.axis_index("tensor")
        self.side = (self.i // 2 + self.i // 4) % 2
        self.x, self.z = [(flip(self.i, b), self.t) for b in (1, 2)]
        self.far = (self.block(6), self.t)
        self.c, self.y = [(self.i, flip(self.t, b)) for b in (1, 2)]

    def greet(self):
        barrier = pltpu.get_barrier_semaphore()
        partners = (self.x, self.z, self.far, self.c, self.y)
        for device in partners:
            pl.semaphore_signal(
                barrier, inc=1, device_id=device, device_id_type=pl.DeviceIdType.MESH
            )
        pl.semaphore_wait(barrier, len(partners))

    def block(self, m):
        d = self.i
        for bit in (1, 2, 4):
            if m & bit:
                d = flip(d, bit)
        return d

    def stripe(self, m):
        s = self.t
        for bit in (1, 2):
            if m & bit:
                s = flip(s, bit)
        return s


class WeightGather:
    def __init__(self, name, place, traffic, moves, half, slot):
        self.name, self.p, self.tr, self.mv = name, place, traffic, moves
        self.half, self.slot = half, slot

    def own(self):
        self.mv.start(self.name + "0", self.half(self.p.side), self.slot(self.p.i))

    def z(self):
        self.tr.send(self.name + "2", self.half(1 - self.p.side), self.slot(self.p.i), self.p.z)

    def far(self):
        self.tr.send(self.name + "6", self.half(self.p.side), self.slot(self.p.i), self.p.far)

    def x(self):
        self.tr.send(self.name + "1", self.half(self.p.side), self.slot(self.p.i), self.p.x)

    def far_next(self):
        self.tr.wait(self.name + "2")
        block = self.slot(self.p.block(2))
        self.tr.send(self.name + "4", block, block, self.p.far)

    def x_next(self, m):
        self.tr.wait(self.name + str(m))
        block = self.slot(self.p.block(m))
        self.tr.send(self.name + str(m + 1), block, block, self.p.x)

    def take(self, *which):
        for m in which:
            if m == 0:
                self.mv.wait(self.name + "0")
            else:
                self.tr.wait(self.name + str(m))

    def end(self):
        self.take(*range(8))


class ActGather:
    def __init__(self, name, place, traffic, slots):
        self.name, self.p, self.tr, self.slots = name, place, traffic, slots

    def at(self, b, m):
        return self.slots.at[b, self.p.stripe(m)]

    def z(self):
        self.tr.send(self.name + "10", self.at(0, 0), self.slots.at[1, self.p.t], self.p.z)

    def y(self):
        self.tr.send(self.name + "02", self.at(0, 0), self.at(0, 0), self.p.y)

    def c(self):
        self.tr.send(self.name + "01", self.at(0, 0), self.at(0, 0), self.p.c)

    def pass_z(self):
        self.tr.wait(self.name + "10")
        block = self.at(1, 0)
        self.tr.send(self.name + "12", block, block, self.p.y)
        self.tr.send(self.name + "11", block, block, self.p.c)

    def pass_y(self, b):
        self.tr.wait(self.name + str(b) + "2")
        block = self.at(b, 2)
        self.tr.send(self.name + str(b) + "3", block, block, self.p.c)

    def take(self, b):
        for m in range(1 - b, 4):
            self.tr.wait(self.name + str(b) + str(m))


def loop_rows(count, step, body):
    def run(k, carry):
        body(pl.multiple_of(k * step, step))
        return carry

    lax.fori_loop(0, count // step, run, 0)


def wide(value):
    return value.astype(jnp.float32)


def add_blocks(out, left, right, rows):
    def body(r):
        at = pl.ds(r, 64)
        out[at, :] = (wide(left[at, :]) + wide(right[at, :])).astype(out.dtype)

    loop_rows(rows, 64, body)


class ActScatter:
    def __init__(self, name, place, traffic, part, got_c, got_y, got_z):
        self.name, self.p, self.tr = name, place, traffic
        self.part, self.got_c, self.got_y, self.got_z = part, got_c, got_y, got_z
        self.rows = part.shape[2]

    def at(self, b, m):
        return self.part.at[b, self.p.stripe(m)]

    def c(self, b):
        for j, m in ((1, 3), (0, 1)):
            name = self.name + "c" + str(b) + str(j)
            self.tr.send(name, self.at(b, m), self.got_c.at[b, j], self.p.c)

    def add(self, b, m, name, got):
        self.tr.wait(self.name + name)
        add_blocks(self.at(b, m), self.at(b, m), got, self.rows)

    def y(self, b):
        self.add(b, 2, "c" + str(b) + "1", self.got_c.at[b, 1])
        self.tr.send(self.name + "y" + str(b), self.at(b, 2), self.got_y.at[b], self.p.y)

    def own(self, b):
        self.add(b, 0, "c" + str(b) + "0", self.got_c.at[b, 0])

    def z(self):
        self.add(1, 0, "y1", self.got_y.at[1])
        self.tr.send(self.name + "z", self.at(1, 0), self.got_z, self.p.z)

    def home(self):
        self.add(0, 0, "y0", self.got_y.at[0])

    def sent(self):
        for key in ("c11", "c01", "c10", "c00", "y1", "y0", "z"):
            self.tr.sent(self.name + key)

    def end(self, out, base):
        self.tr.wait(self.name + "z")
        own = self.at(0, 0)

        def body(r):
            at = pl.ds(r, 64)
            out[at, :] = base[at, :] + (wide(own[at, :]) + wide(self.got_z[at, :]))

        loop_rows(self.rows, 64, body)


def round_rows(src, dst, rows):
    def body(r):
        at = pl.ds(r, 64)
        dst[at, :] = src[at, :].astype(dst.dtype)

    loop_rows(rows, 64, body)


def dot_f32(left, right):
    return jnp.dot(left, right, preferred_element_type=jnp.float32)


def dot_nt(left, right):
    return lax.dot_general(
        left, right, (((1,), (1,)), ((), ())), preferred_element_type=jnp.float32
    )


def dot_tn(left, right):
    return lax.dot_general(
        left, right, (((0,), (0,)), ((), ())), preferred_element_type=jnp.float32
    )


def center_rows(slots, b, at):
    stripes = slots.shape[1]
    rows = jnp.concatenate([wide(slots[b, s, at, :]) for s in range(stripes)], axis=1)
    center = rows - jnp.mean(rows, axis=1, keepdims=True)
    spread = jnp.mean(center * center, axis=1, keepdims=True)
    return center, lax.rsqrt(spread + epsilon)


def norm_rows(slots, b, gain, shift, out):
    rows = slots.shape[2]

    def body(r):
        center, inverse = center_rows(slots, b, pl.ds(r, 128))
        out[pl.ds(b * rows + r, 128), :] = (center * inverse * gain[...] + shift[...]).astype(
            jnp.bfloat16
        )

    loop_rows(rows, 128, body)


def attend(b, qkv, seg_col, seg_row, head_mask, weights, mixed, scale):
    tokens = seg_row.shape[2]
    heads = qkv.shape[2] // HD
    half = tokens // 2
    start = b * tokens
    for h in range(heads):
        cols = pl.ds(h * HD, HD)
        for part in range(2):
            rows = pl.ds(start + part * half, half)
            reach = half * (part + 1)
            query = qkv[0, rows, cols]
            key = qkv[1, pl.ds(start, reach), cols]
            value = qkv[2, pl.ds(start, reach), cols]
            scores = dot_nt(query, key) * scale
            row_id = lax.broadcasted_iota(jnp.int32, (half, reach), 0) + part * half
            col_id = lax.broadcasted_iota(jnp.int32, (half, reach), 1)
            same = seg_col[rows, :] == seg_row[b, :, pl.ds(0, reach)]
            scores = jnp.where(same & (row_id >= col_id), scores, -1000000000.0)
            scores = jnp.exp(scores - jnp.max(scores, axis=1, keepdims=True))
            total = jnp.sum(scores, axis=1, keepdims=True)
            chosen = (scores / total).astype(jnp.bfloat16)
            weights[b * heads + h, pl.ds(part * half, half), pl.ds(0, reach)] = chosen
            mixed[rows, cols] = (dot_f32(chosen, value) * head_mask[rows, :]).astype(jnp.bfloat16)


def sequences(lengths):
    start = 0
    for s in range(lengths.shape[1]):
        length = lengths[0, s]
        yield s, start, length
        start = start + length


def count_row(lengths, width_bucket, lanes):
    lane = lax.broadcasted_iota(jnp.int32, (1, lanes), 1)
    row = jnp.zeros((1, lanes), jnp.float32)
    for s, _, length in sequences(lengths):
        row = row + jnp.where(lane == width_bucket[0, s], wide(length), 0.0)
    return row


def fill_facts(lengths, head_bucket, width_bucket, place_cosine, place_sine, facts):
    lanes = facts.shape[1]
    row = lax.broadcasted_iota(jnp.int32, (8, lanes), 0)
    lane = lax.broadcasted_iota(jnp.int32, (8, lanes), 1)
    count = lengths.shape[1]
    by_lane = jnp.where((row == 0) & (lane >= count), 1e9, 0.0)
    by_row = jnp.where(row >= count, 1e9, 0.0)
    for s, start, length in sequences(lengths):
        end = wide(start + length)
        here = lane == s
        by_lane = by_lane + jnp.where((row == 0) & here, end, 0.0)
        by_lane = by_lane + jnp.where((row == 2) & here, wide(head_bucket[0, s]), 0.0)
        by_lane = by_lane + jnp.where((row == 3) & here, wide(width_bucket[0, s]), 0.0)
        by_row = by_row + jnp.where(row == s, end, 0.0)
        facts[pl.ds(16 + s, 1), :] = place_cosine[pl.ds(start, 1), :]
        facts[pl.ds(20 + s, 1), :] = place_sine[pl.ds(start, 1), :]
    facts[pl.ds(0, 8), :] = by_lane
    facts[pl.ds(8, 8), :] = by_row


def fill_tables(
    infos, place_cosine, place_sine, t, cosine, sine, head_mask, width_mask, seg_col, seg_row
):
    tokens, lanes = place_cosine.shape
    own = wide(t)
    lane = wide(lax.broadcasted_iota(jnp.int32, (tokens, lanes), 1))
    place = wide(lax.broadcasted_iota(jnp.int32, (tokens, lanes), 0))
    sign = jnp.where(lane < lanes // 2, -1.0, 1.0)
    for b in range(2):
        rows = pl.ds(b * tokens, tokens)

        def row(k, b=b):
            return infos[b, pl.ds(k, 1), :]

        segment = jnp.sum(jnp.where(place >= row(0), 1.0, 0.0), axis=1, keepdims=True)
        seg_col[rows, :] = segment
        chosen = jnp.where(lane == segment, 1.0, 0.0)
        head = jnp.sum(chosen * row(2), axis=1, keepdims=True)
        width = jnp.sum(chosen * row(3), axis=1, keepdims=True)
        head_mask[rows, :] = jnp.where(head >= own, 1.0, 0.0)
        width_mask[rows, :] = jnp.where(width >= own, 1.0, 0.0)
        start_cosine, start_sine = 0.0, 0.0
        for s in range(4):
            here = jnp.where(segment == s, 1.0, 0.0)
            start_cosine = start_cosine + here * row(16 + s)
            start_sine = start_sine + here * row(20 + s)
        at_cosine, at_sine = place_cosine[...], place_sine[...]
        cosine[rows, :] = at_cosine * start_cosine + at_sine * start_sine
        sine[rows, :] = (at_sine * start_cosine - at_cosine * start_sine) * sign
        ends = infos[b, pl.ds(8, 8), pl.ds(0, 1)]
        across = wide(lax.broadcasted_iota(jnp.int32, (8, tokens), 1))
        seg_row[b] = jnp.sum(jnp.where(across >= ends, 1.0, 0.0), axis=0, keepdims=True)


def forward_kernel(
    residual_in,
    cotangent_in,
    gain1,
    shift1,
    gain2,
    shift2,
    lengths,
    head_bucket,
    width_bucket,
    place_cosine_in,
    place_sine_in,
    half_qkv,
    half_out,
    half_up,
    half_down,
    cosine_out,
    sine_out,
    head_mask_out,
    all_qkv,
    all_out,
    all_up,
    stream1,
    stream2,
    stream_c,
    normed1,
    normed2,
    heads_out,
    weights_out,
    mixed_out,
    active_out,
    grad_upper_out,
    part_out,
    middle_out,
    w_qkv,
    w_out,
    w_up,
    w_down,
    rows1,
    rows2,
    rows_c,
    normed,
    qkv,
    weights,
    mixed,
    part,
    got_c,
    got_y,
    got_z,
    upper,
    active,
    grad_active,
    middle,
    infos,
    seg_col,
    seg_row,
    width_mask,
    residual,
    cotangent,
    place_cosine,
    place_sine,
    cosine,
    sine,
    head_mask,
    send_sems,
    recv_sems,
    move_sems,
):
    p = Place()
    tr, mv = Traffic(send_sems, recv_sems), Moves(move_sems)
    tokens = residual.shape[0]
    rows_d = half_qkv.shape[1]
    head_cols = w_out.shape[1]

    def row_slot(ref):
        return lambda d: ref.at[pl.ds(pl.multiple_of(d * rows_d, rows_d), rows_d)]

    def first_slot(ref):
        return lambda d: ref.at[d]

    def at_side(k, cut, size):
        return pl.ds(pl.multiple_of(k * size + cut.start, 128), cut.size)

    hidden = w_up.shape[1]
    parts = [pl.ds(0, hidden // 2), pl.ds(hidden // 2, hidden // 2)]

    def rows_at(d):
        return pl.ds(pl.multiple_of(d * rows_d, rows_d), rows_d)

    def up_gather(name, cut):
        return WeightGather(
            name,
            p,
            tr,
            mv,
            lambda k: half_up.at[:, at_side(k, cut, hidden)],
            lambda d: w_up.at[rows_at(d), cut],
        )

    def down_gather(name, cut):
        return WeightGather(
            name,
            p,
            tr,
            mv,
            lambda k: half_down.at[at_side(k, cut, hidden), :],
            lambda d: w_down.at[d, cut, :],
        )

    heads_cut = pl.ds(0, head_cols)
    q = WeightGather(
        "q",
        p,
        tr,
        mv,
        lambda k: half_qkv.at[:, :, at_side(k, heads_cut, head_cols)],
        lambda d: w_qkv.at[:, rows_at(d), :],
    )
    o = WeightGather(
        "o",
        p,
        tr,
        mv,
        lambda k: half_out.at[at_side(k, heads_cut, head_cols), :],
        lambda d: w_out.at[d],
    )
    u, v = [up_gather(n, cut) for n, cut in zip("uv", parts)]
    d, e = [down_gather(n, cut) for n, cut in zip("de", parts)]
    a1 = ActGather("a", p, tr, rows1)
    a2 = ActGather("b", p, tr, rows2)
    ac = ActGather("c", p, tr, rows_c)
    s1 = ActScatter("s", p, tr, part, got_c, got_y, got_z)

    mv.start("residual", residual_in, residual)
    mv.start("place_cosine", place_cosine_in, place_cosine)
    mv.start("place_sine", place_sine_in, place_sine)
    mv.start("cotangent", cotangent_in, cotangent)
    p.greet()
    for one in (q, o, u, v, d, e):
        one.own()
    blocks = w_out.shape[0]
    stripes = part.shape[1]
    per = blocks // stripes
    started = []

    def project(b):
        def body(r):
            at = pl.ds(b * tokens + r, 256)
            for k in range(3):
                got = dot_f32(normed[at, :], w_qkv[k])
                for h in range(head_cols // HD):
                    cols = pl.ds(h * HD, HD)
                    one = got[:, h * HD : (h + 1) * HD]
                    if k < 2:
                        one = one * cosine[at, :] + pltpu.roll(one, HD // 2, 1) * sine[at, :]
                    qkv[k, at, cols] = one.astype(jnp.bfloat16)

        loop_rows(tokens, 256, body)

    def branch(b):
        at = pl.ds(b * tokens, tokens)

        def body(s, carry):
            for j in range(per):
                got = dot_f32(mixed[at, :], w_out[s * per + j])
                part[b, s, :, pl.ds(j * rows_d, rows_d)] = got.astype(jnp.bfloat16)
            return carry

        lax.fori_loop(0, stripes, body, 0)

    def rise(b, cut):
        def body(r):
            at = pl.ds(b * tokens + r, 256)
            for k in range(cut.size // 256):
                cols = pl.ds(cut.start + k * 256, 256)
                got = dot_f32(normed[at, :], w_up[:, cols])
                got = jnp.maximum(got, 0.0) * width_mask[at, :]
                upper[at, cols] = got.astype(jnp.bfloat16)
                active[at, cols] = (got * got).astype(jnp.bfloat16)

        loop_rows(tokens, 256, body)

    def fall(m):
        place = p.block(m)
        s = place // per
        cols = pl.ds(pl.multiple_of((place % per) * rows_d, rows_d), rows_d)
        first = not started
        started.append(m)

        def body(r):
            b, at = r // tokens, pl.ds(pl.multiple_of(r % tokens, 256), 256)
            rows = pl.ds(r, 256)
            part[b, s, at, cols] = dot_f32(active[rows, :], w_down[place]).astype(jnp.bfloat16)
            got = dot_nt(rows_c[b, s, at, cols], w_down[place])
            grad_active[rows, :] = got if first else grad_active[rows, :] + got

        loop_rows(2 * tokens, 256, body)
        for b in range(2):
            mv.start("part" + str(b) + str(m), part.at[b, s, :, cols], part_out.at[b, s, :, cols])

    def turn(r):
        at = pl.ds(r, 64)
        active[at, :] = (grad_active[at, :] * 2.0 * wide(upper[at, :])).astype(jnp.bfloat16)

    q.z()
    mv.wait("residual")
    round_rows(residual, rows1.at[0, p.t], tokens)
    q.x()
    o.z()
    a1.z()
    e.x()
    q.far()
    q.far_next()
    v.x()
    mv.wait("place_cosine", "place_sine")
    fill_facts(lengths, head_bucket, width_bucket, place_cosine, place_sine, infos.at[0])
    tr.send("info", infos.at[0], infos.at[1], p.z)
    o.x_next(2)
    o.far_next()
    a1.y()
    a1.pass_z()
    q.x_next(2)
    a1.c()
    q.x_next(6)
    tr.wait("info")
    fill_tables(
        infos, place_cosine, place_sine, p.t, cosine, sine, head_mask, width_mask, seg_col, seg_row
    )
    mv.start("cosine", cosine, cosine_out)
    mv.start("sine", sine, sine_out)
    mv.start("head_mask", head_mask, head_mask_out)
    o.far()
    q.x_next(4)
    e.z()
    v.z()
    o.x()
    mv.wait("cotangent")
    round_rows(cotangent, rows_c.at[0, p.t], tokens)
    o.x_next(4)
    a1.pass_y(1)
    ac.y()
    u.z()
    d.z()
    a1.take(1)
    norm_rows(rows1, 1, gain1, shift1, normed)
    v.far()
    o.x_next(6)
    q.end()
    project(1)
    u.far()
    a1.pass_y(0)
    v.x_next(2)
    v.far_next()
    attend(
        1, qkv, seg_col, seg_row, head_mask, weights, mixed, HD ** (-0.5)
    )
    o.end()
    branch(1)
    s1.c(1)
    u.x()
    d.x()
    ac.pass_y(0)
    d.x_next(2)
    s1.y(1)
    a1.take(0)
    norm_rows(rows1, 0, gain1, shift1, normed)
    mv.start("stream1", rows1, stream1)
    mv.start("normed1", normed, normed1)
    project(0)
    mv.start("all_qkv", w_qkv, all_qkv)
    attend(
        0, qkv, seg_col, seg_row, head_mask, weights, mixed, HD ** (-0.5)
    )
    mv.start("heads", qkv, heads_out)
    mv.start("weights", weights, weights_out)
    mv.start("mixed", mixed, mixed_out)
    branch(0)
    mv.start("all_out", w_out, all_out)
    s1.own(1)
    s1.c(0)
    u.x_next(6)
    s1.z()
    s1.own(0)
    e.x_next(2)
    s1.y(0)
    u.far_next()
    s1.home()
    v.x_next(6)
    ac.c()
    v.x_next(4)
    s1.end(middle, residual)
    round_rows(middle, rows2.at[0, p.t], tokens)
    mv.start("middle", middle, middle_out)
    a2.z()
    ac.z()
    e.far_next()
    a2.y()
    u.x_next(2)
    d.far_next()
    e.far()
    d.far()
    u.x_next(4)
    a2.pass_z()
    a2.pass_y(0)
    a2.c()
    a2.take(0)
    mv.wait("normed1")
    norm_rows(rows2, 0, gain2, shift2, normed)
    ac.pass_z()
    a2.pass_y(1)
    u.end()
    rise(0, parts[0])
    e.x_next(4)
    v.end()
    rise(0, parts[1])
    a2.take(1)
    norm_rows(rows2, 1, gain2, shift2, normed)
    mv.start("stream2", rows2, stream2)
    mv.start("normed2", normed, normed2)
    rise(1, parts[0])
    d.x_next(4)
    ac.pass_y(1)
    rise(1, parts[1])
    mv.start("active", active, active_out)
    mv.start("all_up", w_up, all_up)
    e.x_next(6)
    ac.take(0)
    ac.take(1)
    s1.sent()
    d.take(4)
    e.take(4)
    fall(4)
    mv.start("stream_c", rows_c, stream_c)
    d.take(1)
    e.take(1)
    fall(1)
    d.take(2)
    e.take(2)
    fall(2)
    d.x_next(6)
    d.take(6)
    e.take(6)
    fall(6)
    d.take(3)
    e.take(3)
    fall(3)
    d.take(0)
    e.take(0)
    fall(0)
    d.take(5)
    e.take(5)
    fall(5)
    d.take(7)
    e.take(7)
    fall(7)
    mv.wait("active")
    loop_rows(2 * tokens, 64, turn)
    mv.start("grad_upper", active, grad_upper_out)
    tr.finish()
    mv.finish()


def forward_call(arrays, weights):
    bf16, f32 = jnp.bfloat16, jnp.float32
    tokens, columns = arrays[0].shape
    w_qkv, w_out, w_up, w_down = weights
    count, stripes = lax.axis_size("dp"), lax.axis_size("tensor")
    rows_d = w_up.shape[0]
    head_cols = w_out.shape[0] // 2
    hidden = w_up.shape[1] // 2
    width = rows_d * count
    heads = head_cols // HD
    slots = (2, stripes, tokens, columns)
    tables = dict(
        cosine=((2 * tokens, HD), f32),
        sine=((2 * tokens, HD), f32),
        head_mask=((2 * tokens, 1), f32),
    )
    shapes = dict(
        all_qkv=((3, width, head_cols), bf16),
        all_out=((count, head_cols, rows_d), bf16),
        all_up=((width, hidden), bf16),
        stream1=(slots, bf16),
        stream2=(slots, bf16),
        stream_c=(slots, bf16),
        normed1=((2 * tokens, width), bf16),
        normed2=((2 * tokens, width), bf16),
        heads=((3, 2 * tokens, head_cols), bf16),
        weights=((2 * heads, tokens, tokens), bf16),
        mixed=((2 * tokens, head_cols), bf16),
        active=((2 * tokens, hidden), bf16),
        grad_upper=((2 * tokens, hidden), bf16),
        part_out=(slots, bf16),
        middle=((tokens, columns), f32),
    )

    def vmem(name):
        return pltpu.VMEM(*shapes[name])

    scratch = [
        vmem("all_qkv"),
        vmem("all_out"),
        vmem("all_up"),
        pltpu.VMEM((count, hidden, rows_d), bf16),
        vmem("stream1"),
        vmem("stream2"),
        vmem("stream_c"),
        vmem("normed1"),
        vmem("heads"),
        vmem("weights"),
        vmem("mixed"),
        pltpu.VMEM(slots, bf16),
        pltpu.VMEM((2, 2, tokens, columns), bf16),
        pltpu.VMEM((2, tokens, columns), bf16),
        pltpu.VMEM((tokens, columns), bf16),
        vmem("active"),
        vmem("active"),
        pltpu.VMEM((2 * tokens, hidden), f32),
        vmem("middle"),
        pltpu.VMEM((2, 24, 128), f32),
        pltpu.VMEM((2 * tokens, 1), f32),
        pltpu.VMEM((2, 1, tokens), f32),
        pltpu.VMEM((2 * tokens, 1), f32),
        vmem("middle"),
        vmem("middle"),
        pltpu.VMEM((tokens, HD), f32),
        pltpu.VMEM((tokens, HD), f32),
        *[pltpu.VMEM(*s) for s in tables.values()],
        pltpu.SemaphoreType.DMA((72,)),
        pltpu.SemaphoreType.DMA((72,)),
        pltpu.SemaphoreType.DMA((48,)),
    ]
    any_spec = pl.BlockSpec(memory_space=pl.ANY)
    vmem_spec = pl.BlockSpec(memory_space=pltpu.VMEM)
    smem_spec = pl.BlockSpec(memory_space=pltpu.SMEM)
    outs = pl.pallas_call(
        forward_kernel,
        out_shape=[jax.ShapeDtypeStruct(*s) for s in (tables | shapes).values()],
        in_specs=[any_spec] * 2 + [vmem_spec] * 4 + [smem_spec] * 3 + [any_spec] * 6,
        out_specs=[any_spec] * (len(tables) + len(shapes)),
        scratch_shapes=scratch,
        compiler_params=pltpu.CompilerParams(
            collective_id=0, has_side_effects=True, vmem_limit_bytes=62 << 20
        ),
    )(*arrays, *weights)
    split = len(tables)
    return outs[:split], dict(zip(shapes, outs[split:]))


class WeightScatter:
    def __init__(self, name, place, traffic, odd, even, got_x, got_far, out):
        self.name, self.p, self.tr = name, place, traffic
        self.odd, self.even, self.got_x, self.got_far, self.out = odd, even, got_x, got_far, out

    def send_x(self, m):
        self.tr.send(self.name + "x" + str(m), self.odd.at[m // 2], self.got_x.at[m // 2], self.p.x)

    def add_x(self, m):
        k, n = m // 2, self.name
        own = self.even.at[k]
        self.tr.wait(n + "x" + str(m + 1))
        add_blocks(own, own, self.got_x.at[k], own.shape[0])
        if m >= 4:
            self.tr.send(n + "f" + str(m), own, self.got_far.at[3 - k], self.p.far)

    def add_far(self, m):
        k, n = m // 2, self.name
        own = self.even.at[k]
        self.tr.wait(n + "f" + str(6 - m))
        add_blocks(own, own, self.got_far.at[k], own.shape[0])
        if m == 2:
            for j, (cut, spot) in enumerate(self.out(self.p.side)):
                self.tr.send(n + "z" + str(j), own.at[:, cut], spot, self.p.z)

    def end(self, moves):
        for j, (cut, spot) in enumerate(self.out(self.p.side)):
            moves.start(self.name + str(j), self.even.at[0, :, cut], spot)
            self.tr.wait(self.name + "z" + str(j))


class SumAll:
    def __init__(self, name, place, traffic, sums, got):
        self.name, self.tr, self.sums, self.got = name, traffic, sums, got
        self.partners = (place.c, place.y, place.x, place.z, place.far)

    def start(self, k):
        self.tr.send(self.name + str(k), self.sums, self.got.at[k], self.partners[k])

    def step(self, k):
        self.tr.wait(self.name + str(k))
        self.tr.sent(self.name + str(k))
        self.sums[...] += self.got[k]
        if k + 1 < len(self.partners):
            self.start(k + 1)


def norm_back(b, part, slots, gain, total, first):
    stripes, rows, columns = part.shape[1:]
    tile = 64
    fold = (tile // 8, 8, stripes * columns)

    def body(r):
        at = pl.ds(r, tile)
        value = wide(slots[at, :])
        center = value - jnp.mean(value, axis=1, keepdims=True)
        spread = jnp.mean(center * center, axis=1, keepdims=True)
        inverse = lax.rsqrt(spread + epsilon)
        unit = center * inverse
        grad = jnp.concatenate([wide(part[b, s, at, :]) for s in range(stripes)], axis=1)
        scaled = grad * gain[...]
        push = inverse * (
            scaled
            - jnp.mean(scaled, axis=1, keepdims=True)
            - unit * jnp.mean(scaled * unit, axis=1, keepdims=True)
        )
        for s in range(stripes):
            part[b, s, at, :] = push[:, s * columns : (s + 1) * columns].astype(jnp.bfloat16)
        total[0] += jnp.sum((grad * unit).reshape(fold), axis=0)
        total[1] += jnp.sum(grad.reshape(fold), axis=0)

    if first:
        total[...] = jnp.zeros_like(total)
    loop_rows(rows, tile, body)


def attend_back(b, qkv, weights, grad_mixed, cosine, sine, out, tokens, scale):
    width = grad_mixed.shape[1]
    heads = width // HD
    half = tokens // 2
    start = b * tokens

    def turn_back(grad, rows):
        return (grad * cosine[rows, :] - pltpu.roll(grad, HD // 2, 1) * sine[rows, :]).astype(
            jnp.bfloat16
        )

    for h in range(heads):
        spots = [pl.ds(k * width + h * HD, HD) for k in range(3)]
        grad_key, grad_value = None, None
        for part in (1, 0):
            rows = pl.ds(start + part * half, half)
            reach = pl.ds(start, half * (part + 1))
            query, key, value = qkv[rows, spots[0]], qkv[reach, spots[1]], qkv[reach, spots[2]]
            given = grad_mixed[rows, pl.ds(h * HD, HD)]
            chosen = weights[b * heads + h, pl.ds(part * half, half), pl.ds(0, half * (part + 1))]
            grad = dot_nt(given, value)
            soft = wide(chosen)
            grad = soft * (grad - jnp.sum(grad * soft, axis=1, keepdims=True))
            raw = (grad * scale).astype(jnp.bfloat16)
            out[rows, spots[0]] = turn_back(dot_f32(raw, key), rows)
            key_part, value_part = dot_tn(raw, query), dot_tn(chosen, given)
            if part == 1:
                grad_key, grad_value = key_part, value_part
        low, high = pl.ds(start, half), pl.ds(start + half, half)
        out[low, spots[1]] = turn_back(grad_key[:half] + key_part, low)
        out[high, spots[1]] = turn_back(grad_key[half:], high)
        out[low, spots[2]] = (grad_value[:half] + value_part).astype(jnp.bfloat16)
        out[high, spots[2]] = grad_value[half:].astype(jnp.bfloat16)


def backward_kernel(
    cotangent_in,
    gain1,
    gain2,
    cosine_in,
    sine_in,
    head_mask_in,
    lengths,
    width_bucket,
    all_qkv,
    all_out,
    all_up,
    stream1,
    stream2,
    stream_c,
    normed1,
    normed2,
    heads,
    weights_in,
    mixed_in,
    active_in,
    grad_upper_in,
    part_in,
    middle_in,
    output,
    grad_input,
    sums2_out,
    sums1_out,
    grad_qkv,
    grad_out,
    grad_up,
    grad_down,
    w_up,
    w_out,
    rows_a,
    rows_b,
    active,
    grad_upper,
    part_a,
    part_b,
    got_ca,
    got_ya,
    got_za,
    got_cb,
    got_yb,
    got_zb,
    stream_b,
    weights,
    mixed,
    grad_mixed,
    odd,
    even_down,
    even_up,
    odd_out,
    even_out,
    gx_down,
    gf_down,
    gx_up,
    gf_up,
    gx_qkv,
    gf_qkv,
    gx_out,
    gf_out,
    middle,
    grad_middle,
    total,
    sums2,
    got2,
    sums1,
    got1,
    cotangent,
    cosine,
    sine,
    head_mask,
    send_sems,
    recv_sems,
    move_sems,
):
    p = Place()
    tr, mv = Traffic(send_sems, recv_sems), Moves(move_sems)
    tokens, columns = cotangent.shape
    stripes, blocks = part_a.shape[1], all_out.shape[0]
    rows_d = all_out.shape[2]
    per = blocks // stripes
    head_cols = mixed.shape[1]
    bf16 = jnp.bfloat16

    def load_stream(name, src, dst):
        for b in range(2):
            for s in range(stripes):
                spot = dst.at[pl.ds(b * tokens, tokens), pl.ds(s * columns, columns)]
                mv.start(name + str(b) + str(s), src.at[b, s], spot)

    def wait_stream(name):
        mv.wait(*[name + str(b) + str(s) for b in range(2) for s in range(stripes)])

    s_out = ActScatter("s", p, tr, part_a, got_ca, got_ya, got_za)
    half = tokens // 2
    halves = [pl.ds(0, half), pl.ds(half, half)]

    def half_scatter(name, cut):
        views = part_b.at[:, :, cut], got_cb.at[:, :, cut], got_yb.at[:, cut], got_zb.at[cut]
        return ActScatter(name, p, tr, *views)

    s2a, s2b = [half_scatter(n, cut) for n, cut in zip("tT", halves)]
    s1a, s1b = [half_scatter(n, cut) for n, cut in zip("rR", halves)]
    aba, abb = [ActGather(n, p, tr, stream_b.at[:, :, cut]) for n, cut in zip("bB", halves)]
    begun = set()
    qkv_cols = pl.ds(0, 3 * head_cols)

    def back(layer, b, h, slots, gain):
        rows = pl.ds(b * tokens + h * half, half)
        first = layer not in begun
        begun.add(layer)
        norm_back(b, part_b.at[:, :, halves[h]], slots.at[rows], gain, total, first)

    hidden = active.shape[1]
    parts = [pl.ds(0, hidden // 2), pl.ds(hidden // 2, hidden // 2)]

    def at_side(k, cut, size):
        return pl.ds(pl.multiple_of(k * size + cut.start, 128), cut.size)

    def scatter(name, odd, even, got_x, got_far, out, cols):
        views = [ref.at[:, :, cols] for ref in (odd, even, got_x, got_far)]

        def spots(k):
            if len(out.shape) == 3:
                return [
                    (pl.ds(j * head_cols, head_cols), out.at[j, :, at_side(k, heads_cut, head_cols)])
                    for j in range(3)
                ]
            spot = out.at[:, at_side(k, cols, out.shape[1] // 2)]
            return [(pl.ds(0, cols.size), spot)]

        return WeightScatter(name, p, tr, *views, spots)

    heads_cut = pl.ds(0, head_cols)

    d, e = [
        scatter(n, odd, even_down, gx_down, gf_down, grad_down, cut) for n, cut in zip("de", parts)
    ]
    u, v = [scatter(n, odd, even_up, gx_up, gf_up, grad_up, cut) for n, cut in zip("uv", parts)]
    q = scatter("q", odd, even_down, gx_qkv, gf_qkv, grad_qkv, qkv_cols)
    o = scatter("o", odd_out, even_out, gx_out, gf_out, grad_out, pl.ds(0, head_cols))
    all2 = SumAll("2", p, tr, sums2, got2)
    all1 = SumAll("1", p, tr, sums1, got1)

    load_stream("c", stream_c, rows_a)
    mv.start("active", active_in, active)
    mv.start("grad_upper", grad_upper_in, grad_upper)
    mv.start("all_up", all_up, w_up)
    load_stream("x2", stream2, rows_b)
    p.greet()

    def load_rest():
        for k in range(blocks):
            mv.start("p" + str(k), all_out.at[k], w_out.at[:, pl.ds(k * rows_d, rows_d)])
        mv.start("cotangent", cotangent_in, cotangent)
        mv.start("head_mask", head_mask_in, head_mask)
        mv.start("cosine", cosine_in, cosine)
        mv.start("sine", sine_in, sine)
        mv.start("mixed", mixed_in, mixed)
        mv.start("weights", weights_in, weights)
        mv.start("part", part_in, part_a)
        mv.start("middle", middle_in, middle)

    def block_cols(m):
        return pl.ds(pl.multiple_of(p.block(m) * rows_d, rows_d), rows_d)

    def grad_block(left, right, m, spot, cols=None):
        value = right[...] if cols is None else right[:, cols]
        spot[...] = dot_tn(left[:, block_cols(m)], value).astype(bf16)

    def down_block(m, spot):
        grad_block(rows_a, active, m, spot)

    def product(b, left, right, cols):
        at = pl.ds(b * tokens, tokens)

        def body(s, carry):
            rows = pl.ds(pl.multiple_of(s * columns, columns), columns)
            part_b[b, s] = dot_nt(left[at, cols], right[rows, cols]).astype(bf16)
            return carry

        lax.fori_loop(0, stripes, body, 0)

    def gather_total(sums):
        depth, lanes = 8, total.shape[2] // 8
        sums[...] = jnp.zeros_like(sums)
        for k in range(2):
            row = jnp.sum(total[k], axis=0, keepdims=True)
            for r in range(depth):
                sums[pl.ds(r, 1), pl.ds(k * lanes, lanes)] = row[:, r * lanes : (r + 1) * lanes]
        sums[pl.ds(0, 1), pl.ds(2 * lanes, HD)] = count_row(lengths, width_bucket, HD)

    def unpack(sums, out):
        depth, lanes = 8, total.shape[2] // 8
        for k in range(2):
            for r in range(depth):
                spot = sums[pl.ds(r, 1), pl.ds(k * lanes, lanes)]
                out[pl.ds(k, 1), pl.ds(r * lanes, lanes)] = spot
        out[pl.ds(2, 1), pl.ds(0, HD)] = sums[pl.ds(0, 1), pl.ds(2 * lanes, HD)]

    def up_block(m, spot):
        grad_block(rows_a, grad_upper, m, spot)

    def up_odd(m):
        tr.sent("dx" + str(m), "ex" + str(m))
        up_block(m, odd.at[m // 2])
        u.send_x(m)
        v.send_x(m)

    def mix(b):
        mv.wait("head_mask", *["p" + str(k) for k in range(blocks)])
        at = pl.ds(b * tokens, tokens)
        got = None
        for s in range(stripes):
            one = dot_nt(stream_b[b, s], w_out[:, pl.ds(s * columns, columns)])
            got = one if got is None else got + one
        grad_mixed[at, :] = (got * head_mask[at, :]).astype(bf16)

    def out_block(m, spot):
        mv.wait("mixed")
        place = p.block(m)
        cols = pl.ds(pl.multiple_of((place % per) * rows_d, rows_d), rows_d)
        near = dot_tn(stream_b[0, place // per, :, cols], mixed[pl.ds(0, tokens), :])
        away = dot_tn(stream_b[1, place // per, :, cols], mixed[pl.ds(tokens, tokens), :])
        spot[...] = (near + away).astype(bf16)

    def qkv_block(m, spot):
        mv.wait("normed1")
        grad_block(rows_b, grad_upper, m, spot, qkv_cols)

    def qkv_odd(m):
        tr.sent("ux" + str(m), "vx" + str(m))
        qkv_block(m, odd.at[m // 2, :, qkv_cols])
        q.send_x(m)

    def qkv_even(m):
        mv.wait("d0", "e0")
        tr.sent("df4", "df6", "dz0", "ef4", "ef6", "ez0")
        qkv_block(m, even_down.at[m // 2, :, qkv_cols])

    wait_stream("c")
    mv.wait("active")
    down_block(5, odd.at[2])
    d.send_x(5)
    e.send_x(5)
    mv.wait("grad_upper", "all_up")
    product(1, grad_upper, w_up, pl.ds(0, w_up.shape[1]))
    wait_stream("x2")
    back(2, 1, 0, rows_b, gain2)
    down_block(4, even_down.at[2])
    d.add_x(4)
    s2a.c(1)
    back(2, 1, 1, rows_b, gain2)
    down_block(3, odd.at[1])
    d.send_x(3)
    e.send_x(3)
    s2a.y(1)
    s2b.c(1)
    product(0, grad_upper, w_up, pl.ds(0, w_up.shape[1]))
    e.add_x(4)
    s2b.y(1)
    down_block(2, even_down.at[1])
    back(2, 0, 0, rows_b, gain2)
    s2b.own(1)
    s2a.c(0)
    s2a.own(1)
    down_block(0, even_down.at[0])
    s2a.z()
    down_block(7, odd.at[3])
    d.send_x(7)
    e.send_x(7)
    down_block(6, even_down.at[3])
    s2a.y(0)
    s2a.own(0)
    back(2, 0, 1, rows_b, gain2)
    down_block(1, odd.at[0])
    d.send_x(1)
    e.send_x(1)
    s2b.c(0)
    s2b.z()
    s2b.y(0)
    s2a.home()
    load_rest()
    s2b.own(0)
    d.add_x(6)
    for k in range(3):
        mv.start("h" + str(k), heads.at[k], active.at[:, pl.ds(k * head_cols, head_cols)])
    mv.start("normed2", normed2, rows_a)
    mv.wait("cotangent")
    s2a.end(grad_middle.at[halves[0]], cotangent.at[halves[0]])
    round_rows(grad_middle.at[halves[0]], stream_b.at[0, p.t, halves[0]], tokens // 2)
    s2b.home()
    e.add_x(2)
    s2b.end(grad_middle.at[halves[1]], cotangent.at[halves[1]])
    round_rows(grad_middle.at[halves[1]], stream_b.at[0, p.t, halves[1]], tokens // 2)
    mv.wait("normed2")
    abb.y()
    up_odd(5)
    up_odd(7)
    abb.z()
    for k in range(3):
        mv.start("w" + str(k), all_qkv.at[k], w_up.at[:, pl.ds(k * head_cols, head_cols)])
    mv.start("normed1", normed1, rows_b)
    d.add_x(0)
    aba.y()
    d.add_x(2)
    e.add_far(2)
    gather_total(sums2)
    all2.start(0)
    aba.z()
    e.add_x(6)
    mv.wait("part")
    up_block(4, even_up.at[2])
    u.add_x(4)
    abb.pass_z()
    up_block(0, even_up.at[0])
    v.add_x(4)
    aba.pass_z()
    up_block(6, even_up.at[3])
    up_odd(3)
    up_odd(1)
    up_block(2, even_up.at[1])
    aba.pass_y(1)
    s_out.c(0)
    aba.pass_y(0)
    abb.pass_y(0)
    d.add_far(0)
    load_stream("x1", stream1, rows_a)
    aba.c()
    abb.c()
    e.add_x(0)
    abb.pass_y(1)
    s_out.c(1)
    e.add_far(0)
    aba.take(1)
    abb.take(1)
    mix(1)
    s_out.own(1)
    v.add_x(6)
    d.add_far(2)
    aba.take(0)
    abb.take(0)
    mix(0)
    u.add_x(2)
    all2.step(0)
    mv.wait("cosine", "sine", "weights", "h0", "h1", "h2")
    attend_back(
        1, active, weights, grad_mixed, cosine, sine, grad_upper, tokens, HD ** (-0.5)
    )
    s2a.sent()
    s2b.sent()
    mv.wait("w0", "w1", "w2")
    product(1, grad_upper, w_up, qkv_cols)
    e.end(mv)
    u.add_x(6)
    s_out.y(1)
    out_block(4, even_out.at[2])
    v.add_x(2)
    u.add_far(2)
    attend_back(
        0, active, weights, grad_mixed, cosine, sine, grad_upper, tokens, HD ** (-0.5)
    )
    product(0, grad_upper, w_up, qkv_cols)
    d.end(mv)
    all2.step(1)
    qkv_even(4)
    s_out.y(0)
    qkv_odd(5)
    out_block(5, odd_out.at[2])
    o.send_x(5)
    wait_stream("x1")
    back(1, 1, 0, rows_a, gain1)
    qkv_even(2)
    qkv_odd(3)
    qkv_even(6)
    v.add_far(2)
    s_out.z()
    back(1, 1, 1, rows_a, gain1)
    s1b.c(1)
    out_block(6, even_out.at[3])
    s_out.own(0)
    back(1, 0, 1, rows_a, gain1)
    s1b.c(0)
    q.add_x(4)
    back(1, 0, 0, rows_a, gain1)
    all2.step(2)
    s1b.y(1)
    out_block(1, odd_out.at[0])
    o.send_x(1)
    s_out.home()
    gather_total(sums1)
    all1.start(0)
    v.add_x(0)
    s1a.c(1)
    qkv_odd(1)
    s1a.c(0)
    o.add_x(4)
    all1.step(0)
    q.add_x(2)
    s1a.y(0)
    s1b.own(1)
    all1.step(1)
    s1b.y(0)
    s1a.y(1)
    out_block(3, odd_out.at[1])
    o.send_x(3)
    s1a.own(1)
    u.add_x(0)
    out_block(2, even_out.at[1])
    v.add_far(0)
    qkv_even(0)
    out_block(0, even_out.at[0])
    mv.wait("middle")
    s_out.end(middle, middle)
    mv.start("output", middle, output)
    qkv_odd(7)
    all2.step(3)
    all1.step(2)
    q.add_far(2)
    s1a.z()
    s1b.own(0)
    o.add_x(2)
    o.add_far(2)
    o.add_x(0)
    s1b.z()
    s1a.own(0)
    v.end(mv)
    s1b.home()
    q.add_x(6)
    out_block(7, odd_out.at[3])
    o.send_x(7)
    all1.step(3)
    o.add_x(6)
    s1b.end(grad_middle.at[halves[1]], grad_middle.at[halves[1]])
    q.add_x(0)
    s1a.home()
    u.add_far(0)
    u.end(mv)
    s1a.end(grad_middle.at[halves[0]], grad_middle.at[halves[0]])
    mv.start("grad_input", grad_middle, grad_input)
    all1.step(4)
    q.add_far(0)
    q.end(mv)
    all2.step(4)
    o.add_far(0)
    o.end(mv)
    unpack(sums2, sums2_out)
    unpack(sums1, sums1_out)
    tr.finish()
    mv.finish()


def backward_call(arrays, saved):
    bf16, f32 = jnp.bfloat16, jnp.float32
    tokens, columns = arrays[0].shape
    count, stripes = lax.axis_size("dp"), lax.axis_size("tensor")
    _, head_cols, rows_d = saved["all_out"].shape
    width, hidden = saved["all_up"].shape
    slots = (2, stripes, tokens, columns)
    wide_rows = (2 * tokens, width)

    def vmem(*shape, dtype=bf16):
        return pltpu.VMEM(shape, dtype)

    def got(cols):
        return [vmem(4, rows_d, cols), vmem(2, rows_d, cols)]

    got_act = [vmem(2, 2, tokens, columns), vmem(2, tokens, columns), vmem(tokens, columns)]
    packed = 2 * width // 8 + HD
    sums = [vmem(8, packed, dtype=f32), vmem(5, 8, packed, dtype=f32)]
    qkv = 3 * head_cols
    scratch = [
        vmem(width, hidden),
        vmem(head_cols, width),
        vmem(*wide_rows),
        vmem(*wide_rows),
        vmem(2 * tokens, hidden),
        vmem(2 * tokens, hidden),
        vmem(*slots),
        vmem(*slots),
        *got_act,
        *got_act,
        vmem(*slots),
        vmem(*saved["weights"].shape),
        vmem(2 * tokens, head_cols),
        vmem(2 * tokens, head_cols),
        vmem(4, rows_d, hidden),
        vmem(4, rows_d, hidden),
        vmem(4, rows_d, hidden),
        vmem(4, rows_d, head_cols),
        vmem(4, rows_d, head_cols),
        *got(hidden),
        *got(hidden),
        *got(qkv),
        *got(head_cols),
        vmem(tokens, columns, dtype=f32),
        vmem(tokens, columns, dtype=f32),
        vmem(2, 8, width, dtype=f32),
        *sums,
        *sums,
        *[vmem(*arrays[k].shape, dtype=f32) for k in (0, 3, 4, 5)],
        pltpu.SemaphoreType.DMA((112,)),
        pltpu.SemaphoreType.DMA((112,)),
        pltpu.SemaphoreType.DMA((80,)),
    ]
    any_spec = pl.BlockSpec(memory_space=pl.ANY)
    vmem_spec = pl.BlockSpec(memory_space=pltpu.VMEM)
    smem_spec = pl.BlockSpec(memory_space=pltpu.SMEM)
    shapes = [
        ((tokens, columns), f32),
        ((tokens, columns), f32),
        ((8, width), f32),
        ((8, width), f32),
        ((3, rows_d, 2 * head_cols), bf16),
        ((rows_d, 2 * head_cols), bf16),
        ((rows_d, 2 * hidden), bf16),
        ((rows_d, 2 * hidden), bf16),
    ]
    names = [k for k in saved]
    return pl.pallas_call(
        backward_kernel,
        out_shape=[jax.ShapeDtypeStruct(*s) for s in shapes],
        in_specs=[any_spec, vmem_spec, vmem_spec] + [any_spec] * 3
        + [smem_spec] * 2
        + [any_spec] * len(names),
        out_specs=[any_spec] * 2 + [vmem_spec] * 2 + [any_spec] * 4,
        scratch_shapes=scratch,
        compiler_params=pltpu.CompilerParams(
            collective_id=1, has_side_effects=True, vmem_limit_bytes=63 << 20
        ),
    )(*arrays, *[saved[n] for n in names])


def finish_kernel(groups, *refs):
    ins, sums, outs, small = refs[:6], refs[6:8], refs[8:14], refs[14:19]
    raw, done, sems = refs[19:25], refs[25:29], refs[29]
    loads = [pltpu.make_async_copy(ins[k], raw[k], sems.at[k]) for k in range(6)]
    for load in loads:
        load.start()
    for k in range(4):
        small[k][...] = sums[k // 2][pl.ds(k % 2, 1), :]
    count = small[4].shape[1]
    small[4][...] = (sums[1][pl.ds(2, 1), pl.ds(0, count)] / groups).astype(jnp.int32)
    stores = []

    def store(k, src):
        stores.append(pltpu.make_async_copy(src, outs[k], sems.at[6 + k]))
        stores[-1].start()

    loads[0].wait()
    rows, columns = raw[0].shape

    def widen(r):
        done[0][pl.ds(r, 32), :] = wide(raw[0][pl.ds(r, 32), :])

    loop_rows(rows, 32, widen)
    store(0, done[0])
    loads[1].wait()

    def turn(src, dst):
        def body(c):
            dst[pl.ds(c, 256), :] = wide(src[:, pl.ds(c, 256)]).T

        loop_rows(src.shape[1], 256, body)

    turn(raw[1], done[1])
    store(1, done[1])
    loads[2].wait()
    for k in range(raw[2].shape[0]):

        def widen_part(r, k=k):
            done[2][k, pl.ds(r, 64), :] = wide(raw[2][k, pl.ds(r, 64), :])

        loop_rows(raw[2].shape[1], 64, widen_part)
    store(2, done[2])
    loads[3].wait()
    turn(raw[3], done[3])
    store(3, done[3])
    for k in (4, 5):
        loads[k].wait()
        store(k, raw[k])
    for one in stores:
        one.wait()


def finish_call(grad_up, grad_down, grad_qkv, grad_out, output, grad_input, sums1, sums2):
    f32 = jnp.float32
    ins = (grad_up, grad_down, grad_qkv, grad_out, output, grad_input)
    shapes = [a.shape for a in ins]
    shapes[1], shapes[3] = shapes[1][::-1], shapes[3][::-1]
    any_spec = pl.BlockSpec(memory_space=pl.ANY)
    vmem_spec = pl.BlockSpec(memory_space=pltpu.VMEM)
    groups = lax.axis_size("tensor")
    return pl.pallas_call(
        functools.partial(finish_kernel, groups),
        out_shape=[jax.ShapeDtypeStruct(s, f32) for s in shapes]
        + [jax.ShapeDtypeStruct((1, sums1.shape[1]), f32)] * 4
        + [jax.ShapeDtypeStruct((1, groups), jnp.int32)],
        in_specs=[any_spec] * 6 + [vmem_spec] * 2,
        out_specs=[any_spec] * 6 + [vmem_spec] * 5,
        scratch_shapes=[pltpu.VMEM(a.shape, a.dtype) for a in ins]
        + [pltpu.VMEM(s, f32) for s in shapes[:4]]
        + [pltpu.SemaphoreType.DMA((12,))],
        compiler_params=pltpu.CompilerParams(vmem_limit_bytes=62 << 20),
    )(*ins, sums1, sums2)


def local_fast(
    residual_in,
    lengths,
    head_bucket,
    width_bucket,
    norm1_gain,
    norm1_shift,
    w_qkv,
    w_out,
    norm2_gain,
    norm2_shift,
    w_up,
    w_down,
    cotangent,
):
    f32 = jnp.float32
    tokens = residual_in.shape[0]
    steps = np.arange(tokens)[:, None] * 10000.0 ** (-2.0 * (np.arange(HD) % (HD // 2)) / HD)
    arrays = (
        residual_in,
        cotangent,
        norm1_gain[None],
        norm1_shift[None],
        norm2_gain[None],
        norm2_shift[None],
        lengths,
        head_bucket,
        width_bucket,
        jnp.asarray(np.cos(steps), f32),
        jnp.asarray(np.sin(steps), f32),
    )
    weights = (jnp.swapaxes(w_qkv, 0, 1), w_out, w_up, w_down)
    (cosine, sine, head_mask), saved = forward_call(arrays, weights)
    arrays = (cotangent, norm1_gain[None], norm2_gain[None], cosine, sine, head_mask)
    output, grad_input, sums2, sums1, grad_qkv, grad_out, grad_up, grad_down = backward_call(
        (*arrays, lengths, width_bucket), saved
    )
    grad_up, grad_down, grad_qkv, grad_out, output, grad_input, *small = finish_call(
        grad_up, grad_down, grad_qkv, grad_out, output, grad_input, sums1, sums2
    )
    gain1_grad, shift1_grad, gain2_grad, shift2_grad, bucket_counts = [one[0] for one in small]
    return (
        output,
        grad_input,
        gain1_grad,
        shift1_grad,
        jnp.swapaxes(grad_qkv, 0, 1),
        grad_out,
        gain2_grad,
        shift2_grad,
        grad_up,
        grad_down,
        bucket_counts,
    )


def local(*args):
    w_out = args[7]
    if lax.axis_size("dp") == 8 and lax.axis_size("tensor") == 4 and w_out.shape[1] % 128 == 0:
        return local_fast(*args)
    return local_general(*args)


def solution(mesh):
    placed = (
        P("dp", "tensor"),
        P("dp", None),
        P("dp", None),
        P("dp", None),
        P(),
        P(),
        P("dp", None, "tensor"),
        P("tensor", "dp"),
        P(),
        P(),
        P("dp", "tensor"),
        P("tensor", "dp"),
        P("dp", "tensor"),
    )
    return jax.shard_map(
        local,
        mesh=mesh,
        in_specs=placed,
        out_specs=(
            P("dp", "tensor"),
            P("dp", "tensor"),
            P(),
            P(),
            P("dp", None, "tensor"),
            P("tensor", "dp"),
            P(),
            P(),
            P("dp", "tensor"),
            P("tensor", "dp"),
            P(),
        ),
        check_vma=False,
    )
```

```python
import functools
import math

import jax
import jax.numpy as jnp
import numpy as np
from jax import lax
from jax.experimental import pallas as pl
from jax.experimental.pallas import tpu as pltpu
from jax.sharding import PartitionSpec as P

HD = 128
HIDDEN_BIT = 2

epsilon = 1e-05


def dp_swap(value, bit):
    count = lax.axis_size("dp")
    return lax.ppermute(value, "dp", [(i, i ^ bit) for i in range(count)])


def tensor_swap(value, bit):
    count = lax.axis_size("tensor")
    return lax.ppermute(value, "tensor", [(i, i ^ bit) for i in range(count)])


def bits_of(count):
    return [1 << i for i in range(count.bit_length() - 1)]


def replica_bits():
    bits = bits_of(lax.axis_size("dp"))
    return [b for b in bits if b > HIDDEN_BIT] + [b for b in bits if b < HIDDEN_BIT]


def gather_weight(mine, other):
    blocks = {0: mine, HIDDEN_BIT: dp_swap(other, HIDDEN_BIT)}
    for bit in replica_bits():
        blocks.update({m | bit: dp_swap(blocks[m], bit) for m in list(blocks)})
    return blocks


def add_low(left, right):
    return (left.astype(jnp.float32) + right.astype(jnp.float32)).astype(jnp.bfloat16)


def scatter_weight(blocks):
    for bit in reversed(replica_bits()):
        arrived = {m ^ bit: dp_swap(blocks[m], bit) for m in blocks if m & bit}
        blocks = {m: add_low(blocks[m], arrived[m]) for m in arrived}
    return blocks[0], dp_swap(blocks[HIDDEN_BIT], HIDDEN_BIT)


def gather_act(rows):
    blocks = {(0, 0): rows, (1, 0): dp_swap(rows, HIDDEN_BIT)}
    for bit in reversed(bits_of(lax.axis_size("tensor"))):
        blocks.update({(b, m | bit): tensor_swap(v, bit) for (b, m), v in list(blocks.items())})
    return blocks


def scatter_act(blocks):
    for bit in bits_of(lax.axis_size("tensor")):
        arrived = {(b, m ^ bit): tensor_swap(v, bit) for (b, m), v in blocks.items() if m & bit}
        blocks = {k: add_low(blocks[k], arrived[k]) for k in arrived}
    return blocks[(0, 0)].astype(jnp.float32) + dp_swap(blocks[(1, 0)], HIDDEN_BIT).astype(
        jnp.float32
    )


def lay(blocks, shape, spots):
    count = len(blocks)

    def kernel(*refs):
        ins, out, sems = refs[:count], refs[count], refs[count + 1]
        copies = []
        for i, spot in enumerate(spots()):
            r, c = blocks[i].shape
            copies.append(
                pltpu.make_async_copy(
                    ins[i],
                    out.at[pl.ds(pl.multiple_of(spot[0], 16), r), pl.ds(pl.multiple_of(spot[1], 128), c)],
                    sems.at[i],
                )
            )
        for copy in copies:
            copy.start()
        for copy in copies:
            copy.wait()

    return pl.pallas_call(
        kernel,
        out_shape=jax.ShapeDtypeStruct(shape, jnp.bfloat16),
        in_specs=[pl.BlockSpec(memory_space=pl.ANY)] * count,
        out_specs=pl.BlockSpec(memory_space=pltpu.VMEM),
        scratch_shapes=[pltpu.SemaphoreType.DMA((count,))],
        compiler_params=pltpu.CompilerParams(vmem_limit_bytes=24 << 20),
    )(*blocks)


def cut(whole, block_shape, count, spots):
    def kernel(*refs):
        src, outs, sems = refs[0], refs[1 : 1 + count], refs[1 + count]
        r, c = block_shape
        copies = []
        for i, spot in enumerate(spots()):
            copies.append(
                pltpu.make_async_copy(
                    src.at[pl.ds(pl.multiple_of(spot[0], 16), r), pl.ds(pl.multiple_of(spot[1], 128), c)],
                    outs[i],
                    sems.at[i],
                )
            )
        for copy in copies:
            copy.start()
        for copy in copies:
            copy.wait()

    return pl.pallas_call(
        kernel,
        out_shape=[jax.ShapeDtypeStruct(block_shape, jnp.bfloat16)] * count,
        in_specs=[pl.BlockSpec(memory_space=pltpu.VMEM)],
        out_specs=[pl.BlockSpec(memory_space=pl.ANY)] * count,
        scratch_shapes=[pltpu.SemaphoreType.DMA((count,))],
        compiler_params=pltpu.CompilerParams(vmem_limit_bytes=24 << 20),
    )(whole)


def lay_weight(blocks, axis):
    count = len(blocks)
    r, c = blocks[0].shape
    if axis == 1 and c % 128:
        order = jnp.bitwise_xor(lax.axis_index("dp"), jnp.arange(count))
        stacked = jnp.stack([blocks[m] for m in range(count)])[order]
        return jnp.swapaxes(stacked, 0, 1).reshape(r, count * c)

    def spots():
        place = lax.axis_index("dp")
        at = [jnp.bitwise_xor(place, m) for m in range(count)]
        return [(d * r, 0) if axis == 0 else (0, d * c) for d in at]

    shape = (r * count, c) if axis == 0 else (r, c * count)
    return lay([blocks[m] for m in range(count)], shape, spots)


def cut_weight(whole, axis):
    count = lax.axis_size("dp")
    r, c = whole.shape
    r, c = (r // count, c) if axis == 0 else (r, c // count)
    if axis == 1 and c % 128:
        order = jnp.bitwise_xor(lax.axis_index("dp"), jnp.arange(count))
        stacked = jnp.swapaxes(whole.reshape(r, count, c), 0, 1)[order]
        return {m: stacked[m] for m in range(count)}

    def spots():
        place = lax.axis_index("dp")
        at = [jnp.bitwise_xor(place, m) for m in range(count)]
        return [(d * r, 0) if axis == 0 else (0, d * c) for d in at]

    return dict(enumerate(cut(whole, (r, c), count, spots)))


def act_keys():
    return [(b, m) for b in range(2) for m in range(lax.axis_size("tensor"))]


def act_spots(r, c):
    place = lax.axis_index("tensor")
    return [(b * r, jnp.bitwise_xor(place, m) * c) for b, m in act_keys()]


def lay_act(blocks):
    r, c = blocks[(0, 0)].shape
    shape = (2 * r, c * lax.axis_size("tensor"))
    return lay([blocks[k] for k in act_keys()], shape, lambda: act_spots(r, c))


def cut_act(whole):
    r, c = whole.shape[0] // 2, whole.shape[1] // lax.axis_size("tensor")
    keys = act_keys()
    return dict(zip(keys, cut(whole, (r, c), len(keys), lambda: act_spots(r, c))))


def whole_stream(rows):
    return lay_act(gather_act(rows.astype(jnp.bfloat16)))


def stream_sum(rows):
    return scatter_act(cut_act(rows.astype(jnp.bfloat16)))


def sum_all(value, axes):
    if "dp" in axes:
        for bit in bits_of(lax.axis_size("dp")):
            value = value + dp_swap(value, bit)
    if "tensor" in axes:
        for bit in bits_of(lax.axis_size("tensor")):
            value = value + tensor_swap(value, bit)
    return value


def token_info(length_row, head_row, width_row, row_count):
    seq_ends = jnp.cumsum(length_row)
    seq_starts = seq_ends - length_row
    places = jnp.arange(row_count, dtype=jnp.int32)
    segment = jnp.sum((places[:, None] >= seq_ends[None, :]).astype(jnp.int32), axis=1)
    labels = jnp.arange(length_row.shape[0], dtype=jnp.int32)
    onehot = (segment[:, None] == labels[None, :]).astype(jnp.int32)
    offset = places - jnp.sum(onehot * seq_starts[None, :], axis=1)
    head_tok = jnp.sum(onehot * head_row[None, :], axis=1)
    width_tok = jnp.sum(onehot * width_row[None, :], axis=1)
    return (segment, offset, head_tok, width_tok)


def rotary_tables(offset, head_size):
    half_size = head_size // 2
    ladder = jnp.arange(half_size, dtype=jnp.float32)
    inverse = jnp.exp(ladder * (-2.0 * math.log(10000.0) / head_size))
    angles = offset.astype(jnp.float32)[:, None] * inverse[None, :]
    return (jnp.cos(angles)[:, None, :], jnp.sin(angles)[:, None, :])


def rotate(values, cosine, sine_part):
    half_size = values.shape[-1] // 2
    front_half = values[..., :half_size]
    back_half = values[..., half_size:]
    return jnp.concatenate(
        [front_half * cosine - back_half * sine_part, back_half * cosine + front_half * sine_part],
        axis=-1,
    )


def norm_forward(values, norm_gain, norm_shift):
    values = values.astype(jnp.float32)
    center = values - jnp.mean(values, axis=-1, keepdims=True)
    spread = jnp.mean(center * center, axis=-1, keepdims=True)
    inverse = lax.rsqrt(spread + epsilon)
    unit_rows = center * inverse
    return (unit_rows * norm_gain + norm_shift, unit_rows, inverse)


def norm_backward(grad_rows, unit_rows, inverse, norm_gain):
    scaled = grad_rows * norm_gain
    grad_in = inverse * (
        scaled
        - jnp.mean(scaled, axis=-1, keepdims=True)
        - unit_rows * jnp.mean(scaled * unit_rows, axis=-1, keepdims=True)
    )
    return (grad_in, jnp.sum(grad_rows * unit_rows, axis=0), jnp.sum(grad_rows, axis=0))


def heads_of(rows, blocks):
    rows = rows.reshape(blocks, rows.shape[0] // blocks, -1, HD)
    return jnp.transpose(rows, (2, 0, 1, 3)).reshape(-1, rows.shape[1], HD)


def rows_of(heads, blocks):
    heads = heads.reshape(-1, blocks, heads.shape[1], HD)
    return jnp.transpose(heads, (1, 2, 0, 3)).reshape(blocks * heads.shape[2], -1)


def local_general(
    residual_in,
    lengths,
    head_bucket,
    width_bucket,
    norm1_gain,
    norm1_shift,
    w_qkv,
    w_out,
    norm2_gain,
    norm2_shift,
    w_up,
    w_down,
    cotangent,
):
    f32, bf16 = jnp.float32, jnp.bfloat16
    dot = functools.partial(jnp.dot, preferred_element_type=f32)
    tensor_index = lax.axis_index("tensor")
    bucket_total = lax.axis_size("tensor")
    tokens = residual_in.shape[0]
    side = (lax.axis_index("dp") // HIDDEN_BIT) % 2

    def halves(weight, axis):
        left, right = jnp.split(weight, 2, axis=axis)
        return jnp.where(side == 0, left, right), jnp.where(side == 0, right, left)

    info = jnp.stack([lengths[0], head_bucket[0], width_bucket[0]])
    far_info = dp_swap(info, HIDDEN_BIT)
    pair = [token_info(i[0], i[1], i[2], tokens) for i in (info, far_info)]
    segment, offset, head_tok, width_tok = [jnp.stack([a, b]) for a, b in zip(*pair)]
    matches = (
        width_bucket[0][:, None] == jnp.arange(bucket_total, dtype=jnp.int32)[None, :]
    ).astype(jnp.int32)
    bucket_counts = sum_all(jnp.sum(lengths[0][:, None] * matches, axis=0), ("dp",))
    head_mask = (head_tok.reshape(-1) >= tensor_index).astype(f32)[:, None]
    width_mask = (width_tok.reshape(-1) >= tensor_index).astype(f32)[:, None]
    places = jnp.arange(tokens, dtype=jnp.int32)
    allowed = (segment[:, :, None] == segment[:, None, :]) & (
        places[:, None] >= places[None, :]
    )
    cosine, sine_part = rotary_tables(offset.reshape(-1), HD)
    score_scale = HD ** (-0.5)

    qkv_halves = [h.reshape(h.shape[0], -1) for h in halves(w_qkv, 2)]
    full_qkv = lay_weight(gather_weight(*qkv_halves), 0)
    full_out = lay_weight(gather_weight(*halves(w_out, 0)), 1)
    full_up = lay_weight(gather_weight(*halves(w_up, 1)), 0)
    full_down = lay_weight(gather_weight(*halves(w_down, 0)), 1)

    inputs = whole_stream(residual_in)
    normed1, unit1, inverse1 = norm_forward(inputs, norm1_gain, norm1_shift)
    normed1 = normed1.astype(bf16)
    projected = dot(normed1, full_qkv).reshape(2 * tokens, 3, -1, HD)
    width = projected.shape[2] * HD
    query = rotate(projected[:, 0], cosine, sine_part).astype(bf16).reshape(-1, width)
    key = rotate(projected[:, 1], cosine, sine_part).astype(bf16).reshape(-1, width)
    value = projected[:, 2].astype(bf16).reshape(-1, width)
    query, key, value = heads_of(query, 2), heads_of(key, 2), heads_of(value, 2)
    allowed = jnp.tile(allowed, (query.shape[0] // 2, 1, 1))
    scores = jnp.einsum("nqd,nkd->nqk", query, key, preferred_element_type=f32) * score_scale
    scores = jnp.where(allowed, scores, -1000000000.0)
    scores = jnp.exp(scores - jnp.max(scores, axis=-1, keepdims=True))
    weights = (scores / jnp.sum(scores, axis=-1, keepdims=True)).astype(bf16)
    mixed = jnp.einsum("nqk,nkd->nqd", weights, value, preferred_element_type=f32)
    mixed = (rows_of(mixed, 2) * head_mask).astype(bf16)
    middle = residual_in + stream_sum(dot(mixed, full_out))
    middle_rows = whole_stream(middle)
    normed2, unit2, inverse2 = norm_forward(middle_rows, norm2_gain, norm2_shift)
    normed2 = normed2.astype(bf16)
    upper = jnp.maximum(dot(normed2, full_up), 0.0) * width_mask
    active = jnp.square(upper).astype(bf16)
    upper = upper.astype(bf16)
    output = middle + stream_sum(dot(active, full_down))

    grad_top = whole_stream(cotangent)
    grad_down = scatter_weight(cut_weight(dot(active.T, grad_top).astype(bf16), 1))
    grad_active = dot(grad_top, full_down.T)
    grad_upper = (grad_active * 2.0 * upper.astype(f32)).astype(bf16)
    grad_normed2 = dot(grad_upper, full_up.T)
    part_middle, gain2_grad, shift2_grad = norm_backward(
        grad_normed2, unit2, inverse2, norm2_gain
    )
    grad_middle = cotangent + stream_sum(part_middle)
    grad_up = scatter_weight(cut_weight(dot(normed2.T, grad_upper).astype(bf16), 0))
    grad_branch = whole_stream(grad_middle)
    grad_wout = scatter_weight(cut_weight(dot(mixed.T, grad_branch).astype(bf16), 1))
    grad_mixed = (dot(grad_branch, full_out.T) * head_mask).astype(bf16)
    grad_mixed = heads_of(grad_mixed, 2)
    grad_weights = jnp.einsum("nqd,nkd->nqk", grad_mixed, value, preferred_element_type=f32)
    grad_value = jnp.einsum("nqk,nqd->nkd", weights, grad_mixed, preferred_element_type=f32)
    wide = weights.astype(f32)
    grad_scores = wide * (grad_weights - jnp.sum(grad_weights * wide, axis=-1, keepdims=True))
    grad_raw = (grad_scores * score_scale).astype(bf16)
    grad_query = jnp.einsum("nqk,nkd->nqd", grad_raw, key, preferred_element_type=f32)
    grad_key = jnp.einsum("nqk,nqd->nkd", grad_raw, query, preferred_element_type=f32)
    grad_query, grad_key = [
        rotate(rows_of(g, 2).reshape(2 * tokens, -1, HD), cosine, -sine_part).reshape(-1, width)
        for g in (grad_query, grad_key)
    ]
    grad_projected = jnp.concatenate([grad_query, grad_key, rows_of(grad_value, 2)], axis=1)
    grad_projected = grad_projected.astype(bf16)
    grad_normed1 = dot(grad_projected, full_qkv.T)
    part_input, gain1_grad, shift1_grad = norm_backward(
        grad_normed1, unit1, inverse1, norm1_gain
    )
    grad_input = grad_middle + stream_sum(part_input)
    grad_qkv = scatter_weight(cut_weight(dot(normed1.T, grad_projected).astype(bf16), 0))

    def join(pair, axis):
        left = jnp.where(side == 0, pair[0], pair[1])
        right = jnp.where(side == 0, pair[1], pair[0])
        return jnp.concatenate([left, right], axis=axis).astype(f32)

    grad_qkv = join([g.reshape(g.shape[0], 3, width) for g in grad_qkv], 2)
    grad_wout, grad_up, grad_down = join(grad_wout, 0), join(grad_up, 1), join(grad_down, 0)
    gain2_grad, shift2_grad = sum_all(jnp.stack([gain2_grad, shift2_grad]), ("dp", "tensor"))
    gain1_grad, shift1_grad = sum_all(jnp.stack([gain1_grad, shift1_grad]), ("dp", "tensor"))
    return (
        output,
        grad_input,
        gain1_grad,
        shift1_grad,
        grad_qkv,
        grad_wout,
        gain2_grad,
        shift2_grad,
        grad_up,
        grad_down,
        bucket_counts,
    )


def flip(i, bit):
    return i + bit - 2 * bit * ((i // bit) % 2)


class Traffic:
    def __init__(self, send_sems, recv_sems):
        self.send_sems, self.recv_sems = send_sems, recv_sems
        self.copies, self.gone, self.come = {}, set(), set()

    def send(self, name, src, dst, device):
        k = len(self.copies)
        copy = pltpu.make_async_remote_copy(
            src_ref=src,
            dst_ref=dst,
            send_sem=self.send_sems.at[k],
            recv_sem=self.recv_sems.at[k],
            device_id=device,
            device_id_type=pl.DeviceIdType.MESH,
        )
        copy.start()
        self.copies[name] = copy

    def wait(self, *names):
        for name in names:
            if name not in self.come:
                self.copies[name].wait_recv()
                self.come.add(name)

    def sent(self, *names):
        for name in names:
            if name not in self.gone:
                self.copies[name].wait_send()
                self.gone.add(name)

    def finish(self):
        self.sent(*self.copies)


class Moves:
    def __init__(self, sems):
        self.sems, self.copies = sems, {}

    def start(self, name, src, dst):
        copy = pltpu.make_async_copy(src, dst, self.sems.at[len(self.copies)])
        copy.start()
        self.copies[name] = [copy, False]

    def wait(self, *names):
        for name in names:
            if not self.copies[name][1]:
                self.copies[name][0].wait()
                self.copies[name][1] = True

    def finish(self):
        self.wait(*self.copies)


class Place:
    def __init__(self):
        self.i, self.t = lax.axis_index("dp"), lax.axis_index("tensor")
        self.side = (self.i // 2 + self.i // 4) % 2
        self.x, self.z = [(flip(self.i, b), self.t) for b in (1, 2)]
        self.far = (self.block(6), self.t)
        self.c, self.y = [(self.i, flip(self.t, b)) for b in (1, 2)]

    def greet(self):
        barrier = pltpu.get_barrier_semaphore()
        partners = (self.x, self.z, self.far, self.c, self.y)
        for device in partners:
            pl.semaphore_signal(
                barrier, inc=1, device_id=device, device_id_type=pl.DeviceIdType.MESH
            )
        pl.semaphore_wait(barrier, len(partners))

    def block(self, m):
        d = self.i
        for bit in (1, 2, 4):
            if m & bit:
                d = flip(d, bit)
        return d

    def stripe(self, m):
        s = self.t
        for bit in (1, 2):
            if m & bit:
                s = flip(s, bit)
        return s


class WeightGather:
    def __init__(self, name, place, traffic, moves, half, slot):
        self.name, self.p, self.tr, self.mv = name, place, traffic, moves
        self.half, self.slot = half, slot

    def own(self):
        self.mv.start(self.name + "0", self.half(self.p.side), self.slot(self.p.i))

    def z(self):
        self.tr.send(self.name + "2", self.half(1 - self.p.side), self.slot(self.p.i), self.p.z)

    def far(self):
        self.tr.send(self.name + "6", self.half(self.p.side), self.slot(self.p.i), self.p.far)

    def x(self):
        self.tr.send(self.name + "1", self.half(self.p.side), self.slot(self.p.i), self.p.x)

    def far_next(self):
        self.tr.wait(self.name + "2")
        block = self.slot(self.p.block(2))
        self.tr.send(self.name + "4", block, block, self.p.far)

    def x_next(self, m):
        self.tr.wait(self.name + str(m))
        block = self.slot(self.p.block(m))
        self.tr.send(self.name + str(m + 1), block, block, self.p.x)

    def take(self, *which):
        for m in which:
            if m == 0:
                self.mv.wait(self.name + "0")
            else:
                self.tr.wait(self.name + str(m))

    def end(self):
        self.take(*range(8))


class ActGather:
    def __init__(self, name, place, traffic, slots):
        self.name, self.p, self.tr, self.slots = name, place, traffic, slots

    def at(self, b, m):
        return self.slots.at[b, self.p.stripe(m)]

    def z(self):
        self.tr.send(self.name + "10", self.at(0, 0), self.slots.at[1, self.p.t], self.p.z)

    def y(self):
        self.tr.send(self.name + "02", self.at(0, 0), self.at(0, 0), self.p.y)

    def c(self):
        self.tr.send(self.name + "01", self.at(0, 0), self.at(0, 0), self.p.c)

    def pass_z(self):
        self.tr.wait(self.name + "10")
        block = self.at(1, 0)
        self.tr.send(self.name + "12", block, block, self.p.y)
        self.tr.send(self.name + "11", block, block, self.p.c)

    def pass_y(self, b):
        self.tr.wait(self.name + str(b) + "2")
        block = self.at(b, 2)
        self.tr.send(self.name + str(b) + "3", block, block, self.p.c)

    def take(self, b):
        for m in range(1 - b, 4):
            self.tr.wait(self.name + str(b) + str(m))


def loop_rows(count, step, body):
    def run(k, carry):
        body(pl.multiple_of(k * step, step))
        return carry

    lax.fori_loop(0, count // step, run, 0)


def wide(value):
    return value.astype(jnp.float32)


def add_blocks(out, left, right, rows):
    def body(r):
        at = pl.ds(r, 64)
        out[at, :] = (wide(left[at, :]) + wide(right[at, :])).astype(out.dtype)

    loop_rows(rows, 64, body)


class ActScatter:
    def __init__(self, name, place, traffic, part, got_c, got_y, got_z):
        self.name, self.p, self.tr = name, place, traffic
        self.part, self.got_c, self.got_y, self.got_z = part, got_c, got_y, got_z
        self.rows = part.shape[2]

    def at(self, b, m):
        return self.part.at[b, self.p.stripe(m)]

    def c(self, b):
        for j, m in ((1, 3), (0, 1)):
            name = self.name + "c" + str(b) + str(j)
            self.tr.send(name, self.at(b, m), self.got_c.at[b, j], self.p.c)

    def add(self, b, m, name, got):
        self.tr.wait(self.name + name)
        add_blocks(self.at(b, m), self.at(b, m), got, self.rows)

    def y(self, b):
        self.add(b, 2, "c" + str(b) + "1", self.got_c.at[b, 1])
        self.tr.send(self.name + "y" + str(b), self.at(b, 2), self.got_y.at[b], self.p.y)

    def own(self, b):
        self.add(b, 0, "c" + str(b) + "0", self.got_c.at[b, 0])

    def z(self):
        self.add(1, 0, "y1", self.got_y.at[1])
        self.tr.send(self.name + "z", self.at(1, 0), self.got_z, self.p.z)

    def home(self):
        self.add(0, 0, "y0", self.got_y.at[0])

    def sent(self):
        for key in ("c11", "c01", "c10", "c00", "y1", "y0", "z"):
            self.tr.sent(self.name + key)

    def end(self, out, base):
        self.tr.wait(self.name + "z")
        own = self.at(0, 0)

        def body(r):
            at = pl.ds(r, 64)
            out[at, :] = base[at, :] + (wide(own[at, :]) + wide(self.got_z[at, :]))

        loop_rows(self.rows, 64, body)


def round_rows(src, dst, rows):
    def body(r):
        at = pl.ds(r, 64)
        dst[at, :] = src[at, :].astype(dst.dtype)

    loop_rows(rows, 64, body)


def dot_f32(left, right):
    return jnp.dot(left, right, preferred_element_type=jnp.float32)


def dot_nt(left, right):
    return lax.dot_general(
        left, right, (((1,), (1,)), ((), ())), preferred_element_type=jnp.float32
    )


def dot_tn(left, right):
    return lax.dot_general(
        left, right, (((0,), (0,)), ((), ())), preferred_element_type=jnp.float32
    )


def center_rows(slots, b, at):
    stripes = slots.shape[1]
    rows = jnp.concatenate([wide(slots[b, s, at, :]) for s in range(stripes)], axis=1)
    center = rows - jnp.mean(rows, axis=1, keepdims=True)
    spread = jnp.mean(center * center, axis=1, keepdims=True)
    return center, lax.rsqrt(spread + epsilon)


def norm_rows(slots, b, gain, shift, out):
    rows = slots.shape[2]

    def body(r):
        center, inverse = center_rows(slots, b, pl.ds(r, 128))
        out[pl.ds(b * rows + r, 128), :] = (center * inverse * gain[...] + shift[...]).astype(
            jnp.bfloat16
        )

    loop_rows(rows, 128, body)


def attend(b, qkv, seg_col, seg_row, head_mask, weights, mixed, scale):
    tokens = seg_row.shape[2]
    heads = qkv.shape[2] // HD
    half = tokens // 2
    start = b * tokens
    for h in range(heads):
        cols = pl.ds(h * HD, HD)
        for part in range(2):
            rows = pl.ds(start + part * half, half)
            reach = half * (part + 1)
            query = qkv[0, rows, cols]
            key = qkv[1, pl.ds(start, reach), cols]
            value = qkv[2, pl.ds(start, reach), cols]
            scores = dot_nt(query, key) * scale
            row_id = lax.broadcasted_iota(jnp.int32, (half, reach), 0) + part * half
            col_id = lax.broadcasted_iota(jnp.int32, (half, reach), 1)
            same = seg_col[rows, :] == seg_row[b, :, pl.ds(0, reach)]
            scores = jnp.where(same & (row_id >= col_id), scores, -1000000000.0)
            scores = jnp.exp(scores - jnp.max(scores, axis=1, keepdims=True))
            total = jnp.sum(scores, axis=1, keepdims=True)
            chosen = (scores / total).astype(jnp.bfloat16)
            weights[b * heads + h, pl.ds(part * half, half), pl.ds(0, reach)] = chosen
            mixed[rows, cols] = (dot_f32(chosen, value) * head_mask[rows, :]).astype(jnp.bfloat16)


def sequences(lengths):
    start = 0
    for s in range(lengths.shape[1]):
        length = lengths[0, s]
        yield s, start, length
        start = start + length


def count_row(lengths, width_bucket, lanes):
    lane = lax.broadcasted_iota(jnp.int32, (1, lanes), 1)
    row = jnp.zeros((1, lanes), jnp.float32)
    for s, _, length in sequences(lengths):
        row = row + jnp.where(lane == width_bucket[0, s], wide(length), 0.0)
    return row


def fill_facts(lengths, head_bucket, width_bucket, place_cosine, place_sine, facts):
    lanes = facts.shape[1]
    row = lax.broadcasted_iota(jnp.int32, (8, lanes), 0)
    lane = lax.broadcasted_iota(jnp.int32, (8, lanes), 1)
    count = lengths.shape[1]
    by_lane = jnp.where((row == 0) & (lane >= count), 1e9, 0.0)
    by_row = jnp.where(row >= count, 1e9, 0.0)
    for s, start, length in sequences(lengths):
        end = wide(start + length)
        here = lane == s
        by_lane = by_lane + jnp.where((row == 0) & here, end, 0.0)
        by_lane = by_lane + jnp.where((row == 2) & here, wide(head_bucket[0, s]), 0.0)
        by_lane = by_lane + jnp.where((row == 3) & here, wide(width_bucket[0, s]), 0.0)
        by_row = by_row + jnp.where(row == s, end, 0.0)
        facts[pl.ds(16 + s, 1), :] = place_cosine[pl.ds(start, 1), :]
        facts[pl.ds(20 + s, 1), :] = place_sine[pl.ds(start, 1), :]
    facts[pl.ds(0, 8), :] = by_lane
    facts[pl.ds(8, 8), :] = by_row


def fill_tables(
    infos, place_cosine, place_sine, t, cosine, sine, head_mask, width_mask, seg_col, seg_row
):
    tokens, lanes = place_cosine.shape
    own = wide(t)
    lane = wide(lax.broadcasted_iota(jnp.int32, (tokens, lanes), 1))
    place = wide(lax.broadcasted_iota(jnp.int32, (tokens, lanes), 0))
    sign = jnp.where(lane < lanes // 2, -1.0, 1.0)
    for b in range(2):
        rows = pl.ds(b * tokens, tokens)

        def row(k, b=b):
            return infos[b, pl.ds(k, 1), :]

        segment = jnp.sum(jnp.where(place >= row(0), 1.0, 0.0), axis=1, keepdims=True)
        seg_col[rows, :] = segment
        chosen = jnp.where(lane == segment, 1.0, 0.0)
        head = jnp.sum(chosen * row(2), axis=1, keepdims=True)
        width = jnp.sum(chosen * row(3), axis=1, keepdims=True)
        head_mask[rows, :] = jnp.where(head >= own, 1.0, 0.0)
        width_mask[rows, :] = jnp.where(width >= own, 1.0, 0.0)
        start_cosine, start_sine = 0.0, 0.0
        for s in range(4):
            here = jnp.where(segment == s, 1.0, 0.0)
            start_cosine = start_cosine + here * row(16 + s)
            start_sine = start_sine + here * row(20 + s)
        at_cosine, at_sine = place_cosine[...], place_sine[...]
        cosine[rows, :] = at_cosine * start_cosine + at_sine * start_sine
        sine[rows, :] = (at_sine * start_cosine - at_cosine * start_sine) * sign
        ends = infos[b, pl.ds(8, 8), pl.ds(0, 1)]
        across = wide(lax.broadcasted_iota(jnp.int32, (8, tokens), 1))
        seg_row[b] = jnp.sum(jnp.where(across >= ends, 1.0, 0.0), axis=0, keepdims=True)


def forward_kernel(
    residual_in,
    cotangent_in,
    gain1,
    shift1,
    gain2,
    shift2,
    lengths,
    head_bucket,
    width_bucket,
    place_cosine_in,
    place_sine_in,
    half_qkv,
    half_out,
    half_up,
    half_down,
    cosine_out,
    sine_out,
    head_mask_out,
    all_qkv,
    all_out,
    all_up,
    stream1,
    stream2,
    stream_c,
    normed1,
    normed2,
    heads_out,
    weights_out,
    mixed_out,
    active_out,
    grad_upper_out,
    part_out,
    middle_out,
    w_qkv,
    w_out,
    w_up,
    w_down,
    rows1,
    rows2,
    rows_c,
    normed,
    qkv,
    weights,
    mixed,
    part,
    got_c,
    got_y,
    got_z,
    upper,
    active,
    grad_active,
    middle,
    infos,
    seg_col,
    seg_row,
    width_mask,
    residual,
    cotangent,
    place_cosine,
    place_sine,
    cosine,
    sine,
    head_mask,
    send_sems,
    recv_sems,
    move_sems,
):
    p = Place()
    tr, mv = Traffic(send_sems, recv_sems), Moves(move_sems)
    tokens = residual.shape[0]
    rows_d = half_qkv.shape[1]
    head_cols = w_out.shape[1]

    def row_slot(ref):
        return lambda d: ref.at[pl.ds(pl.multiple_of(d * rows_d, rows_d), rows_d)]

    def first_slot(ref):
        return lambda d: ref.at[d]

    def at_side(k, cut, size):
        return pl.ds(pl.multiple_of(k * size + cut.start, 128), cut.size)

    hidden = w_up.shape[1]
    parts = [pl.ds(0, hidden // 2), pl.ds(hidden // 2, hidden // 2)]

    def rows_at(d):
        return pl.ds(pl.multiple_of(d * rows_d, rows_d), rows_d)

    def up_gather(name, cut):
        return WeightGather(
            name,
            p,
            tr,
            mv,
            lambda k: half_up.at[:, at_side(k, cut, hidden)],
            lambda d: w_up.at[rows_at(d), cut],
        )

    def down_gather(name, cut):
        return WeightGather(
            name,
            p,
            tr,
            mv,
            lambda k: half_down.at[at_side(k, cut, hidden), :],
            lambda d: w_down.at[d, cut, :],
        )

    heads_cut = pl.ds(0, head_cols)
    q = WeightGather(
        "q",
        p,
        tr,
        mv,
        lambda k: half_qkv.at[:, :, at_side(k, heads_cut, head_cols)],
        lambda d: w_qkv.at[:, rows_at(d), :],
    )
    o = WeightGather(
        "o",
        p,
        tr,
        mv,
        lambda k: half_out.at[at_side(k, heads_cut, head_cols), :],
        lambda d: w_out.at[d],
    )
    u, v = [up_gather(n, cut) for n, cut in zip("uv", parts)]
    d, e = [down_gather(n, cut) for n, cut in zip("de", parts)]
    a1 = ActGather("a", p, tr, rows1)
    a2 = ActGather("b", p, tr, rows2)
    ac = ActGather("c", p, tr, rows_c)
    s1 = ActScatter("s", p, tr, part, got_c, got_y, got_z)

    mv.start("residual", residual_in, residual)
    mv.start("place_cosine", place_cosine_in, place_cosine)
    mv.start("place_sine", place_sine_in, place_sine)
    mv.start("cotangent", cotangent_in, cotangent)
    p.greet()
    for one in (q, o, u, v, d, e):
        one.own()
    blocks = w_out.shape[0]
    stripes = part.shape[1]
    per = blocks // stripes
    started = []

    def project(b):
        def body(r):
            at = pl.ds(b * tokens + r, 256)
            for k in range(3):
                got = dot_f32(normed[at, :], w_qkv[k])
                for h in range(head_cols // HD):
                    cols = pl.ds(h * HD, HD)
                    one = got[:, h * HD : (h + 1) * HD]
                    if k < 2:
                        one = one * cosine[at, :] + pltpu.roll(one, HD // 2, 1) * sine[at, :]
                    qkv[k, at, cols] = one.astype(jnp.bfloat16)

        loop_rows(tokens, 256, body)

    def branch(b):
        at = pl.ds(b * tokens, tokens)

        def body(s, carry):
            for j in range(per):
                got = dot_f32(mixed[at, :], w_out[s * per + j])
                part[b, s, :, pl.ds(j * rows_d, rows_d)] = got.astype(jnp.bfloat16)
            return carry

        lax.fori_loop(0, stripes, body, 0)

    def rise(b, cut):
        def body(r):
            at = pl.ds(b * tokens + r, 256)
            for k in range(cut.size // 256):
                cols = pl.ds(cut.start + k * 256, 256)
                got = dot_f32(normed[at, :], w_up[:, cols])
                got = jnp.maximum(got, 0.0) * width_mask[at, :]
                upper[at, cols] = got.astype(jnp.bfloat16)
                active[at, cols] = (got * got).astype(jnp.bfloat16)

        loop_rows(tokens, 256, body)

    def fall(m):
        place = p.block(m)
        s = place // per
        cols = pl.ds(pl.multiple_of((place % per) * rows_d, rows_d), rows_d)
        first = not started
        started.append(m)

        def body(r):
            b, at = r // tokens, pl.ds(pl.multiple_of(r % tokens, 256), 256)
            rows = pl.ds(r, 256)
            part[b, s, at, cols] = dot_f32(active[rows, :], w_down[place]).astype(jnp.bfloat16)
            got = dot_nt(rows_c[b, s, at, cols], w_down[place])
            grad_active[rows, :] = got if first else grad_active[rows, :] + got

        loop_rows(2 * tokens, 256, body)
        for b in range(2):
            mv.start("part" + str(b) + str(m), part.at[b, s, :, cols], part_out.at[b, s, :, cols])

    def turn(r):
        at = pl.ds(r, 64)
        active[at, :] = (grad_active[at, :] * 2.0 * wide(upper[at, :])).astype(jnp.bfloat16)

    o.z()
    q.far()
    o.x()
    mv.wait("residual")
    round_rows(residual, rows1.at[0, p.t], tokens)
    a1.y()
    q.z()
    o.far_next()
    a1.z()
    e.x()
    q.x()
    mv.wait("place_cosine", "place_sine")
    fill_facts(lengths, head_bucket, width_bucket, place_cosine, place_sine, infos.at[0])
    tr.send("info", infos.at[0], infos.at[1], p.z)
    q.far_next()
    q.x_next(6)
    a1.c()
    v.z()
    a1.pass_y(0)
    o.far()
    o.x_next(2)
    o.x_next(4)
    e.z()
    a1.pass_z()
    q.x_next(2)
    q.x_next(4)
    u.far()
    a1.take(0)
    norm_rows(rows1, 0, gain1, shift1, normed)
    a1.pass_y(1)
    tr.wait("info")
    fill_tables(
        infos, place_cosine, place_sine, p.t, cosine, sine, head_mask, width_mask, seg_col, seg_row
    )
    mv.start("cosine", cosine, cosine_out)
    mv.start("sine", sine, sine_out)
    mv.start("head_mask", head_mask, head_mask_out)
    o.x_next(6)
    a1.take(1)
    norm_rows(rows1, 1, gain1, shift1, normed)
    mv.start("stream1", rows1, stream1)
    mv.start("normed1", normed, normed1)
    u.z()
    v.far()
    q.end()
    project(1)
    attend(
        1, qkv, seg_col, seg_row, head_mask, weights, mixed, HD ** (-0.5)
    )
    o.end()
    branch(1)
    s1.c(1)
    d.z()
    s1.y(1)
    e.x_next(2)
    project(0)
    mv.start("all_qkv", w_qkv, all_qkv)
    attend(
        0, qkv, seg_col, seg_row, head_mask, weights, mixed, HD ** (-0.5)
    )
    mv.start("heads", qkv, heads_out)
    mv.start("weights", weights, weights_out)
    mv.start("mixed", mixed, mixed_out)
    branch(0)
    mv.start("all_out", w_out, all_out)
    u.x()
    d.x()
    v.x_next(2)
    s1.c(0)
    v.far_next()
    s1.own(1)
    u.x_next(6)
    s1.y(0)
    s1.z()
    s1.own(0)
    mv.wait("cotangent")
    round_rows(cotangent, rows_c.at[0, p.t], tokens)
    v.x()
    u.far_next()
    ac.y()
    s1.home()
    s1.end(middle, residual)
    round_rows(middle, rows2.at[0, p.t], tokens)
    mv.start("middle", middle, middle_out)
    v.x_next(4)
    a2.z()
    u.x_next(2)
    v.x_next(6)
    ac.z()
    d.far_next()
    e.far()
    e.far_next()
    ac.c()
    a2.y()
    a2.c()
    a2.pass_y(0)
    u.x_next(4)
    a2.pass_z()
    d.x_next(2)
    ac.pass_y(0)
    d.far()
    a2.take(0)
    mv.wait("normed1")
    norm_rows(rows2, 0, gain2, shift2, normed)
    ac.pass_z()
    a2.pass_y(1)
    d.x_next(4)
    a2.take(1)
    norm_rows(rows2, 1, gain2, shift2, normed)
    mv.start("stream2", rows2, stream2)
    mv.start("normed2", normed, normed2)
    u.end()
    rise(1, parts[0])
    e.x_next(6)
    rise(0, parts[0])
    ac.pass_y(1)
    v.end()
    rise(1, parts[1])
    rise(0, parts[1])
    mv.start("active", active, active_out)
    mv.start("all_up", w_up, all_up)
    e.x_next(4)
    ac.take(0)
    ac.take(1)
    s1.sent()
    d.take(4)
    e.take(4)
    fall(4)
    mv.start("stream_c", rows_c, stream_c)
    d.take(2)
    e.take(2)
    fall(2)
    d.take(0)
    e.take(0)
    fall(0)
    d.x_next(6)
    d.take(6)
    e.take(6)
    fall(6)
    d.take(1)
    e.take(1)
    fall(1)
    d.take(5)
    e.take(5)
    fall(5)
    d.take(3)
    e.take(3)
    fall(3)
    d.take(7)
    e.take(7)
    fall(7)
    mv.wait("active")
    loop_rows(2 * tokens, 64, turn)
    mv.start("grad_upper", active, grad_upper_out)
    tr.finish()
    mv.finish()


def forward_call(arrays, weights):
    bf16, f32 = jnp.bfloat16, jnp.float32
    tokens, columns = arrays[0].shape
    w_qkv, w_out, w_up, w_down = weights
    count, stripes = lax.axis_size("dp"), lax.axis_size("tensor")
    rows_d = w_up.shape[0]
    head_cols = w_out.shape[0] // 2
    hidden = w_up.shape[1] // 2
    width = rows_d * count
    heads = head_cols // HD
    slots = (2, stripes, tokens, columns)
    tables = dict(
        cosine=((2 * tokens, HD), f32),
        sine=((2 * tokens, HD), f32),
        head_mask=((2 * tokens, 1), f32),
    )
    shapes = dict(
        all_qkv=((3, width, head_cols), bf16),
        all_out=((count, head_cols, rows_d), bf16),
        all_up=((width, hidden), bf16),
        stream1=(slots, bf16),
        stream2=(slots, bf16),
        stream_c=(slots, bf16),
        normed1=((2 * tokens, width), bf16),
        normed2=((2 * tokens, width), bf16),
        heads=((3, 2 * tokens, head_cols), bf16),
        weights=((2 * heads, tokens, tokens), bf16),
        mixed=((2 * tokens, head_cols), bf16),
        active=((2 * tokens, hidden), bf16),
        grad_upper=((2 * tokens, hidden), bf16),
        part_out=(slots, bf16),
        middle=((tokens, columns), f32),
    )

    def vmem(name):
        return pltpu.VMEM(*shapes[name])

    scratch = [
        vmem("all_qkv"),
        vmem("all_out"),
        vmem("all_up"),
        pltpu.VMEM((count, hidden, rows_d), bf16),
        vmem("stream1"),
        vmem("stream2"),
        vmem("stream_c"),
        vmem("normed1"),
        vmem("heads"),
        vmem("weights"),
        vmem("mixed"),
        pltpu.VMEM(slots, bf16),
        pltpu.VMEM((2, 2, tokens, columns), bf16),
        pltpu.VMEM((2, tokens, columns), bf16),
        pltpu.VMEM((tokens, columns), bf16),
        vmem("active"),
        vmem("active"),
        pltpu.VMEM((2 * tokens, hidden), f32),
        vmem("middle"),
        pltpu.VMEM((2, 24, 128), f32),
        pltpu.VMEM((2 * tokens, 1), f32),
        pltpu.VMEM((2, 1, tokens), f32),
        pltpu.VMEM((2 * tokens, 1), f32),
        vmem("middle"),
        vmem("middle"),
        pltpu.VMEM((tokens, HD), f32),
        pltpu.VMEM((tokens, HD), f32),
        *[pltpu.VMEM(*s) for s in tables.values()],
        pltpu.SemaphoreType.DMA((72,)),
        pltpu.SemaphoreType.DMA((72,)),
        pltpu.SemaphoreType.DMA((48,)),
    ]
    any_spec = pl.BlockSpec(memory_space=pl.ANY)
    vmem_spec = pl.BlockSpec(memory_space=pltpu.VMEM)
    smem_spec = pl.BlockSpec(memory_space=pltpu.SMEM)
    outs = pl.pallas_call(
        forward_kernel,
        out_shape=[jax.ShapeDtypeStruct(*s) for s in (tables | shapes).values()],
        in_specs=[any_spec] * 2 + [vmem_spec] * 4 + [smem_spec] * 3 + [any_spec] * 6,
        out_specs=[any_spec] * (len(tables) + len(shapes)),
        scratch_shapes=scratch,
        compiler_params=pltpu.CompilerParams(
            collective_id=0, has_side_effects=True, vmem_limit_bytes=62 << 20
        ),
    )(*arrays, *weights)
    split = len(tables)
    return outs[:split], dict(zip(shapes, outs[split:]))


class WeightScatter:
    def __init__(self, name, place, traffic, odd, even, got_x, got_far, out):
        self.name, self.p, self.tr = name, place, traffic
        self.odd, self.even, self.got_x, self.got_far, self.out = odd, even, got_x, got_far, out

    def send_x(self, m):
        self.tr.send(self.name + "x" + str(m), self.odd.at[m // 2], self.got_x.at[m // 2], self.p.x)

    def add_x(self, m):
        k, n = m // 2, self.name
        own = self.even.at[k]
        self.tr.wait(n + "x" + str(m + 1))
        add_blocks(own, own, self.got_x.at[k], own.shape[0])
        if m >= 4:
            self.tr.send(n + "f" + str(m), own, self.got_far.at[3 - k], self.p.far)

    def add_far(self, m):
        k, n = m // 2, self.name
        own = self.even.at[k]
        self.tr.wait(n + "f" + str(6 - m))
        add_blocks(own, own, self.got_far.at[k], own.shape[0])
        if m == 2:
            for j, (cut, spot) in enumerate(self.out(self.p.side)):
                self.tr.send(n + "z" + str(j), own.at[:, cut], spot, self.p.z)

    def end(self, moves):
        for j, (cut, spot) in enumerate(self.out(self.p.side)):
            moves.start(self.name + str(j), self.even.at[0, :, cut], spot)
            self.tr.wait(self.name + "z" + str(j))


class SumAll:
    def __init__(self, name, place, traffic, sums, got):
        self.name, self.tr, self.sums, self.got = name, traffic, sums, got
        self.partners = (place.c, place.y, place.x, place.z, place.far)

    def start(self, k):
        self.tr.send(self.name + str(k), self.sums, self.got.at[k], self.partners[k])

    def step(self, k):
        self.tr.wait(self.name + str(k))
        self.tr.sent(self.name + str(k))
        self.sums[...] += self.got[k]
        if k + 1 < len(self.partners):
            self.start(k + 1)


def norm_back(b, part, slots, gain, total, first):
    stripes, rows, columns = part.shape[1:]
    tile = 64
    fold = (tile // 8, 8, stripes * columns)

    def body(r):
        at = pl.ds(r, tile)
        value = wide(slots[at, :])
        center = value - jnp.mean(value, axis=1, keepdims=True)
        spread = jnp.mean(center * center, axis=1, keepdims=True)
        inverse = lax.rsqrt(spread + epsilon)
        unit = center * inverse
        grad = jnp.concatenate([wide(part[b, s, at, :]) for s in range(stripes)], axis=1)
        scaled = grad * gain[...]
        push = inverse * (
            scaled
            - jnp.mean(scaled, axis=1, keepdims=True)
            - unit * jnp.mean(scaled * unit, axis=1, keepdims=True)
        )
        for s in range(stripes):
            part[b, s, at, :] = push[:, s * columns : (s + 1) * columns].astype(jnp.bfloat16)
        total[0] += jnp.sum((grad * unit).reshape(fold), axis=0)
        total[1] += jnp.sum(grad.reshape(fold), axis=0)

    if first:
        total[...] = jnp.zeros_like(total)
    loop_rows(rows, tile, body)


def attend_back(b, qkv, weights, grad_mixed, cosine, sine, out, tokens, scale):
    width = grad_mixed.shape[1]
    heads = width // HD
    half = tokens // 2
    start = b * tokens

    def turn_back(grad, rows):
        return (grad * cosine[rows, :] - pltpu.roll(grad, HD // 2, 1) * sine[rows, :]).astype(
            jnp.bfloat16
        )

    for h in range(heads):
        spots = [pl.ds(k * width + h * HD, HD) for k in range(3)]
        grad_key, grad_value = None, None
        for part in (1, 0):
            rows = pl.ds(start + part * half, half)
            reach = pl.ds(start, half * (part + 1))
            query, key, value = qkv[rows, spots[0]], qkv[reach, spots[1]], qkv[reach, spots[2]]
            given = grad_mixed[rows, pl.ds(h * HD, HD)]
            chosen = weights[b * heads + h, pl.ds(part * half, half), pl.ds(0, half * (part + 1))]
            grad = dot_nt(given, value)
            soft = wide(chosen)
            grad = soft * (grad - jnp.sum(grad * soft, axis=1, keepdims=True))
            raw = (grad * scale).astype(jnp.bfloat16)
            out[rows, spots[0]] = turn_back(dot_f32(raw, key), rows)
            key_part, value_part = dot_tn(raw, query), dot_tn(chosen, given)
            if part == 1:
                grad_key, grad_value = key_part, value_part
        low, high = pl.ds(start, half), pl.ds(start + half, half)
        out[low, spots[1]] = turn_back(grad_key[:half] + key_part, low)
        out[high, spots[1]] = turn_back(grad_key[half:], high)
        out[low, spots[2]] = (grad_value[:half] + value_part).astype(jnp.bfloat16)
        out[high, spots[2]] = grad_value[half:].astype(jnp.bfloat16)


def backward_kernel(
    cotangent_in,
    gain1,
    gain2,
    cosine_in,
    sine_in,
    head_mask_in,
    lengths,
    width_bucket,
    all_qkv,
    all_out,
    all_up,
    stream1,
    stream2,
    stream_c,
    normed1,
    normed2,
    heads,
    weights_in,
    mixed_in,
    active_in,
    grad_upper_in,
    part_in,
    middle_in,
    output,
    grad_input,
    sums2_out,
    sums1_out,
    grad_qkv,
    grad_out,
    grad_up,
    grad_down,
    w_up,
    w_out,
    rows_a,
    rows_b,
    active,
    grad_upper,
    part_a,
    part_b,
    got_ca,
    got_ya,
    got_za,
    got_cb,
    got_yb,
    got_zb,
    stream_b,
    weights,
    mixed,
    grad_mixed,
    odd,
    even_down,
    even_up,
    odd_out,
    even_out,
    gx_down,
    gf_down,
    gx_up,
    gf_up,
    gx_qkv,
    gf_qkv,
    gx_out,
    gf_out,
    middle,
    grad_middle,
    total,
    sums2,
    got2,
    sums1,
    got1,
    cotangent,
    cosine,
    sine,
    head_mask,
    send_sems,
    recv_sems,
    move_sems,
):
    p = Place()
    tr, mv = Traffic(send_sems, recv_sems), Moves(move_sems)
    tokens, columns = cotangent.shape
    stripes, blocks = part_a.shape[1], all_out.shape[0]
    rows_d = all_out.shape[2]
    per = blocks // stripes
    head_cols = mixed.shape[1]
    bf16 = jnp.bfloat16

    def load_stream(name, src, dst):
        for b in range(2):
            for s in range(stripes):
                spot = dst.at[pl.ds(b * tokens, tokens), pl.ds(s * columns, columns)]
                mv.start(name + str(b) + str(s), src.at[b, s], spot)

    def wait_stream(name):
        mv.wait(*[name + str(b) + str(s) for b in range(2) for s in range(stripes)])

    s_out = ActScatter("s", p, tr, part_a, got_ca, got_ya, got_za)
    half = tokens // 2
    halves = [pl.ds(0, half), pl.ds(half, half)]

    def half_scatter(name, cut):
        views = part_b.at[:, :, cut], got_cb.at[:, :, cut], got_yb.at[:, cut], got_zb.at[cut]
        return ActScatter(name, p, tr, *views)

    s2a, s2b = [half_scatter(n, cut) for n, cut in zip("tT", halves)]
    s1a, s1b = [half_scatter(n, cut) for n, cut in zip("rR", halves)]
    aba, abb = [ActGather(n, p, tr, stream_b.at[:, :, cut]) for n, cut in zip("bB", halves)]
    begun = set()
    qkv_cols = pl.ds(0, 3 * head_cols)

    def back(layer, b, h, slots, gain):
        rows = pl.ds(b * tokens + h * half, half)
        first = layer not in begun
        begun.add(layer)
        norm_back(b, part_b.at[:, :, halves[h]], slots.at[rows], gain, total, first)

    hidden = active.shape[1]
    parts = [pl.ds(0, hidden // 2), pl.ds(hidden // 2, hidden // 2)]

    def at_side(k, cut, size):
        return pl.ds(pl.multiple_of(k * size + cut.start, 128), cut.size)

    def scatter(name, odd, even, got_x, got_far, out, cols):
        views = [ref.at[:, :, cols] for ref in (odd, even, got_x, got_far)]

        def spots(k):
            if len(out.shape) == 3:
                return [
                    (pl.ds(j * head_cols, head_cols), out.at[j, :, at_side(k, heads_cut, head_cols)])
                    for j in range(3)
                ]
            spot = out.at[:, at_side(k, cols, out.shape[1] // 2)]
            return [(pl.ds(0, cols.size), spot)]

        return WeightScatter(name, p, tr, *views, spots)

    heads_cut = pl.ds(0, head_cols)

    d, e = [
        scatter(n, odd, even_down, gx_down, gf_down, grad_down, cut) for n, cut in zip("de", parts)
    ]
    u, v = [scatter(n, odd, even_up, gx_up, gf_up, grad_up, cut) for n, cut in zip("uv", parts)]
    q = scatter("q", odd, even_down, gx_qkv, gf_qkv, grad_qkv, qkv_cols)
    o = scatter("o", odd_out, even_out, gx_out, gf_out, grad_out, pl.ds(0, head_cols))
    all2 = SumAll("2", p, tr, sums2, got2)
    all1 = SumAll("1", p, tr, sums1, got1)

    load_stream("c", stream_c, rows_a)
    mv.start("active", active_in, active)
    mv.start("grad_upper", grad_upper_in, grad_upper)
    mv.start("all_up", all_up, w_up)
    load_stream("x2", stream2, rows_b)
    p.greet()

    def load_rest():
        for k in range(blocks):
            mv.start("p" + str(k), all_out.at[k], w_out.at[:, pl.ds(k * rows_d, rows_d)])
        mv.start("cotangent", cotangent_in, cotangent)
        mv.start("head_mask", head_mask_in, head_mask)
        mv.start("cosine", cosine_in, cosine)
        mv.start("sine", sine_in, sine)
        mv.start("mixed", mixed_in, mixed)
        mv.start("weights", weights_in, weights)
        mv.start("part", part_in, part_a)
        mv.start("middle", middle_in, middle)

    def block_cols(m):
        return pl.ds(pl.multiple_of(p.block(m) * rows_d, rows_d), rows_d)

    def grad_block(left, right, m, spot, cols=None):
        value = right[...] if cols is None else right[:, cols]
        spot[...] = dot_tn(left[:, block_cols(m)], value).astype(bf16)

    def down_block(m, spot):
        grad_block(rows_a, active, m, spot)

    def product(b, left, right, cols):
        at = pl.ds(b * tokens, tokens)

        def body(s, carry):
            rows = pl.ds(pl.multiple_of(s * columns, columns), columns)
            part_b[b, s] = dot_nt(left[at, cols], right[rows, cols]).astype(bf16)
            return carry

        lax.fori_loop(0, stripes, body, 0)

    def gather_total(sums):
        depth, lanes = 8, total.shape[2] // 8
        sums[...] = jnp.zeros_like(sums)
        for k in range(2):
            row = jnp.sum(total[k], axis=0, keepdims=True)
            for r in range(depth):
                sums[pl.ds(r, 1), pl.ds(k * lanes, lanes)] = row[:, r * lanes : (r + 1) * lanes]
        sums[pl.ds(0, 1), pl.ds(2 * lanes, HD)] = count_row(lengths, width_bucket, HD)

    def unpack(sums, out):
        depth, lanes = 8, total.shape[2] // 8
        for k in range(2):
            for r in range(depth):
                spot = sums[pl.ds(r, 1), pl.ds(k * lanes, lanes)]
                out[pl.ds(k, 1), pl.ds(r * lanes, lanes)] = spot
        out[pl.ds(2, 1), pl.ds(0, HD)] = sums[pl.ds(0, 1), pl.ds(2 * lanes, HD)]

    def up_block(m, spot):
        grad_block(rows_a, grad_upper, m, spot)

    def up_odd(m):
        tr.sent("dx" + str(m), "ex" + str(m))
        up_block(m, odd.at[m // 2])
        u.send_x(m)
        v.send_x(m)

    def mix(b):
        mv.wait("head_mask", *["p" + str(k) for k in range(blocks)])
        at = pl.ds(b * tokens, tokens)
        got = None
        for s in range(stripes):
            one = dot_nt(stream_b[b, s], w_out[:, pl.ds(s * columns, columns)])
            got = one if got is None else got + one
        grad_mixed[at, :] = (got * head_mask[at, :]).astype(bf16)

    def out_block(m, spot):
        mv.wait("mixed")
        place = p.block(m)
        cols = pl.ds(pl.multiple_of((place % per) * rows_d, rows_d), rows_d)
        near = dot_tn(stream_b[0, place // per, :, cols], mixed[pl.ds(0, tokens), :])
        away = dot_tn(stream_b[1, place // per, :, cols], mixed[pl.ds(tokens, tokens), :])
        spot[...] = (near + away).astype(bf16)

    def qkv_block(m, spot):
        mv.wait("normed1")
        grad_block(rows_b, grad_upper, m, spot, qkv_cols)

    def qkv_odd(m):
        tr.sent("ux" + str(m), "vx" + str(m))
        qkv_block(m, odd.at[m // 2, :, qkv_cols])
        q.send_x(m)

    def qkv_even(m):
        mv.wait("d0", "e0")
        tr.sent("df4", "df6", "dz0", "ef4", "ef6", "ez0")
        qkv_block(m, even_down.at[m // 2, :, qkv_cols])

    wait_stream("c")
    mv.wait("active")
    down_block(5, odd.at[2])
    d.send_x(5)
    e.send_x(5)
    down_block(2, even_down.at[1])
    mv.wait("grad_upper", "all_up")
    down_block(4, even_down.at[2])
    product(1, grad_upper, w_up, pl.ds(0, w_up.shape[1]))
    wait_stream("x2")
    back(2, 1, 1, rows_b, gain2)
    d.add_x(4)
    down_block(6, even_down.at[3])
    s2b.c(1)
    down_block(7, odd.at[3])
    d.send_x(7)
    e.send_x(7)
    product(0, grad_upper, w_up, pl.ds(0, w_up.shape[1]))
    e.add_x(4)
    s2b.own(1)
    load_rest()
    back(2, 1, 0, rows_b, gain2)
    s2a.c(1)
    s2b.y(1)
    back(2, 0, 0, rows_b, gain2)
    d.add_x(6)
    back(2, 0, 1, rows_b, gain2)
    down_block(1, odd.at[0])
    d.send_x(1)
    e.send_x(1)
    down_block(0, even_down.at[0])
    gather_total(sums2)
    all2.start(0)
    s2a.y(1)
    s2b.c(0)
    down_block(3, odd.at[1])
    d.send_x(3)
    e.send_x(3)
    s2a.c(0)
    s2b.z()
    for k in range(3):
        mv.start("h" + str(k), heads.at[k], active.at[:, pl.ds(k * head_cols, head_cols)])
    mv.start("normed2", normed2, rows_a)
    s2a.own(0)
    e.add_x(6)
    mv.wait("normed2")
    mv.wait("part")
    s2a.own(1)
    s2b.y(0)
    up_odd(5)
    s2a.z()
    s2b.own(0)
    s2b.home()
    s2a.y(0)
    up_block(4, even_up.at[2])
    mv.wait("cotangent")
    s2b.end(grad_middle.at[halves[1]], cotangent.at[halves[1]])
    round_rows(grad_middle.at[halves[1]], stream_b.at[0, p.t, halves[1]], tokens // 2)
    up_odd(7)
    abb.z()
    s2a.home()
    s2a.end(grad_middle.at[halves[0]], cotangent.at[halves[0]])
    round_rows(grad_middle.at[halves[0]], stream_b.at[0, p.t, halves[0]], tokens // 2)
    for k in range(3):
        mv.start("w" + str(k), all_qkv.at[k], w_up.at[:, pl.ds(k * head_cols, head_cols)])
    mv.start("normed1", normed1, rows_b)
    aba.z()
    abb.y()
    all2.step(0)
    s_out.c(1)
    abb.pass_z()
    up_odd(3)
    e.add_x(0)
    d.add_x(2)
    u.add_x(4)
    aba.pass_z()
    e.add_x(2)
    v.add_x(4)
    aba.y()
    d.add_far(2)
    up_block(6, even_up.at[3])
    d.add_x(0)
    up_block(2, even_up.at[1])
    aba.pass_y(1)
    e.add_far(0)
    abb.pass_y(1)
    s_out.y(1)
    up_odd(1)
    aba.c()
    s_out.own(1)
    abb.pass_y(0)
    up_block(0, even_up.at[0])
    e.add_far(2)
    aba.pass_y(0)
    v.add_x(6)
    abb.c()
    all2.step(1)
    aba.take(0)
    abb.take(0)
    mix(0)
    u.add_x(6)
    aba.take(1)
    abb.take(1)
    mix(1)
    mv.wait("cosine", "sine", "weights", "h0", "h1", "h2")
    attend_back(
        1, active, weights, grad_mixed, cosine, sine, grad_upper, tokens, HD ** (-0.5)
    )
    u.add_x(2)
    out_block(7, odd_out.at[3])
    o.send_x(7)
    attend_back(
        0, active, weights, grad_mixed, cosine, sine, grad_upper, tokens, HD ** (-0.5)
    )
    s2a.sent()
    s2b.sent()
    mv.wait("w0", "w1", "w2")
    product(0, grad_upper, w_up, qkv_cols)
    s_out.z()
    out_block(6, even_out.at[3])
    product(1, grad_upper, w_up, qkv_cols)
    out_block(5, odd_out.at[2])
    o.send_x(5)
    u.add_x(0)
    load_stream("x1", stream1, rows_a)
    out_block(1, odd_out.at[0])
    o.send_x(1)
    v.add_x(2)
    wait_stream("x1")
    back(1, 0, 0, rows_a, gain1)
    u.add_far(2)
    back(1, 1, 0, rows_a, gain1)
    v.add_far(2)
    back(1, 0, 1, rows_a, gain1)
    back(1, 1, 1, rows_a, gain1)
    gather_total(sums1)
    all1.start(0)
    qkv_odd(5)
    d.add_far(0)
    d.end(mv)
    s1a.c(0)
    s1b.c(1)
    s1a.own(0)
    s1b.own(1)
    s_out.c(0)
    out_block(3, odd_out.at[1])
    o.send_x(3)
    e.end(mv)
    s1a.c(1)
    out_block(4, even_out.at[2])
    qkv_odd(3)
    all1.step(0)
    s1b.y(1)
    qkv_even(6)
    o.add_x(4)
    s1b.c(0)
    s1a.y(1)
    qkv_odd(7)
    u.add_far(0)
    s1b.y(0)
    s1b.z()
    v.add_x(0)
    v.add_far(0)
    all1.step(1)
    s1a.own(1)
    v.end(mv)
    o.add_x(6)
    qkv_even(0)
    u.end(mv)
    qkv_even(2)
    s1a.y(0)
    s1b.own(0)
    out_block(2, even_out.at[1])
    qkv_even(4)
    q.add_x(4)
    o.add_x(2)
    s1a.z()
    out_block(0, even_out.at[0])
    o.add_x(0)
    all1.step(2)
    all2.step(2)
    s1a.home()
    q.add_x(2)
    q.add_x(6)
    s1b.home()
    qkv_odd(1)
    s_out.own(0)
    s_out.y(0)
    o.add_far(2)
    s_out.home()
    q.add_x(0)
    all1.step(3)
    all2.step(3)
    q.add_far(2)
    o.add_far(0)
    mv.wait("middle")
    s_out.end(middle, middle)
    mv.start("output", middle, output)
    all1.step(4)
    o.end(mv)
    q.add_far(0)
    all2.step(4)
    s1a.end(grad_middle.at[halves[0]], grad_middle.at[halves[0]])
    s1b.end(grad_middle.at[halves[1]], grad_middle.at[halves[1]])
    mv.start("grad_input", grad_middle, grad_input)
    q.end(mv)
    unpack(sums2, sums2_out)
    unpack(sums1, sums1_out)
    tr.finish()
    mv.finish()


def backward_call(arrays, saved):
    bf16, f32 = jnp.bfloat16, jnp.float32
    tokens, columns = arrays[0].shape
    count, stripes = lax.axis_size("dp"), lax.axis_size("tensor")
    _, head_cols, rows_d = saved["all_out"].shape
    width, hidden = saved["all_up"].shape
    slots = (2, stripes, tokens, columns)
    wide_rows = (2 * tokens, width)

    def vmem(*shape, dtype=bf16):
        return pltpu.VMEM(shape, dtype)

    def got(cols):
        return [vmem(4, rows_d, cols), vmem(2, rows_d, cols)]

    got_act = [vmem(2, 2, tokens, columns), vmem(2, tokens, columns), vmem(tokens, columns)]
    packed = 2 * width // 8 + HD
    sums = [vmem(8, packed, dtype=f32), vmem(5, 8, packed, dtype=f32)]
    qkv = 3 * head_cols
    scratch = [
        vmem(width, hidden),
        vmem(head_cols, width),
        vmem(*wide_rows),
        vmem(*wide_rows),
        vmem(2 * tokens, hidden),
        vmem(2 * tokens, hidden),
        vmem(*slots),
        vmem(*slots),
        *got_act,
        *got_act,
        vmem(*slots),
        vmem(*saved["weights"].shape),
        vmem(2 * tokens, head_cols),
        vmem(2 * tokens, head_cols),
        vmem(4, rows_d, hidden),
        vmem(4, rows_d, hidden),
        vmem(4, rows_d, hidden),
        vmem(4, rows_d, head_cols),
        vmem(4, rows_d, head_cols),
        *got(hidden),
        *got(hidden),
        *got(qkv),
        *got(head_cols),
        vmem(tokens, columns, dtype=f32),
        vmem(tokens, columns, dtype=f32),
        vmem(2, 8, width, dtype=f32),
        *sums,
        *sums,
        *[vmem(*arrays[k].shape, dtype=f32) for k in (0, 3, 4, 5)],
        pltpu.SemaphoreType.DMA((112,)),
        pltpu.SemaphoreType.DMA((112,)),
        pltpu.SemaphoreType.DMA((80,)),
    ]
    any_spec = pl.BlockSpec(memory_space=pl.ANY)
    vmem_spec = pl.BlockSpec(memory_space=pltpu.VMEM)
    smem_spec = pl.BlockSpec(memory_space=pltpu.SMEM)
    shapes = [
        ((tokens, columns), f32),
        ((tokens, columns), f32),
        ((8, width), f32),
        ((8, width), f32),
        ((3, rows_d, 2 * head_cols), bf16),
        ((rows_d, 2 * head_cols), bf16),
        ((rows_d, 2 * hidden), bf16),
        ((rows_d, 2 * hidden), bf16),
    ]
    names = [k for k in saved]
    return pl.pallas_call(
        backward_kernel,
        out_shape=[jax.ShapeDtypeStruct(*s) for s in shapes],
        in_specs=[any_spec, vmem_spec, vmem_spec] + [any_spec] * 3
        + [smem_spec] * 2
        + [any_spec] * len(names),
        out_specs=[any_spec] * 2 + [vmem_spec] * 2 + [any_spec] * 4,
        scratch_shapes=scratch,
        compiler_params=pltpu.CompilerParams(
            collective_id=1, has_side_effects=True, vmem_limit_bytes=63 << 20
        ),
    )(*arrays, *[saved[n] for n in names])


def finish_kernel(groups, *refs):
    ins, sums, outs, small = refs[:6], refs[6:8], refs[8:14], refs[14:19]
    raw, done, sems = refs[19:25], refs[25:29], refs[29]
    loads = [pltpu.make_async_copy(ins[k], raw[k], sems.at[k]) for k in range(6)]
    for load in loads:
        load.start()
    for k in range(4):
        small[k][...] = sums[k // 2][pl.ds(k % 2, 1), :]
    count = small[4].shape[1]
    small[4][...] = (sums[1][pl.ds(2, 1), pl.ds(0, count)] / groups).astype(jnp.int32)
    stores = []

    def store(k, src):
        stores.append(pltpu.make_async_copy(src, outs[k], sems.at[6 + k]))
        stores[-1].start()

    loads[0].wait()
    rows, columns = raw[0].shape

    def widen(r):
        done[0][pl.ds(r, 32), :] = wide(raw[0][pl.ds(r, 32), :])

    loop_rows(rows, 32, widen)
    store(0, done[0])
    loads[1].wait()

    def turn(src, dst):
        def body(c):
            dst[pl.ds(c, 256), :] = wide(src[:, pl.ds(c, 256)]).T

        loop_rows(src.shape[1], 256, body)

    turn(raw[1], done[1])
    store(1, done[1])
    loads[2].wait()
    for k in range(raw[2].shape[0]):

        def widen_part(r, k=k):
            done[2][k, pl.ds(r, 64), :] = wide(raw[2][k, pl.ds(r, 64), :])

        loop_rows(raw[2].shape[1], 64, widen_part)
    store(2, done[2])
    loads[3].wait()
    turn(raw[3], done[3])
    store(3, done[3])
    for k in (4, 5):
        loads[k].wait()
        store(k, raw[k])
    for one in stores:
        one.wait()


def finish_call(grad_up, grad_down, grad_qkv, grad_out, output, grad_input, sums1, sums2):
    f32 = jnp.float32
    ins = (grad_up, grad_down, grad_qkv, grad_out, output, grad_input)
    shapes = [a.shape for a in ins]
    shapes[1], shapes[3] = shapes[1][::-1], shapes[3][::-1]
    any_spec = pl.BlockSpec(memory_space=pl.ANY)
    vmem_spec = pl.BlockSpec(memory_space=pltpu.VMEM)
    groups = lax.axis_size("tensor")
    return pl.pallas_call(
        functools.partial(finish_kernel, groups),
        out_shape=[jax.ShapeDtypeStruct(s, f32) for s in shapes]
        + [jax.ShapeDtypeStruct((1, sums1.shape[1]), f32)] * 4
        + [jax.ShapeDtypeStruct((1, groups), jnp.int32)],
        in_specs=[any_spec] * 6 + [vmem_spec] * 2,
        out_specs=[any_spec] * 6 + [vmem_spec] * 5,
        scratch_shapes=[pltpu.VMEM(a.shape, a.dtype) for a in ins]
        + [pltpu.VMEM(s, f32) for s in shapes[:4]]
        + [pltpu.SemaphoreType.DMA((12,))],
        compiler_params=pltpu.CompilerParams(vmem_limit_bytes=62 << 20),
    )(*ins, sums1, sums2)


def local_fast(
    residual_in,
    lengths,
    head_bucket,
    width_bucket,
    norm1_gain,
    norm1_shift,
    w_qkv,
    w_out,
    norm2_gain,
    norm2_shift,
    w_up,
    w_down,
    cotangent,
):
    f32 = jnp.float32
    tokens = residual_in.shape[0]
    steps = np.arange(tokens)[:, None] * 10000.0 ** (-2.0 * (np.arange(HD) % (HD // 2)) / HD)
    arrays = (
        residual_in,
        cotangent,
        norm1_gain[None],
        norm1_shift[None],
        norm2_gain[None],
        norm2_shift[None],
        lengths,
        head_bucket,
        width_bucket,
        jnp.asarray(np.cos(steps), f32),
        jnp.asarray(np.sin(steps), f32),
    )
    weights = (jnp.swapaxes(w_qkv, 0, 1), w_out, w_up, w_down)
    (cosine, sine, head_mask), saved = forward_call(arrays, weights)
    arrays = (cotangent, norm1_gain[None], norm2_gain[None], cosine, sine, head_mask)
    output, grad_input, sums2, sums1, grad_qkv, grad_out, grad_up, grad_down = backward_call(
        (*arrays, lengths, width_bucket), saved
    )
    grad_up, grad_down, grad_qkv, grad_out, output, grad_input, *small = finish_call(
        grad_up, grad_down, grad_qkv, grad_out, output, grad_input, sums1, sums2
    )
    gain1_grad, shift1_grad, gain2_grad, shift2_grad, bucket_counts = [one[0] for one in small]
    return (
        output,
        grad_input,
        gain1_grad,
        shift1_grad,
        jnp.swapaxes(grad_qkv, 0, 1),
        grad_out,
        gain2_grad,
        shift2_grad,
        grad_up,
        grad_down,
        bucket_counts,
    )


def local(*args):
    w_out = args[7]
    if lax.axis_size("dp") == 8 and lax.axis_size("tensor") == 4 and w_out.shape[1] % 128 == 0:
        return local_fast(*args)
    return local_general(*args)


def solution(mesh):
    placed = (
        P("dp", "tensor"),
        P("dp", None),
        P("dp", None),
        P("dp", None),
        P(),
        P(),
        P("dp", None, "tensor"),
        P("tensor", "dp"),
        P(),
        P(),
        P("dp", "tensor"),
        P("tensor", "dp"),
        P("dp", "tensor"),
    )
    return jax.shard_map(
        local,
        mesh=mesh,
        in_specs=placed,
        out_specs=(
            P("dp", "tensor"),
            P("dp", "tensor"),
            P(),
            P(),
            P("dp", None, "tensor"),
            P("tensor", "dp"),
            P(),
            P(),
            P("dp", "tensor"),
            P("tensor", "dp"),
            P(),
        ),
        check_vma=False,
    )
```

```python
import functools
import math

import jax
import jax.numpy as jnp
import numpy as np
from jax import lax
from jax.experimental import pallas as pl
from jax.experimental.pallas import tpu as pltpu
from jax.sharding import PartitionSpec as P

HD = 128
HIDDEN_BIT = 2

epsilon = 1e-05


def dp_swap(value, bit):
    count = lax.axis_size("dp")
    return lax.ppermute(value, "dp", [(i, i ^ bit) for i in range(count)])


def tensor_swap(value, bit):
    count = lax.axis_size("tensor")
    return lax.ppermute(value, "tensor", [(i, i ^ bit) for i in range(count)])


def bits_of(count):
    return [1 << i for i in range(count.bit_length() - 1)]


def replica_bits():
    bits = bits_of(lax.axis_size("dp"))
    return [b for b in bits if b > HIDDEN_BIT] + [b for b in bits if b < HIDDEN_BIT]


def gather_weight(mine, other):
    blocks = {0: mine, HIDDEN_BIT: dp_swap(other, HIDDEN_BIT)}
    for bit in replica_bits():
        blocks.update({m | bit: dp_swap(blocks[m], bit) for m in list(blocks)})
    return blocks


def add_low(left, right):
    return (left.astype(jnp.float32) + right.astype(jnp.float32)).astype(jnp.bfloat16)


def scatter_weight(blocks):
    for bit in reversed(replica_bits()):
        arrived = {m ^ bit: dp_swap(blocks[m], bit) for m in blocks if m & bit}
        blocks = {m: add_low(blocks[m], arrived[m]) for m in arrived}
    return blocks[0], dp_swap(blocks[HIDDEN_BIT], HIDDEN_BIT)


def gather_act(rows):
    blocks = {(0, 0): rows, (1, 0): dp_swap(rows, HIDDEN_BIT)}
    for bit in reversed(bits_of(lax.axis_size("tensor"))):
        blocks.update({(b, m | bit): tensor_swap(v, bit) for (b, m), v in list(blocks.items())})
    return blocks


def scatter_act(blocks):
    for bit in bits_of(lax.axis_size("tensor")):
        arrived = {(b, m ^ bit): tensor_swap(v, bit) for (b, m), v in blocks.items() if m & bit}
        blocks = {k: add_low(blocks[k], arrived[k]) for k in arrived}
    return blocks[(0, 0)].astype(jnp.float32) + dp_swap(blocks[(1, 0)], HIDDEN_BIT).astype(
        jnp.float32
    )


def lay(blocks, shape, spots):
    count = len(blocks)

    def kernel(*refs):
        ins, out, sems = refs[:count], refs[count], refs[count + 1]
        copies = []
        for i, spot in enumerate(spots()):
            r, c = blocks[i].shape
            copies.append(
                pltpu.make_async_copy(
                    ins[i],
                    out.at[pl.ds(pl.multiple_of(spot[0], 16), r), pl.ds(pl.multiple_of(spot[1], 128), c)],
                    sems.at[i],
                )
            )
        for copy in copies:
            copy.start()
        for copy in copies:
            copy.wait()

    return pl.pallas_call(
        kernel,
        out_shape=jax.ShapeDtypeStruct(shape, jnp.bfloat16),
        in_specs=[pl.BlockSpec(memory_space=pl.ANY)] * count,
        out_specs=pl.BlockSpec(memory_space=pltpu.VMEM),
        scratch_shapes=[pltpu.SemaphoreType.DMA((count,))],
        compiler_params=pltpu.CompilerParams(vmem_limit_bytes=24 << 20),
    )(*blocks)


def cut(whole, block_shape, count, spots):
    def kernel(*refs):
        src, outs, sems = refs[0], refs[1 : 1 + count], refs[1 + count]
        r, c = block_shape
        copies = []
        for i, spot in enumerate(spots()):
            copies.append(
                pltpu.make_async_copy(
                    src.at[pl.ds(pl.multiple_of(spot[0], 16), r), pl.ds(pl.multiple_of(spot[1], 128), c)],
                    outs[i],
                    sems.at[i],
                )
            )
        for copy in copies:
            copy.start()
        for copy in copies:
            copy.wait()

    return pl.pallas_call(
        kernel,
        out_shape=[jax.ShapeDtypeStruct(block_shape, jnp.bfloat16)] * count,
        in_specs=[pl.BlockSpec(memory_space=pltpu.VMEM)],
        out_specs=[pl.BlockSpec(memory_space=pl.ANY)] * count,
        scratch_shapes=[pltpu.SemaphoreType.DMA((count,))],
        compiler_params=pltpu.CompilerParams(vmem_limit_bytes=24 << 20),
    )(whole)


def lay_weight(blocks, axis):
    count = len(blocks)
    r, c = blocks[0].shape
    if axis == 1 and c % 128:
        order = jnp.bitwise_xor(lax.axis_index("dp"), jnp.arange(count))
        stacked = jnp.stack([blocks[m] for m in range(count)])[order]
        return jnp.swapaxes(stacked, 0, 1).reshape(r, count * c)

    def spots():
        place = lax.axis_index("dp")
        at = [jnp.bitwise_xor(place, m) for m in range(count)]
        return [(d * r, 0) if axis == 0 else (0, d * c) for d in at]

    shape = (r * count, c) if axis == 0 else (r, c * count)
    return lay([blocks[m] for m in range(count)], shape, spots)


def cut_weight(whole, axis):
    count = lax.axis_size("dp")
    r, c = whole.shape
    r, c = (r // count, c) if axis == 0 else (r, c // count)
    if axis == 1 and c % 128:
        order = jnp.bitwise_xor(lax.axis_index("dp"), jnp.arange(count))
        stacked = jnp.swapaxes(whole.reshape(r, count, c), 0, 1)[order]
        return {m: stacked[m] for m in range(count)}

    def spots():
        place = lax.axis_index("dp")
        at = [jnp.bitwise_xor(place, m) for m in range(count)]
        return [(d * r, 0) if axis == 0 else (0, d * c) for d in at]

    return dict(enumerate(cut(whole, (r, c), count, spots)))


def act_keys():
    return [(b, m) for b in range(2) for m in range(lax.axis_size("tensor"))]


def act_spots(r, c):
    place = lax.axis_index("tensor")
    return [(b * r, jnp.bitwise_xor(place, m) * c) for b, m in act_keys()]


def lay_act(blocks):
    r, c = blocks[(0, 0)].shape
    shape = (2 * r, c * lax.axis_size("tensor"))
    return lay([blocks[k] for k in act_keys()], shape, lambda: act_spots(r, c))


def cut_act(whole):
    r, c = whole.shape[0] // 2, whole.shape[1] // lax.axis_size("tensor")
    keys = act_keys()
    return dict(zip(keys, cut(whole, (r, c), len(keys), lambda: act_spots(r, c))))


def whole_stream(rows):
    return lay_act(gather_act(rows.astype(jnp.bfloat16)))


def stream_sum(rows):
    return scatter_act(cut_act(rows.astype(jnp.bfloat16)))


def sum_all(value, axes):
    if "dp" in axes:
        for bit in bits_of(lax.axis_size("dp")):
            value = value + dp_swap(value, bit)
    if "tensor" in axes:
        for bit in bits_of(lax.axis_size("tensor")):
            value = value + tensor_swap(value, bit)
    return value


def token_info(length_row, head_row, width_row, row_count):
    seq_ends = jnp.cumsum(length_row)
    seq_starts = seq_ends - length_row
    places = jnp.arange(row_count, dtype=jnp.int32)
    segment = jnp.sum((places[:, None] >= seq_ends[None, :]).astype(jnp.int32), axis=1)
    labels = jnp.arange(length_row.shape[0], dtype=jnp.int32)
    onehot = (segment[:, None] == labels[None, :]).astype(jnp.int32)
    offset = places - jnp.sum(onehot * seq_starts[None, :], axis=1)
    head_tok = jnp.sum(onehot * head_row[None, :], axis=1)
    width_tok = jnp.sum(onehot * width_row[None, :], axis=1)
    return (segment, offset, head_tok, width_tok)


def rotary_tables(offset, head_size):
    half_size = head_size // 2
    ladder = jnp.arange(half_size, dtype=jnp.float32)
    inverse = jnp.exp(ladder * (-2.0 * math.log(10000.0) / head_size))
    angles = offset.astype(jnp.float32)[:, None] * inverse[None, :]
    return (jnp.cos(angles)[:, None, :], jnp.sin(angles)[:, None, :])


def rotate(values, cosine, sine_part):
    half_size = values.shape[-1] // 2
    front_half = values[..., :half_size]
    back_half = values[..., half_size:]
    return jnp.concatenate(
        [front_half * cosine - back_half * sine_part, back_half * cosine + front_half * sine_part],
        axis=-1,
    )


def norm_forward(values, norm_gain, norm_shift):
    values = values.astype(jnp.float32)
    center = values - jnp.mean(values, axis=-1, keepdims=True)
    spread = jnp.mean(center * center, axis=-1, keepdims=True)
    inverse = lax.rsqrt(spread + epsilon)
    unit_rows = center * inverse
    return (unit_rows * norm_gain + norm_shift, unit_rows, inverse)


def norm_backward(grad_rows, unit_rows, inverse, norm_gain):
    scaled = grad_rows * norm_gain
    grad_in = inverse * (
        scaled
        - jnp.mean(scaled, axis=-1, keepdims=True)
        - unit_rows * jnp.mean(scaled * unit_rows, axis=-1, keepdims=True)
    )
    return (grad_in, jnp.sum(grad_rows * unit_rows, axis=0), jnp.sum(grad_rows, axis=0))


def heads_of(rows, blocks):
    rows = rows.reshape(blocks, rows.shape[0] // blocks, -1, HD)
    return jnp.transpose(rows, (2, 0, 1, 3)).reshape(-1, rows.shape[1], HD)


def rows_of(heads, blocks):
    heads = heads.reshape(-1, blocks, heads.shape[1], HD)
    return jnp.transpose(heads, (1, 2, 0, 3)).reshape(blocks * heads.shape[2], -1)


def local_general(
    residual_in,
    lengths,
    head_bucket,
    width_bucket,
    norm1_gain,
    norm1_shift,
    w_qkv,
    w_out,
    norm2_gain,
    norm2_shift,
    w_up,
    w_down,
    cotangent,
):
    f32, bf16 = jnp.float32, jnp.bfloat16
    dot = functools.partial(jnp.dot, preferred_element_type=f32)
    tensor_index = lax.axis_index("tensor")
    bucket_total = lax.axis_size("tensor")
    tokens = residual_in.shape[0]
    side = (lax.axis_index("dp") // HIDDEN_BIT) % 2

    def halves(weight, axis):
        left, right = jnp.split(weight, 2, axis=axis)
        return jnp.where(side == 0, left, right), jnp.where(side == 0, right, left)

    info = jnp.stack([lengths[0], head_bucket[0], width_bucket[0]])
    far_info = dp_swap(info, HIDDEN_BIT)
    pair = [token_info(i[0], i[1], i[2], tokens) for i in (info, far_info)]
    segment, offset, head_tok, width_tok = [jnp.stack([a, b]) for a, b in zip(*pair)]
    matches = (
        width_bucket[0][:, None] == jnp.arange(bucket_total, dtype=jnp.int32)[None, :]
    ).astype(jnp.int32)
    bucket_counts = sum_all(jnp.sum(lengths[0][:, None] * matches, axis=0), ("dp",))
    head_mask = (head_tok.reshape(-1) >= tensor_index).astype(f32)[:, None]
    width_mask = (width_tok.reshape(-1) >= tensor_index).astype(f32)[:, None]
    places = jnp.arange(tokens, dtype=jnp.int32)
    allowed = (segment[:, :, None] == segment[:, None, :]) & (
        places[:, None] >= places[None, :]
    )
    cosine, sine_part = rotary_tables(offset.reshape(-1), HD)
    score_scale = HD ** (-0.5)

    qkv_halves = [h.reshape(h.shape[0], -1) for h in halves(w_qkv, 2)]
    full_qkv = lay_weight(gather_weight(*qkv_halves), 0)
    full_out = lay_weight(gather_weight(*halves(w_out, 0)), 1)
    full_up = lay_weight(gather_weight(*halves(w_up, 1)), 0)
    full_down = lay_weight(gather_weight(*halves(w_down, 0)), 1)

    inputs = whole_stream(residual_in)
    normed1, unit1, inverse1 = norm_forward(inputs, norm1_gain, norm1_shift)
    normed1 = normed1.astype(bf16)
    projected = dot(normed1, full_qkv).reshape(2 * tokens, 3, -1, HD)
    width = projected.shape[2] * HD
    query = rotate(projected[:, 0], cosine, sine_part).astype(bf16).reshape(-1, width)
    key = rotate(projected[:, 1], cosine, sine_part).astype(bf16).reshape(-1, width)
    value = projected[:, 2].astype(bf16).reshape(-1, width)
    query, key, value = heads_of(query, 2), heads_of(key, 2), heads_of(value, 2)
    allowed = jnp.tile(allowed, (query.shape[0] // 2, 1, 1))
    scores = jnp.einsum("nqd,nkd->nqk", query, key, preferred_element_type=f32) * score_scale
    scores = jnp.where(allowed, scores, -1000000000.0)
    scores = jnp.exp(scores - jnp.max(scores, axis=-1, keepdims=True))
    weights = (scores / jnp.sum(scores, axis=-1, keepdims=True)).astype(bf16)
    mixed = jnp.einsum("nqk,nkd->nqd", weights, value, preferred_element_type=f32)
    mixed = (rows_of(mixed, 2) * head_mask).astype(bf16)
    middle = residual_in + stream_sum(dot(mixed, full_out))
    middle_rows = whole_stream(middle)
    normed2, unit2, inverse2 = norm_forward(middle_rows, norm2_gain, norm2_shift)
    normed2 = normed2.astype(bf16)
    upper = jnp.maximum(dot(normed2, full_up), 0.0) * width_mask
    active = jnp.square(upper).astype(bf16)
    upper = upper.astype(bf16)
    output = middle + stream_sum(dot(active, full_down))

    grad_top = whole_stream(cotangent)
    grad_down = scatter_weight(cut_weight(dot(active.T, grad_top).astype(bf16), 1))
    grad_active = dot(grad_top, full_down.T)
    grad_upper = (grad_active * 2.0 * upper.astype(f32)).astype(bf16)
    grad_normed2 = dot(grad_upper, full_up.T)
    part_middle, gain2_grad, shift2_grad = norm_backward(
        grad_normed2, unit2, inverse2, norm2_gain
    )
    grad_middle = cotangent + stream_sum(part_middle)
    grad_up = scatter_weight(cut_weight(dot(normed2.T, grad_upper).astype(bf16), 0))
    grad_branch = whole_stream(grad_middle)
    grad_wout = scatter_weight(cut_weight(dot(mixed.T, grad_branch).astype(bf16), 1))
    grad_mixed = (dot(grad_branch, full_out.T) * head_mask).astype(bf16)
    grad_mixed = heads_of(grad_mixed, 2)
    grad_weights = jnp.einsum("nqd,nkd->nqk", grad_mixed, value, preferred_element_type=f32)
    grad_value = jnp.einsum("nqk,nqd->nkd", weights, grad_mixed, preferred_element_type=f32)
    wide = weights.astype(f32)
    grad_scores = wide * (grad_weights - jnp.sum(grad_weights * wide, axis=-1, keepdims=True))
    grad_raw = (grad_scores * score_scale).astype(bf16)
    grad_query = jnp.einsum("nqk,nkd->nqd", grad_raw, key, preferred_element_type=f32)
    grad_key = jnp.einsum("nqk,nqd->nkd", grad_raw, query, preferred_element_type=f32)
    grad_query, grad_key = [
        rotate(rows_of(g, 2).reshape(2 * tokens, -1, HD), cosine, -sine_part).reshape(-1, width)
        for g in (grad_query, grad_key)
    ]
    grad_projected = jnp.concatenate([grad_query, grad_key, rows_of(grad_value, 2)], axis=1)
    grad_projected = grad_projected.astype(bf16)
    grad_normed1 = dot(grad_projected, full_qkv.T)
    part_input, gain1_grad, shift1_grad = norm_backward(
        grad_normed1, unit1, inverse1, norm1_gain
    )
    grad_input = grad_middle + stream_sum(part_input)
    grad_qkv = scatter_weight(cut_weight(dot(normed1.T, grad_projected).astype(bf16), 0))

    def join(pair, axis):
        left = jnp.where(side == 0, pair[0], pair[1])
        right = jnp.where(side == 0, pair[1], pair[0])
        return jnp.concatenate([left, right], axis=axis).astype(f32)

    grad_qkv = join([g.reshape(g.shape[0], 3, width) for g in grad_qkv], 2)
    grad_wout, grad_up, grad_down = join(grad_wout, 0), join(grad_up, 1), join(grad_down, 0)
    gain2_grad, shift2_grad = sum_all(jnp.stack([gain2_grad, shift2_grad]), ("dp", "tensor"))
    gain1_grad, shift1_grad = sum_all(jnp.stack([gain1_grad, shift1_grad]), ("dp", "tensor"))
    return (
        output,
        grad_input,
        gain1_grad,
        shift1_grad,
        grad_qkv,
        grad_wout,
        gain2_grad,
        shift2_grad,
        grad_up,
        grad_down,
        bucket_counts,
    )


def flip(i, bit):
    return i + bit - 2 * bit * ((i // bit) % 2)


class Traffic:
    def __init__(self, send_sems, recv_sems):
        self.send_sems, self.recv_sems = send_sems, recv_sems
        self.copies, self.gone, self.come = {}, set(), set()

    def send(self, name, src, dst, device):
        k = len(self.copies)
        copy = pltpu.make_async_remote_copy(
            src_ref=src,
            dst_ref=dst,
            send_sem=self.send_sems.at[k],
            recv_sem=self.recv_sems.at[k],
            device_id=device,
            device_id_type=pl.DeviceIdType.MESH,
        )
        copy.start()
        self.copies[name] = copy

    def wait(self, *names):
        for name in names:
            if name not in self.come:
                self.copies[name].wait_recv()
                self.come.add(name)

    def sent(self, *names):
        for name in names:
            if name not in self.gone:
                self.copies[name].wait_send()
                self.gone.add(name)

    def finish(self):
        self.sent(*self.copies)


class Moves:
    def __init__(self, sems):
        self.sems, self.copies = sems, {}

    def start(self, name, src, dst):
        copy = pltpu.make_async_copy(src, dst, self.sems.at[len(self.copies)])
        copy.start()
        self.copies[name] = [copy, False]

    def wait(self, *names):
        for name in names:
            if not self.copies[name][1]:
                self.copies[name][0].wait()
                self.copies[name][1] = True

    def finish(self):
        self.wait(*self.copies)


class Place:
    def __init__(self):
        self.i, self.t = lax.axis_index("dp"), lax.axis_index("tensor")
        self.side = (self.i // 2 + self.i // 4) % 2
        self.x, self.z = [(flip(self.i, b), self.t) for b in (1, 2)]
        self.far = (self.block(6), self.t)
        self.c, self.y = [(self.i, flip(self.t, b)) for b in (1, 2)]

    def greet(self):
        barrier = pltpu.get_barrier_semaphore()
        partners = (self.x, self.z, self.far, self.c, self.y)
        for device in partners:
            pl.semaphore_signal(
                barrier, inc=1, device_id=device, device_id_type=pl.DeviceIdType.MESH
            )
        pl.semaphore_wait(barrier, len(partners))

    def block(self, m):
        d = self.i
        for bit in (1, 2, 4):
            if m & bit:
                d = flip(d, bit)
        return d

    def stripe(self, m):
        s = self.t
        for bit in (1, 2):
            if m & bit:
                s = flip(s, bit)
        return s


class WeightGather:
    def __init__(self, name, place, traffic, moves, half, slot):
        self.name, self.p, self.tr, self.mv = name, place, traffic, moves
        self.half, self.slot = half, slot

    def own(self):
        self.mv.start(self.name + "0", self.half(self.p.side), self.slot(self.p.i))

    def z(self):
        self.tr.send(self.name + "2", self.half(1 - self.p.side), self.slot(self.p.i), self.p.z)

    def far(self):
        self.tr.send(self.name + "6", self.half(self.p.side), self.slot(self.p.i), self.p.far)

    def x(self):
        self.tr.send(self.name + "1", self.half(self.p.side), self.slot(self.p.i), self.p.x)

    def far_next(self):
        self.tr.wait(self.name + "2")
        block = self.slot(self.p.block(2))
        self.tr.send(self.name + "4", block, block, self.p.far)

    def x_next(self, m):
        self.tr.wait(self.name + str(m))
        block = self.slot(self.p.block(m))
        self.tr.send(self.name + str(m + 1), block, block, self.p.x)

    def take(self, *which):
        for m in which:
            if m == 0:
                self.mv.wait(self.name + "0")
            else:
                self.tr.wait(self.name + str(m))

    def end(self):
        self.take(*range(8))


class ActGather:
    def __init__(self, name, place, traffic, slots):
        self.name, self.p, self.tr, self.slots = name, place, traffic, slots

    def at(self, b, m):
        return self.slots.at[b, self.p.stripe(m)]

    def z(self):
        self.tr.send(self.name + "10", self.at(0, 0), self.slots.at[1, self.p.t], self.p.z)

    def y(self):
        self.tr.send(self.name + "02", self.at(0, 0), self.at(0, 0), self.p.y)

    def c(self):
        self.tr.send(self.name + "01", self.at(0, 0), self.at(0, 0), self.p.c)

    def pass_z(self):
        self.tr.wait(self.name + "10")
        block = self.at(1, 0)
        self.tr.send(self.name + "12", block, block, self.p.y)
        self.tr.send(self.name + "11", block, block, self.p.c)

    def pass_y(self, b):
        self.tr.wait(self.name + str(b) + "2")
        block = self.at(b, 2)
        self.tr.send(self.name + str(b) + "3", block, block, self.p.c)

    def take(self, b):
        for m in range(1 - b, 4):
            self.tr.wait(self.name + str(b) + str(m))


def loop_rows(count, step, body):
    def run(k, carry):
        body(pl.multiple_of(k * step, step))
        return carry

    lax.fori_loop(0, count // step, run, 0)


def wide(value):
    return value.astype(jnp.float32)


def add_blocks(out, left, right, rows):
    def body(r):
        at = pl.ds(r, 64)
        out[at, :] = (wide(left[at, :]) + wide(right[at, :])).astype(out.dtype)

    loop_rows(rows, 64, body)


class ActScatter:
    def __init__(self, name, place, traffic, part, got_c, got_y, got_z):
        self.name, self.p, self.tr = name, place, traffic
        self.part, self.got_c, self.got_y, self.got_z = part, got_c, got_y, got_z
        self.rows = part.shape[2]

    def at(self, b, m):
        return self.part.at[b, self.p.stripe(m)]

    def c(self, b):
        for j, m in ((1, 3), (0, 1)):
            name = self.name + "c" + str(b) + str(j)
            self.tr.send(name, self.at(b, m), self.got_c.at[b, j], self.p.c)

    def add(self, b, m, name, got):
        self.tr.wait(self.name + name)
        add_blocks(self.at(b, m), self.at(b, m), got, self.rows)

    def y(self, b):
        self.add(b, 2, "c" + str(b) + "1", self.got_c.at[b, 1])
        self.tr.send(self.name + "y" + str(b), self.at(b, 2), self.got_y.at[b], self.p.y)

    def own(self, b):
        self.add(b, 0, "c" + str(b) + "0", self.got_c.at[b, 0])

    def z(self):
        self.add(1, 0, "y1", self.got_y.at[1])
        self.tr.send(self.name + "z", self.at(1, 0), self.got_z, self.p.z)

    def home(self):
        self.add(0, 0, "y0", self.got_y.at[0])

    def sent(self):
        for key in ("c11", "c01", "c10", "c00", "y1", "y0", "z"):
            self.tr.sent(self.name + key)

    def end(self, out, base):
        self.tr.wait(self.name + "z")
        own = self.at(0, 0)

        def body(r):
            at = pl.ds(r, 64)
            out[at, :] = base[at, :] + (wide(own[at, :]) + wide(self.got_z[at, :]))

        loop_rows(self.rows, 64, body)


def round_rows(src, dst, rows):
    def body(r):
        at = pl.ds(r, 64)
        dst[at, :] = src[at, :].astype(dst.dtype)

    loop_rows(rows, 64, body)


def dot_f32(left, right):
    return jnp.dot(left, right, preferred_element_type=jnp.float32)


def dot_nt(left, right):
    return lax.dot_general(
        left, right, (((1,), (1,)), ((), ())), preferred_element_type=jnp.float32
    )


def dot_tn(left, right):
    return lax.dot_general(
        left, right, (((0,), (0,)), ((), ())), preferred_element_type=jnp.float32
    )


def center_rows(slots, b, at):
    stripes = slots.shape[1]
    rows = jnp.concatenate([wide(slots[b, s, at, :]) for s in range(stripes)], axis=1)
    center = rows - jnp.mean(rows, axis=1, keepdims=True)
    spread = jnp.mean(center * center, axis=1, keepdims=True)
    return center, lax.rsqrt(spread + epsilon)


def norm_rows(slots, b, gain, shift, out):
    rows = slots.shape[2]

    def body(r):
        center, inverse = center_rows(slots, b, pl.ds(r, 128))
        out[pl.ds(b * rows + r, 128), :] = (center * inverse * gain[...] + shift[...]).astype(
            jnp.bfloat16
        )

    loop_rows(rows, 128, body)


def attend(b, qkv, seg_col, seg_row, head_mask, weights, mixed, scale):
    tokens = seg_row.shape[2]
    heads = qkv.shape[2] // HD
    half = tokens // 2
    start = b * tokens
    for h in range(heads):
        cols = pl.ds(h * HD, HD)
        for part in range(2):
            rows = pl.ds(start + part * half, half)
            reach = half * (part + 1)
            query = qkv[0, rows, cols]
            key = qkv[1, pl.ds(start, reach), cols]
            value = qkv[2, pl.ds(start, reach), cols]
            scores = dot_nt(query, key) * scale
            row_id = lax.broadcasted_iota(jnp.int32, (half, reach), 0) + part * half
            col_id = lax.broadcasted_iota(jnp.int32, (half, reach), 1)
            same = seg_col[rows, :] == seg_row[b, :, pl.ds(0, reach)]
            scores = jnp.where(same & (row_id >= col_id), scores, -1000000000.0)
            scores = jnp.exp(scores - jnp.max(scores, axis=1, keepdims=True))
            total = jnp.sum(scores, axis=1, keepdims=True)
            chosen = (scores / total).astype(jnp.bfloat16)
            weights[b * heads + h, pl.ds(part * half, half), pl.ds(0, reach)] = chosen
            mixed[rows, cols] = (dot_f32(chosen, value) * head_mask[rows, :]).astype(jnp.bfloat16)


def sequences(lengths):
    start = 0
    for s in range(lengths.shape[1]):
        length = lengths[0, s]
        yield s, start, length
        start = start + length


def count_row(lengths, width_bucket, lanes):
    lane = lax.broadcasted_iota(jnp.int32, (1, lanes), 1)
    row = jnp.zeros((1, lanes), jnp.float32)
    for s, _, length in sequences(lengths):
        row = row + jnp.where(lane == width_bucket[0, s], wide(length), 0.0)
    return row


def fill_facts(lengths, head_bucket, width_bucket, place_cosine, place_sine, facts):
    lanes = facts.shape[1]
    row = lax.broadcasted_iota(jnp.int32, (8, lanes), 0)
    lane = lax.broadcasted_iota(jnp.int32, (8, lanes), 1)
    count = lengths.shape[1]
    by_lane = jnp.where((row == 0) & (lane >= count), 1e9, 0.0)
    by_row = jnp.where(row >= count, 1e9, 0.0)
    for s, start, length in sequences(lengths):
        end = wide(start + length)
        here = lane == s
        by_lane = by_lane + jnp.where((row == 0) & here, end, 0.0)
        by_lane = by_lane + jnp.where((row == 2) & here, wide(head_bucket[0, s]), 0.0)
        by_lane = by_lane + jnp.where((row == 3) & here, wide(width_bucket[0, s]), 0.0)
        by_row = by_row + jnp.where(row == s, end, 0.0)
        facts[pl.ds(16 + s, 1), :] = place_cosine[pl.ds(start, 1), :]
        facts[pl.ds(20 + s, 1), :] = place_sine[pl.ds(start, 1), :]
    facts[pl.ds(0, 8), :] = by_lane
    facts[pl.ds(8, 8), :] = by_row


def fill_tables(
    infos, place_cosine, place_sine, t, cosine, sine, head_mask, width_mask, seg_col, seg_row
):
    tokens, lanes = place_cosine.shape
    own = wide(t)
    lane = wide(lax.broadcasted_iota(jnp.int32, (tokens, lanes), 1))
    place = wide(lax.broadcasted_iota(jnp.int32, (tokens, lanes), 0))
    sign = jnp.where(lane < lanes // 2, -1.0, 1.0)
    for b in range(2):
        rows = pl.ds(b * tokens, tokens)

        def row(k, b=b):
            return infos[b, pl.ds(k, 1), :]

        segment = jnp.sum(jnp.where(place >= row(0), 1.0, 0.0), axis=1, keepdims=True)
        seg_col[rows, :] = segment
        chosen = jnp.where(lane == segment, 1.0, 0.0)
        head = jnp.sum(chosen * row(2), axis=1, keepdims=True)
        width = jnp.sum(chosen * row(3), axis=1, keepdims=True)
        head_mask[rows, :] = jnp.where(head >= own, 1.0, 0.0)
        width_mask[rows, :] = jnp.where(width >= own, 1.0, 0.0)
        start_cosine, start_sine = 0.0, 0.0
        for s in range(4):
            here = jnp.where(segment == s, 1.0, 0.0)
            start_cosine = start_cosine + here * row(16 + s)
            start_sine = start_sine + here * row(20 + s)
        at_cosine, at_sine = place_cosine[...], place_sine[...]
        cosine[rows, :] = at_cosine * start_cosine + at_sine * start_sine
        sine[rows, :] = (at_sine * start_cosine - at_cosine * start_sine) * sign
        ends = infos[b, pl.ds(8, 8), pl.ds(0, 1)]
        across = wide(lax.broadcasted_iota(jnp.int32, (8, tokens), 1))
        seg_row[b] = jnp.sum(jnp.where(across >= ends, 1.0, 0.0), axis=0, keepdims=True)


def forward_kernel(
    residual_in,
    cotangent_in,
    gain1,
    shift1,
    gain2,
    shift2,
    lengths,
    head_bucket,
    width_bucket,
    place_cosine_in,
    place_sine_in,
    half_qkv,
    half_out,
    half_up,
    half_down,
    cosine_out,
    sine_out,
    head_mask_out,
    all_qkv,
    all_out,
    all_up,
    stream1,
    stream2,
    stream_c,
    normed1,
    normed2,
    heads_out,
    weights_out,
    mixed_out,
    active_out,
    grad_upper_out,
    part_out,
    middle_out,
    w_qkv,
    w_out,
    w_up,
    w_down,
    rows1,
    rows2,
    rows_c,
    normed,
    qkv,
    weights,
    mixed,
    part,
    got_c,
    got_y,
    got_z,
    upper,
    active,
    grad_active,
    middle,
    infos,
    seg_col,
    seg_row,
    width_mask,
    residual,
    cotangent,
    place_cosine,
    place_sine,
    cosine,
    sine,
    head_mask,
    send_sems,
    recv_sems,
    move_sems,
):
    p = Place()
    tr, mv = Traffic(send_sems, recv_sems), Moves(move_sems)
    tokens = residual.shape[0]
    rows_d = half_qkv.shape[1]
    head_cols = w_out.shape[1]

    def row_slot(ref):
        return lambda d: ref.at[pl.ds(pl.multiple_of(d * rows_d, rows_d), rows_d)]

    def first_slot(ref):
        return lambda d: ref.at[d]

    def at_side(k, cut, size):
        return pl.ds(pl.multiple_of(k * size + cut.start, 128), cut.size)

    hidden = w_up.shape[1]
    parts = [pl.ds(0, hidden // 2), pl.ds(hidden // 2, hidden // 2)]

    def rows_at(d):
        return pl.ds(pl.multiple_of(d * rows_d, rows_d), rows_d)

    def up_gather(name, cut):
        return WeightGather(
            name,
            p,
            tr,
            mv,
            lambda k: half_up.at[:, at_side(k, cut, hidden)],
            lambda d: w_up.at[rows_at(d), cut],
        )

    def down_gather(name, cut):
        return WeightGather(
            name,
            p,
            tr,
            mv,
            lambda k: half_down.at[at_side(k, cut, hidden), :],
            lambda d: w_down.at[d, cut, :],
        )

    heads_cut = pl.ds(0, head_cols)
    q = WeightGather(
        "q",
        p,
        tr,
        mv,
        lambda k: half_qkv.at[:, :, at_side(k, heads_cut, head_cols)],
        lambda d: w_qkv.at[:, rows_at(d), :],
    )
    o = WeightGather(
        "o",
        p,
        tr,
        mv,
        lambda k: half_out.at[at_side(k, heads_cut, head_cols), :],
        lambda d: w_out.at[d],
    )
    u, v = [up_gather(n, cut) for n, cut in zip("uv", parts)]
    d, e = [down_gather(n, cut) for n, cut in zip("de", parts)]
    a1 = ActGather("a", p, tr, rows1)
    a2 = ActGather("b", p, tr, rows2)
    ac = ActGather("c", p, tr, rows_c)
    s1 = ActScatter("s", p, tr, part, got_c, got_y, got_z)

    mv.start("residual", residual_in, residual)
    mv.start("place_cosine", place_cosine_in, place_cosine)
    mv.start("place_sine", place_sine_in, place_sine)
    mv.start("cotangent", cotangent_in, cotangent)
    p.greet()
    for one in (q, o, u, v, d, e):
        one.own()
    blocks = w_out.shape[0]
    stripes = part.shape[1]
    per = blocks // stripes
    started = []

    def project(b):
        def body(r):
            at = pl.ds(b * tokens + r, 512)
            for k in range(3):
                got = dot_f32(normed[at, :], w_qkv[k])
                for h in range(head_cols // HD):
                    cols = pl.ds(h * HD, HD)
                    one = got[:, h * HD : (h + 1) * HD]
                    if k < 2:
                        one = one * cosine[at, :] + pltpu.roll(one, HD // 2, 1) * sine[at, :]
                    qkv[k, at, cols] = one.astype(jnp.bfloat16)

        loop_rows(tokens, 512, body)

    def branch(b):
        at = pl.ds(b * tokens, tokens)

        def body(s, carry):
            for j in range(per):
                got = dot_f32(mixed[at, :], w_out[s * per + j])
                part[b, s, :, pl.ds(j * rows_d, rows_d)] = got.astype(jnp.bfloat16)
            return carry

        lax.fori_loop(0, stripes, body, 0)

    def rise(b, cut):
        def body(r):
            at = pl.ds(b * tokens + r, 512)
            for k in range(cut.size // 256):
                cols = pl.ds(cut.start + k * 256, 256)
                got = dot_f32(normed[at, :], w_up[:, cols])
                got = jnp.maximum(got, 0.0) * width_mask[at, :]
                upper[at, cols] = got.astype(jnp.bfloat16)
                active[at, cols] = (got * got).astype(jnp.bfloat16)

        loop_rows(tokens, 512, body)

    def fall(m):
        place = p.block(m)
        s = place // per
        cols = pl.ds(pl.multiple_of((place % per) * rows_d, rows_d), rows_d)
        first = not started
        started.append(m)

        def body(r):
            b, at = r // tokens, pl.ds(pl.multiple_of(r % tokens, 512), 512)
            rows = pl.ds(r, 512)
            part[b, s, at, cols] = dot_f32(active[rows, :], w_down[place]).astype(jnp.bfloat16)
            got = dot_nt(rows_c[b, s, at, cols], w_down[place])
            grad_active[rows, :] = got if first else grad_active[rows, :] + got

        loop_rows(2 * tokens, 512, body)
        for b in range(2):
            mv.start("part" + str(b) + str(m), part.at[b, s, :, cols], part_out.at[b, s, :, cols])

    def turn(r):
        at = pl.ds(r, 64)
        active[at, :] = (grad_active[at, :] * 2.0 * wide(upper[at, :])).astype(jnp.bfloat16)

    o.z()
    q.far()
    o.x()
    mv.wait("residual")
    round_rows(residual, rows1.at[0, p.t], tokens)
    a1.y()
    q.z()
    o.far_next()
    a1.z()
    e.x()
    q.x()
    mv.wait("place_cosine", "place_sine")
    fill_facts(lengths, head_bucket, width_bucket, place_cosine, place_sine, infos.at[0])
    tr.send("info", infos.at[0], infos.at[1], p.z)
    q.far_next()
    q.x_next(6)
    a1.c()
    v.z()
    a1.pass_y(0)
    o.far()
    o.x_next(2)
    o.x_next(4)
    e.z()
    a1.pass_z()
    q.x_next(2)
    q.x_next(4)
    u.far()
    a1.take(0)
    norm_rows(rows1, 0, gain1, shift1, normed)
    a1.pass_y(1)
    tr.wait("info")
    fill_tables(
        infos, place_cosine, place_sine, p.t, cosine, sine, head_mask, width_mask, seg_col, seg_row
    )
    mv.start("cosine", cosine, cosine_out)
    mv.start("sine", sine, sine_out)
    mv.start("head_mask", head_mask, head_mask_out)
    o.x_next(6)
    a1.take(1)
    norm_rows(rows1, 1, gain1, shift1, normed)
    mv.start("stream1", rows1, stream1)
    mv.start("normed1", normed, normed1)
    u.z()
    v.far()
    q.end()
    project(1)
    attend(
        1, qkv, seg_col, seg_row, head_mask, weights, mixed, HD ** (-0.5)
    )
    o.end()
    branch(1)
    s1.c(1)
    d.z()
    s1.y(1)
    e.x_next(2)
    project(0)
    mv.start("all_qkv", w_qkv, all_qkv)
    attend(
        0, qkv, seg_col, seg_row, head_mask, weights, mixed, HD ** (-0.5)
    )
    mv.start("heads", qkv, heads_out)
    mv.start("weights", weights, weights_out)
    mv.start("mixed", mixed, mixed_out)
    branch(0)
    mv.start("all_out", w_out, all_out)
    u.x()
    d.x()
    v.x_next(2)
    s1.c(0)
    v.far_next()
    s1.own(1)
    u.x_next(6)
    s1.y(0)
    s1.z()
    s1.own(0)
    mv.wait("cotangent")
    round_rows(cotangent, rows_c.at[0, p.t], tokens)
    v.x()
    u.far_next()
    ac.y()
    s1.home()
    s1.end(middle, residual)
    round_rows(middle, rows2.at[0, p.t], tokens)
    mv.start("middle", middle, middle_out)
    v.x_next(4)
    a2.z()
    u.x_next(2)
    v.x_next(6)
    ac.z()
    d.far_next()
    e.far()
    e.far_next()
    ac.c()
    a2.y()
    a2.c()
    a2.pass_y(0)
    u.x_next(4)
    a2.pass_z()
    d.x_next(2)
    ac.pass_y(0)
    d.far()
    a2.take(0)
    mv.wait("normed1")
    norm_rows(rows2, 0, gain2, shift2, normed)
    ac.pass_z()
    a2.pass_y(1)
    d.x_next(4)
    a2.take(1)
    norm_rows(rows2, 1, gain2, shift2, normed)
    mv.start("stream2", rows2, stream2)
    mv.start("normed2", normed, normed2)
    u.end()
    rise(1, parts[0])
    e.x_next(6)
    rise(0, parts[0])
    ac.pass_y(1)
    v.end()
    rise(1, parts[1])
    rise(0, parts[1])
    mv.start("active", active, active_out)
    mv.start("all_up", w_up, all_up)
    e.x_next(4)
    ac.take(0)
    ac.take(1)
    s1.sent()
    d.take(4)
    e.take(4)
    fall(4)
    mv.start("stream_c", rows_c, stream_c)
    d.take(2)
    e.take(2)
    fall(2)
    d.take(0)
    e.take(0)
    fall(0)
    d.x_next(6)
    d.take(6)
    e.take(6)
    fall(6)
    d.take(1)
    e.take(1)
    fall(1)
    d.take(5)
    e.take(5)
    fall(5)
    d.take(3)
    e.take(3)
    fall(3)
    d.take(7)
    e.take(7)
    fall(7)
    mv.wait("active")
    loop_rows(2 * tokens, 64, turn)
    mv.start("grad_upper", active, grad_upper_out)
    tr.finish()
    mv.finish()


def forward_call(arrays, weights):
    bf16, f32 = jnp.bfloat16, jnp.float32
    tokens, columns = arrays[0].shape
    w_qkv, w_out, w_up, w_down = weights
    count, stripes = lax.axis_size("dp"), lax.axis_size("tensor")
    rows_d = w_up.shape[0]
    head_cols = w_out.shape[0] // 2
    hidden = w_up.shape[1] // 2
    width = rows_d * count
    heads = head_cols // HD
    slots = (2, stripes, tokens, columns)
    tables = dict(
        cosine=((2 * tokens, HD), f32),
        sine=((2 * tokens, HD), f32),
        head_mask=((2 * tokens, 1), f32),
    )
    shapes = dict(
        all_qkv=((3, width, head_cols), bf16),
        all_out=((count, head_cols, rows_d), bf16),
        all_up=((width, hidden), bf16),
        stream1=(slots, bf16),
        stream2=(slots, bf16),
        stream_c=(slots, bf16),
        normed1=((2 * tokens, width), bf16),
        normed2=((2 * tokens, width), bf16),
        heads=((3, 2 * tokens, head_cols), bf16),
        weights=((2 * heads, tokens, tokens), bf16),
        mixed=((2 * tokens, head_cols), bf16),
        active=((2 * tokens, hidden), bf16),
        grad_upper=((2 * tokens, hidden), bf16),
        part_out=(slots, bf16),
        middle=((tokens, columns), f32),
    )

    def vmem(name):
        return pltpu.VMEM(*shapes[name])

    scratch = [
        vmem("all_qkv"),
        vmem("all_out"),
        vmem("all_up"),
        pltpu.VMEM((count, hidden, rows_d), bf16),
        vmem("stream1"),
        vmem("stream2"),
        vmem("stream_c"),
        vmem("normed1"),
        vmem("heads"),
        vmem("weights"),
        vmem("mixed"),
        pltpu.VMEM(slots, bf16),
        pltpu.VMEM((2, 2, tokens, columns), bf16),
        pltpu.VMEM((2, tokens, columns), bf16),
        pltpu.VMEM((tokens, columns), bf16),
        vmem("active"),
        vmem("active"),
        pltpu.VMEM((2 * tokens, hidden), f32),
        vmem("middle"),
        pltpu.VMEM((2, 24, 128), f32),
        pltpu.VMEM((2 * tokens, 1), f32),
        pltpu.VMEM((2, 1, tokens), f32),
        pltpu.VMEM((2 * tokens, 1), f32),
        vmem("middle"),
        vmem("middle"),
        pltpu.VMEM((tokens, HD), f32),
        pltpu.VMEM((tokens, HD), f32),
        *[pltpu.VMEM(*s) for s in tables.values()],
        pltpu.SemaphoreType.DMA((72,)),
        pltpu.SemaphoreType.DMA((72,)),
        pltpu.SemaphoreType.DMA((48,)),
    ]
    any_spec = pl.BlockSpec(memory_space=pl.ANY)
    vmem_spec = pl.BlockSpec(memory_space=pltpu.VMEM)
    smem_spec = pl.BlockSpec(memory_space=pltpu.SMEM)
    outs = pl.pallas_call(
        forward_kernel,
        out_shape=[jax.ShapeDtypeStruct(*s) for s in (tables | shapes).values()],
        in_specs=[any_spec] * 2 + [vmem_spec] * 4 + [smem_spec] * 3 + [any_spec] * 6,
        out_specs=[any_spec] * (len(tables) + len(shapes)),
        scratch_shapes=scratch,
        compiler_params=pltpu.CompilerParams(
            collective_id=0, has_side_effects=True, vmem_limit_bytes=62 << 20
        ),
    )(*arrays, *weights)
    split = len(tables)
    return outs[:split], dict(zip(shapes, outs[split:]))


class WeightScatter:
    def __init__(self, name, place, traffic, odd, even, got_x, got_far, out):
        self.name, self.p, self.tr = name, place, traffic
        self.odd, self.even, self.got_x, self.got_far, self.out = odd, even, got_x, got_far, out

    def send_x(self, m):
        self.tr.send(self.name + "x" + str(m), self.odd.at[m // 2], self.got_x.at[m // 2], self.p.x)

    def add_x(self, m):
        k, n = m // 2, self.name
        own = self.even.at[k]
        self.tr.wait(n + "x" + str(m + 1))
        add_blocks(own, own, self.got_x.at[k], own.shape[0])
        if m >= 4:
            self.tr.send(n + "f" + str(m), own, self.got_far.at[3 - k], self.p.far)

    def add_far(self, m):
        k, n = m // 2, self.name
        own = self.even.at[k]
        self.tr.wait(n + "f" + str(6 - m))
        add_blocks(own, own, self.got_far.at[k], own.shape[0])
        if m == 2:
            for j, (cut, spot) in enumerate(self.out(self.p.side)):
                self.tr.send(n + "z" + str(j), own.at[:, cut], spot, self.p.z)

    def end(self, moves):
        for j, (cut, spot) in enumerate(self.out(self.p.side)):
            moves.start(self.name + str(j), self.even.at[0, :, cut], spot)
            self.tr.wait(self.name + "z" + str(j))


class SumAll:
    def __init__(self, name, place, traffic, sums, got):
        self.name, self.tr, self.sums, self.got = name, traffic, sums, got
        self.partners = (place.c, place.y, place.x, place.z, place.far)

    def start(self, k):
        self.tr.send(self.name + str(k), self.sums, self.got.at[k], self.partners[k])

    def step(self, k):
        self.tr.wait(self.name + str(k))
        self.tr.sent(self.name + str(k))
        self.sums[...] += self.got[k]
        if k + 1 < len(self.partners):
            self.start(k + 1)


def norm_back(b, part, slots, gain, total, first):
    stripes, rows, columns = part.shape[1:]
    tile = 64
    fold = (tile // 8, 8, stripes * columns)

    def body(r):
        at = pl.ds(r, tile)
        value = wide(slots[at, :])
        center = value - jnp.mean(value, axis=1, keepdims=True)
        spread = jnp.mean(center * center, axis=1, keepdims=True)
        inverse = lax.rsqrt(spread + epsilon)
        unit = center * inverse
        grad = jnp.concatenate([wide(part[b, s, at, :]) for s in range(stripes)], axis=1)
        scaled = grad * gain[...]
        push = inverse * (
            scaled
            - jnp.mean(scaled, axis=1, keepdims=True)
            - unit * jnp.mean(scaled * unit, axis=1, keepdims=True)
        )
        for s in range(stripes):
            part[b, s, at, :] = push[:, s * columns : (s + 1) * columns].astype(jnp.bfloat16)
        total[0] += jnp.sum((grad * unit).reshape(fold), axis=0)
        total[1] += jnp.sum(grad.reshape(fold), axis=0)

    if first:
        total[...] = jnp.zeros_like(total)
    loop_rows(rows, tile, body)


def attend_back(b, qkv, weights, grad_mixed, cosine, sine, out, tokens, scale):
    width = grad_mixed.shape[1]
    heads = width // HD
    half = tokens // 2
    start = b * tokens

    def turn_back(grad, rows):
        return (grad * cosine[rows, :] - pltpu.roll(grad, HD // 2, 1) * sine[rows, :]).astype(
            jnp.bfloat16
        )

    for h in range(heads):
        spots = [pl.ds(k * width + h * HD, HD) for k in range(3)]
        grad_key, grad_value = None, None
        for part in (1, 0):
            rows = pl.ds(start + part * half, half)
            reach = pl.ds(start, half * (part + 1))
            query, key, value = qkv[rows, spots[0]], qkv[reach, spots[1]], qkv[reach, spots[2]]
            given = grad_mixed[rows, pl.ds(h * HD, HD)]
            chosen = weights[b * heads + h, pl.ds(part * half, half), pl.ds(0, half * (part + 1))]
            grad = dot_nt(given, value)
            soft = wide(chosen)
            grad = soft * (grad - jnp.sum(grad * soft, axis=1, keepdims=True))
            raw = (grad * scale).astype(jnp.bfloat16)
            out[rows, spots[0]] = turn_back(dot_f32(raw, key), rows)
            key_part, value_part = dot_tn(raw, query), dot_tn(chosen, given)
            if part == 1:
                grad_key, grad_value = key_part, value_part
        low, high = pl.ds(start, half), pl.ds(start + half, half)
        out[low, spots[1]] = turn_back(grad_key[:half] + key_part, low)
        out[high, spots[1]] = turn_back(grad_key[half:], high)
        out[low, spots[2]] = (grad_value[:half] + value_part).astype(jnp.bfloat16)
        out[high, spots[2]] = grad_value[half:].astype(jnp.bfloat16)


def backward_kernel(
    cotangent_in,
    gain1,
    gain2,
    cosine_in,
    sine_in,
    head_mask_in,
    lengths,
    width_bucket,
    all_qkv,
    all_out,
    all_up,
    stream1,
    stream2,
    stream_c,
    normed1,
    normed2,
    heads,
    weights_in,
    mixed_in,
    active_in,
    grad_upper_in,
    part_in,
    middle_in,
    output,
    grad_input,
    sums2_out,
    sums1_out,
    grad_qkv,
    grad_out,
    grad_up,
    grad_down,
    w_up,
    w_out,
    rows_a,
    rows_b,
    active,
    grad_upper,
    part_a,
    part_b,
    got_ca,
    got_ya,
    got_za,
    got_cb,
    got_yb,
    got_zb,
    stream_b,
    weights,
    mixed,
    grad_mixed,
    odd,
    even_down,
    even_up,
    odd_out,
    even_out,
    gx_down,
    gf_down,
    gx_up,
    gf_up,
    gx_qkv,
    gf_qkv,
    gx_out,
    gf_out,
    middle,
    grad_middle,
    total,
    sums2,
    got2,
    sums1,
    got1,
    cotangent,
    cosine,
    sine,
    head_mask,
    send_sems,
    recv_sems,
    move_sems,
):
    p = Place()
    tr, mv = Traffic(send_sems, recv_sems), Moves(move_sems)
    tokens, columns = cotangent.shape
    stripes, blocks = part_a.shape[1], all_out.shape[0]
    rows_d = all_out.shape[2]
    per = blocks // stripes
    head_cols = mixed.shape[1]
    bf16 = jnp.bfloat16

    def load_stream(name, src, dst):
        for b in range(2):
            for s in range(stripes):
                spot = dst.at[pl.ds(b * tokens, tokens), pl.ds(s * columns, columns)]
                mv.start(name + str(b) + str(s), src.at[b, s], spot)

    def wait_stream(name):
        mv.wait(*[name + str(b) + str(s) for b in range(2) for s in range(stripes)])

    s_out = ActScatter("s", p, tr, part_a, got_ca, got_ya, got_za)
    half = tokens // 2
    halves = [pl.ds(0, half), pl.ds(half, half)]

    def half_scatter(name, cut):
        views = part_b.at[:, :, cut], got_cb.at[:, :, cut], got_yb.at[:, cut], got_zb.at[cut]
        return ActScatter(name, p, tr, *views)

    s2a, s2b = [half_scatter(n, cut) for n, cut in zip("tT", halves)]
    s1a, s1b = [half_scatter(n, cut) for n, cut in zip("rR", halves)]
    aba, abb = [ActGather(n, p, tr, stream_b.at[:, :, cut]) for n, cut in zip("bB", halves)]
    begun = set()
    qkv_cols = pl.ds(0, 3 * head_cols)

    def back(layer, b, h, slots, gain):
        rows = pl.ds(b * tokens + h * half, half)
        first = layer not in begun
        begun.add(layer)
        norm_back(b, part_b.at[:, :, halves[h]], slots.at[rows], gain, total, first)

    hidden = active.shape[1]
    parts = [pl.ds(0, hidden // 2), pl.ds(hidden // 2, hidden // 2)]

    def at_side(k, cut, size):
        return pl.ds(pl.multiple_of(k * size + cut.start, 128), cut.size)

    def scatter(name, odd, even, got_x, got_far, out, cols):
        views = [ref.at[:, :, cols] for ref in (odd, even, got_x, got_far)]

        def spots(k):
            if len(out.shape) == 3:
                return [
                    (pl.ds(j * head_cols, head_cols), out.at[j, :, at_side(k, heads_cut, head_cols)])
                    for j in range(3)
                ]
            spot = out.at[:, at_side(k, cols, out.shape[1] // 2)]
            return [(pl.ds(0, cols.size), spot)]

        return WeightScatter(name, p, tr, *views, spots)

    heads_cut = pl.ds(0, head_cols)

    d, e = [
        scatter(n, odd, even_down, gx_down, gf_down, grad_down, cut) for n, cut in zip("de", parts)
    ]
    u, v = [scatter(n, odd, even_up, gx_up, gf_up, grad_up, cut) for n, cut in zip("uv", parts)]
    q = scatter("q", odd, even_down, gx_qkv, gf_qkv, grad_qkv, qkv_cols)
    o = scatter("o", odd_out, even_out, gx_out, gf_out, grad_out, pl.ds(0, head_cols))
    all2 = SumAll("2", p, tr, sums2, got2)
    all1 = SumAll("1", p, tr, sums1, got1)

    per = blocks // stripes

    def load_cotangent(j):
        stripe = p.block(5) // per
        for bit in (1, 2):
            if j & bit:
                stripe = flip(stripe, bit)
        cols = pl.ds(pl.multiple_of(stripe * columns, columns), columns)
        for b in range(2):
            spot = rows_a.at[pl.ds(b * tokens, tokens), cols]
            mv.start("c" + str(b) + str(j), stream_c.at[b, stripe], spot)

    load_cotangent(0)
    mv.start("active0", active_in.at[:, parts[0]], active.at[:, parts[0]])
    mv.start("active1", active_in.at[:, parts[1]], active.at[:, parts[1]])
    p.greet()
    for j in range(1, stripes):
        load_cotangent(j)
    mv.start("grad_upper", grad_upper_in, grad_upper)
    mv.start("all_up", all_up, w_up)
    load_stream("x2", stream2, rows_b)

    def load_rest():
        for k in range(blocks):
            mv.start("p" + str(k), all_out.at[k], w_out.at[:, pl.ds(k * rows_d, rows_d)])
        mv.start("cotangent", cotangent_in, cotangent)
        mv.start("head_mask", head_mask_in, head_mask)
        mv.start("cosine", cosine_in, cosine)
        mv.start("sine", sine_in, sine)
        mv.start("mixed", mixed_in, mixed)
        mv.start("weights", weights_in, weights)
        mv.start("part", part_in, part_a)
        mv.start("middle", middle_in, middle)

    def block_cols(m):
        return pl.ds(pl.multiple_of(p.block(m) * rows_d, rows_d), rows_d)

    def grad_block(left, right, m, spot, cols=None):
        value = right[...] if cols is None else right[:, cols]
        spot[...] = dot_tn(left[:, block_cols(m)], value).astype(bf16)

    def down_block(m, spot):
        grad_block(rows_a, active, m, spot)

    def product(b, left, right, cols):
        at = pl.ds(b * tokens, tokens)

        def body(s, carry):
            rows = pl.ds(pl.multiple_of(s * columns, columns), columns)
            part_b[b, s] = dot_nt(left[at, cols], right[rows, cols]).astype(bf16)
            return carry

        lax.fori_loop(0, stripes, body, 0)

    def gather_total(sums):
        depth, lanes = 8, total.shape[2] // 8
        sums[...] = jnp.zeros_like(sums)
        for k in range(2):
            row = jnp.sum(total[k], axis=0, keepdims=True)
            for r in range(depth):
                sums[pl.ds(r, 1), pl.ds(k * lanes, lanes)] = row[:, r * lanes : (r + 1) * lanes]
        sums[pl.ds(0, 1), pl.ds(2 * lanes, HD)] = count_row(lengths, width_bucket, HD)

    def unpack(sums, out):
        depth, lanes = 8, total.shape[2] // 8
        for k in range(2):
            for r in range(depth):
                spot = sums[pl.ds(r, 1), pl.ds(k * lanes, lanes)]
                out[pl.ds(k, 1), pl.ds(r * lanes, lanes)] = spot
        out[pl.ds(2, 1), pl.ds(0, HD)] = sums[pl.ds(0, 1), pl.ds(2 * lanes, HD)]

    def up_block(m, spot):
        grad_block(rows_a, grad_upper, m, spot)

    def up_odd(m):
        tr.sent("dx" + str(m), "ex" + str(m))
        up_block(m, odd.at[m // 2])
        u.send_x(m)
        v.send_x(m)

    def mix(b):
        mv.wait("head_mask", *["p" + str(k) for k in range(blocks)])
        at = pl.ds(b * tokens, tokens)
        got = None
        for s in range(stripes):
            one = dot_nt(stream_b[b, s], w_out[:, pl.ds(s * columns, columns)])
            got = one if got is None else got + one
        grad_mixed[at, :] = (got * head_mask[at, :]).astype(bf16)

    def out_block(m, spot):
        mv.wait("mixed")
        place = p.block(m)
        cols = pl.ds(pl.multiple_of((place % per) * rows_d, rows_d), rows_d)
        near = dot_tn(stream_b[0, place // per, :, cols], mixed[pl.ds(0, tokens), :])
        away = dot_tn(stream_b[1, place // per, :, cols], mixed[pl.ds(tokens, tokens), :])
        spot[...] = (near + away).astype(bf16)

    def qkv_block(m, spot):
        mv.wait("normed1")
        grad_block(rows_b, grad_upper, m, spot, qkv_cols)

    def qkv_odd(m):
        tr.sent("ux" + str(m), "vx" + str(m))
        qkv_block(m, odd.at[m // 2, :, qkv_cols])
        q.send_x(m)

    def qkv_even(m):
        mv.wait("d0", "e0")
        tr.sent("df4", "df6", "dz0", "ef4", "ef6", "ez0")
        qkv_block(m, even_down.at[m // 2, :, qkv_cols])

    mv.wait("c00", "c10", "active0", "active1")
    down_block(5, odd.at[2])
    d.send_x(5)
    e.send_x(5)
    wait_stream("c")
    down_block(4, even_down.at[2])
    mv.wait("grad_upper", "all_up")
    product(1, grad_upper, w_up, pl.ds(0, w_up.shape[1]))
    wait_stream("x2")
    back(2, 1, 1, rows_b, gain2)
    d.add_x(4)
    s2b.c(1)
    back(2, 1, 0, rows_b, gain2)
    load_rest()
    down_block(7, odd.at[3])
    d.send_x(7)
    e.send_x(7)
    s2b.y(1)
    down_block(6, even_down.at[3])
    down_block(3, odd.at[1])
    d.send_x(3)
    e.send_x(3)
    s2a.c(1)
    s2b.own(1)
    e.add_x(4)
    product(0, grad_upper, w_up, pl.ds(0, w_up.shape[1]))
    d.add_x(6)
    s2a.y(1)
    mv.wait("part")
    down_block(2, even_down.at[1])
    back(2, 0, 1, rows_b, gain2)
    s_out.c(0)
    down_block(0, even_down.at[0])
    s2b.c(0)
    s2b.z()
    s2a.own(1)
    back(2, 0, 0, rows_b, gain2)
    down_block(1, odd.at[0])
    d.send_x(1)
    e.send_x(1)
    for k in range(3):
        mv.start("h" + str(k), heads.at[k], active.at[:, pl.ds(k * head_cols, head_cols)])
    mv.start("normed2", normed2, rows_a)
    s2a.c(0)
    mv.wait("normed2")
    e.add_x(6)
    s2b.y(0)
    s2b.own(0)
    s2a.z()
    gather_total(sums2)
    all2.start(0)
    s2b.home()
    s2a.own(0)
    d.add_x(2)
    up_block(4, even_up.at[2])
    s_out.c(1)
    mv.wait("cotangent")
    s2b.end(grad_middle.at[halves[1]], cotangent.at[halves[1]])
    round_rows(grad_middle.at[halves[1]], stream_b.at[0, p.t, halves[1]], tokens // 2)
    up_odd(5)
    s2a.y(0)
    up_block(6, even_up.at[3])
    abb.z()
    abb.y()
    up_block(2, even_up.at[1])
    d.add_x(0)
    up_odd(7)
    s_out.own(0)
    s2a.home()
    e.add_x(2)
    s2a.end(grad_middle.at[halves[0]], cotangent.at[halves[0]])
    round_rows(grad_middle.at[halves[0]], stream_b.at[0, p.t, halves[0]], tokens // 2)
    aba.z()
    aba.y()
    abb.pass_z()
    e.add_far(2)
    aba.pass_z()
    up_odd(3)
    abb.c()
    abb.pass_y(0)
    aba.pass_y(0)
    d.add_far(2)
    aba.c()
    e.add_x(0)
    u.add_x(4)
    aba.take(0)
    abb.take(0)
    mix(0)
    s_out.own(1)
    aba.pass_y(1)
    abb.pass_y(1)
    v.add_x(4)
    up_block(0, even_up.at[0])
    up_odd(1)
    aba.take(1)
    abb.take(1)
    out_block(4, even_out.at[2])
    s_out.y(1)
    mix(1)
    out_block(5, odd_out.at[2])
    o.send_x(5)
    out_block(2, even_out.at[1])
    v.add_x(6)
    mv.wait("cosine", "sine", "weights", "h0", "h1", "h2")
    attend_back(
        1, active, weights, grad_mixed, cosine, sine, grad_upper, tokens, HD ** (-0.5)
    )
    out_block(7, odd_out.at[3])
    o.send_x(7)
    out_block(0, even_out.at[0])
    out_block(6, even_out.at[3])
    u.add_x(6)
    attend_back(
        0, active, weights, grad_mixed, cosine, sine, grad_upper, tokens, HD ** (-0.5)
    )
    all2.step(0)
    for k in range(3):
        mv.start("w" + str(k), all_qkv.at[k], w_up.at[:, pl.ds(k * head_cols, head_cols)])
    mv.start("normed1", normed1, rows_b)
    d.add_far(0)
    s2a.sent()
    s2b.sent()
    mv.wait("w0", "w1", "w2")
    product(0, grad_upper, w_up, qkv_cols)
    out_block(3, odd_out.at[1])
    o.send_x(3)
    s_out.z()
    product(1, grad_upper, w_up, qkv_cols)
    u.add_x(0)
    u.add_x(2)
    v.add_x(2)
    load_stream("x1", stream1, rows_a)
    u.add_far(2)
    all2.step(1)
    s_out.y(0)
    wait_stream("x1")
    back(1, 0, 1, rows_a, gain1)
    e.add_far(0)
    back(1, 1, 0, rows_a, gain1)
    back(1, 1, 1, rows_a, gain1)
    back(1, 0, 0, rows_a, gain1)
    o.add_x(4)
    o.add_x(6)
    qkv_odd(5)
    o.add_x(2)
    e.end(mv)
    out_block(1, odd_out.at[0])
    o.send_x(1)
    s1a.c(1)
    d.end(mv)
    s1b.c(1)
    s1a.c(0)
    s1b.c(0)
    gather_total(sums1)
    all1.start(0)
    all1.step(0)
    qkv_odd(7)
    v.add_x(0)
    s1a.own(1)
    all2.step(2)
    qkv_even(4)
    s1a.y(1)
    qkv_even(2)
    v.add_far(2)
    s1b.y(1)
    s1a.own(0)
    qkv_odd(3)
    all1.step(1)
    q.add_x(4)
    qkv_odd(1)
    o.add_far(2)
    s1b.own(1)
    o.add_x(0)
    s_out.home()
    s1a.z()
    all2.step(3)
    o.add_far(0)
    qkv_even(0)
    qkv_even(6)
    q.add_x(6)
    all1.step(2)
    s1a.y(0)
    u.add_far(0)
    s1b.y(0)
    s1a.home()
    s1a.end(grad_middle.at[halves[0]], grad_middle.at[halves[0]])
    s1b.z()
    q.add_x(0)
    u.end(mv)
    v.add_far(0)
    v.end(mv)
    q.add_x(2)
    o.end(mv)
    s1b.own(0)
    s1b.home()
    mv.wait("middle")
    s_out.end(middle, middle)
    mv.start("output", middle, output)
    all1.step(3)
    q.add_far(2)
    all2.step(4)
    q.add_far(0)
    s1b.end(grad_middle.at[halves[1]], grad_middle.at[halves[1]])
    mv.start("grad_input", grad_middle, grad_input)
    all1.step(4)
    q.end(mv)
    unpack(sums2, sums2_out)
    unpack(sums1, sums1_out)
    tr.finish()
    mv.finish()


def backward_call(arrays, saved):
    bf16, f32 = jnp.bfloat16, jnp.float32
    tokens, columns = arrays[0].shape
    count, stripes = lax.axis_size("dp"), lax.axis_size("tensor")
    _, head_cols, rows_d = saved["all_out"].shape
    width, hidden = saved["all_up"].shape
    slots = (2, stripes, tokens, columns)
    wide_rows = (2 * tokens, width)

    def vmem(*shape, dtype=bf16):
        return pltpu.VMEM(shape, dtype)

    def got(cols):
        return [vmem(4, rows_d, cols), vmem(2, rows_d, cols)]

    got_act = [vmem(2, 2, tokens, columns), vmem(2, tokens, columns), vmem(tokens, columns)]
    packed = 2 * width // 8 + HD
    sums = [vmem(8, packed, dtype=f32), vmem(5, 8, packed, dtype=f32)]
    qkv = 3 * head_cols
    scratch = [
        vmem(width, hidden),
        vmem(head_cols, width),
        vmem(*wide_rows),
        vmem(*wide_rows),
        vmem(2 * tokens, hidden),
        vmem(2 * tokens, hidden),
        vmem(*slots),
        vmem(*slots),
        *got_act,
        *got_act,
        vmem(*slots),
        vmem(*saved["weights"].shape),
        vmem(2 * tokens, head_cols),
        vmem(2 * tokens, head_cols),
        vmem(4, rows_d, hidden),
        vmem(4, rows_d, hidden),
        vmem(4, rows_d, hidden),
        vmem(4, rows_d, head_cols),
        vmem(4, rows_d, head_cols),
        *got(hidden),
        *got(hidden),
        *got(qkv),
        *got(head_cols),
        vmem(tokens, columns, dtype=f32),
        vmem(tokens, columns, dtype=f32),
        vmem(2, 8, width, dtype=f32),
        *sums,
        *sums,
        *[vmem(*arrays[k].shape, dtype=f32) for k in (0, 3, 4, 5)],
        pltpu.SemaphoreType.DMA((112,)),
        pltpu.SemaphoreType.DMA((112,)),
        pltpu.SemaphoreType.DMA((80,)),
    ]
    any_spec = pl.BlockSpec(memory_space=pl.ANY)
    vmem_spec = pl.BlockSpec(memory_space=pltpu.VMEM)
    smem_spec = pl.BlockSpec(memory_space=pltpu.SMEM)
    shapes = [
        ((tokens, columns), f32),
        ((tokens, columns), f32),
        ((8, width), f32),
        ((8, width), f32),
        ((3, rows_d, 2 * head_cols), bf16),
        ((rows_d, 2 * head_cols), bf16),
        ((rows_d, 2 * hidden), bf16),
        ((rows_d, 2 * hidden), bf16),
    ]
    names = [k for k in saved]
    return pl.pallas_call(
        backward_kernel,
        out_shape=[jax.ShapeDtypeStruct(*s) for s in shapes],
        in_specs=[any_spec, vmem_spec, vmem_spec] + [any_spec] * 3
        + [smem_spec] * 2
        + [any_spec] * len(names),
        out_specs=[any_spec] * 2 + [vmem_spec] * 2 + [any_spec] * 4,
        scratch_shapes=scratch,
        compiler_params=pltpu.CompilerParams(
            collective_id=1, has_side_effects=True, vmem_limit_bytes=63 << 20
        ),
    )(*arrays, *[saved[n] for n in names])


def finish_kernel(groups, *refs):
    ins, sums, outs, small = refs[:6], refs[6:8], refs[8:14], refs[14:19]
    raw, done, sems = refs[19:25], refs[25:29], refs[29]
    loads = [pltpu.make_async_copy(ins[k], raw[k], sems.at[k]) for k in range(6)]
    for load in loads:
        load.start()
    for k in range(4):
        small[k][...] = sums[k // 2][pl.ds(k % 2, 1), :]
    count = small[4].shape[1]
    small[4][...] = (sums[1][pl.ds(2, 1), pl.ds(0, count)] / groups).astype(jnp.int32)
    stores = []

    def store(k, src):
        stores.append(pltpu.make_async_copy(src, outs[k], sems.at[6 + k]))
        stores[-1].start()

    loads[0].wait()
    rows, columns = raw[0].shape

    def widen(r):
        done[0][pl.ds(r, 32), :] = wide(raw[0][pl.ds(r, 32), :])

    loop_rows(rows, 32, widen)
    store(0, done[0])
    loads[1].wait()

    def turn(src, dst):
        def body(c):
            dst[pl.ds(c, 256), :] = wide(src[:, pl.ds(c, 256)]).T

        loop_rows(src.shape[1], 256, body)

    turn(raw[1], done[1])
    store(1, done[1])
    loads[2].wait()
    for k in range(raw[2].shape[0]):

        def widen_part(r, k=k):
            done[2][k, pl.ds(r, 64), :] = wide(raw[2][k, pl.ds(r, 64), :])

        loop_rows(raw[2].shape[1], 64, widen_part)
    store(2, done[2])
    loads[3].wait()
    turn(raw[3], done[3])
    store(3, done[3])
    for k in (4, 5):
        loads[k].wait()
        store(k, raw[k])
    for one in stores:
        one.wait()


def finish_call(grad_up, grad_down, grad_qkv, grad_out, output, grad_input, sums1, sums2):
    f32 = jnp.float32
    ins = (grad_up, grad_down, grad_qkv, grad_out, output, grad_input)
    shapes = [a.shape for a in ins]
    shapes[1], shapes[3] = shapes[1][::-1], shapes[3][::-1]
    any_spec = pl.BlockSpec(memory_space=pl.ANY)
    vmem_spec = pl.BlockSpec(memory_space=pltpu.VMEM)
    groups = lax.axis_size("tensor")
    return pl.pallas_call(
        functools.partial(finish_kernel, groups),
        out_shape=[jax.ShapeDtypeStruct(s, f32) for s in shapes]
        + [jax.ShapeDtypeStruct((1, sums1.shape[1]), f32)] * 4
        + [jax.ShapeDtypeStruct((1, groups), jnp.int32)],
        in_specs=[any_spec] * 6 + [vmem_spec] * 2,
        out_specs=[any_spec] * 6 + [vmem_spec] * 5,
        scratch_shapes=[pltpu.VMEM(a.shape, a.dtype) for a in ins]
        + [pltpu.VMEM(s, f32) for s in shapes[:4]]
        + [pltpu.SemaphoreType.DMA((12,))],
        compiler_params=pltpu.CompilerParams(vmem_limit_bytes=62 << 20),
    )(*ins, sums1, sums2)


def local_fast(
    residual_in,
    lengths,
    head_bucket,
    width_bucket,
    norm1_gain,
    norm1_shift,
    w_qkv,
    w_out,
    norm2_gain,
    norm2_shift,
    w_up,
    w_down,
    cotangent,
):
    f32 = jnp.float32
    tokens = residual_in.shape[0]
    steps = np.arange(tokens)[:, None] * 10000.0 ** (-2.0 * (np.arange(HD) % (HD // 2)) / HD)
    arrays = (
        residual_in,
        cotangent,
        norm1_gain[None],
        norm1_shift[None],
        norm2_gain[None],
        norm2_shift[None],
        lengths,
        head_bucket,
        width_bucket,
        jnp.asarray(np.cos(steps), f32),
        jnp.asarray(np.sin(steps), f32),
    )
    weights = (jnp.swapaxes(w_qkv, 0, 1), w_out, w_up, w_down)
    (cosine, sine, head_mask), saved = forward_call(arrays, weights)
    arrays = (cotangent, norm1_gain[None], norm2_gain[None], cosine, sine, head_mask)
    output, grad_input, sums2, sums1, grad_qkv, grad_out, grad_up, grad_down = backward_call(
        (*arrays, lengths, width_bucket), saved
    )
    grad_up, grad_down, grad_qkv, grad_out, output, grad_input, *small = finish_call(
        grad_up, grad_down, grad_qkv, grad_out, output, grad_input, sums1, sums2
    )
    gain1_grad, shift1_grad, gain2_grad, shift2_grad, bucket_counts = [one[0] for one in small]
    return (
        output,
        grad_input,
        gain1_grad,
        shift1_grad,
        jnp.swapaxes(grad_qkv, 0, 1),
        grad_out,
        gain2_grad,
        shift2_grad,
        grad_up,
        grad_down,
        bucket_counts,
    )


def local(*args):
    w_out = args[7]
    if lax.axis_size("dp") == 8 and lax.axis_size("tensor") == 4 and w_out.shape[1] % 128 == 0:
        return local_fast(*args)
    return local_general(*args)


def solution(mesh):
    placed = (
        P("dp", "tensor"),
        P("dp", None),
        P("dp", None),
        P("dp", None),
        P(),
        P(),
        P("dp", None, "tensor"),
        P("tensor", "dp"),
        P(),
        P(),
        P("dp", "tensor"),
        P("tensor", "dp"),
        P("dp", "tensor"),
    )
    return jax.shard_map(
        local,
        mesh=mesh,
        in_specs=placed,
        out_specs=(
            P("dp", "tensor"),
            P("dp", "tensor"),
            P(),
            P(),
            P("dp", None, "tensor"),
            P("tensor", "dp"),
            P(),
            P(),
            P("dp", "tensor"),
            P("tensor", "dp"),
            P(),
        ),
        check_vma=False,
    )
```

```python
import functools
import math

import jax
import jax.numpy as jnp
import numpy as np
from jax import lax
from jax.experimental import pallas as pl
from jax.experimental.pallas import tpu as pltpu
from jax.sharding import PartitionSpec as P

HD = 128
HIDDEN_BIT = 2

epsilon = 1e-05


def dp_swap(value, bit):
    count = lax.axis_size("dp")
    return lax.ppermute(value, "dp", [(i, i ^ bit) for i in range(count)])


def tensor_swap(value, bit):
    count = lax.axis_size("tensor")
    return lax.ppermute(value, "tensor", [(i, i ^ bit) for i in range(count)])


def bits_of(count):
    return [1 << i for i in range(count.bit_length() - 1)]


def replica_bits():
    bits = bits_of(lax.axis_size("dp"))
    return [b for b in bits if b > HIDDEN_BIT] + [b for b in bits if b < HIDDEN_BIT]


def gather_weight(mine, other):
    blocks = {0: mine, HIDDEN_BIT: dp_swap(other, HIDDEN_BIT)}
    for bit in replica_bits():
        blocks.update({m | bit: dp_swap(blocks[m], bit) for m in list(blocks)})
    return blocks


def add_low(left, right):
    return (left.astype(jnp.float32) + right.astype(jnp.float32)).astype(jnp.bfloat16)


def scatter_weight(blocks):
    for bit in reversed(replica_bits()):
        arrived = {m ^ bit: dp_swap(blocks[m], bit) for m in blocks if m & bit}
        blocks = {m: add_low(blocks[m], arrived[m]) for m in arrived}
    return blocks[0], dp_swap(blocks[HIDDEN_BIT], HIDDEN_BIT)


def gather_act(rows):
    blocks = {(0, 0): rows, (1, 0): dp_swap(rows, HIDDEN_BIT)}
    for bit in reversed(bits_of(lax.axis_size("tensor"))):
        blocks.update({(b, m | bit): tensor_swap(v, bit) for (b, m), v in list(blocks.items())})
    return blocks


def scatter_act(blocks):
    for bit in bits_of(lax.axis_size("tensor")):
        arrived = {(b, m ^ bit): tensor_swap(v, bit) for (b, m), v in blocks.items() if m & bit}
        blocks = {k: add_low(blocks[k], arrived[k]) for k in arrived}
    return blocks[(0, 0)].astype(jnp.float32) + dp_swap(blocks[(1, 0)], HIDDEN_BIT).astype(
        jnp.float32
    )


def lay(blocks, shape, spots):
    count = len(blocks)

    def kernel(*refs):
        ins, out, sems = refs[:count], refs[count], refs[count + 1]
        copies = []
        for i, spot in enumerate(spots()):
            r, c = blocks[i].shape
            copies.append(
                pltpu.make_async_copy(
                    ins[i],
                    out.at[pl.ds(pl.multiple_of(spot[0], 16), r), pl.ds(pl.multiple_of(spot[1], 128), c)],
                    sems.at[i],
                )
            )
        for copy in copies:
            copy.start()
        for copy in copies:
            copy.wait()

    return pl.pallas_call(
        kernel,
        out_shape=jax.ShapeDtypeStruct(shape, jnp.bfloat16),
        in_specs=[pl.BlockSpec(memory_space=pl.ANY)] * count,
        out_specs=pl.BlockSpec(memory_space=pltpu.VMEM),
        scratch_shapes=[pltpu.SemaphoreType.DMA((count,))],
        compiler_params=pltpu.CompilerParams(vmem_limit_bytes=24 << 20),
    )(*blocks)


def cut(whole, block_shape, count, spots):
    def kernel(*refs):
        src, outs, sems = refs[0], refs[1 : 1 + count], refs[1 + count]
        r, c = block_shape
        copies = []
        for i, spot in enumerate(spots()):
            copies.append(
                pltpu.make_async_copy(
                    src.at[pl.ds(pl.multiple_of(spot[0], 16), r), pl.ds(pl.multiple_of(spot[1], 128), c)],
                    outs[i],
                    sems.at[i],
                )
            )
        for copy in copies:
            copy.start()
        for copy in copies:
            copy.wait()

    return pl.pallas_call(
        kernel,
        out_shape=[jax.ShapeDtypeStruct(block_shape, jnp.bfloat16)] * count,
        in_specs=[pl.BlockSpec(memory_space=pltpu.VMEM)],
        out_specs=[pl.BlockSpec(memory_space=pl.ANY)] * count,
        scratch_shapes=[pltpu.SemaphoreType.DMA((count,))],
        compiler_params=pltpu.CompilerParams(vmem_limit_bytes=24 << 20),
    )(whole)


def lay_weight(blocks, axis):
    count = len(blocks)
    r, c = blocks[0].shape
    if axis == 1 and c % 128:
        order = jnp.bitwise_xor(lax.axis_index("dp"), jnp.arange(count))
        stacked = jnp.stack([blocks[m] for m in range(count)])[order]
        return jnp.swapaxes(stacked, 0, 1).reshape(r, count * c)

    def spots():
        place = lax.axis_index("dp")
        at = [jnp.bitwise_xor(place, m) for m in range(count)]
        return [(d * r, 0) if axis == 0 else (0, d * c) for d in at]

    shape = (r * count, c) if axis == 0 else (r, c * count)
    return lay([blocks[m] for m in range(count)], shape, spots)


def cut_weight(whole, axis):
    count = lax.axis_size("dp")
    r, c = whole.shape
    r, c = (r // count, c) if axis == 0 else (r, c // count)
    if axis == 1 and c % 128:
        order = jnp.bitwise_xor(lax.axis_index("dp"), jnp.arange(count))
        stacked = jnp.swapaxes(whole.reshape(r, count, c), 0, 1)[order]
        return {m: stacked[m] for m in range(count)}

    def spots():
        place = lax.axis_index("dp")
        at = [jnp.bitwise_xor(place, m) for m in range(count)]
        return [(d * r, 0) if axis == 0 else (0, d * c) for d in at]

    return dict(enumerate(cut(whole, (r, c), count, spots)))


def act_keys():
    return [(b, m) for b in range(2) for m in range(lax.axis_size("tensor"))]


def act_spots(r, c):
    place = lax.axis_index("tensor")
    return [(b * r, jnp.bitwise_xor(place, m) * c) for b, m in act_keys()]


def lay_act(blocks):
    r, c = blocks[(0, 0)].shape
    shape = (2 * r, c * lax.axis_size("tensor"))
    return lay([blocks[k] for k in act_keys()], shape, lambda: act_spots(r, c))


def cut_act(whole):
    r, c = whole.shape[0] // 2, whole.shape[1] // lax.axis_size("tensor")
    keys = act_keys()
    return dict(zip(keys, cut(whole, (r, c), len(keys), lambda: act_spots(r, c))))


def whole_stream(rows):
    return lay_act(gather_act(rows.astype(jnp.bfloat16)))


def stream_sum(rows):
    return scatter_act(cut_act(rows.astype(jnp.bfloat16)))


def sum_all(value, axes):
    if "dp" in axes:
        for bit in bits_of(lax.axis_size("dp")):
            value = value + dp_swap(value, bit)
    if "tensor" in axes:
        for bit in bits_of(lax.axis_size("tensor")):
            value = value + tensor_swap(value, bit)
    return value


def token_info(length_row, head_row, width_row, row_count):
    seq_ends = jnp.cumsum(length_row)
    seq_starts = seq_ends - length_row
    places = jnp.arange(row_count, dtype=jnp.int32)
    segment = jnp.sum((places[:, None] >= seq_ends[None, :]).astype(jnp.int32), axis=1)
    labels = jnp.arange(length_row.shape[0], dtype=jnp.int32)
    onehot = (segment[:, None] == labels[None, :]).astype(jnp.int32)
    offset = places - jnp.sum(onehot * seq_starts[None, :], axis=1)
    head_tok = jnp.sum(onehot * head_row[None, :], axis=1)
    width_tok = jnp.sum(onehot * width_row[None, :], axis=1)
    return (segment, offset, head_tok, width_tok)


def rotary_tables(offset, head_size):
    half_size = head_size // 2
    ladder = jnp.arange(half_size, dtype=jnp.float32)
    inverse = jnp.exp(ladder * (-2.0 * math.log(10000.0) / head_size))
    angles = offset.astype(jnp.float32)[:, None] * inverse[None, :]
    return (jnp.cos(angles)[:, None, :], jnp.sin(angles)[:, None, :])


def rotate(values, cosine, sine_part):
    half_size = values.shape[-1] // 2
    front_half = values[..., :half_size]
    back_half = values[..., half_size:]
    return jnp.concatenate(
        [front_half * cosine - back_half * sine_part, back_half * cosine + front_half * sine_part],
        axis=-1,
    )


def norm_forward(values, norm_gain, norm_shift):
    values = values.astype(jnp.float32)
    center = values - jnp.mean(values, axis=-1, keepdims=True)
    spread = jnp.mean(center * center, axis=-1, keepdims=True)
    inverse = lax.rsqrt(spread + epsilon)
    unit_rows = center * inverse
    return (unit_rows * norm_gain + norm_shift, unit_rows, inverse)


def norm_backward(grad_rows, unit_rows, inverse, norm_gain):
    scaled = grad_rows * norm_gain
    grad_in = inverse * (
        scaled
        - jnp.mean(scaled, axis=-1, keepdims=True)
        - unit_rows * jnp.mean(scaled * unit_rows, axis=-1, keepdims=True)
    )
    return (grad_in, jnp.sum(grad_rows * unit_rows, axis=0), jnp.sum(grad_rows, axis=0))


def heads_of(rows, blocks):
    rows = rows.reshape(blocks, rows.shape[0] // blocks, -1, HD)
    return jnp.transpose(rows, (2, 0, 1, 3)).reshape(-1, rows.shape[1], HD)


def rows_of(heads, blocks):
    heads = heads.reshape(-1, blocks, heads.shape[1], HD)
    return jnp.transpose(heads, (1, 2, 0, 3)).reshape(blocks * heads.shape[2], -1)


def local_general(
    residual_in,
    lengths,
    head_bucket,
    width_bucket,
    norm1_gain,
    norm1_shift,
    w_qkv,
    w_out,
    norm2_gain,
    norm2_shift,
    w_up,
    w_down,
    cotangent,
):
    f32, bf16 = jnp.float32, jnp.bfloat16
    dot = functools.partial(jnp.dot, preferred_element_type=f32)
    tensor_index = lax.axis_index("tensor")
    bucket_total = lax.axis_size("tensor")
    tokens = residual_in.shape[0]
    side = (lax.axis_index("dp") // HIDDEN_BIT) % 2

    def halves(weight, axis):
        left, right = jnp.split(weight, 2, axis=axis)
        return jnp.where(side == 0, left, right), jnp.where(side == 0, right, left)

    info = jnp.stack([lengths[0], head_bucket[0], width_bucket[0]])
    far_info = dp_swap(info, HIDDEN_BIT)
    pair = [token_info(i[0], i[1], i[2], tokens) for i in (info, far_info)]
    segment, offset, head_tok, width_tok = [jnp.stack([a, b]) for a, b in zip(*pair)]
    matches = (
        width_bucket[0][:, None] == jnp.arange(bucket_total, dtype=jnp.int32)[None, :]
    ).astype(jnp.int32)
    bucket_counts = sum_all(jnp.sum(lengths[0][:, None] * matches, axis=0), ("dp",))
    head_mask = (head_tok.reshape(-1) >= tensor_index).astype(f32)[:, None]
    width_mask = (width_tok.reshape(-1) >= tensor_index).astype(f32)[:, None]
    places = jnp.arange(tokens, dtype=jnp.int32)
    allowed = (segment[:, :, None] == segment[:, None, :]) & (
        places[:, None] >= places[None, :]
    )
    cosine, sine_part = rotary_tables(offset.reshape(-1), HD)
    score_scale = HD ** (-0.5)

    qkv_halves = [h.reshape(h.shape[0], -1) for h in halves(w_qkv, 2)]
    full_qkv = lay_weight(gather_weight(*qkv_halves), 0)
    full_out = lay_weight(gather_weight(*halves(w_out, 0)), 1)
    full_up = lay_weight(gather_weight(*halves(w_up, 1)), 0)
    full_down = lay_weight(gather_weight(*halves(w_down, 0)), 1)

    inputs = whole_stream(residual_in)
    normed1, unit1, inverse1 = norm_forward(inputs, norm1_gain, norm1_shift)
    normed1 = normed1.astype(bf16)
    projected = dot(normed1, full_qkv).reshape(2 * tokens, 3, -1, HD)
    width = projected.shape[2] * HD
    query = rotate(projected[:, 0], cosine, sine_part).astype(bf16).reshape(-1, width)
    key = rotate(projected[:, 1], cosine, sine_part).astype(bf16).reshape(-1, width)
    value = projected[:, 2].astype(bf16).reshape(-1, width)
    query, key, value = heads_of(query, 2), heads_of(key, 2), heads_of(value, 2)
    allowed = jnp.tile(allowed, (query.shape[0] // 2, 1, 1))
    scores = jnp.einsum("nqd,nkd->nqk", query, key, preferred_element_type=f32) * score_scale
    scores = jnp.where(allowed, scores, -1000000000.0)
    scores = jnp.exp(scores - jnp.max(scores, axis=-1, keepdims=True))
    weights = (scores / jnp.sum(scores, axis=-1, keepdims=True)).astype(bf16)
    mixed = jnp.einsum("nqk,nkd->nqd", weights, value, preferred_element_type=f32)
    mixed = (rows_of(mixed, 2) * head_mask).astype(bf16)
    middle = residual_in + stream_sum(dot(mixed, full_out))
    middle_rows = whole_stream(middle)
    normed2, unit2, inverse2 = norm_forward(middle_rows, norm2_gain, norm2_shift)
    normed2 = normed2.astype(bf16)
    upper = jnp.maximum(dot(normed2, full_up), 0.0) * width_mask
    active = jnp.square(upper).astype(bf16)
    upper = upper.astype(bf16)
    output = middle + stream_sum(dot(active, full_down))

    grad_top = whole_stream(cotangent)
    grad_down = scatter_weight(cut_weight(dot(active.T, grad_top).astype(bf16), 1))
    grad_active = dot(grad_top, full_down.T)
    grad_upper = (grad_active * 2.0 * upper.astype(f32)).astype(bf16)
    grad_normed2 = dot(grad_upper, full_up.T)
    part_middle, gain2_grad, shift2_grad = norm_backward(
        grad_normed2, unit2, inverse2, norm2_gain
    )
    grad_middle = cotangent + stream_sum(part_middle)
    grad_up = scatter_weight(cut_weight(dot(normed2.T, grad_upper).astype(bf16), 0))
    grad_branch = whole_stream(grad_middle)
    grad_wout = scatter_weight(cut_weight(dot(mixed.T, grad_branch).astype(bf16), 1))
    grad_mixed = (dot(grad_branch, full_out.T) * head_mask).astype(bf16)
    grad_mixed = heads_of(grad_mixed, 2)
    grad_weights = jnp.einsum("nqd,nkd->nqk", grad_mixed, value, preferred_element_type=f32)
    grad_value = jnp.einsum("nqk,nqd->nkd", weights, grad_mixed, preferred_element_type=f32)
    wide = weights.astype(f32)
    grad_scores = wide * (grad_weights - jnp.sum(grad_weights * wide, axis=-1, keepdims=True))
    grad_raw = (grad_scores * score_scale).astype(bf16)
    grad_query = jnp.einsum("nqk,nkd->nqd", grad_raw, key, preferred_element_type=f32)
    grad_key = jnp.einsum("nqk,nqd->nkd", grad_raw, query, preferred_element_type=f32)
    grad_query, grad_key = [
        rotate(rows_of(g, 2).reshape(2 * tokens, -1, HD), cosine, -sine_part).reshape(-1, width)
        for g in (grad_query, grad_key)
    ]
    grad_projected = jnp.concatenate([grad_query, grad_key, rows_of(grad_value, 2)], axis=1)
    grad_projected = grad_projected.astype(bf16)
    grad_normed1 = dot(grad_projected, full_qkv.T)
    part_input, gain1_grad, shift1_grad = norm_backward(
        grad_normed1, unit1, inverse1, norm1_gain
    )
    grad_input = grad_middle + stream_sum(part_input)
    grad_qkv = scatter_weight(cut_weight(dot(normed1.T, grad_projected).astype(bf16), 0))

    def join(pair, axis):
        left = jnp.where(side == 0, pair[0], pair[1])
        right = jnp.where(side == 0, pair[1], pair[0])
        return jnp.concatenate([left, right], axis=axis).astype(f32)

    grad_qkv = join([g.reshape(g.shape[0], 3, width) for g in grad_qkv], 2)
    grad_wout, grad_up, grad_down = join(grad_wout, 0), join(grad_up, 1), join(grad_down, 0)
    gain2_grad, shift2_grad = sum_all(jnp.stack([gain2_grad, shift2_grad]), ("dp", "tensor"))
    gain1_grad, shift1_grad = sum_all(jnp.stack([gain1_grad, shift1_grad]), ("dp", "tensor"))
    return (
        output,
        grad_input,
        gain1_grad,
        shift1_grad,
        grad_qkv,
        grad_wout,
        gain2_grad,
        shift2_grad,
        grad_up,
        grad_down,
        bucket_counts,
    )


def flip(i, bit):
    return i + bit - 2 * bit * ((i // bit) % 2)


class Traffic:
    def __init__(self, send_sems, recv_sems):
        self.send_sems, self.recv_sems = send_sems, recv_sems
        self.copies, self.gone, self.come = {}, set(), set()

    def send(self, name, src, dst, device):
        k = len(self.copies)
        copy = pltpu.make_async_remote_copy(
            src_ref=src,
            dst_ref=dst,
            send_sem=self.send_sems.at[k],
            recv_sem=self.recv_sems.at[k],
            device_id=device,
            device_id_type=pl.DeviceIdType.MESH,
        )
        copy.start()
        self.copies[name] = copy

    def wait(self, *names):
        for name in names:
            if name not in self.come:
                self.copies[name].wait_recv()
                self.come.add(name)

    def sent(self, *names):
        for name in names:
            if name not in self.gone:
                self.copies[name].wait_send()
                self.gone.add(name)

    def finish(self):
        self.sent(*self.copies)


class Moves:
    def __init__(self, sems):
        self.sems, self.copies = sems, {}

    def start(self, name, src, dst):
        copy = pltpu.make_async_copy(src, dst, self.sems.at[len(self.copies)])
        copy.start()
        self.copies[name] = [copy, False]

    def wait(self, *names):
        for name in names:
            if not self.copies[name][1]:
                self.copies[name][0].wait()
                self.copies[name][1] = True

    def finish(self):
        self.wait(*self.copies)


class Place:
    def __init__(self):
        self.i, self.t = lax.axis_index("dp"), lax.axis_index("tensor")
        self.side = (self.i // 2 + self.i // 4) % 2
        self.x, self.z = [(flip(self.i, b), self.t) for b in (1, 2)]
        self.far = (self.block(6), self.t)
        self.c, self.y = [(self.i, flip(self.t, b)) for b in (1, 2)]

    def greet(self):
        barrier = pltpu.get_barrier_semaphore()
        partners = (self.x, self.z, self.far, self.c, self.y)
        for device in partners:
            pl.semaphore_signal(
                barrier, inc=1, device_id=device, device_id_type=pl.DeviceIdType.MESH
            )
        pl.semaphore_wait(barrier, len(partners))

    def block(self, m):
        d = self.i
        for bit in (1, 2, 4):
            if m & bit:
                d = flip(d, bit)
        return d

    def stripe(self, m):
        s = self.t
        for bit in (1, 2):
            if m & bit:
                s = flip(s, bit)
        return s


class WeightGather:
    def __init__(self, name, place, traffic, moves, half, slot):
        self.name, self.p, self.tr, self.mv = name, place, traffic, moves
        self.half, self.slot = half, slot

    def own(self):
        self.mv.start(self.name + "0", self.half(self.p.side), self.slot(self.p.i))

    def z(self):
        self.tr.send(self.name + "2", self.half(1 - self.p.side), self.slot(self.p.i), self.p.z)

    def far(self):
        self.tr.send(self.name + "6", self.half(self.p.side), self.slot(self.p.i), self.p.far)

    def x(self):
        self.tr.send(self.name + "1", self.half(self.p.side), self.slot(self.p.i), self.p.x)

    def far_next(self):
        self.tr.wait(self.name + "2")
        block = self.slot(self.p.block(2))
        self.tr.send(self.name + "4", block, block, self.p.far)

    def x_next(self, m):
        self.tr.wait(self.name + str(m))
        block = self.slot(self.p.block(m))
        self.tr.send(self.name + str(m + 1), block, block, self.p.x)

    def take(self, *which):
        for m in which:
            if m == 0:
                self.mv.wait(self.name + "0")
            else:
                self.tr.wait(self.name + str(m))

    def end(self):
        self.take(*range(8))


class ActGather:
    def __init__(self, name, place, traffic, slots):
        self.name, self.p, self.tr, self.slots = name, place, traffic, slots

    def at(self, b, m):
        return self.slots.at[b, self.p.stripe(m)]

    def z(self):
        self.tr.send(self.name + "10", self.at(0, 0), self.slots.at[1, self.p.t], self.p.z)

    def y(self):
        self.tr.send(self.name + "02", self.at(0, 0), self.at(0, 0), self.p.y)

    def c(self):
        self.tr.send(self.name + "01", self.at(0, 0), self.at(0, 0), self.p.c)

    def pass_z(self):
        self.tr.wait(self.name + "10")
        block = self.at(1, 0)
        self.tr.send(self.name + "12", block, block, self.p.y)
        self.tr.send(self.name + "11", block, block, self.p.c)

    def pass_y(self, b):
        self.tr.wait(self.name + str(b) + "2")
        block = self.at(b, 2)
        self.tr.send(self.name + str(b) + "3", block, block, self.p.c)

    def take(self, b):
        for m in range(1 - b, 4):
            self.tr.wait(self.name + str(b) + str(m))


def loop_rows(count, step, body):
    def run(k, carry):
        body(pl.multiple_of(k * step, step))
        return carry

    lax.fori_loop(0, count // step, run, 0)


def wide(value):
    return value.astype(jnp.float32)


def add_blocks(out, left, right, rows):
    def body(r):
        at = pl.ds(r, 64)
        out[at, :] = (wide(left[at, :]) + wide(right[at, :])).astype(out.dtype)

    loop_rows(rows, 64, body)


class ActScatter:
    def __init__(self, name, place, traffic, part, got_c, got_y, got_z):
        self.name, self.p, self.tr = name, place, traffic
        self.part, self.got_c, self.got_y, self.got_z = part, got_c, got_y, got_z
        self.rows = part.shape[2]

    def at(self, b, m):
        return self.part.at[b, self.p.stripe(m)]

    def c(self, b):
        for j, m in ((1, 3), (0, 1)):
            name = self.name + "c" + str(b) + str(j)
            self.tr.send(name, self.at(b, m), self.got_c.at[b, j], self.p.c)

    def add(self, b, m, name, got):
        self.tr.wait(self.name + name)
        add_blocks(self.at(b, m), self.at(b, m), got, self.rows)

    def y(self, b):
        self.add(b, 2, "c" + str(b) + "1", self.got_c.at[b, 1])
        self.tr.send(self.name + "y" + str(b), self.at(b, 2), self.got_y.at[b], self.p.y)

    def own(self, b):
        self.add(b, 0, "c" + str(b) + "0", self.got_c.at[b, 0])

    def z(self):
        self.add(1, 0, "y1", self.got_y.at[1])
        self.tr.send(self.name + "z", self.at(1, 0), self.got_z, self.p.z)

    def home(self):
        self.add(0, 0, "y0", self.got_y.at[0])

    def sent(self):
        for key in ("c11", "c01", "c10", "c00", "y1", "y0", "z"):
            self.tr.sent(self.name + key)

    def end(self, out, base):
        self.tr.wait(self.name + "z")
        own = self.at(0, 0)

        def body(r):
            at = pl.ds(r, 64)
            out[at, :] = base[at, :] + (wide(own[at, :]) + wide(self.got_z[at, :]))

        loop_rows(self.rows, 64, body)


def round_rows(src, dst, rows):
    def body(r):
        at = pl.ds(r, 64)
        dst[at, :] = src[at, :].astype(dst.dtype)

    loop_rows(rows, 64, body)


def dot_f32(left, right):
    return jnp.dot(left, right, preferred_element_type=jnp.float32)


def dot_nt(left, right):
    return lax.dot_general(
        left, right, (((1,), (1,)), ((), ())), preferred_element_type=jnp.float32
    )


def dot_tn(left, right):
    return lax.dot_general(
        left, right, (((0,), (0,)), ((), ())), preferred_element_type=jnp.float32
    )


def center_rows(slots, b, at):
    stripes = slots.shape[1]
    rows = jnp.concatenate([wide(slots[b, s, at, :]) for s in range(stripes)], axis=1)
    center = rows - jnp.mean(rows, axis=1, keepdims=True)
    spread = jnp.mean(center * center, axis=1, keepdims=True)
    return center, lax.rsqrt(spread + epsilon)


def norm_rows(slots, b, gain, shift, out):
    rows = slots.shape[2]

    def body(r):
        center, inverse = center_rows(slots, b, pl.ds(r, 128))
        out[pl.ds(b * rows + r, 128), :] = (center * inverse * gain[...] + shift[...]).astype(
            jnp.bfloat16
        )

    loop_rows(rows, 128, body)


def attend(b, qkv, seg_col, seg_row, head_mask, weights, mixed, scale):
    tokens = seg_row.shape[2]
    heads = qkv.shape[2] // HD
    half = tokens // 2
    start = b * tokens
    for h in range(heads):
        cols = pl.ds(h * HD, HD)
        for part in range(2):
            rows = pl.ds(start + part * half, half)
            reach = half * (part + 1)
            query = qkv[0, rows, cols]
            key = qkv[1, pl.ds(start, reach), cols]
            value = qkv[2, pl.ds(start, reach), cols]
            scores = dot_nt(query, key) * scale
            row_id = lax.broadcasted_iota(jnp.int32, (half, reach), 0) + part * half
            col_id = lax.broadcasted_iota(jnp.int32, (half, reach), 1)
            same = seg_col[rows, :] == seg_row[b, :, pl.ds(0, reach)]
            scores = jnp.where(same & (row_id >= col_id), scores, -1000000000.0)
            scores = jnp.exp(scores - jnp.max(scores, axis=1, keepdims=True))
            total = jnp.sum(scores, axis=1, keepdims=True)
            chosen = (scores / total).astype(jnp.bfloat16)
            weights[b * heads + h, pl.ds(part * half, half), pl.ds(0, reach)] = chosen
            mixed[rows, cols] = (dot_f32(chosen, value) * head_mask[rows, :]).astype(jnp.bfloat16)


def sequences(lengths):
    start = 0
    for s in range(lengths.shape[1]):
        length = lengths[0, s]
        yield s, start, length
        start = start + length


def count_row(lengths, width_bucket, lanes):
    lane = lax.broadcasted_iota(jnp.int32, (1, lanes), 1)
    row = jnp.zeros((1, lanes), jnp.float32)
    for s, _, length in sequences(lengths):
        row = row + jnp.where(lane == width_bucket[0, s], wide(length), 0.0)
    return row


def fill_facts(lengths, head_bucket, width_bucket, place_cosine, place_sine, facts):
    lanes = facts.shape[1]
    row = lax.broadcasted_iota(jnp.int32, (8, lanes), 0)
    lane = lax.broadcasted_iota(jnp.int32, (8, lanes), 1)
    count = lengths.shape[1]
    by_lane = jnp.where((row == 0) & (lane >= count), 1e9, 0.0)
    by_row = jnp.where(row >= count, 1e9, 0.0)
    for s, start, length in sequences(lengths):
        end = wide(start + length)
        here = lane == s
        by_lane = by_lane + jnp.where((row == 0) & here, end, 0.0)
        by_lane = by_lane + jnp.where((row == 2) & here, wide(head_bucket[0, s]), 0.0)
        by_lane = by_lane + jnp.where((row == 3) & here, wide(width_bucket[0, s]), 0.0)
        by_row = by_row + jnp.where(row == s, end, 0.0)
        facts[pl.ds(16 + s, 1), :] = place_cosine[pl.ds(start, 1), :]
        facts[pl.ds(20 + s, 1), :] = place_sine[pl.ds(start, 1), :]
    facts[pl.ds(0, 8), :] = by_lane
    facts[pl.ds(8, 8), :] = by_row


def fill_tables(
    infos, place_cosine, place_sine, t, cosine, sine, head_mask, width_mask, seg_col, seg_row
):
    tokens, lanes = place_cosine.shape
    own = wide(t)
    lane = wide(lax.broadcasted_iota(jnp.int32, (tokens, lanes), 1))
    place = wide(lax.broadcasted_iota(jnp.int32, (tokens, lanes), 0))
    sign = jnp.where(lane < lanes // 2, -1.0, 1.0)
    for b in range(2):
        rows = pl.ds(b * tokens, tokens)

        def row(k, b=b):
            return infos[b, pl.ds(k, 1), :]

        segment = jnp.sum(jnp.where(place >= row(0), 1.0, 0.0), axis=1, keepdims=True)
        seg_col[rows, :] = segment
        chosen = jnp.where(lane == segment, 1.0, 0.0)
        head = jnp.sum(chosen * row(2), axis=1, keepdims=True)
        width = jnp.sum(chosen * row(3), axis=1, keepdims=True)
        head_mask[rows, :] = jnp.where(head >= own, 1.0, 0.0)
        width_mask[rows, :] = jnp.where(width >= own, 1.0, 0.0)
        start_cosine, start_sine = 0.0, 0.0
        for s in range(4):
            here = jnp.where(segment == s, 1.0, 0.0)
            start_cosine = start_cosine + here * row(16 + s)
            start_sine = start_sine + here * row(20 + s)
        at_cosine, at_sine = place_cosine[...], place_sine[...]
        cosine[rows, :] = at_cosine * start_cosine + at_sine * start_sine
        sine[rows, :] = (at_sine * start_cosine - at_cosine * start_sine) * sign
        ends = infos[b, pl.ds(8, 8), pl.ds(0, 1)]
        across = wide(lax.broadcasted_iota(jnp.int32, (8, tokens), 1))
        seg_row[b] = jnp.sum(jnp.where(across >= ends, 1.0, 0.0), axis=0, keepdims=True)


def forward_kernel(
    residual_in,
    cotangent_in,
    gain1,
    shift1,
    gain2,
    shift2,
    lengths,
    head_bucket,
    width_bucket,
    place_cosine_in,
    place_sine_in,
    half_qkv,
    half_out,
    half_up,
    half_down,
    cosine_out,
    sine_out,
    head_mask_out,
    all_qkv,
    all_out,
    all_up,
    stream1,
    stream2,
    stream_c,
    normed1,
    normed2,
    heads_out,
    weights_out,
    mixed_out,
    active_out,
    grad_upper_out,
    part_out,
    middle_out,
    w_qkv,
    w_out,
    w_up,
    w_down,
    rows1,
    rows2,
    rows_c,
    normed,
    qkv,
    weights,
    mixed,
    part,
    got_c,
    got_y,
    got_z,
    upper,
    active,
    grad_active,
    middle,
    infos,
    seg_col,
    seg_row,
    width_mask,
    residual,
    cotangent,
    place_cosine,
    place_sine,
    cosine,
    sine,
    head_mask,
    send_sems,
    recv_sems,
    move_sems,
):
    p = Place()
    tr, mv = Traffic(send_sems, recv_sems), Moves(move_sems)
    tokens = residual.shape[0]
    rows_d = half_qkv.shape[1]
    head_cols = w_out.shape[1]

    def row_slot(ref):
        return lambda d: ref.at[pl.ds(pl.multiple_of(d * rows_d, rows_d), rows_d)]

    def first_slot(ref):
        return lambda d: ref.at[d]

    def at_side(k, cut, size):
        return pl.ds(pl.multiple_of(k * size + cut.start, 128), cut.size)

    hidden = w_up.shape[1]
    parts = [pl.ds(0, hidden // 2), pl.ds(hidden // 2, hidden // 2)]

    def rows_at(d):
        return pl.ds(pl.multiple_of(d * rows_d, rows_d), rows_d)

    def up_gather(name, cut):
        return WeightGather(
            name,
            p,
            tr,
            mv,
            lambda k: half_up.at[:, at_side(k, cut, hidden)],
            lambda d: w_up.at[rows_at(d), cut],
        )

    def down_gather(name, cut):
        return WeightGather(
            name,
            p,
            tr,
            mv,
            lambda k: half_down.at[at_side(k, cut, hidden), :],
            lambda d: w_down.at[d, cut, :],
        )

    heads_cut = pl.ds(0, head_cols)
    q = WeightGather(
        "q",
        p,
        tr,
        mv,
        lambda k: half_qkv.at[:, :, at_side(k, heads_cut, head_cols)],
        lambda d: w_qkv.at[:, rows_at(d), :],
    )
    o = WeightGather(
        "o",
        p,
        tr,
        mv,
        lambda k: half_out.at[at_side(k, heads_cut, head_cols), :],
        lambda d: w_out.at[d],
    )
    u, v = [up_gather(n, cut) for n, cut in zip("uv", parts)]
    d, e = [down_gather(n, cut) for n, cut in zip("de", parts)]
    a1 = ActGather("a", p, tr, rows1)
    a2 = ActGather("b", p, tr, rows2)
    ac = ActGather("c", p, tr, rows_c)
    s1 = ActScatter("s", p, tr, part, got_c, got_y, got_z)

    mv.start("residual", residual_in, residual)
    mv.start("place_cosine", place_cosine_in, place_cosine)
    mv.start("place_sine", place_sine_in, place_sine)
    mv.start("cotangent", cotangent_in, cotangent)
    p.greet()
    for one in (q, o, u, v, d, e):
        one.own()
    blocks = w_out.shape[0]
    stripes = part.shape[1]
    per = blocks // stripes
    started = []

    def project(b):
        def body(r):
            at = pl.ds(b * tokens + r, 512)
            for k in range(3):
                got = dot_f32(normed[at, :], w_qkv[k])
                for h in range(head_cols // HD):
                    cols = pl.ds(h * HD, HD)
                    one = got[:, h * HD : (h + 1) * HD]
                    if k < 2:
                        one = one * cosine[at, :] + pltpu.roll(one, HD // 2, 1) * sine[at, :]
                    qkv[k, at, cols] = one.astype(jnp.bfloat16)

        loop_rows(tokens, 512, body)

    def branch(b):
        at = pl.ds(b * tokens, tokens)

        def body(s, carry):
            for j in range(per):
                got = dot_f32(mixed[at, :], w_out[s * per + j])
                part[b, s, :, pl.ds(j * rows_d, rows_d)] = got.astype(jnp.bfloat16)
            return carry

        lax.fori_loop(0, stripes, body, 0)

    def rise(b, cut):
        def body(r):
            at = pl.ds(b * tokens + r, 512)
            for k in range(cut.size // 256):
                cols = pl.ds(cut.start + k * 256, 256)
                got = dot_f32(normed[at, :], w_up[:, cols])
                got = jnp.maximum(got, 0.0) * width_mask[at, :]
                upper[at, cols] = got.astype(jnp.bfloat16)
                active[at, cols] = (got * got).astype(jnp.bfloat16)

        loop_rows(tokens, 512, body)

    def fall(m):
        place = p.block(m)
        s = place // per
        cols = pl.ds(pl.multiple_of((place % per) * rows_d, rows_d), rows_d)
        first = not started
        started.append(m)

        def body(r):
            b, at = r // tokens, pl.ds(pl.multiple_of(r % tokens, 512), 512)
            rows = pl.ds(r, 512)
            part[b, s, at, cols] = dot_f32(active[rows, :], w_down[place]).astype(jnp.bfloat16)
            got = dot_nt(rows_c[b, s, at, cols], w_down[place])
            grad_active[rows, :] = got if first else grad_active[rows, :] + got

        loop_rows(2 * tokens, 512, body)
        for b in range(2):
            mv.start("part" + str(b) + str(m), part.at[b, s, :, cols], part_out.at[b, s, :, cols])

    def turn(r):
        at = pl.ds(r, 64)
        active[at, :] = (grad_active[at, :] * 2.0 * wide(upper[at, :])).astype(jnp.bfloat16)

    o.z()
    q.far()
    o.x()
    mv.wait("residual")
    round_rows(residual, rows1.at[0, p.t], tokens)
    a1.y()
    q.z()
    o.far_next()
    a1.z()
    e.x()
    q.x()
    mv.wait("place_cosine", "place_sine")
    fill_facts(lengths, head_bucket, width_bucket, place_cosine, place_sine, infos.at[0])
    tr.send("info", infos.at[0], infos.at[1], p.z)
    q.far_next()
    q.x_next(6)
    a1.c()
    v.z()
    a1.pass_y(0)
    o.far()
    o.x_next(2)
    o.x_next(4)
    e.z()
    a1.pass_z()
    q.x_next(2)
    q.x_next(4)
    u.far()
    a1.take(0)
    norm_rows(rows1, 0, gain1, shift1, normed)
    a1.pass_y(1)
    tr.wait("info")
    fill_tables(
        infos, place_cosine, place_sine, p.t, cosine, sine, head_mask, width_mask, seg_col, seg_row
    )
    mv.start("cosine", cosine, cosine_out)
    mv.start("sine", sine, sine_out)
    mv.start("head_mask", head_mask, head_mask_out)
    o.x_next(6)
    a1.take(1)
    norm_rows(rows1, 1, gain1, shift1, normed)
    mv.start("stream1", rows1, stream1)
    mv.start("normed1", normed, normed1)
    u.z()
    v.far()
    q.end()
    project(1)
    attend(
        1, qkv, seg_col, seg_row, head_mask, weights, mixed, HD ** (-0.5)
    )
    o.end()
    branch(1)
    s1.c(1)
    d.z()
    s1.y(1)
    e.x_next(2)
    project(0)
    mv.start("all_qkv", w_qkv, all_qkv)
    attend(
        0, qkv, seg_col, seg_row, head_mask, weights, mixed, HD ** (-0.5)
    )
    mv.start("heads", qkv, heads_out)
    mv.start("weights", weights, weights_out)
    mv.start("mixed", mixed, mixed_out)
    branch(0)
    mv.start("all_out", w_out, all_out)
    u.x()
    d.x()
    v.x_next(2)
    s1.c(0)
    v.far_next()
    s1.own(1)
    u.x_next(6)
    s1.y(0)
    s1.z()
    s1.own(0)
    mv.wait("cotangent")
    round_rows(cotangent, rows_c.at[0, p.t], tokens)
    v.x()
    u.far_next()
    ac.y()
    s1.home()
    s1.end(middle, residual)
    round_rows(middle, rows2.at[0, p.t], tokens)
    mv.start("middle", middle, middle_out)
    v.x_next(4)
    a2.z()
    u.x_next(2)
    v.x_next(6)
    ac.z()
    d.far_next()
    e.far()
    e.far_next()
    ac.c()
    a2.y()
    a2.c()
    a2.pass_y(0)
    u.x_next(4)
    a2.pass_z()
    d.x_next(2)
    ac.pass_y(0)
    d.far()
    a2.take(0)
    mv.wait("normed1")
    norm_rows(rows2, 0, gain2, shift2, normed)
    ac.pass_z()
    a2.pass_y(1)
    d.x_next(4)
    a2.take(1)
    norm_rows(rows2, 1, gain2, shift2, normed)
    mv.start("stream2", rows2, stream2)
    mv.start("normed2", normed, normed2)
    u.end()
    rise(1, parts[0])
    e.x_next(6)
    rise(0, parts[0])
    ac.pass_y(1)
    v.end()
    rise(1, parts[1])
    rise(0, parts[1])
    mv.start("active", active, active_out)
    mv.start("all_up", w_up, all_up)
    e.x_next(4)
    ac.take(0)
    ac.take(1)
    s1.sent()
    d.take(4)
    e.take(4)
    fall(4)
    mv.start("stream_c", rows_c, stream_c)
    d.take(2)
    e.take(2)
    fall(2)
    d.take(0)
    e.take(0)
    fall(0)
    d.x_next(6)
    d.take(6)
    e.take(6)
    fall(6)
    d.take(1)
    e.take(1)
    fall(1)
    d.take(5)
    e.take(5)
    fall(5)
    d.take(3)
    e.take(3)
    fall(3)
    d.take(7)
    e.take(7)
    fall(7)
    mv.wait("active")
    loop_rows(2 * tokens, 64, turn)
    mv.start("grad_upper", active, grad_upper_out)
    tr.finish()
    mv.finish()


def forward_call(arrays, weights):
    bf16, f32 = jnp.bfloat16, jnp.float32
    tokens, columns = arrays[0].shape
    w_qkv, w_out, w_up, w_down = weights
    count, stripes = lax.axis_size("dp"), lax.axis_size("tensor")
    rows_d = w_up.shape[0]
    head_cols = w_out.shape[0] // 2
    hidden = w_up.shape[1] // 2
    width = rows_d * count
    heads = head_cols // HD
    slots = (2, stripes, tokens, columns)
    tables = dict(
        cosine=((2 * tokens, HD), f32),
        sine=((2 * tokens, HD), f32),
        head_mask=((2 * tokens, 1), f32),
    )
    shapes = dict(
        all_qkv=((3, width, head_cols), bf16),
        all_out=((count, head_cols, rows_d), bf16),
        all_up=((width, hidden), bf16),
        stream1=(slots, bf16),
        stream2=(slots, bf16),
        stream_c=(slots, bf16),
        normed1=((2 * tokens, width), bf16),
        normed2=((2 * tokens, width), bf16),
        heads=((3, 2 * tokens, head_cols), bf16),
        weights=((2 * heads, tokens, tokens), bf16),
        mixed=((2 * tokens, head_cols), bf16),
        active=((2 * tokens, hidden), bf16),
        grad_upper=((2 * tokens, hidden), bf16),
        part_out=(slots, bf16),
        middle=((tokens, columns), f32),
    )

    def vmem(name):
        return pltpu.VMEM(*shapes[name])

    scratch = [
        vmem("all_qkv"),
        vmem("all_out"),
        vmem("all_up"),
        pltpu.VMEM((count, hidden, rows_d), bf16),
        vmem("stream1"),
        vmem("stream2"),
        vmem("stream_c"),
        vmem("normed1"),
        vmem("heads"),
        vmem("weights"),
        vmem("mixed"),
        pltpu.VMEM(slots, bf16),
        pltpu.VMEM((2, 2, tokens, columns), bf16),
        pltpu.VMEM((2, tokens, columns), bf16),
        pltpu.VMEM((tokens, columns), bf16),
        vmem("active"),
        vmem("active"),
        pltpu.VMEM((2 * tokens, hidden), f32),
        vmem("middle"),
        pltpu.VMEM((2, 24, 128), f32),
        pltpu.VMEM((2 * tokens, 1), f32),
        pltpu.VMEM((2, 1, tokens), f32),
        pltpu.VMEM((2 * tokens, 1), f32),
        vmem("middle"),
        vmem("middle"),
        pltpu.VMEM((tokens, HD), f32),
        pltpu.VMEM((tokens, HD), f32),
        *[pltpu.VMEM(*s) for s in tables.values()],
        pltpu.SemaphoreType.DMA((72,)),
        pltpu.SemaphoreType.DMA((72,)),
        pltpu.SemaphoreType.DMA((48,)),
    ]
    any_spec = pl.BlockSpec(memory_space=pl.ANY)
    vmem_spec = pl.BlockSpec(memory_space=pltpu.VMEM)
    smem_spec = pl.BlockSpec(memory_space=pltpu.SMEM)
    outs = pl.pallas_call(
        forward_kernel,
        out_shape=[jax.ShapeDtypeStruct(*s) for s in (tables | shapes).values()],
        in_specs=[any_spec] * 2 + [vmem_spec] * 4 + [smem_spec] * 3 + [any_spec] * 6,
        out_specs=[any_spec] * (len(tables) + len(shapes)),
        scratch_shapes=scratch,
        compiler_params=pltpu.CompilerParams(
            collective_id=0, has_side_effects=True, vmem_limit_bytes=62 << 20
        ),
    )(*arrays, *weights)
    split = len(tables)
    return outs[:split], dict(zip(shapes, outs[split:]))


class WeightScatter:
    def __init__(self, name, place, traffic, odd, even, got_x, got_far, out):
        self.name, self.p, self.tr = name, place, traffic
        self.odd, self.even, self.got_x, self.got_far, self.out = odd, even, got_x, got_far, out

    def send_x(self, m):
        self.tr.send(self.name + "x" + str(m), self.odd.at[m // 2], self.got_x.at[m // 2], self.p.x)

    def add_x(self, m):
        k, n = m // 2, self.name
        own = self.even.at[k]
        self.tr.wait(n + "x" + str(m + 1))
        add_blocks(own, own, self.got_x.at[k], own.shape[0])
        if m >= 4:
            self.tr.send(n + "f" + str(m), own, self.got_far.at[3 - k], self.p.far)

    def add_far(self, m):
        k, n = m // 2, self.name
        own = self.even.at[k]
        self.tr.wait(n + "f" + str(6 - m))
        add_blocks(own, own, self.got_far.at[k], own.shape[0])
        if m == 2:
            for j, (cut, spot) in enumerate(self.out(self.p.side)):
                self.tr.send(n + "z" + str(j), own.at[:, cut], spot, self.p.z)

    def end(self, moves):
        for j, (cut, spot) in enumerate(self.out(self.p.side)):
            moves.start(self.name + str(j), self.even.at[0, :, cut], spot)
            self.tr.wait(self.name + "z" + str(j))


class SumAll:
    def __init__(self, name, place, traffic, sums, got):
        self.name, self.tr, self.sums, self.got = name, traffic, sums, got
        self.partners = (place.c, place.y, place.x, place.z, place.far)

    def start(self, k):
        self.tr.send(self.name + str(k), self.sums, self.got.at[k], self.partners[k])

    def step(self, k):
        self.tr.wait(self.name + str(k))
        self.tr.sent(self.name + str(k))
        self.sums[...] += self.got[k]
        if k + 1 < len(self.partners):
            self.start(k + 1)


def norm_back(b, part, slots, gain, total, first):
    stripes, rows, columns = part.shape[1:]
    tile = 64
    fold = (tile // 8, 8, stripes * columns)

    def body(r):
        at = pl.ds(r, tile)
        value = wide(slots[at, :])
        center = value - jnp.mean(value, axis=1, keepdims=True)
        spread = jnp.mean(center * center, axis=1, keepdims=True)
        inverse = lax.rsqrt(spread + epsilon)
        unit = center * inverse
        grad = jnp.concatenate([wide(part[b, s, at, :]) for s in range(stripes)], axis=1)
        scaled = grad * gain[...]
        push = inverse * (
            scaled
            - jnp.mean(scaled, axis=1, keepdims=True)
            - unit * jnp.mean(scaled * unit, axis=1, keepdims=True)
        )
        for s in range(stripes):
            part[b, s, at, :] = push[:, s * columns : (s + 1) * columns].astype(jnp.bfloat16)
        total[0] += jnp.sum((grad * unit).reshape(fold), axis=0)
        total[1] += jnp.sum(grad.reshape(fold), axis=0)

    if first:
        total[...] = jnp.zeros_like(total)
    loop_rows(rows, tile, body)


def attend_back(b, qkv, weights, grad_mixed, cosine, sine, out, tokens, scale):
    width = grad_mixed.shape[1]
    heads = width // HD
    half = tokens // 2
    start = b * tokens

    def turn_back(grad, rows):
        return (grad * cosine[rows, :] - pltpu.roll(grad, HD // 2, 1) * sine[rows, :]).astype(
            jnp.bfloat16
        )

    for h in range(heads):
        spots = [pl.ds(k * width + h * HD, HD) for k in range(3)]
        grad_key, grad_value = None, None
        for part in (1, 0):
            rows = pl.ds(start + part * half, half)
            reach = pl.ds(start, half * (part + 1))
            query, key, value = qkv[rows, spots[0]], qkv[reach, spots[1]], qkv[reach, spots[2]]
            given = grad_mixed[rows, pl.ds(h * HD, HD)]
            chosen = weights[b * heads + h, pl.ds(part * half, half), pl.ds(0, half * (part + 1))]
            grad = dot_nt(given, value)
            soft = wide(chosen)
            grad = soft * (grad - jnp.sum(grad * soft, axis=1, keepdims=True))
            raw = (grad * scale).astype(jnp.bfloat16)
            out[rows, spots[0]] = turn_back(dot_f32(raw, key), rows)
            key_part, value_part = dot_tn(raw, query), dot_tn(chosen, given)
            if part == 1:
                grad_key, grad_value = key_part, value_part
        low, high = pl.ds(start, half), pl.ds(start + half, half)
        out[low, spots[1]] = turn_back(grad_key[:half] + key_part, low)
        out[high, spots[1]] = turn_back(grad_key[half:], high)
        out[low, spots[2]] = (grad_value[:half] + value_part).astype(jnp.bfloat16)
        out[high, spots[2]] = grad_value[half:].astype(jnp.bfloat16)


def backward_kernel(
    cotangent_in,
    gain1,
    gain2,
    cosine_in,
    sine_in,
    head_mask_in,
    lengths,
    width_bucket,
    all_qkv,
    all_out,
    all_up,
    stream1,
    stream2,
    stream_c,
    normed1,
    normed2,
    heads,
    weights_in,
    mixed_in,
    active_in,
    grad_upper_in,
    part_in,
    middle_in,
    output,
    grad_input,
    sums2_out,
    sums1_out,
    grad_qkv,
    grad_out,
    grad_up,
    grad_down,
    w_up,
    w_out,
    rows_a,
    rows_b,
    active,
    grad_upper,
    part_a,
    part_b,
    got_ca,
    got_ya,
    got_za,
    got_cb,
    got_yb,
    got_zb,
    stream_b,
    weights,
    mixed,
    grad_mixed,
    odd,
    even_down,
    even_up,
    odd_out,
    even_out,
    gx_down,
    gf_down,
    gx_up,
    gf_up,
    gx_qkv,
    gf_qkv,
    gx_out,
    gf_out,
    middle,
    grad_middle,
    total,
    sums2,
    got2,
    sums1,
    got1,
    cotangent,
    cosine,
    sine,
    head_mask,
    send_sems,
    recv_sems,
    move_sems,
):
    p = Place()
    tr, mv = Traffic(send_sems, recv_sems), Moves(move_sems)
    tokens, columns = cotangent.shape
    stripes, blocks = part_a.shape[1], all_out.shape[0]
    rows_d = all_out.shape[2]
    per = blocks // stripes
    head_cols = mixed.shape[1]
    bf16 = jnp.bfloat16

    def load_stream(name, src, dst):
        for b in range(2):
            for s in range(stripes):
                spot = dst.at[pl.ds(b * tokens, tokens), pl.ds(s * columns, columns)]
                mv.start(name + str(b) + str(s), src.at[b, s], spot)

    def wait_stream(name):
        mv.wait(*[name + str(b) + str(s) for b in range(2) for s in range(stripes)])

    s_out = ActScatter("s", p, tr, part_a, got_ca, got_ya, got_za)
    half = tokens // 2
    halves = [pl.ds(0, half), pl.ds(half, half)]

    def half_scatter(name, cut):
        views = part_b.at[:, :, cut], got_cb.at[:, :, cut], got_yb.at[:, cut], got_zb.at[cut]
        return ActScatter(name, p, tr, *views)

    s2a, s2b = [half_scatter(n, cut) for n, cut in zip("tT", halves)]
    s1a, s1b = [half_scatter(n, cut) for n, cut in zip("rR", halves)]
    aba, abb = [ActGather(n, p, tr, stream_b.at[:, :, cut]) for n, cut in zip("bB", halves)]
    begun = set()
    qkv_cols = pl.ds(0, 3 * head_cols)

    def back(layer, b, h, slots, gain):
        rows = pl.ds(b * tokens + h * half, half)
        first = layer not in begun
        begun.add(layer)
        norm_back(b, part_b.at[:, :, halves[h]], slots.at[rows], gain, total, first)

    hidden = active.shape[1]
    parts = [pl.ds(0, hidden // 2), pl.ds(hidden // 2, hidden // 2)]

    def at_side(k, cut, size):
        return pl.ds(pl.multiple_of(k * size + cut.start, 128), cut.size)

    def scatter(name, odd, even, got_x, got_far, out, cols):
        views = [ref.at[:, :, cols] for ref in (odd, even, got_x, got_far)]

        def spots(k):
            if len(out.shape) == 3:
                return [
                    (pl.ds(j * head_cols, head_cols), out.at[j, :, at_side(k, heads_cut, head_cols)])
                    for j in range(3)
                ]
            spot = out.at[:, at_side(k, cols, out.shape[1] // 2)]
            return [(pl.ds(0, cols.size), spot)]

        return WeightScatter(name, p, tr, *views, spots)

    heads_cut = pl.ds(0, head_cols)

    d, e = [
        scatter(n, odd, even_down, gx_down, gf_down, grad_down, cut) for n, cut in zip("de", parts)
    ]
    u, v = [scatter(n, odd, even_up, gx_up, gf_up, grad_up, cut) for n, cut in zip("uv", parts)]
    q = scatter("q", odd, even_down, gx_qkv, gf_qkv, grad_qkv, qkv_cols)
    o = scatter("o", odd_out, even_out, gx_out, gf_out, grad_out, pl.ds(0, head_cols))
    all2 = SumAll("2", p, tr, sums2, got2)
    all1 = SumAll("1", p, tr, sums1, got1)

    per = blocks // stripes

    def load_cotangent(j):
        stripe = p.block(5) // per
        for bit in (1, 2):
            if j & bit:
                stripe = flip(stripe, bit)
        cols = pl.ds(pl.multiple_of(stripe * columns, columns), columns)
        for b in range(2):
            spot = rows_a.at[pl.ds(b * tokens, tokens), cols]
            mv.start("c" + str(b) + str(j), stream_c.at[b, stripe], spot)

    load_cotangent(0)
    mv.start("active0", active_in.at[:, parts[0]], active.at[:, parts[0]])
    mv.start("active1", active_in.at[:, parts[1]], active.at[:, parts[1]])
    p.greet()
    for j in range(1, stripes):
        load_cotangent(j)
    mv.start("grad_upper", grad_upper_in, grad_upper)
    mv.start("all_up", all_up, w_up)
    load_stream("x2", stream2, rows_b)

    def load_rest():
        for k in range(blocks):
            mv.start("p" + str(k), all_out.at[k], w_out.at[:, pl.ds(k * rows_d, rows_d)])
        mv.start("cotangent", cotangent_in, cotangent)
        mv.start("head_mask", head_mask_in, head_mask)
        mv.start("cosine", cosine_in, cosine)
        mv.start("sine", sine_in, sine)
        mv.start("mixed", mixed_in, mixed)
        mv.start("weights", weights_in, weights)
        mv.start("part", part_in, part_a)
        mv.start("middle", middle_in, middle)

    def block_cols(m):
        return pl.ds(pl.multiple_of(p.block(m) * rows_d, rows_d), rows_d)

    def grad_block(left, right, m, spot, cols=None):
        value = right[...] if cols is None else right[:, cols]
        spot[...] = dot_tn(left[:, block_cols(m)], value).astype(bf16)

    def down_block(m, spot):
        grad_block(rows_a, active, m, spot)

    def product(b, left, right, cols):
        at = pl.ds(b * tokens, tokens)

        def body(s, carry):
            rows = pl.ds(pl.multiple_of(s * columns, columns), columns)
            part_b[b, s] = dot_nt(left[at, cols], right[rows, cols]).astype(bf16)
            return carry

        lax.fori_loop(0, stripes, body, 0)

    def gather_total(sums):
        depth, lanes = 8, total.shape[2] // 8
        sums[...] = jnp.zeros_like(sums)
        for k in range(2):
            row = jnp.sum(total[k], axis=0, keepdims=True)
            for r in range(depth):
                sums[pl.ds(r, 1), pl.ds(k * lanes, lanes)] = row[:, r * lanes : (r + 1) * lanes]
        sums[pl.ds(0, 1), pl.ds(2 * lanes, HD)] = count_row(lengths, width_bucket, HD)

    def unpack(sums, out):
        depth, lanes = 8, total.shape[2] // 8
        for k in range(2):
            for r in range(depth):
                spot = sums[pl.ds(r, 1), pl.ds(k * lanes, lanes)]
                out[pl.ds(k, 1), pl.ds(r * lanes, lanes)] = spot
        out[pl.ds(2, 1), pl.ds(0, HD)] = sums[pl.ds(0, 1), pl.ds(2 * lanes, HD)]

    def up_block(m, spot):
        grad_block(rows_a, grad_upper, m, spot)

    def up_odd(m):
        tr.sent("dx" + str(m), "ex" + str(m))
        up_block(m, odd.at[m // 2])
        u.send_x(m)
        v.send_x(m)

    def mix(b):
        mv.wait("head_mask", *["p" + str(k) for k in range(blocks)])
        at = pl.ds(b * tokens, tokens)
        got = None
        for s in range(stripes):
            one = dot_nt(stream_b[b, s], w_out[:, pl.ds(s * columns, columns)])
            got = one if got is None else got + one
        grad_mixed[at, :] = (got * head_mask[at, :]).astype(bf16)

    def out_block(m, spot):
        mv.wait("mixed")
        place = p.block(m)
        cols = pl.ds(pl.multiple_of((place % per) * rows_d, rows_d), rows_d)
        near = dot_tn(stream_b[0, place // per, :, cols], mixed[pl.ds(0, tokens), :])
        away = dot_tn(stream_b[1, place // per, :, cols], mixed[pl.ds(tokens, tokens), :])
        spot[...] = (near + away).astype(bf16)

    def qkv_block(m, spot):
        mv.wait("normed1")
        grad_block(rows_b, grad_upper, m, spot, qkv_cols)

    def qkv_odd(m):
        tr.sent("ux" + str(m), "vx" + str(m))
        qkv_block(m, odd.at[m // 2, :, qkv_cols])
        q.send_x(m)

    def qkv_even(m):
        mv.wait("d0", "e0")
        tr.sent("df4", "df6", "dz0", "ef4", "ef6", "ez0")
        qkv_block(m, even_down.at[m // 2, :, qkv_cols])

    mv.wait("c00", "c10", "active0", "active1")
    down_block(5, odd.at[2])
    d.send_x(5)
    e.send_x(5)
    wait_stream("c")
    down_block(4, even_down.at[2])
    mv.wait("grad_upper", "all_up")
    product(1, grad_upper, w_up, pl.ds(0, w_up.shape[1]))
    wait_stream("x2")
    back(2, 1, 1, rows_b, gain2)
    d.add_x(4)
    s2b.c(1)
    back(2, 1, 0, rows_b, gain2)
    load_rest()
    down_block(7, odd.at[3])
    d.send_x(7)
    e.send_x(7)
    s2b.y(1)
    down_block(6, even_down.at[3])
    down_block(3, odd.at[1])
    d.send_x(3)
    e.send_x(3)
    s2a.c(1)
    s2b.own(1)
    e.add_x(4)
    product(0, grad_upper, w_up, pl.ds(0, w_up.shape[1]))
    d.add_x(6)
    s2a.y(1)
    mv.wait("part")
    down_block(2, even_down.at[1])
    back(2, 0, 1, rows_b, gain2)
    s_out.c(0)
    down_block(0, even_down.at[0])
    s2b.c(0)
    s2b.z()
    s2a.own(1)
    back(2, 0, 0, rows_b, gain2)
    down_block(1, odd.at[0])
    d.send_x(1)
    e.send_x(1)
    for k in range(3):
        mv.start("h" + str(k), heads.at[k], active.at[:, pl.ds(k * head_cols, head_cols)])
    mv.start("normed2", normed2, rows_a)
    s2a.c(0)
    mv.wait("normed2")
    e.add_x(6)
    s2b.y(0)
    s2b.own(0)
    s2a.z()
    gather_total(sums2)
    all2.start(0)
    s2b.home()
    s2a.own(0)
    d.add_x(2)
    up_block(4, even_up.at[2])
    s_out.c(1)
    mv.wait("cotangent")
    s2b.end(grad_middle.at[halves[1]], cotangent.at[halves[1]])
    round_rows(grad_middle.at[halves[1]], stream_b.at[0, p.t, halves[1]], tokens // 2)
    up_odd(5)
    s2a.y(0)
    up_block(6, even_up.at[3])
    abb.z()
    abb.y()
    up_block(2, even_up.at[1])
    d.add_x(0)
    up_odd(7)
    s_out.own(0)
    s2a.home()
    e.add_x(2)
    s2a.end(grad_middle.at[halves[0]], cotangent.at[halves[0]])
    round_rows(grad_middle.at[halves[0]], stream_b.at[0, p.t, halves[0]], tokens // 2)
    aba.z()
    aba.y()
    abb.pass_z()
    e.add_far(2)
    aba.pass_z()
    up_odd(3)
    abb.c()
    abb.pass_y(0)
    aba.pass_y(0)
    d.add_far(2)
    aba.c()
    e.add_x(0)
    u.add_x(4)
    aba.take(0)
    abb.take(0)
    mix(0)
    s_out.own(1)
    aba.pass_y(1)
    abb.pass_y(1)
    v.add_x(4)
    up_block(0, even_up.at[0])
    up_odd(1)
    aba.take(1)
    abb.take(1)
    out_block(4, even_out.at[2])
    s_out.y(1)
    mix(1)
    out_block(5, odd_out.at[2])
    o.send_x(5)
    out_block(2, even_out.at[1])
    v.add_x(6)
    mv.wait("cosine", "sine", "weights", "h0", "h1", "h2")
    attend_back(
        1, active, weights, grad_mixed, cosine, sine, grad_upper, tokens, HD ** (-0.5)
    )
    out_block(7, odd_out.at[3])
    o.send_x(7)
    out_block(0, even_out.at[0])
    out_block(6, even_out.at[3])
    u.add_x(6)
    attend_back(
        0, active, weights, grad_mixed, cosine, sine, grad_upper, tokens, HD ** (-0.5)
    )
    all2.step(0)
    for k in range(3):
        mv.start("w" + str(k), all_qkv.at[k], w_up.at[:, pl.ds(k * head_cols, head_cols)])
    mv.start("normed1", normed1, rows_b)
    d.add_far(0)
    s2a.sent()
    s2b.sent()
    mv.wait("w0", "w1", "w2")
    product(0, grad_upper, w_up, qkv_cols)
    out_block(3, odd_out.at[1])
    o.send_x(3)
    s_out.z()
    product(1, grad_upper, w_up, qkv_cols)
    u.add_x(0)
    u.add_x(2)
    v.add_x(2)
    load_stream("x1", stream1, rows_a)
    u.add_far(2)
    all2.step(1)
    s_out.y(0)
    wait_stream("x1")
    back(1, 0, 1, rows_a, gain1)
    e.add_far(0)
    back(1, 1, 0, rows_a, gain1)
    back(1, 1, 1, rows_a, gain1)
    back(1, 0, 0, rows_a, gain1)
    o.add_x(4)
    o.add_x(6)
    qkv_odd(5)
    o.add_x(2)
    e.end(mv)
    out_block(1, odd_out.at[0])
    o.send_x(1)
    s1a.c(1)
    d.end(mv)
    s1b.c(1)
    s1a.c(0)
    s1b.c(0)
    gather_total(sums1)
    all1.start(0)
    all1.step(0)
    qkv_odd(7)
    v.add_x(0)
    s1a.own(1)
    all2.step(2)
    qkv_even(4)
    s1a.y(1)
    qkv_even(2)
    v.add_far(2)
    s1b.y(1)
    s1a.own(0)
    qkv_odd(3)
    all1.step(1)
    q.add_x(4)
    qkv_odd(1)
    o.add_far(2)
    s1b.own(1)
    o.add_x(0)
    s_out.home()
    s1a.z()
    all2.step(3)
    o.add_far(0)
    qkv_even(0)
    qkv_even(6)
    q.add_x(6)
    all1.step(2)
    s1a.y(0)
    u.add_far(0)
    s1b.y(0)
    s1a.home()
    s1a.end(grad_middle.at[halves[0]], grad_middle.at[halves[0]])
    s1b.z()
    q.add_x(0)
    u.end(mv)
    v.add_far(0)
    v.end(mv)
    q.add_x(2)
    o.end(mv)
    s1b.own(0)
    s1b.home()
    mv.wait("middle")
    s_out.end(middle, middle)
    mv.start("output", middle, output)
    all1.step(3)
    q.add_far(2)
    all2.step(4)
    q.add_far(0)
    s1b.end(grad_middle.at[halves[1]], grad_middle.at[halves[1]])
    mv.start("grad_input", grad_middle, grad_input)
    all1.step(4)
    q.end(mv)
    unpack(sums2, sums2_out)
    unpack(sums1, sums1_out)
    tr.finish()
    mv.finish()


def backward_call(arrays, saved):
    bf16, f32 = jnp.bfloat16, jnp.float32
    tokens, columns = arrays[0].shape
    count, stripes = lax.axis_size("dp"), lax.axis_size("tensor")
    _, head_cols, rows_d = saved["all_out"].shape
    width, hidden = saved["all_up"].shape
    slots = (2, stripes, tokens, columns)
    wide_rows = (2 * tokens, width)

    def vmem(*shape, dtype=bf16):
        return pltpu.VMEM(shape, dtype)

    def got(cols):
        return [vmem(4, rows_d, cols), vmem(2, rows_d, cols)]

    got_act = [vmem(2, 2, tokens, columns), vmem(2, tokens, columns), vmem(tokens, columns)]
    packed = 2 * width // 8 + HD
    sums = [vmem(8, packed, dtype=f32), vmem(5, 8, packed, dtype=f32)]
    qkv = 3 * head_cols
    scratch = [
        vmem(width, hidden),
        vmem(head_cols, width),
        vmem(*wide_rows),
        vmem(*wide_rows),
        vmem(2 * tokens, hidden),
        vmem(2 * tokens, hidden),
        vmem(*slots),
        vmem(*slots),
        *got_act,
        *got_act,
        vmem(*slots),
        vmem(*saved["weights"].shape),
        vmem(2 * tokens, head_cols),
        vmem(2 * tokens, head_cols),
        vmem(4, rows_d, hidden),
        vmem(4, rows_d, hidden),
        vmem(4, rows_d, hidden),
        vmem(4, rows_d, head_cols),
        vmem(4, rows_d, head_cols),
        *got(hidden),
        *got(hidden),
        *got(qkv),
        *got(head_cols),
        vmem(tokens, columns, dtype=f32),
        vmem(tokens, columns, dtype=f32),
        vmem(2, 8, width, dtype=f32),
        *sums,
        *sums,
        *[vmem(*arrays[k].shape, dtype=f32) for k in (0, 3, 4, 5)],
        pltpu.SemaphoreType.DMA((112,)),
        pltpu.SemaphoreType.DMA((112,)),
        pltpu.SemaphoreType.DMA((80,)),
    ]
    any_spec = pl.BlockSpec(memory_space=pl.ANY)
    vmem_spec = pl.BlockSpec(memory_space=pltpu.VMEM)
    smem_spec = pl.BlockSpec(memory_space=pltpu.SMEM)
    shapes = [
        ((tokens, columns), f32),
        ((tokens, columns), f32),
        ((8, width), f32),
        ((8, width), f32),
        ((3, rows_d, 2 * head_cols), bf16),
        ((rows_d, 2 * head_cols), bf16),
        ((rows_d, 2 * hidden), bf16),
        ((rows_d, 2 * hidden), bf16),
    ]
    names = [k for k in saved]
    return pl.pallas_call(
        backward_kernel,
        out_shape=[jax.ShapeDtypeStruct(*s) for s in shapes],
        in_specs=[any_spec, vmem_spec, vmem_spec] + [any_spec] * 3
        + [smem_spec] * 2
        + [any_spec] * len(names),
        out_specs=[any_spec] * 2 + [vmem_spec] * 2 + [any_spec] * 4,
        scratch_shapes=scratch,
        compiler_params=pltpu.CompilerParams(
            collective_id=1, has_side_effects=True, vmem_limit_bytes=63 << 20
        ),
    )(*arrays, *[saved[n] for n in names])


def finish_kernel(groups, *refs):
    ins, sums, outs, small = refs[:6], refs[6:8], refs[8:14], refs[14:19]
    raw, done, sems = refs[19:25], refs[25:29], refs[29]
    loads = [pltpu.make_async_copy(ins[k], raw[k], sems.at[k]) for k in range(6)]
    for k in (0, 4, 5, 1, 2, 3):
        loads[k].start()
    for k in range(4):
        small[k][...] = sums[k // 2][pl.ds(k % 2, 1), :]
    count = small[4].shape[1]
    small[4][...] = (sums[1][pl.ds(2, 1), pl.ds(0, count)] / groups).astype(jnp.int32)
    stores = []

    def store(k, src):
        stores.append(pltpu.make_async_copy(src, outs[k], sems.at[6 + k]))
        stores[-1].start()

    loads[0].wait()
    rows, columns = raw[0].shape

    def widen(r):
        done[0][pl.ds(r, 32), :] = wide(raw[0][pl.ds(r, 32), :])

    loop_rows(rows, 32, widen)
    store(0, done[0])
    for k in (4, 5):
        loads[k].wait()
        store(k, raw[k])
    loads[1].wait()

    def turn(src, dst):
        def body(c):
            dst[pl.ds(c, 256), :] = wide(src[:, pl.ds(c, 256)]).T

        loop_rows(src.shape[1], 256, body)

    turn(raw[1], done[1])
    store(1, done[1])
    loads[2].wait()
    for k in range(raw[2].shape[0]):

        def widen_part(r, k=k):
            done[2][k, pl.ds(r, 64), :] = wide(raw[2][k, pl.ds(r, 64), :])

        loop_rows(raw[2].shape[1], 64, widen_part)
    store(2, done[2])
    loads[3].wait()
    turn(raw[3], done[3])
    store(3, done[3])
    for one in stores:
        one.wait()


def finish_call(grad_up, grad_down, grad_qkv, grad_out, output, grad_input, sums1, sums2):
    f32 = jnp.float32
    ins = (grad_up, grad_down, grad_qkv, grad_out, output, grad_input)
    shapes = [a.shape for a in ins]
    shapes[1], shapes[3] = shapes[1][::-1], shapes[3][::-1]
    any_spec = pl.BlockSpec(memory_space=pl.ANY)
    vmem_spec = pl.BlockSpec(memory_space=pltpu.VMEM)
    groups = lax.axis_size("tensor")
    return pl.pallas_call(
        functools.partial(finish_kernel, groups),
        out_shape=[jax.ShapeDtypeStruct(s, f32) for s in shapes]
        + [jax.ShapeDtypeStruct((1, sums1.shape[1]), f32)] * 4
        + [jax.ShapeDtypeStruct((1, groups), jnp.int32)],
        in_specs=[any_spec] * 6 + [vmem_spec] * 2,
        out_specs=[any_spec] * 6 + [vmem_spec] * 5,
        scratch_shapes=[pltpu.VMEM(a.shape, a.dtype) for a in ins]
        + [pltpu.VMEM(s, f32) for s in shapes[:4]]
        + [pltpu.SemaphoreType.DMA((12,))],
        compiler_params=pltpu.CompilerParams(vmem_limit_bytes=62 << 20),
    )(*ins, sums1, sums2)


def local_fast(
    residual_in,
    lengths,
    head_bucket,
    width_bucket,
    norm1_gain,
    norm1_shift,
    w_qkv,
    w_out,
    norm2_gain,
    norm2_shift,
    w_up,
    w_down,
    cotangent,
):
    f32 = jnp.float32
    tokens = residual_in.shape[0]
    steps = np.arange(tokens)[:, None] * 10000.0 ** (-2.0 * (np.arange(HD) % (HD // 2)) / HD)
    arrays = (
        residual_in,
        cotangent,
        norm1_gain[None],
        norm1_shift[None],
        norm2_gain[None],
        norm2_shift[None],
        lengths,
        head_bucket,
        width_bucket,
        jnp.asarray(np.cos(steps), f32),
        jnp.asarray(np.sin(steps), f32),
    )
    weights = (jnp.swapaxes(w_qkv, 0, 1), w_out, w_up, w_down)
    (cosine, sine, head_mask), saved = forward_call(arrays, weights)
    arrays = (cotangent, norm1_gain[None], norm2_gain[None], cosine, sine, head_mask)
    output, grad_input, sums2, sums1, grad_qkv, grad_out, grad_up, grad_down = backward_call(
        (*arrays, lengths, width_bucket), saved
    )
    grad_up, grad_down, grad_qkv, grad_out, output, grad_input, *small = finish_call(
        grad_up, grad_down, grad_qkv, grad_out, output, grad_input, sums1, sums2
    )
    gain1_grad, shift1_grad, gain2_grad, shift2_grad, bucket_counts = [one[0] for one in small]
    return (
        output,
        grad_input,
        gain1_grad,
        shift1_grad,
        jnp.swapaxes(grad_qkv, 0, 1),
        grad_out,
        gain2_grad,
        shift2_grad,
        grad_up,
        grad_down,
        bucket_counts,
    )


def local(*args):
    w_out = args[7]
    if lax.axis_size("dp") == 8 and lax.axis_size("tensor") == 4 and w_out.shape[1] % 128 == 0:
        return local_fast(*args)
    return local_general(*args)


def solution(mesh):
    placed = (
        P("dp", "tensor"),
        P("dp", None),
        P("dp", None),
        P("dp", None),
        P(),
        P(),
        P("dp", None, "tensor"),
        P("tensor", "dp"),
        P(),
        P(),
        P("dp", "tensor"),
        P("tensor", "dp"),
        P("dp", "tensor"),
    )
    return jax.shard_map(
        local,
        mesh=mesh,
        in_specs=placed,
        out_specs=(
            P("dp", "tensor"),
            P("dp", "tensor"),
            P(),
            P(),
            P("dp", None, "tensor"),
            P("tensor", "dp"),
            P(),
            P(),
            P("dp", "tensor"),
            P("tensor", "dp"),
            P(),
        ),
        check_vma=False,
    )
```
